32 devices in a mesh: dp: 8 (over y, x, core), rep: 4 (over z).
Axes of the slice: x: 2, y: 2, z: 4, core: 2. Of those that a mesh axis runs over, the one named last changes fastest.
Arguments:
- inputs: bfloat16 [2, 4, 2048, 1024], P(None, 'rep', 'dp'), may hold values from -6 to 6
- skips: bfloat16 [2, 4, 2048, 1024], P(None, 'rep', 'dp'), may hold values from -6 to 6
- cotangent: bfloat16 [2, 4, 2048, 1024], P(None, 'rep', 'dp'), may hold values from -6 to 6
- dest_slot: int32 [2, 4, 256], P(None, 'rep', 'dp'), may hold values from 0 to 255, as said below
- pack_segments: int32 [2, 4, 2048], P(None, 'rep', 'dp'), may hold values from 0 to 15, as said below
- block_live: int32 [2, 4, 256], P(None, 'rep', 'dp'), may hold values from 4 to 8
- counts: int32 [8, 4], P('dp', 'rep'), may hold values from 64 to 208
- w_skip: bfloat16 [2048, 1024], P('rep'), may hold values from -0.125 to 0.125
- b_skip: float32 [1024], replicated, may hold values from -3 to 3
- g_one: float32 [1024], replicated, may hold values from 0.1 to 1.9
- b_one: float32 [1024], replicated, may hold values from -3 to 3
- w_qkv: bfloat16 [1024, 3072], P('rep'), may hold values from -0.25 to 0.25
- w_out: bfloat16 [1024, 1024], P('rep'), may hold values from -0.75 to 0.75
- b_out: float32 [1024], replicated, may hold values from -3 to 3
- g_two: float32 [1024], replicated, may hold values from 0.1 to 1.9
- b_two: float32 [1024], replicated, may hold values from -3 to 3
- w_up: bfloat16 [1024, 4096], P('rep'), may hold values from -0.1875 to 0.1875
- c_up: float32 [4096], replicated, may hold values from -3 to 3
- w_down: bfloat16 [4096, 1024], P('rep'), may hold values from -0.09375 to 0.09375
- c_down: float32 [1024], replicated, may hold values from -3 to 3
Outputs:
- output: bfloat16 [2, 4, 2048, 1024], P(None, 'rep', 'dp')
- input_grad: bfloat16 [2, 4, 2048, 1024], P(None, 'rep', 'dp')
- skip_grad: bfloat16 [2, 4, 2048, 1024], P(None, 'rep', 'dp')
- grad_w_skip: float32 [2048, 1024], P('dp')
- grad_b_skip: float32 [1024], replicated
- grad_g_one: float32 [1024], replicated
- grad_b_one: float32 [1024], replicated
- grad_w_qkv: float32 [1024, 3072], P('dp')
- grad_w_out: float32 [1024, 1024], P('dp')
- grad_b_out: float32 [1024], replicated
- grad_g_two: float32 [1024], replicated
- grad_b_two: float32 [1024], replicated
- grad_w_up: float32 [1024, 4096], P('dp')
- grad_c_up: float32 [4096], replicated
- grad_w_down: float32 [4096, 1024], P('dp')
- grad_c_down: float32 [1024], replicated
The draws below stay inside these ranges and needn't reach their ends.
Inputs may be any that keep to these rules, and one draw needn't show every extreme that they name: `dest_slot`: for each micro-batch and replica, each slot is named by exactly one block; of one device's 32 blocks, the same number name slots of each device's range d * 32 to d * 32 + 31. `pack_segments`: within the 256 frames of one pack, ids never fall and start at 0; in every draw some pack holds a single utterance, and some pack reaches the largest id.
All inputs are finite; a program needn't handle non-finite values.
Results may differ from the reference program's by a relative error of at most 0.02.
Values may be sent and summed in bfloat16 or wider, within the bound.
No kernel may reach another device: no remote copies, remote signals or barrier semaphores. Data moves between devices by JAX's collectives and lax.ppermute only.
A program may use at most 256 MiB of HBM per device.

```python
import jax
import jax.numpy as jnp
from jax import lax

D = 1024
HEADS = 16
FF = 4096
HEAD = 64
BLK = 8
MB = 2
OWN = 32
OWNERS = 8
GROUPS = 4
SLOTS = 256
FRAMES = 2048


def draw_dest_slot(key, part):
    key = jax.random.fold_in(key, 11)
    first_key, second_key = jax.random.split(key)
    per_pair = OWN // OWNERS
    batches = MB * GROUPS * OWNERS
    sigma = jax.vmap(lambda single: jax.random.permutation(single, OWN))(jax.random.split(first_key, batches))
    sigma = sigma.reshape(MB, GROUPS, OWNERS, OWN).astype(jnp.int32)
    arrival_order = jax.vmap(lambda single: jax.random.permutation(single, OWN))(jax.random.split(second_key, batches))
    arrival_order = arrival_order.reshape(MB, GROUPS, OWNERS * OWN).astype(jnp.int32)
    target = sigma // per_pair
    within = sigma % per_pair
    source = jnp.arange(OWNERS, dtype=jnp.int32)[None, None, :, None]
    arrival = source * per_pair + within
    index = (target * OWN + arrival).reshape(MB, GROUPS, OWNERS * OWN)
    placed = jnp.take_along_axis(arrival_order, index, axis=2).reshape(MB, GROUPS, OWNERS, OWN)
    slot_value = target * OWN + placed
    return slot_value.reshape(MB, GROUPS, SLOTS).astype(jnp.int32)


def draw_pack_segments(key, part):
    key = jax.random.fold_in(key, 23)
    first_key, second_key = jax.random.split(key)
    pack_frames = OWN * BLK
    top_id = pack_frames // 16 - 1
    flags = (jax.random.randint(first_key, (MB, GROUPS, OWNERS, pack_frames), 0, 48) == 0).astype(jnp.int32)
    flags = flags.at[:, :, :, 0].set(0)
    chosen = jax.random.randint(second_key, (), 0, OWNERS)
    other = (chosen + 1) % OWNERS
    first_cell = (jnp.arange(MB) == 0)[:, None, None, None] & (jnp.arange(GROUPS) == 0)[None, :, None, None]
    single = (jnp.arange(OWNERS) == chosen)[None, None, :, None] & first_cell
    regular = (jnp.arange(OWNERS) == other)[None, None, :, None] & first_cell
    frame_index = jnp.arange(pack_frames, dtype=jnp.int32)
    regular_flags = ((frame_index % 16 == 0) & (frame_index > 0)).astype(jnp.int32)[None, None, None, :]
    flags = jnp.where(single, 0, flags)
    flags = jnp.where(regular, regular_flags, flags)
    ids = jnp.minimum(jnp.cumsum(flags, axis=3), top_id)
    return ids.reshape(MB, GROUPS, FRAMES).astype(jnp.int32)


def draw_counts(key, part):
    key = jax.random.fold_in(key, 37)
    device_total = OWNERS * GROUPS
    flat = jnp.arange(device_total, dtype=jnp.int32)
    jitter = jax.random.randint(key, (device_total,), 0, 17)
    jitter = jnp.where(flat == 0, 0, jnp.where(flat == device_total - 1, 16, jitter))
    value = 64 + 128 * flat // max(device_total - 1, 1) + jitter
    return value.reshape(OWNERS, GROUPS).astype(jnp.int32)


def place_ends(drawn, stream_key, smallest, top_value):
    longest = drawn.shape.index(max(drawn.shape))
    spots = []
    for shift in (0, 1):
        where = [jax.random.randint(jax.random.fold_in(stream_key, axis), (), 0, length) for axis, length in enumerate(drawn.shape)]
        where[longest] = (where[longest] + shift) % drawn.shape[longest]
        spots.append(tuple(where))
    return drawn.at[spots[0]].set(smallest).at[spots[1]].set(top_value)


def level_of(rng, dims, pieces, least, high):
    def one(axis_at, blocks):
        heights = jax.random.uniform(jax.random.fold_in(jax.random.fold_in(rng, 6), axis_at), (blocks,), jnp.float32, least / len(pieces), high / len(pieces))
        return jnp.repeat(jnp.exp(heights), dims[axis_at] // blocks).reshape((-1,) + (1,) * (len(dims) - axis_at - 1))

    loudness = one(*pieces[0])
    for cut in pieces[1:]:
        loudness = loudness * one(*cut)
    return loudness


def bell_draw(key, dims, scale, limit, pieces=(), kind=jnp.bfloat16):
    array = jax.random.normal(key, dims, jnp.float32) * scale
    if len(pieces) > 0:
        array = level_of(key, dims, pieces, -0.22, 0.18) * array
    return jnp.clip(array, min=-limit, max=limit).astype(kind)


def setup_inputs(seed: int = 0) -> dict:
    key_list = jax.random.split(jax.random.key(seed), 21)
    return {
        "inputs": bell_draw(key_list[0], (MB, GROUPS, FRAMES, D), 1.0, 6.0, ((1, 4), (2, 8))),
        "skips": bell_draw(key_list[1], (MB, GROUPS, FRAMES, D), 1.0, 6.0, ((1, 4), (2, 8))),
        "cotangent": bell_draw(key_list[2], (MB, GROUPS, FRAMES, D), 1.0, 6.0, ((1, 4), (2, 8))),
        "dest_slot": draw_dest_slot(jax.random.fold_in(key_list[20], 71), 0),
        "pack_segments": draw_pack_segments(jax.random.fold_in(key_list[20], 71), 0),
        "block_live": place_ends(jax.random.randint(key_list[5], (MB, GROUPS, SLOTS), BLK // 2, BLK + 1), jax.random.fold_in(key_list[5], 1), BLK // 2, BLK).astype(jnp.int32),
        "counts": draw_counts(jax.random.fold_in(key_list[20], 71), 0),
        "w_skip": bell_draw(key_list[7], (2 * D, D), (2 * D) ** -0.5, 0.125, ((0, 4),)),
        "b_skip": bell_draw(key_list[8], (D,), 0.5, 3.0, (), jnp.float32),
        "g_one": jnp.clip(1.0 + 0.18 * jax.random.normal(key_list[9], (D,), jnp.float32), 0.1, 1.9),
        "b_one": bell_draw(key_list[10], (D,), 0.5, 3.0, (), jnp.float32),
        "w_qkv": bell_draw(key_list[11], (D, 3 * D), (D // 2) ** -0.5, 0.25, ((0, 4),)),
        "w_out": bell_draw(key_list[12], (D, D), (D // 16) ** -0.5, 0.75, ((0, 4),)),
        "b_out": bell_draw(key_list[13], (D,), 0.5, 3.0, (), jnp.float32),
        "g_two": jnp.clip(1.0 + 0.18 * jax.random.normal(key_list[14], (D,), jnp.float32), 0.1, 1.9),
        "b_two": bell_draw(key_list[15], (D,), 0.5, 3.0, (), jnp.float32),
        "w_up": bell_draw(key_list[16], (D, FF), D ** -0.5, 0.1875, ((0, 4),)),
        "c_up": bell_draw(key_list[17], (FF,), 0.5, 3.0, (), jnp.float32),
        "w_down": bell_draw(key_list[18], (FF, D), FF ** -0.5, 0.09375, ((0, 4),)),
        "c_down": bell_draw(key_list[19], (D,), 0.5, 3.0, (), jnp.float32),
    }


@jax.custom_vjp
def low(v):
    return lax.optimization_barrier(v.astype(jnp.bfloat16)).astype(jnp.float32)

@jax.custom_vjp
def low_back(v):
    return v

def low_keep(v):
    return (low(v), None)

def low_pass(kept, grad):
    return (grad,)

def back_keep(v):
    return (v, None)

def back_low(kept, grad):
    return (low(grad),)
low.defvjp(low_keep, low_pass)
low_back.defvjp(back_keep, back_low)
highest = lax.Precision.HIGHEST
epsilon = 1e-05

def layer_norm(values, norm_gain, norm_shift):
    average = lax.optimization_barrier(jnp.mean(values, axis=-1, keepdims=True))
    centred = values - average
    spread = lax.optimization_barrier(jnp.mean(centred * centred, axis=-1, keepdims=True))
    return centred * lax.rsqrt(spread + epsilon) * norm_gain + norm_shift

def matmul_high(left, right):
    return jnp.dot(left, right, precision=highest)

def head_slopes(head_count):
    return 2.0 ** (-8.0 * (jnp.arange(head_count, dtype=jnp.float32) + 1.0) / head_count)

def pack_forward(params, packed):
    w_skip, b_skip, g_one, b_one, w_qkv, w_out, b_out, g_two, b_two, w_up, c_up, w_down, c_down = params
    entering, skipped, segment, live = packed
    frames = entering.shape[0]
    position = jnp.arange(frames)
    live_mask = position % BLK < jnp.repeat(live, BLK)
    joined = jnp.concatenate([entering, skipped], axis=1)
    base_rows = low_back(matmul_high(joined, w_skip)) + b_skip
    normed = low(layer_norm(base_rows, g_one, b_one))
    triple = low_back(low(matmul_high(normed, w_qkv)))
    queries = triple[:, :D].reshape(frames, HEADS, HEAD)
    key_rows = triple[:, D:2 * D].reshape(frames, HEADS, HEAD)
    value_rows = triple[:, 2 * D:].reshape(frames, HEADS, HEAD)
    scores = jnp.einsum('qhd,khd->hqk', queries, key_rows, precision=highest) * HEAD ** (-0.5)
    distance = jnp.abs(position[:, None] - position[None, :]).astype(jnp.float32)
    scores = low_back(scores - head_slopes(HEADS)[:, None, None] * distance[None])
    allowed = (segment[:, None] == segment[None, :]) & (live_mask[None, :] | (position[:, None] == position[None, :]))
    scores = jnp.where(allowed[None], scores, -1e+30)
    highest_score = lax.optimization_barrier(jnp.max(scores, axis=-1, keepdims=True))
    raised = jnp.exp(scores - highest_score)
    attention = low(raised / lax.optimization_barrier(jnp.sum(raised, axis=-1, keepdims=True)))
    attended = jnp.einsum('hqk,khd->qhd', attention, value_rows, precision=highest).reshape(frames, D)
    attended = low_back(low(attended))
    mixed_rows = base_rows + low_back(matmul_high(attended, w_out)) + b_out
    normed_two = low(layer_norm(mixed_rows, g_two, b_two))
    hidden = low_back(matmul_high(normed_two, w_up)) + c_up
    active = low(jax.nn.gelu(hidden, approximate=False))
    result = mixed_rows + matmul_high(active, w_down) + c_down
    return result * live_mask.astype(jnp.float32)[:, None]

def reference(inputs, skips, cotangent, dest_slot, pack_segments, block_live, counts, w_skip, b_skip, g_one, b_one, w_qkv, w_out, b_out, g_two, b_two, w_up, c_up, w_down, c_down):
    devices = OWNERS * GROUPS
    count_total = jnp.sum(counts).astype(jnp.float32)
    share = counts.astype(jnp.float32) * devices / count_total
    frame_share = jnp.repeat(jnp.transpose(share), OWN * BLK, axis=1)
    scaled = low(cotangent.astype(jnp.float32) * frame_share[None, :, :, None])

    def to_packs(values):
        blocks = values.reshape(MB, GROUPS, SLOTS, BLK, -1)
        placed = jax.vmap(jax.vmap(lambda piece, target: jnp.zeros_like(piece).at[target].set(piece)))(blocks, dest_slot)
        return placed.reshape(MB * GROUPS * OWNERS, OWN * BLK, -1)

    def to_owners(values):
        blocks = values.reshape(MB, GROUPS, SLOTS, BLK, -1)
        taken = jax.vmap(jax.vmap(lambda piece, source: piece[source]))(blocks, dest_slot)
        return taken.reshape(MB, GROUPS, FRAMES, -1)
    segments = pack_segments.reshape(MB * GROUPS * OWNERS, OWN * BLK)
    lives = block_live.reshape(MB * GROUPS * OWNERS, OWN)

    def forward(inputs_full, skips_full, *params):
        packed_in = to_packs(inputs_full)
        packed_skip = to_packs(skips_full)
        single = jax.checkpoint(lambda item: pack_forward(params, item))
        results = lax.map(single, (packed_in, packed_skip, segments, lives))
        return to_owners(results)
    weights = (w_skip.astype(jnp.float32), b_skip, g_one, b_one, w_qkv.astype(jnp.float32), w_out.astype(jnp.float32), b_out, g_two, b_two, w_up.astype(jnp.float32), c_up, w_down.astype(jnp.float32), c_down)
    result, pull = jax.vjp(forward, inputs.astype(jnp.float32), skips.astype(jnp.float32), *weights)
    grads = pull(scaled)
    return (result.astype(jnp.bfloat16), grads[0].astype(jnp.bfloat16), grads[1].astype(jnp.bfloat16), grads[2], grads[3], grads[4], grads[5], grads[6], grads[7], grads[8], grads[9], grads[10], grads[11], grads[12], grads[13], grads[14])
```

```python
import jax
import jax.numpy as jnp
from jax import lax
from jax.experimental import pallas as pl
from jax.experimental.pallas import tpu as pltpu
from jax.sharding import PartitionSpec as P

HEADS = 16
HEAD = 64
EPS = 1e-05
F32 = jnp.float32
BF16 = jnp.bfloat16


def flip(value, bit):
    n = lax.axis_size("dp")
    return lax.ppermute(value, "dp", [(i, i ^ bit) for i in range(n)])


def assemble(w_local, pieces, place, group):
    rep = lax.axis_size("rep")
    shard_rows, columns = w_local.shape
    rows = shard_rows // group
    rels = sorted(pieces)
    arrays = [pieces[rel] for rel in rels]
    count = len(rels) * (rep - 1) + 1

    def body(place_ref, local_ref, *refs):
        piece_refs = refs[: len(rels)]
        out_ref, sems = refs[len(rels)], refs[len(rels) + 1]
        z = place_ref[0]
        e = place_ref[1]
        copies = [
            pltpu.make_async_copy(
                local_ref,
                out_ref.at[pl.ds(pl.multiple_of(z * shard_rows, 16), shard_rows), :],
                sems.at[0],
            )
        ]
        for i, rel in enumerate(rels):
            chunk = jnp.bitwise_xor(e, rel)
            for s in range(1, rep):
                shard = lax.rem(z - s + rep, rep)
                start = pl.multiple_of(shard * shard_rows + chunk * rows, 16)
                copies.append(
                    pltpu.make_async_copy(
                        piece_refs[i].at[pl.ds((s - 1) * rows, rows), :],
                        out_ref.at[pl.ds(start, rows), :],
                        sems.at[len(copies)],
                    )
                )
        for copy in copies:
            copy.start()
        for copy in copies:
            copy.wait()

    return pl.pallas_call(
        body,
        out_shape=jax.ShapeDtypeStruct((shard_rows * rep, columns), w_local.dtype),
        in_specs=[pl.BlockSpec(memory_space=pltpu.SMEM)]
        + [pl.BlockSpec(memory_space=pl.ANY)] * (1 + len(rels)),
        out_specs=pl.BlockSpec(memory_space=pl.ANY),
        scratch_shapes=[pltpu.SemaphoreType.DMA((count,))],
        cost_estimate=pl.CostEstimate(
            flops=0, bytes_accessed=4 * shard_rows * rep * columns, transcendentals=0
        ),
        name="assemble",
    )(place, w_local, *arrays)


def gather_matrix(w_local, place, order):
    rep = lax.axis_size("rep")
    group = 8
    rows = w_local.shape[0] // group
    own = lax.dynamic_slice_in_dim(w_local, place[1] * rows, rows, 0)
    far = [
        lax.ppermute(own, "rep", [(i, (i + s) % rep) for i in range(rep)])
        for s in range(1, rep)
    ]
    start = jnp.concatenate(far, axis=0)
    first, second = order
    pieces = {0: start}
    pieces[first] = flip(start, first)
    pieces[second] = flip(start, second)
    pieces[first | second] = flip(pieces[first], second)
    for rel in (0, first, second, first | second):
        pieces[rel | 1] = flip(pieces[rel], 1)
    return assemble(w_local, pieces, place, group)


def reduce_rows(full, order):
    dp = lax.axis_size("dp")
    bits = dp.bit_length() - 1
    d = lax.axis_index("dp")
    rows = full.shape[0] // dp
    value = full.reshape((2,) * bits + (rows, full.shape[1]))
    left = list(range(bits - 1, -1, -1))
    for bit in order:
        at = left.index(bit)
        mine = lax.bitwise_and(lax.shift_right_logical(d, bit), 1)
        send = lax.dynamic_index_in_dim(value, 1 - mine, at, keepdims=False)
        keep = lax.dynamic_index_in_dim(value, mine, at, keepdims=False)
        got = flip(send, 1 << bit)
        value = (keep.astype(F32) + got.astype(F32)).astype(full.dtype)
        left.remove(bit)
    return value


def sum_over_rep(value):
    rep = lax.axis_size("rep")
    z = lax.axis_index("rep")
    half = rep // 2
    for i in range(half - 1):
        got = lax.ppermute(value, "rep", [(i, i + 1), (rep - 1 - i, rep - 2 - i)])
        value = value + got
    got = lax.ppermute(value, "rep", [(half - 1, half), (half, half - 1)])
    value = value + got
    for i in reversed(range(half - 1)):
        got = lax.ppermute(value, "rep", [(i + 1, i), (rep - 2 - i, rep - 1 - i)])
        value = jnp.where((z == i) | (z == rep - 1 - i), got, value)
    return value


def matmul(left, right):
    return jnp.dot(left, right, preferred_element_type=F32)


def matmul_nt(left, right):
    return lax.dot_general(left, right, (((1,), (1,)), ((), ())), preferred_element_type=F32)


def matmul_tn(left, right):
    return lax.dot_general(left, right, (((0,), (0,)), ((), ())), preferred_element_type=F32)


def norm_parts(values):
    average = jnp.mean(values, axis=-1, keepdims=True)
    centred = values - average
    spread = jnp.mean(centred * centred, axis=-1, keepdims=True)
    scale = lax.rsqrt(spread + EPS)
    return centred * scale, scale


def norm_back(grad, gain, unit, scale):
    e = grad * gain
    return scale * (
        e
        - jnp.mean(e, axis=-1, keepdims=True)
        - unit * jnp.mean(e * unit, axis=-1, keepdims=True)
    )


def shards(
    inputs,
    skips,
    cotangent,
    dest_slot,
    pack_segments,
    block_live,
    counts,
    w_skip,
    b_skip,
    g_one,
    b_one,
    w_qkv,
    w_out,
    b_out,
    g_two,
    b_two,
    w_up,
    c_up,
    w_down,
    c_down,
):
    dp = lax.axis_size("dp")
    rep = lax.axis_size("rep")
    d = lax.axis_index("dp")
    z = lax.axis_index("rep")
    micro = inputs.shape[0]
    frames = inputs.shape[2]
    width = inputs.shape[3]
    blocks = dest_slot.shape[2]
    block = frames // blocks
    per_pair = blocks // dp
    total = micro * frames
    bits = dp.bit_length() - 1
    place = jnp.stack([z, lax.rem(d, 8)]).astype(jnp.int32)
    xs = list(range(1, bits))
    order_x = [0] + xs
    order_y = [0] + xs[::-1]

    full_skip = gather_matrix(w_skip, place, (2, 4))
    full_qkv = gather_matrix(w_qkv, place, (4, 2))
    full_out = gather_matrix(w_out, place, (4, 2))
    full_up = gather_matrix(w_up, place, (2, 4))
    full_down = gather_matrix(w_down, place, (4, 2))

    slots = dest_slot[:, 0, :]
    small = jnp.concatenate(
        [slots.reshape(-1), block_live[:, 0, :].reshape(-1), counts.reshape(-1)]
    )
    every = lax.all_gather(small, "dp")
    span = micro * blocks
    all_slots = every[:, :span].reshape(dp, micro, blocks)
    all_live = every[:, span : 2 * span].reshape(dp, micro, blocks)
    group_total = jnp.sum(every[:, 2 * span]).astype(F32).reshape(1, 1)
    count_total = sum_over_rep(group_total)[0, 0]
    share = counts[0, 0].astype(F32) * (dp * rep) / count_total

    rank = jnp.sum(
        (all_slots[:, :, None, :] < all_slots[:, :, :, None]).astype(jnp.int32), axis=3
    )
    mine_rank = jnp.sum((slots[:, None, :] < slots[:, :, None]).astype(jnp.int32), axis=2)
    here = (all_slots // blocks) == d
    arrive = jnp.arange(dp)[:, None, None] * per_pair + rank % per_pair
    arrive = jnp.where(here, arrive, -1)
    match = arrive[None] == jnp.arange(blocks)[:, None, None, None]
    placing = jnp.sum(jnp.where(match, (all_slots % blocks)[None], 0), axis=(1, 3)).T
    pick = placing[:, :, None] == jnp.arange(blocks)[None, None, :]
    seg_blocks = pack_segments[:, 0, :].reshape(micro, blocks, block)
    segment = jnp.sum(jnp.where(pick[..., None], seg_blocks[:, None], 0), axis=2)
    segment = segment.reshape(micro, frames)
    live_count = jnp.sum(jnp.where(pick, block_live[:, 0, None, :], 0), axis=2)
    inner = jnp.arange(frames) % block
    live = inner[None] < jnp.repeat(live_count, block, axis=1)
    position = jnp.repeat(placing * block, block, axis=1) + inner[None]
    flat_live = jnp.transpose(all_live, (1, 0, 2)).reshape(micro, dp * blocks)
    own_live = jnp.sum(
        jnp.where(slots[:, :, None] == jnp.arange(dp * blocks), flat_live[:, None], 0), axis=2
    )
    keep_rows = (inner[None] < jnp.repeat(own_live, block, axis=1)).astype(F32)
    keep_rows = keep_rows.reshape(total, 1)

    target = mine_rank // per_pair
    row = (target * micro + jnp.arange(micro)[:, None]) * per_pair + mine_rank % per_pair
    row = jnp.repeat(row.reshape(-1) * block, block) + jnp.tile(jnp.arange(block), micro * blocks)
    shuffle = (jnp.arange(total)[:, None] == row[None, :]).astype(BF16)

    def to_packs(values):
        sent = matmul(shuffle, values).astype(BF16)
        got = lax.all_to_all(
            sent.reshape(dp, total // dp, width), "dp", split_axis=0, concat_axis=0, tiled=True
        )
        got = got.reshape(dp, micro, per_pair * block, width)
        return jnp.transpose(got, (1, 0, 2, 3)).reshape(total, width)

    def to_owners(values):
        sent = values.reshape(micro, dp, per_pair * block, width)
        sent = jnp.transpose(sent, (1, 0, 2, 3)).reshape(dp, total // dp, width)
        got = lax.all_to_all(sent, "dp", split_axis=0, concat_axis=0, tiled=True)
        return matmul_tn(shuffle, got.reshape(total, width))

    joined = jnp.concatenate(
        [inputs.reshape(total, width), skips.reshape(total, width)], axis=1
    )
    base = matmul(joined, full_skip) + b_skip
    unit_one, scale_one = norm_parts(base)
    normed = to_packs((unit_one * g_one + b_one).astype(BF16))
    triple = matmul(normed, full_qkv).astype(BF16)
    triple = triple.reshape(micro, frames, 3, HEADS, HEAD)
    queries, keys, values = triple[:, :, 0], triple[:, :, 1], triple[:, :, 2]
    slopes = 2.0 ** (-8.0 * (jnp.arange(HEADS, dtype=F32) + 1.0) / HEADS)
    distance = jnp.abs(position[:, :, None] - position[:, None, :]).astype(F32)
    allowed = (segment[:, :, None] == segment[:, None, :]) & (
        live[:, None, :] | (position[:, :, None] == position[:, None, :])
    )
    score_scale = HEAD ** (-0.5)
    scores = jnp.einsum("mqhd,mkhd->mhqk", queries, keys, preferred_element_type=F32)
    scores = scores * score_scale - slopes[None, :, None, None] * distance[:, None]
    scores = jnp.where(allowed[:, None], scores, -1e30)
    raised = jnp.exp(scores - jnp.max(scores, axis=-1, keepdims=True))
    attention = raised / jnp.sum(raised, axis=-1, keepdims=True)
    attention_low = attention.astype(BF16)
    attended = jnp.einsum("mhqk,mkhd->mqhd", attention_low, values, preferred_element_type=F32)
    attended = to_owners(attended.reshape(total, width).astype(BF16)).astype(BF16)
    mixed = base + matmul(attended, full_out) + b_out
    unit_two, scale_two = norm_parts(mixed)
    normed_two = (unit_two * g_two + b_two).astype(BF16)
    hidden = matmul(normed_two, full_up) + c_up
    phi = 0.5 * (1.0 + lax.erf(hidden * (0.5**0.5)))
    active = (hidden * phi).astype(BF16)
    slope = (phi + hidden * jnp.exp(-0.5 * hidden * hidden) * ((2 * jnp.pi) ** -0.5)).astype(BF16)

    scaled = (cotangent.reshape(total, width).astype(F32) * share).astype(BF16)
    grad_result = scaled * keep_rows.astype(BF16)
    grad_w_down = matmul_tn(active, grad_result).astype(BF16)
    part_down = reduce_rows(grad_w_down, order_x)
    result = mixed + matmul(active, full_down) + c_down
    output = (result * keep_rows).astype(BF16)
    grad_result_full = grad_result.astype(F32)
    grad_active = matmul_nt(grad_result, full_down)
    grad_hidden = slope.astype(F32) * grad_active
    hidden_low = grad_hidden.astype(BF16)
    grad_w_up = matmul_tn(normed_two, hidden_low).astype(BF16)
    part_up = reduce_rows(grad_w_up, order_y)
    grad_normed_two = matmul_nt(hidden_low, full_up)
    grad_mixed = grad_result_full + norm_back(grad_normed_two, g_two, unit_two, scale_two)
    mixed_low = grad_mixed.astype(BF16)
    grad_w_out = matmul_tn(attended, mixed_low).astype(BF16)
    part_out = reduce_rows(grad_w_out, order_x)
    grad_attended = to_packs(matmul_nt(mixed_low, full_out).astype(BF16))
    grad_attended = grad_attended.reshape(micro, frames, HEADS, HEAD)
    grad_values = jnp.einsum(
        "mhqk,mqhd->mkhd", attention_low, grad_attended, preferred_element_type=F32
    )
    grad_probs = jnp.einsum("mqhd,mkhd->mhqk", grad_attended, values, preferred_element_type=F32)
    grad_scores = attention * (
        grad_probs - jnp.sum(grad_probs * attention, axis=-1, keepdims=True)
    )
    scores_low = grad_scores.astype(BF16)
    grad_queries = score_scale * jnp.einsum(
        "mhqk,mkhd->mqhd", scores_low, keys, preferred_element_type=F32
    )
    grad_keys = score_scale * jnp.einsum(
        "mhqk,mqhd->mkhd", scores_low, queries, preferred_element_type=F32
    )
    grad_triple = jnp.concatenate(
        [g.reshape(total, width).astype(BF16) for g in (grad_queries, grad_keys, grad_values)],
        axis=1,
    )
    grad_w_qkv = matmul_tn(normed, grad_triple).astype(BF16)
    part_qkv = reduce_rows(grad_w_qkv, order_y)
    grad_normed = to_owners(matmul_nt(grad_triple, full_qkv).astype(BF16))
    grad_base = grad_mixed + norm_back(grad_normed, g_one, unit_one, scale_one)
    base_low = grad_base.astype(BF16)
    grad_w_skip = matmul_tn(joined, base_low).astype(BF16)
    part_skip = reduce_rows(grad_w_skip, order_x)
    grad_joined = matmul_nt(base_low, full_skip).astype(BF16)

    finals = [
        sum_over_rep(part).astype(F32)
        for part in (part_down, part_up, part_out, part_qkv, part_skip)
    ]
    vectors = (
        jnp.sum(grad_base, axis=0),
        jnp.sum(grad_normed * unit_one, axis=0),
        jnp.sum(grad_normed, axis=0),
        jnp.sum(grad_mixed, axis=0),
        jnp.sum(grad_normed_two * unit_two, axis=0),
        jnp.sum(grad_normed_two, axis=0),
        jnp.sum(grad_hidden, axis=0),
        jnp.sum(grad_result_full, axis=0),
    )
    lengths = [v.shape[0] for v in vectors]
    summed = jnp.concatenate(vectors).reshape(-1, 128)
    for bit in range(bits):
        summed = summed + flip(summed, 1 << bit)
    summed = sum_over_rep(summed).reshape(-1)
    sums = []
    offset = 0
    for length in lengths:
        sums.append(summed[offset : offset + length])
        offset += length

    def as_owned(values):
        return values.reshape(inputs.shape)

    return (
        as_owned(output),
        as_owned(grad_joined[:, :width]),
        as_owned(grad_joined[:, width:]),
        finals[4],
        sums[0],
        sums[1],
        sums[2],
        finals[3],
        finals[2],
        sums[3],
        sums[4],
        sums[5],
        finals[1],
        sums[6],
        finals[0],
        sums[7],
    )


def solution(mesh):
    frames = P(None, "rep", "dp", None)
    slots = P(None, "rep", "dp")
    rows = P("rep", None)
    whole = P()
    in_specs = (
        (frames,) * 3
        + (slots,) * 3
        + (P("dp", "rep"), rows, whole, whole, whole, rows, rows)
        + (whole,) * 3
        + (rows, whole, rows, whole)
    )
    split = P("dp", None)
    out_specs = (
        (frames,) * 3
        + (split,)
        + (whole,) * 3
        + (split, split)
        + (whole,) * 3
        + (split, whole, split, whole)
    )
    return jax.shard_map(shards, mesh=mesh, in_specs=in_specs, out_specs=out_specs, check_vma=False)
```

```python
import jax
import jax.numpy as jnp
from jax import lax
from jax.experimental import pallas as pl
from jax.experimental.pallas import tpu as pltpu
from jax.sharding import PartitionSpec as P

HEADS = 16
HEAD = 64
EPS = 1e-05
F32 = jnp.float32
BF16 = jnp.bfloat16


def flip(value, bit):
    n = lax.axis_size("dp")
    return lax.ppermute(value, "dp", [(i, i ^ bit) for i in range(n)])


def after(value, *earlier):
    return lax.optimization_barrier((value,) + earlier)[0]


def assemble(w_local, parts, place, group):
    rep = lax.axis_size("rep")
    shard_rows, columns = w_local.shape
    rows = shard_rows // group
    arrays = [part[0] for part in parts]
    count = 1 + sum(len(part[2]) for part in parts) * (rep - 1)

    def body(place_ref, local_ref, *refs):
        out_ref, sems = refs[len(parts)], refs[len(parts) + 1]
        z = place_ref[0]
        e = place_ref[1]
        copies = [
            pltpu.make_async_copy(
                local_ref,
                out_ref.at[pl.ds(pl.multiple_of(z * shard_rows, 16), shard_rows), :],
                sems.at[0],
            )
        ]
        for ref, (_, column, rels) in zip(refs, parts):
            for k, rel in enumerate(rels):
                chunk = jnp.bitwise_xor(e, rel)
                for s in range(1, rep):
                    shard = lax.rem(z + s, rep)
                    start = pl.multiple_of(shard * shard_rows + chunk * rows, 16)
                    copies.append(
                        pltpu.make_async_copy(
                            ref.at[pl.ds((k * (rep - 1) + s - 1) * rows, rows), :],
                            out_ref.at[pl.ds(start, rows), pl.ds(column, ref.shape[1])],
                            sems.at[len(copies)],
                        )
                    )
        for copy in copies:
            copy.start()
        for copy in copies:
            copy.wait()

    return pl.pallas_call(
        body,
        out_shape=jax.ShapeDtypeStruct((shard_rows * rep, columns), w_local.dtype),
        in_specs=[pl.BlockSpec(memory_space=pltpu.SMEM)]
        + [pl.BlockSpec(memory_space=pl.ANY)] * (1 + len(parts)),
        out_specs=pl.BlockSpec(memory_space=pltpu.VMEM),
        scratch_shapes=[pltpu.SemaphoreType.DMA((count,))],
        compiler_params=pltpu.CompilerParams(vmem_limit_bytes=24 * 2**20),
        cost_estimate=pl.CostEstimate(
            flops=0, bytes_accessed=4 * shard_rows * rep * columns, transcendentals=0
        ),
        name="assemble",
    )(place, w_local, *arrays)


def fetch_far(w_local, place, previous):
    rep = lax.axis_size("rep")
    rows = w_local.shape[0] // 8
    own = lax.dynamic_slice_in_dim(w_local, place[1] * rows, rows, 0)
    if previous is not None:
        own = after(own, previous)
    every = lax.all_gather(own, "rep", axis=0)
    far = [
        lax.dynamic_index_in_dim(every, lax.rem(place[0] + s, rep), 0, keepdims=False)
        for s in range(1, rep)
    ]
    return every, far


def spread_pieces(far):
    half = far[0].shape[1] // 2
    parts = []
    firsts = []
    for first, second, column in ((2, 4, 0), (4, 2, half)):
        start = jnp.concatenate([piece[:, column : column + half] for piece in far], axis=0)
        firsts.append((start, flip(start, first), first, second, column))
    for start, got, first, second, column in firsts:
        pair = jnp.concatenate([start, got], axis=0)
        parts.append((pair, column, [0, first]))
        parts.append((flip(pair, second), column, [second, first | second]))
    others = []
    for array, column, rels in parts:
        others.append((flip(array, 1), column, [rel | 1 for rel in rels]))
    return parts + others


def rep_flip(value, bit):
    n = lax.axis_size("rep")
    return lax.ppermute(value, "rep", [(i, i ^ bit) for i in range(n)])


def gradient_blocks(left, right, d, order, odd):
    dp = lax.axis_size("dp")
    total, all_rows = left.shape
    columns = right.shape[1]
    rows = all_rows // dp
    count = dp // 2
    tile = min(columns, 1024)
    steps = order[1:]

    def absolute(p, d_ref):
        rel = jnp.int32(odd)
        for k, bit in enumerate(steps):
            chosen = lax.bitwise_and(lax.shift_right_logical(p, len(steps) - 1 - k), 1)
            rel = rel + lax.shift_left(chosen, bit)
        return lax.bitwise_xor(d_ref[0], rel)

    def body(d_ref, left_ref, right_ref, out_ref):
        product = lax.dot_general(
            left_ref[...], right_ref[...], (((0,), (0,)), ((), ())), preferred_element_type=F32
        )
        out_ref[0] = product.astype(BF16)

    lanes = rows
    if rows % 128 != 0:
        product = lax.dot_general(left, right, (((0,), (0,)), ((), ())), preferred_element_type=F32)
        product = product.astype(BF16).reshape(dp, rows, columns)
        p = jnp.arange(count)
        rel = jnp.full((count,), odd)
        for k, bit in enumerate(steps):
            rel = rel + (((p >> (len(steps) - 1 - k)) & 1) << bit)
        return product[jnp.bitwise_xor(rel, d)]
    return pl.pallas_call(
        body,
        out_shape=jax.ShapeDtypeStruct((count, rows, columns), BF16),
        grid_spec=pltpu.PrefetchScalarGridSpec(
            num_scalar_prefetch=1,
            grid=(columns // tile, count),
            in_specs=[
                pl.BlockSpec((total, lanes), lambda c, p, d_ref: (0, absolute(p, d_ref))),
                pl.BlockSpec((total, tile), lambda c, p, d_ref: (0, c)),
            ],
            out_specs=pl.BlockSpec((1, rows, tile), lambda c, p, d_ref: (p, 0, c)),
        ),
        compiler_params=pltpu.CompilerParams(vmem_limit_bytes=24 * 2**20),
        cost_estimate=pl.CostEstimate(
            flops=total * all_rows * columns,
            bytes_accessed=total * all_rows + 2 * total * columns + all_rows * columns,
            transcendentals=0,
        ),
        name="gradient",
    )(d.reshape(1).astype(jnp.int32), left, right)


class Reduction:
    def __init__(self, left, right, d, dims, hold=None):
        self.dims = dims
        send = gradient_blocks(left, right, d, [0] + dims, 1)
        self.sent = send
        self.got = flip(send, 1)
        self.kept = gradient_blocks(left, after(right, send), d, [0] + dims, 0)
        self.halves = None

    def step(self, ready=None):
        if self.halves is None:
            shape = (2,) * len(self.dims) + self.kept.shape[1:]
            half = self.kept.shape[2] // 2
            whole_keep = self.kept.reshape(shape)
            whole_got = self.got.reshape(shape)
            halves = []
            for column, order in ((0, self.dims), (half, self.dims[::-1])):
                halves.append(
                    (
                        whole_keep[..., column : column + half],
                        whole_got[..., column : column + half],
                        list(order),
                        list(self.dims),
                    )
                )
        else:
            halves = self.halves
        self.halves = []
        tokens = []
        for keep, got, order, left in halves:
            bit = order[0]
            at = left.index(bit)

            def total(index):
                a = lax.index_in_dim(keep, index, at, keepdims=False)
                b = lax.index_in_dim(got, index, at, keepdims=False)
                return (a.astype(F32) + b.astype(F32)).astype(BF16)

            send, stay = total(1), total(0)
            if ready is not None:
                send = after(send, ready)
            tokens.append(send)
            self.halves.append((stay, flip(send, 1 << bit), order[1:], [b for b in left if b != bit]))
        return tokens

    def finish(self, previous=None):
        while self.halves[0][2]:
            self.step()
        pieces = [
            (keep.astype(F32) + got.astype(F32)).astype(BF16) for keep, got, _, _ in self.halves
        ]
        value = jnp.concatenate(pieces, axis=1)
        if previous is not None:
            value = after(value, previous)
        return lax.psum(value, "rep")


def matmul(left, right):
    return jnp.dot(left, right, preferred_element_type=F32)


def matmul_nt(left, right):
    return lax.dot_general(left, right, (((1,), (1,)), ((), ())), preferred_element_type=F32)


def matmul_tn(left, right):
    return lax.dot_general(left, right, (((0,), (0,)), ((), ())), preferred_element_type=F32)


def norm_parts(values):
    average = jnp.mean(values, axis=-1, keepdims=True)
    centred = values - average
    spread = jnp.mean(centred * centred, axis=-1, keepdims=True)
    scale = lax.rsqrt(spread + EPS)
    return centred * scale, scale


def norm_back(grad, gain, unit, scale):
    e = grad * gain
    return scale * (
        e
        - jnp.mean(e, axis=-1, keepdims=True)
        - unit * jnp.mean(e * unit, axis=-1, keepdims=True)
    )


def shards(
    inputs,
    skips,
    cotangent,
    dest_slot,
    pack_segments,
    block_live,
    counts,
    w_skip,
    b_skip,
    g_one,
    b_one,
    w_qkv,
    w_out,
    b_out,
    g_two,
    b_two,
    w_up,
    c_up,
    w_down,
    c_down,
):
    dp = lax.axis_size("dp")
    rep = lax.axis_size("rep")
    d = lax.axis_index("dp")
    z = lax.axis_index("rep")
    micro = inputs.shape[0]
    frames = inputs.shape[2]
    width = inputs.shape[3]
    blocks = dest_slot.shape[2]
    block = frames // blocks
    per_pair = blocks // dp
    total = micro * frames
    bits = dp.bit_length() - 1
    place = jnp.stack([z, lax.rem(d, 8)]).astype(jnp.int32)
    dims = list(range(1, bits))
    moved, far_skip = fetch_far(w_skip, place, None)
    moved_qkv, far_qkv = fetch_far(w_qkv, place, moved)
    moved_out, far_out = fetch_far(w_out, place, moved_qkv)
    moved_up, far_up = fetch_far(w_up, place, moved_out)
    moved_down, far_down = fetch_far(w_down, place, moved_up)
    parts_skip = spread_pieces(far_skip)
    far_qkv = [after(far, parts_skip[0][0]) for far in far_qkv]
    parts_qkv = spread_pieces(far_qkv)
    far_out = [after(far, parts_qkv[0][0]) for far in far_out]
    parts_out = spread_pieces(far_out)
    far_up = [after(far, parts_out[0][0]) for far in far_up]
    parts_up = spread_pieces(far_up)
    far_down = [after(far, parts_up[0][0]) for far in far_down]
    parts_down = spread_pieces(far_down)
    full_skip = assemble(w_skip, parts_skip, place, 8)
    full_qkv = assemble(w_qkv, parts_qkv, place, 8)
    full_out = assemble(w_out, parts_out, place, 8)
    full_up = assemble(w_up, parts_up, place, 8)
    full_down = assemble(w_down, parts_down, place, 8)

    slots = dest_slot[:, 0, :]
    small = jnp.concatenate(
        [slots.reshape(-1), block_live[:, 0, :].reshape(-1), counts.reshape(-1)]
    )
    small, _ = lax.optimization_barrier((small, moved))
    every = small[None]
    for bit in range(bits):
        every = jnp.concatenate([every, flip(every, 1 << bit)], axis=0)
    span = micro * blocks
    all_slots = every[:, :span].reshape(dp, micro, blocks)
    all_live = every[:, span : 2 * span].reshape(dp, micro, blocks)
    source = jnp.bitwise_xor(jnp.arange(dp), d)
    count_total = jnp.sum(every[:, 2 * span]).astype(F32).reshape(1, 1)
    for bit in range(rep.bit_length() - 1):
        count_total = count_total + rep_flip(count_total, 1 << bit)
    share = counts[0, 0].astype(F32) * (dp * rep) / count_total[0, 0]

    rank = jnp.sum(
        (all_slots[:, :, None, :] < all_slots[:, :, :, None]).astype(jnp.int32), axis=3
    )
    mine_rank = jnp.sum((slots[:, None, :] < slots[:, :, None]).astype(jnp.int32), axis=2)
    here = (all_slots // blocks) == d
    arrive = source[:, None, None] * per_pair + rank % per_pair
    arrive = jnp.where(here, arrive, -1)
    match = arrive[None] == jnp.arange(blocks)[:, None, None, None]
    placing = jnp.sum(jnp.where(match, (all_slots % blocks)[None], 0), axis=(1, 3)).T
    pick = placing[:, :, None] == jnp.arange(blocks)[None, None, :]
    seg_blocks = pack_segments[:, 0, :].reshape(micro, blocks, block)
    segment = jnp.sum(jnp.where(pick[..., None], seg_blocks[:, None], 0), axis=2)
    segment = segment.reshape(micro, frames)
    live_count = jnp.sum(jnp.where(pick, block_live[:, 0, None, :], 0), axis=2)
    inner = jnp.arange(frames) % block
    live = inner[None] < jnp.repeat(live_count, block, axis=1)
    position = jnp.repeat(placing * block, block, axis=1) + inner[None]
    flat_live = jnp.transpose(all_live, (1, 0, 2)).reshape(micro, dp * blocks)
    flat_slot = (source[:, None] * blocks + jnp.arange(blocks)).reshape(-1)
    own_live = jnp.sum(jnp.where(slots[:, :, None] == flat_slot, flat_live[:, None], 0), axis=2)
    keep_rows = (inner[None] < jnp.repeat(own_live, block, axis=1)).astype(F32)
    keep_rows = keep_rows.reshape(total, 1)

    target = mine_rank // per_pair
    row = (target * micro + jnp.arange(micro)[:, None]) * per_pair + mine_rank % per_pair
    row = jnp.repeat(row.reshape(-1) * block, block) + jnp.tile(jnp.arange(block), micro * blocks)
    shuffle = (jnp.arange(total)[:, None] == row[None, :]).astype(BF16)

    def to_packs(values):
        sent = matmul(shuffle, values).astype(BF16)
        got = lax.all_to_all(
            sent.reshape(dp, total // dp, width), "dp", split_axis=0, concat_axis=0, tiled=True
        )
        got = got.reshape(dp, micro, per_pair * block, width)
        return jnp.transpose(got, (1, 0, 2, 3)).reshape(total, width)

    def to_owners(values):
        sent = values.reshape(micro, dp, per_pair * block, width)
        sent = jnp.transpose(sent, (1, 0, 2, 3)).reshape(dp, total // dp, width)
        got = lax.all_to_all(sent, "dp", split_axis=0, concat_axis=0, tiled=True)
        return matmul_tn(shuffle, got.reshape(total, width))

    joined = jnp.concatenate(
        [inputs.reshape(total, width), skips.reshape(total, width)], axis=1
    )
    base = matmul(joined, full_skip) + b_skip
    unit_one, scale_one = norm_parts(base)
    normed = to_packs((unit_one * g_one + b_one).astype(BF16))
    triple = matmul(normed, full_qkv).astype(BF16)
    triple = triple.reshape(micro, frames, 3, HEADS, HEAD)
    queries, keys, values = triple[:, :, 0], triple[:, :, 1], triple[:, :, 2]
    slopes = 2.0 ** (-8.0 * (jnp.arange(HEADS, dtype=F32) + 1.0) / HEADS)
    distance = jnp.abs(position[:, :, None] - position[:, None, :]).astype(F32)
    allowed = (segment[:, :, None] == segment[:, None, :]) & (
        live[:, None, :] | (position[:, :, None] == position[:, None, :])
    )
    score_scale = HEAD ** (-0.5)
    scores = jnp.einsum("mqhd,mkhd->mhqk", queries, keys, preferred_element_type=F32)
    scores = scores * score_scale - slopes[None, :, None, None] * distance[:, None]
    scores = jnp.where(allowed[:, None], scores, -1e30)
    raised = jnp.exp(scores - jnp.max(scores, axis=-1, keepdims=True))
    attention = raised / jnp.sum(raised, axis=-1, keepdims=True)
    attention_low = attention.astype(BF16)
    attended = jnp.einsum("mhqk,mkhd->mqhd", attention_low, values, preferred_element_type=F32)
    attended = to_owners(attended.reshape(total, width).astype(BF16)).astype(BF16)
    mixed = base + matmul(attended, full_out) + b_out
    unit_two, scale_two = norm_parts(mixed)
    normed_two = (unit_two * g_two + b_two).astype(BF16)
    hidden = matmul(normed_two, full_up) + c_up
    phi = 0.5 * (1.0 + lax.erf(hidden * (0.5**0.5)))
    active = (hidden * phi).astype(BF16)
    slope = (phi + hidden * jnp.exp(-0.5 * hidden * hidden) * ((2 * jnp.pi) ** -0.5)).astype(BF16)

    scaled = (cotangent.reshape(total, width).astype(F32) * share).astype(BF16)
    grad_result = scaled * keep_rows.astype(BF16)
    red_down = Reduction(active, grad_result, d, dims)
    grad_result = after(grad_result, red_down.kept)
    grad_result_full = grad_result.astype(F32)
    grad_active = matmul_nt(grad_result, full_down)
    grad_hidden = slope.astype(F32) * grad_active
    hidden_low = grad_hidden.astype(BF16)
    red_up = Reduction(normed_two, hidden_low, d, dims)
    tokens = red_down.step()
    hidden_low = after(hidden_low, red_up.kept, *tokens)
    grad_normed_two = matmul_nt(hidden_low, full_up)
    grad_mixed = grad_result_full + norm_back(grad_normed_two, g_two, unit_two, scale_two)
    mixed_low = grad_mixed.astype(BF16)
    red_out = Reduction(attended, mixed_low, d, dims)
    mixed_low = after(mixed_low, red_out.kept)
    tokens = red_up.step()
    grad_attended = to_packs(after(matmul_nt(mixed_low, full_out).astype(BF16), *tokens))
    result = mixed + matmul(active, full_down) + c_down
    output = (result * keep_rows).astype(BF16)
    tokens = red_out.step()
    grad_attended = after(grad_attended, output, *tokens)
    grad_attended = grad_attended.reshape(micro, frames, HEADS, HEAD)
    grad_values = jnp.einsum(
        "mhqk,mqhd->mkhd", attention_low, grad_attended, preferred_element_type=F32
    )
    grad_probs = jnp.einsum("mqhd,mkhd->mhqk", grad_attended, values, preferred_element_type=F32)
    grad_scores = attention * (
        grad_probs - jnp.sum(grad_probs * attention, axis=-1, keepdims=True)
    )
    scores_low = grad_scores.astype(BF16)
    grad_queries = score_scale * jnp.einsum(
        "mhqk,mkhd->mqhd", scores_low, keys, preferred_element_type=F32
    )
    grad_keys = score_scale * jnp.einsum(
        "mhqk,mqhd->mkhd", scores_low, queries, preferred_element_type=F32
    )
    grad_triple = jnp.concatenate(
        [g.reshape(total, width).astype(BF16) for g in (grad_queries, grad_keys, grad_values)],
        axis=1,
    )
    tokens = red_down.step()
    grad_triple = after(grad_triple, *tokens)
    red_qkv = Reduction(normed, grad_triple, d, dims)
    grad_triple = after(grad_triple, red_qkv.kept)
    grad_normed = to_owners(matmul_nt(grad_triple, full_qkv).astype(BF16))
    tokens = red_qkv.step()
    tokens += red_up.step()
    final_down = red_down.finish()
    grad_normed = after(grad_normed, *tokens)
    grad_base = grad_mixed + norm_back(grad_normed, g_one, unit_one, scale_one)
    base_low = grad_base.astype(BF16)
    red_skip = Reduction(joined, base_low, d, dims)
    base_low = after(base_low, red_skip.kept)
    grad_joined = matmul_nt(base_low, full_skip).astype(BF16)
    red_out.step()
    red_skip.step()
    red_qkv.step()
    red_skip.step()
    final_up = red_up.finish(final_down)
    final_out = red_out.finish(final_up)
    final_qkv = red_qkv.finish(final_out)
    final_skip = red_skip.finish(final_qkv)
    finals = [v.astype(F32) for v in (final_down, final_up, final_out, final_qkv, final_skip)]
    vectors = (
        jnp.sum(grad_base, axis=0),
        jnp.sum(grad_normed * unit_one, axis=0),
        jnp.sum(grad_normed, axis=0),
        jnp.sum(grad_mixed, axis=0),
        jnp.sum(grad_normed_two * unit_two, axis=0),
        jnp.sum(grad_normed_two, axis=0),
        jnp.sum(grad_hidden, axis=0),
        jnp.sum(grad_result_full, axis=0),
    )
    lengths = [v.shape[0] for v in vectors]
    summed = jnp.concatenate(vectors).reshape(-1, 128)
    for bit in range(bits):
        summed = summed + flip(summed, 1 << bit)
    for bit in range(rep.bit_length() - 1):
        summed = summed + rep_flip(summed, 1 << bit)
    summed = summed.reshape(-1)
    sums = []
    offset = 0
    for length in lengths:
        sums.append(summed[offset : offset + length])
        offset += length

    def as_owned(values):
        return values.reshape(inputs.shape)

    return (
        as_owned(output),
        as_owned(grad_joined[:, :width]),
        as_owned(grad_joined[:, width:]),
        finals[4],
        sums[0],
        sums[1],
        sums[2],
        finals[3],
        finals[2],
        sums[3],
        sums[4],
        sums[5],
        finals[1],
        sums[6],
        finals[0],
        sums[7],
    )


def solution(mesh):
    frames = P(None, "rep", "dp", None)
    slots = P(None, "rep", "dp")
    rows = P("rep", None)
    whole = P()
    in_specs = (
        (frames,) * 3
        + (slots,) * 3
        + (P("dp", "rep"), rows, whole, whole, whole, rows, rows)
        + (whole,) * 3
        + (rows, whole, rows, whole)
    )
    split = P("dp", None)
    out_specs = (
        (frames,) * 3
        + (split,)
        + (whole,) * 3
        + (split, split)
        + (whole,) * 3
        + (split, whole, split, whole)
    )
    return jax.shard_map(shards, mesh=mesh, in_specs=in_specs, out_specs=out_specs, check_vma=False)
```

```python
import jax
import jax.numpy as jnp
from jax import lax
from jax.experimental import pallas as pl
from jax.experimental.pallas import tpu as pltpu
from jax.sharding import PartitionSpec as P

HEADS = 16
HEAD = 64
EPS = 1e-05
F32 = jnp.float32
BF16 = jnp.bfloat16


def flip(value, bit):
    n = lax.axis_size("dp")
    return lax.ppermute(value, "dp", [(i, i ^ bit) for i in range(n)])


def after(value, *earlier):
    return lax.optimization_barrier((value,) + earlier)[0]


def assemble(w_local, parts, place, row_at, tiles):
    rep = lax.axis_size("rep")
    shard_rows, columns = w_local.shape
    rows = shard_rows // 8
    tile = columns // tiles
    half = tile // 2
    chunk_rows = parts[0][0].shape[0] // (len(parts[0][2]) * (rep - 1))
    arrays = [part[0] for part in parts]
    count = 1 + sum(len(part[2]) for part in parts) * (rep - 1) * tiles

    def body(place_ref, local_ref, *refs):
        out_ref, sems = refs[len(parts)], refs[len(parts) + 1]
        z = place_ref[0]
        e = place_ref[1]
        copies = [
            pltpu.make_async_copy(
                local_ref,
                out_ref.at[pl.ds(pl.multiple_of(z * shard_rows, 16), shard_rows), :],
                sems.at[0],
            )
        ]
        for ref, (_, side, rels) in zip(refs, parts):
            for k, rel in enumerate(rels):
                chunk = jnp.bitwise_xor(e, rel)
                for s in range(1, rep):
                    shard = lax.rem(z - s + rep, rep)
                    start = pl.multiple_of(shard * shard_rows + chunk * rows, 16)
                    for t in range(tiles):
                        at = (k * (rep - 1) + s - 1) * chunk_rows + row_at + t * rows
                        copies.append(
                            pltpu.make_async_copy(
                                ref.at[pl.ds(at, rows), :],
                                out_ref.at[pl.ds(start, rows), pl.ds(t * tile + side * half, half)],
                                sems.at[len(copies)],
                            )
                        )
        for copy in copies:
            copy.start()
        for copy in copies:
            copy.wait()

    return pl.pallas_call(
        body,
        out_shape=jax.ShapeDtypeStruct((shard_rows * rep, columns), w_local.dtype),
        in_specs=[pl.BlockSpec(memory_space=pltpu.SMEM)]
        + [pl.BlockSpec(memory_space=pl.ANY)] * (1 + len(parts)),
        out_specs=pl.BlockSpec(memory_space=pltpu.VMEM),
        scratch_shapes=[pltpu.SemaphoreType.DMA((count,))],
        compiler_params=pltpu.CompilerParams(vmem_limit_bytes=24 * 2**20),
        cost_estimate=pl.CostEstimate(
            flops=0, bytes_accessed=4 * shard_rows * rep * columns, transcendentals=0
        ),
        name="assemble",
    )(place, w_local, *arrays)


def own_chunk(place, width, *shards_local):
    pieces = []
    for w_local in shards_local:
        rows = w_local.shape[0] // 8
        own = lax.dynamic_slice_in_dim(w_local, place[1] * rows, rows, 0)
        for t in range(w_local.shape[1] // width):
            pieces.append(own[:, t * width : (t + 1) * width])
    return jnp.concatenate(pieces, axis=0)


def fetch_far(own, previous):
    rep = lax.axis_size("rep")
    if previous is not None:
        own = after(own, previous)
    return [
        lax.ppermute(own, "rep", [(i, (i + s) % rep) for i in range(rep)])
        for s in range(1, rep)
    ]


def spread_pieces(far):
    half = far[0].shape[1] // 2
    parts = []
    firsts = []
    for first, second, side in ((2, 4, 0), (4, 2, 1)):
        start = jnp.concatenate([piece[:, side * half : (side + 1) * half] for piece in far], axis=0)
        firsts.append((start, flip(start, first), first, second, side))
    for start, got, first, second, side in firsts:
        pair = jnp.concatenate([start, got], axis=0)
        parts.append((pair, side, [0, first]))
        parts.append((flip(pair, second), side, [second, first | second]))
    others = []
    for array, side, rels in parts:
        others.append((flip(array, 1), side, [rel | 1 for rel in rels]))
    return parts + others


def rep_flip(value, bit):
    n = lax.axis_size("rep")
    return lax.ppermute(value, "rep", [(i, i ^ bit) for i in range(n)])


def gradient_blocks(left, right, d, order, odd):
    dp = lax.axis_size("dp")
    total, all_rows = left.shape
    tiles, _, width = right.shape
    rows = all_rows // dp
    count = dp // 2
    steps = order[1:]
    tile = min(width, 512)
    split = width // tile

    def distance(p):
        rel = odd
        for k, bit in enumerate(steps):
            rel += ((p >> (len(steps) - 1 - k)) & 1) << bit
        return rel

    if rows % 128 != 0:
        flat = jnp.transpose(right, (1, 0, 2)).reshape(total, tiles * width)
        product = matmul_tn(left, flat).astype(BF16).reshape(dp, rows, tiles * width)
        rel = jnp.array([distance(p) for p in range(count)], jnp.int32)
        return product[jnp.bitwise_xor(rel, d)]

    def body(d_ref, left_ref, right_ref, out_ref, turned_ref):
        @pl.when(pl.program_id(0) == 0)
        def _():
            for p in range(count):
                at = pl.multiple_of(jnp.bitwise_xor(d_ref[0], distance(p)) * rows, 128)
                turned_ref[pl.ds(p * rows, rows), :] = left_ref[:, pl.ds(at, rows)].T

        step = min(count * rows, 512)
        for r in range(count * rows // step):
            product = jnp.dot(
                turned_ref[pl.ds(r * step, step), :], right_ref[0], preferred_element_type=F32
            ).astype(BF16)
            for q in range(max(step // rows, 1)):
                size = min(rows, step)
                at = r * step + q * size
                out_ref[at // rows, pl.ds(at % rows, size), :] = product[q * size : (q + 1) * size]

    return pl.pallas_call(
        body,
        out_shape=jax.ShapeDtypeStruct((count, rows, tiles * width), BF16),
        grid_spec=pltpu.PrefetchScalarGridSpec(
            num_scalar_prefetch=1,
            grid=(tiles * split,),
            in_specs=[
                pl.BlockSpec((total, all_rows), lambda c, d_ref: (0, 0)),
                pl.BlockSpec((1, total, tile), lambda c, d_ref: (c // split, 0, c % split)),
            ],
            out_specs=pl.BlockSpec((count, rows, tile), lambda c, d_ref: (0, 0, c)),
            scratch_shapes=[pltpu.VMEM((count * rows, total), BF16)],
        ),
        compiler_params=pltpu.CompilerParams(vmem_limit_bytes=40 * 2**20),
        cost_estimate=pl.CostEstimate(
            flops=total * all_rows * tiles * width,
            bytes_accessed=2 * total * (all_rows + tiles * width) + all_rows * tiles * width,
            transcendentals=0,
        ),
        name="gradient",
    )(d.reshape(1).astype(jnp.int32), left, right)


def head_probs(q, k, far, slope):
    scores = lax.dot_general(q, k, (((1,), (1,)), ((), ())), preferred_element_type=F32)
    scores = scores * (HEAD ** (-0.5)) - slope * far
    raised = jnp.exp(scores - jnp.max(scores, axis=-1, keepdims=True))
    return raised * (1.0 / jnp.sum(raised, axis=-1, keepdims=True))


def flat_frames(block):
    sources, _, rows, lanes = block.shape
    if rows % 16 == 0:
        return block.reshape(sources * rows, lanes)
    return block.astype(F32).reshape(sources * rows, lanes).astype(BF16)


def by_source(value, like):
    sources, _, rows, lanes = like
    if rows % 16 == 0:
        return value.astype(BF16).reshape(sources, 1, rows, lanes)
    return value.reshape(sources, 1, rows, lanes).astype(BF16)


def attend(triple, far, slopes):
    dp, micro, rows, wide = triple.shape
    frames = dp * rows
    width = wide // 3
    pairs = width // 128
    shape = (dp, 1, rows, 128)

    def body(slope_ref, q_ref, k_ref, v_ref, far_ref, out_ref):
        h = pl.program_id(1)
        q, k, v = (flat_frames(ref[...]) for ref in (q_ref, k_ref, v_ref))
        first = lax.broadcasted_iota(jnp.int32, (frames, 128), 1) < HEAD
        zero = jnp.zeros_like(q)
        outs = []
        for j, own in enumerate((jnp.where(first, q, zero), jnp.where(first, zero, q))):
            probs = head_probs(own, k, far_ref[0], slope_ref[h * 2 + j])
            outs.append(jnp.dot(probs.astype(BF16), v, preferred_element_type=F32))
        out_ref[...] = by_source(jnp.where(first, outs[0], outs[1]), shape)

    def spec(offset):
        return pl.BlockSpec(shape, lambda m, h, s: (0, m, 0, h + offset))

    return pl.pallas_call(
        body,
        out_shape=jax.ShapeDtypeStruct((dp, micro, rows, width), BF16),
        grid_spec=pltpu.PrefetchScalarGridSpec(
            num_scalar_prefetch=1,
            grid=(micro, pairs),
            in_specs=[
                spec(0),
                spec(pairs),
                spec(2 * pairs),
                pl.BlockSpec((1, frames, frames), lambda m, h, s: (m, 0, 0)),
            ],
            out_specs=spec(0),
        ),
        compiler_params=pltpu.CompilerParams(vmem_limit_bytes=24 * 2**20),
        cost_estimate=pl.CostEstimate(
            flops=8 * micro * frames * frames * width,
            bytes_accessed=8 * micro * frames * width,
            transcendentals=micro * HEADS * frames * frames,
        ),
        name="attend",
    )(slopes, triple, triple, triple, far)


def attend_back(triple, grad, far, slopes):
    dp, micro, rows, wide = triple.shape
    frames = dp * rows
    width = wide // 3
    pairs = width // 128
    shape = (dp, 1, rows, 128)
    scale = HEAD ** (-0.5)

    def turned(left, right):
        return lax.dot_general(left, right, (((0,), (0,)), ((), ())), preferred_element_type=F32)

    def body(slope_ref, q_ref, k_ref, v_ref, g_ref, far_ref, out_ref):
        h = pl.program_id(1)
        q, k, v, g = (flat_frames(ref[...]) for ref in (q_ref, k_ref, v_ref, g_ref))
        first = lax.broadcasted_iota(jnp.int32, (frames, 128), 1) < HEAD
        zero = jnp.zeros_like(q)
        grads = []
        for j in range(2):
            own_q = jnp.where(first, q, zero) if j == 0 else jnp.where(first, zero, q)
            own_g = jnp.where(first, g, zero) if j == 0 else jnp.where(first, zero, g)
            probs = head_probs(own_q, k, far_ref[0], slope_ref[h * 2 + j])
            back = lax.dot_general(own_g, v, (((1,), (1,)), ((), ())), preferred_element_type=F32)
            back = probs * (back - jnp.sum(back * probs, axis=-1, keepdims=True))
            low = back.astype(BF16)
            grads.append(
                (
                    jnp.dot(low, k, preferred_element_type=F32) * scale,
                    turned(low, q) * scale,
                    turned(probs.astype(BF16), g),
                )
            )
        for i in range(3):
            out_ref[i] = by_source(jnp.where(first, grads[0][i], grads[1][i]), shape)

    def spec(offset):
        return pl.BlockSpec(shape, lambda m, h, s: (0, m, 0, h + offset))

    return pl.pallas_call(
        body,
        out_shape=jax.ShapeDtypeStruct((3, dp, micro, rows, width), BF16),
        grid_spec=pltpu.PrefetchScalarGridSpec(
            num_scalar_prefetch=1,
            grid=(micro, pairs),
            in_specs=[
                spec(0),
                spec(pairs),
                spec(2 * pairs),
                spec(0),
                pl.BlockSpec((1, frames, frames), lambda m, h, s: (m, 0, 0)),
            ],
            out_specs=pl.BlockSpec((3,) + shape, lambda m, h, s: (0, 0, m, 0, h)),
        ),
        compiler_params=pltpu.CompilerParams(vmem_limit_bytes=24 * 2**20),
        cost_estimate=pl.CostEstimate(
            flops=20 * micro * frames * frames * width,
            bytes_accessed=14 * micro * frames * width,
            transcendentals=micro * HEADS * frames * frames,
        ),
        name="attend_back",
    )(slopes, triple, triple, triple, grad, far)


class Reduction:
    def __init__(self, left, right, d, dims):
        self.dims = dims
        if right.ndim == 2:
            right = right[None]
        send = gradient_blocks(left, right, d, [0] + dims, 1)
        self.sent = send
        self.got = flip(send, 1)
        self.kept = gradient_blocks(left, after(right, send), d, [0] + dims, 0)
        self.halves = None

    def step(self, ready=None):
        if self.halves is None:
            shape = (2,) * len(self.dims) + self.kept.shape[1:]
            half = self.kept.shape[2] // 2
            whole_keep = self.kept.reshape(shape)
            whole_got = self.got.reshape(shape)
            halves = []
            for column, order in ((0, self.dims), (half, self.dims[::-1])):
                halves.append(
                    (
                        whole_keep[..., column : column + half],
                        whole_got[..., column : column + half],
                        list(order),
                        list(self.dims),
                    )
                )
        else:
            halves = self.halves
        self.halves = []
        tokens = []
        for keep, got, order, left in halves:
            bit = order[0]
            at = left.index(bit)

            def total(index):
                a = lax.index_in_dim(keep, index, at, keepdims=False)
                b = lax.index_in_dim(got, index, at, keepdims=False)
                return (a.astype(F32) + b.astype(F32)).astype(BF16)

            send, stay = total(1), total(0)
            if ready is not None:
                send = after(send, ready)
            tokens.append(send)
            self.halves.append((stay, flip(send, 1 << bit), order[1:], [b for b in left if b != bit]))
        return tokens

    def line(self):
        while self.halves[0][2]:
            self.step()
        pieces = [
            (keep.astype(F32) + got.astype(F32)).astype(BF16) for keep, got, _, _ in self.halves
        ]
        self.value = jnp.concatenate(pieces, axis=1)
        self.stage = 0
        return self.along()

    def along(self):
        rep = lax.axis_size("rep")
        z = lax.axis_index("rep")
        half = rep // 2
        k = self.stage
        self.stage += 1
        value = self.value
        if k < half - 1:
            got = lax.ppermute(value, "rep", [(k, k + 1), (rep - 1 - k, rep - 2 - k)])
            self.value = (value.astype(F32) + got.astype(F32)).astype(BF16)
        elif k == half - 1:
            got = lax.ppermute(value, "rep", [(k, k + 1), (k + 1, k)])
            self.value = (value.astype(F32) + got.astype(F32)).astype(BF16)
        else:
            i = rep - 2 - k
            got = lax.ppermute(value, "rep", [(i + 1, i), (rep - 2 - i, rep - 1 - i)])
            self.value = jnp.where((z == i) | (z == rep - 1 - i), got, value)
        return self.value

    def finish(self):
        while self.stage < lax.axis_size("rep") - 1:
            self.along()
        return self.value.astype(F32)


def matmul(left, right):
    return jnp.dot(left, right, preferred_element_type=F32)


def matmul_nt(left, right):
    return lax.dot_general(left, right, (((1,), (1,)), ((), ())), preferred_element_type=F32)


def matmul_tn(left, right):
    return lax.dot_general(left, right, (((0,), (0,)), ((), ())), preferred_element_type=F32)


def norm_parts(values):
    average = jnp.mean(values, axis=-1, keepdims=True)
    centred = values - average
    spread = jnp.mean(centred * centred, axis=-1, keepdims=True)
    scale = lax.rsqrt(spread + EPS)
    return centred * scale, scale


def norm_back(grad, gain, unit, scale):
    e = grad * gain
    return scale * (
        e
        - jnp.mean(e, axis=-1, keepdims=True)
        - unit * jnp.mean(e * unit, axis=-1, keepdims=True)
    )


def shards(
    inputs,
    skips,
    cotangent,
    dest_slot,
    pack_segments,
    block_live,
    counts,
    w_skip,
    b_skip,
    g_one,
    b_one,
    w_qkv,
    w_out,
    b_out,
    g_two,
    b_two,
    w_up,
    c_up,
    w_down,
    c_down,
):
    dp = lax.axis_size("dp")
    rep = lax.axis_size("rep")
    d = lax.axis_index("dp")
    z = lax.axis_index("rep")
    micro = inputs.shape[0]
    frames = inputs.shape[2]
    width = inputs.shape[3]
    blocks = dest_slot.shape[2]
    block = frames // blocks
    per_pair = blocks // dp
    total = micro * frames
    bits = dp.bit_length() - 1
    place = jnp.stack([z, lax.rem(d, 8)]).astype(jnp.int32)
    dims = list(range(1, bits))
    own_skip = own_chunk(place, width, w_skip)
    own_mid = own_chunk(place, width, w_qkv, w_out)
    own_up = own_chunk(place, width, w_up)
    own_down = own_chunk(place, width, w_down)
    far_skip = fetch_far(own_skip, None)
    moved = far_skip[0]
    far_mid = fetch_far(own_mid, moved)
    parts_skip = spread_pieces(far_skip)
    far_up = fetch_far(own_up, far_mid[0])
    far_mid = [after(far, parts_skip[0][0]) for far in far_mid]
    parts_mid = spread_pieces(far_mid)
    far_down = fetch_far(own_down, far_up[0])
    far_up = [after(far, parts_mid[0][0]) for far in far_up]
    parts_up = spread_pieces(far_up)
    far_down = [after(far, parts_up[0][0]) for far in far_down]
    parts_down = spread_pieces(far_down)
    mid_rows = w_qkv.shape[0] // 8
    full_skip = assemble(w_skip, parts_skip, place, 0, 1)
    full_qkv = assemble(w_qkv, parts_mid, place, 0, 3)
    full_out = assemble(w_out, parts_mid, place, 3 * mid_rows, 1)
    full_up = assemble(w_up, parts_up, place, 0, w_up.shape[1] // width)
    full_down = assemble(w_down, parts_down, place, 0, 1)

    slots = dest_slot[:, 0, :]
    small = jnp.concatenate(
        [slots.reshape(-1), block_live[:, 0, :].reshape(-1), counts.reshape(-1)]
    )
    small, _ = lax.optimization_barrier((small, moved))
    every = small[None]
    for bit in range(bits):
        every = jnp.concatenate([every, flip(every, 1 << bit)], axis=0)
    span = micro * blocks
    all_slots = every[:, :span].reshape(dp, micro, blocks)
    all_live = every[:, span : 2 * span].reshape(dp, micro, blocks)
    source = jnp.bitwise_xor(jnp.arange(dp), d)
    count_total = jnp.sum(every[:, 2 * span]).astype(F32).reshape(1, 1)
    for bit in range(rep.bit_length() - 1):
        count_total = count_total + rep_flip(count_total, 1 << bit)
    share = counts[0, 0].astype(F32) * (dp * rep) / count_total[0, 0]

    rank = jnp.sum(
        (all_slots[:, :, None, :] < all_slots[:, :, :, None]).astype(jnp.int32), axis=3
    )
    mine_rank = jnp.sum((slots[:, None, :] < slots[:, :, None]).astype(jnp.int32), axis=2)
    here = (all_slots // blocks) == d
    arrive = source[:, None, None] * per_pair + rank % per_pair
    arrive = jnp.where(here, arrive, -1)
    match = arrive[None] == jnp.arange(blocks)[:, None, None, None]
    placing = jnp.sum(jnp.where(match, (all_slots % blocks)[None], 0), axis=(1, 3)).T
    pick = placing[:, :, None] == jnp.arange(blocks)[None, None, :]
    seg_blocks = pack_segments[:, 0, :].reshape(micro, blocks, block)
    segment = jnp.sum(jnp.where(pick[..., None], seg_blocks[:, None], 0), axis=2)
    segment = segment.reshape(micro, frames)
    live_count = jnp.sum(jnp.where(pick, block_live[:, 0, None, :], 0), axis=2)
    inner = jnp.arange(frames) % block
    live = inner[None] < jnp.repeat(live_count, block, axis=1)
    position = jnp.repeat(placing * block, block, axis=1) + inner[None]
    flat_live = jnp.transpose(all_live, (1, 0, 2)).reshape(micro, dp * blocks)
    flat_slot = (source[:, None] * blocks + jnp.arange(blocks)).reshape(-1)
    own_live = jnp.sum(jnp.where(slots[:, :, None] == flat_slot, flat_live[:, None], 0), axis=2)
    keep_rows = (inner[None] < jnp.repeat(own_live, block, axis=1)).astype(F32)
    keep_rows = keep_rows.reshape(total, 1)

    target = mine_rank // per_pair
    row = (target * micro + jnp.arange(micro)[:, None]) * per_pair + mine_rank % per_pair
    row = jnp.repeat(row.reshape(-1) * block, block) + jnp.tile(jnp.arange(block), micro * blocks)
    shuffle = (jnp.arange(total)[:, None] == row[None, :]).astype(BF16)

    def to_packs(values):
        sent = matmul(shuffle, values).astype(BF16)
        got = lax.all_to_all(
            sent.reshape(dp, total // dp, width), "dp", split_axis=0, concat_axis=0, tiled=True
        )
        return got.reshape(total, width)

    def to_owners(values):
        sent = values.reshape(dp, total // dp, width)
        got = lax.all_to_all(sent, "dp", split_axis=0, concat_axis=0, tiled=True)
        return matmul_tn(shuffle, got.reshape(total, width))

    joined = jnp.concatenate(
        [inputs.reshape(total, width), skips.reshape(total, width)], axis=1
    )
    base = matmul(joined, full_skip) + b_skip
    unit_one, scale_one = norm_parts(base)
    normed = to_packs((unit_one * g_one + b_one).astype(BF16))
    triple = matmul(normed, full_qkv).astype(BF16)
    triple = triple.reshape(dp, micro, per_pair * block, 3 * width)
    slopes = 2.0 ** (-8.0 * (jnp.arange(HEADS, dtype=F32) + 1.0) / HEADS)
    distance = jnp.abs(position[:, :, None] - position[:, None, :]).astype(F32)
    allowed = (segment[:, :, None] == segment[:, None, :]) & (
        live[:, None, :] | (position[:, :, None] == position[:, None, :])
    )
    far = jnp.where(allowed, distance, 1e32)
    attended = attend(triple, far, slopes)
    attended = to_owners(attended).astype(BF16)
    mixed = base + matmul(attended, full_out) + b_out
    unit_two, scale_two = norm_parts(mixed)
    normed_two = (unit_two * g_two + b_two).astype(BF16)
    hidden = matmul(normed_two, full_up) + c_up
    phi = 0.5 * (1.0 + lax.erf(hidden * (0.5**0.5)))
    active = (hidden * phi).astype(BF16)
    slope = (phi + hidden * jnp.exp(-0.5 * hidden * hidden) * ((2 * jnp.pi) ** -0.5)).astype(BF16)

    scaled = (cotangent.reshape(total, width).astype(F32) * share).astype(BF16)
    grad_result = scaled * keep_rows.astype(BF16)
    red_down = Reduction(active, grad_result, d, dims)
    grad_result = after(grad_result, red_down.kept)
    grad_result_full = grad_result.astype(F32)
    grad_active = matmul_nt(grad_result, full_down)
    grad_hidden = slope.astype(F32) * grad_active
    hidden_low = grad_hidden.astype(BF16)
    red_up = Reduction(normed_two, hidden_low, d, dims)
    tokens = red_down.step()
    hidden_low = after(hidden_low, red_up.kept, *tokens)
    grad_normed_two = matmul_nt(hidden_low, full_up)
    grad_mixed = grad_result_full + norm_back(grad_normed_two, g_two, unit_two, scale_two)
    mixed_low = grad_mixed.astype(BF16)
    red_out = Reduction(attended, mixed_low, d, dims)
    mixed_low = after(mixed_low, red_out.kept)
    tokens = red_up.step()
    grad_attended = to_packs(after(matmul_nt(mixed_low, full_out).astype(BF16), *tokens))
    result = mixed + matmul(active, full_down) + c_down
    output = (result * keep_rows).astype(BF16)
    tokens = red_out.step() + red_down.step()
    grad_attended = after(grad_attended, output, *tokens)
    grad_attended = grad_attended.reshape(dp, micro, per_pair * block, width)
    grad_triple = attend_back(triple, grad_attended, far, slopes).reshape(3, total, width)
    tokens = [red_down.line()] + red_up.step()
    grad_triple = after(grad_triple, *tokens)
    red_qkv = Reduction(normed, grad_triple, d, dims)
    tokens = red_out.step()
    grad_triple = after(grad_triple, red_qkv.kept, *tokens)
    grad_normed = sum(
        matmul_nt(grad_triple[i], full_qkv[:, i * width : (i + 1) * width]) for i in range(3)
    )
    grad_normed = to_owners(grad_normed.astype(BF16))
    tokens = [red_down.along()] + red_qkv.step() + [red_up.line(), red_out.line()]
    grad_normed = after(grad_normed, *tokens)
    grad_base = grad_mixed + norm_back(grad_normed, g_one, unit_one, scale_one)
    base_low = grad_base.astype(BF16)
    red_skip = Reduction(joined, base_low, d, dims)
    tokens = red_qkv.step() + [red_up.along()]
    base_low = after(base_low, red_skip.kept, *tokens)
    grad_joined = matmul_nt(base_low, full_skip).astype(BF16)
    red_skip.step()
    red_qkv.line()
    red_skip.step()
    red_skip.line()
    finals = [red.finish() for red in (red_down, red_up, red_out, red_qkv, red_skip)]
    vectors = (
        jnp.sum(grad_base, axis=0),
        jnp.sum(grad_normed * unit_one, axis=0),
        jnp.sum(grad_normed, axis=0),
        jnp.sum(grad_mixed, axis=0),
        jnp.sum(grad_normed_two * unit_two, axis=0),
        jnp.sum(grad_normed_two, axis=0),
        jnp.sum(grad_hidden, axis=0),
        jnp.sum(grad_result_full, axis=0),
    )
    lengths = [v.shape[0] for v in vectors]
    summed = jnp.concatenate(vectors).reshape(-1, 128)
    for bit in range(bits):
        summed = summed + flip(summed, 1 << bit)
    for bit in range(rep.bit_length() - 1):
        summed = summed + rep_flip(summed, 1 << bit)
    summed = summed.reshape(-1)
    sums = []
    offset = 0
    for length in lengths:
        sums.append(summed[offset : offset + length])
        offset += length

    def as_owned(values):
        return values.reshape(inputs.shape)

    return (
        as_owned(output),
        as_owned(grad_joined[:, :width]),
        as_owned(grad_joined[:, width:]),
        finals[4],
        sums[0],
        sums[1],
        sums[2],
        finals[3],
        finals[2],
        sums[3],
        sums[4],
        sums[5],
        finals[1],
        sums[6],
        finals[0],
        sums[7],
    )


def solution(mesh):
    frames = P(None, "rep", "dp", None)
    slots = P(None, "rep", "dp")
    rows = P("rep", None)
    whole = P()
    in_specs = (
        (frames,) * 3
        + (slots,) * 3
        + (P("dp", "rep"), rows, whole, whole, whole, rows, rows)
        + (whole,) * 3
        + (rows, whole, rows, whole)
    )
    split = P("dp", None)
    out_specs = (
        (frames,) * 3
        + (split,)
        + (whole,) * 3
        + (split, split)
        + (whole,) * 3
        + (split, whole, split, whole)
    )
    return jax.shard_map(shards, mesh=mesh, in_specs=in_specs, out_specs=out_specs, check_vma=False)
```

```python
import jax
import jax.numpy as jnp
from jax import lax
from jax.experimental import pallas as pl
from jax.experimental.pallas import tpu as pltpu
from jax.sharding import PartitionSpec as P

HEADS = 16
HEAD = 64
EPS = 1e-05
F32 = jnp.float32
BF16 = jnp.bfloat16


def flip(value, bit):
    n = lax.axis_size("dp")
    return lax.ppermute(value, "dp", [(i, i ^ bit) for i in range(n)])


def rep_flip(value, bit):
    n = lax.axis_size("rep")
    return lax.ppermute(value, "rep", [(i, i ^ bit) for i in range(n)])


def after(value, *earlier):
    return lax.optimization_barrier((value,) + earlier)[0]


def assemble(w_local, parts, place, row_at, tiles):
    rep = lax.axis_size("rep")
    shard_rows, columns = w_local.shape
    rows = shard_rows // 8
    tile = columns // tiles
    half = tile // 2
    chunk_rows = parts[0][0].shape[0] // (len(parts[0][2]) * (rep - 1))
    arrays = [part[0] for part in parts]
    count = 1 + sum(len(part[2]) for part in parts) * (rep - 1) * tiles

    def body(place_ref, local_ref, *refs):
        out_ref, sems = refs[len(parts)], refs[len(parts) + 1]
        z = place_ref[0]
        e = place_ref[1]
        copies = [
            pltpu.make_async_copy(
                local_ref,
                out_ref.at[pl.ds(pl.multiple_of(z * shard_rows, 16), shard_rows), :],
                sems.at[0],
            )
        ]
        for ref, (_, side, rels) in zip(refs, parts):
            for k, rel in enumerate(rels):
                chunk = jnp.bitwise_xor(e, rel)
                for s in range(1, rep):
                    shard = jnp.bitwise_xor(z, s)
                    start = pl.multiple_of(shard * shard_rows + chunk * rows, 16)
                    for t in range(tiles):
                        at = (k * (rep - 1) + s - 1) * chunk_rows + row_at + t * rows
                        copies.append(
                            pltpu.make_async_copy(
                                ref.at[pl.ds(at, rows), :],
                                out_ref.at[pl.ds(start, rows), pl.ds(t * tile + side * half, half)],
                                sems.at[len(copies)],
                            )
                        )
        for copy in copies:
            copy.start()
        for copy in copies:
            copy.wait()

    return pl.pallas_call(
        body,
        out_shape=jax.ShapeDtypeStruct((shard_rows * rep, columns), w_local.dtype),
        in_specs=[pl.BlockSpec(memory_space=pltpu.SMEM)]
        + [pl.BlockSpec(memory_space=pl.ANY)] * (1 + len(parts)),
        out_specs=pl.BlockSpec(memory_space=pltpu.VMEM),
        scratch_shapes=[pltpu.SemaphoreType.DMA((count,))],
        compiler_params=pltpu.CompilerParams(vmem_limit_bytes=24 * 2**20),
        cost_estimate=pl.CostEstimate(
            flops=0, bytes_accessed=4 * shard_rows * rep * columns, transcendentals=0
        ),
        name="assemble",
    )(place, w_local, *arrays)


def own_chunk(place, width, *shards_local):
    pieces = []
    for w_local in shards_local:
        rows = w_local.shape[0] // 8
        own = lax.dynamic_slice_in_dim(w_local, place[1] * rows, rows, 0)
        for t in range(w_local.shape[1] // width):
            pieces.append(own[:, t * width : (t + 1) * width])
    return jnp.concatenate(pieces, axis=0)


def fetch_far(own, previous):
    rep = lax.axis_size("rep")
    if previous is not None:
        own = after(own, previous)
    pieces = own
    for bit in range(rep.bit_length() - 1):
        pieces = jnp.concatenate([pieces, rep_flip(pieces, 1 << bit)], axis=0)
    return pieces[own.shape[0] :]


def spread_pieces(far, previous):
    half = far.shape[1] // 2
    parts = []
    firsts = []
    if previous is not None:
        far = after(far, *previous)
    for first, second, side in ((2, 4, 0), (4, 2, 1)):
        start = far[:, side * half : (side + 1) * half]
        firsts.append((start, flip(start, first), first, second, side))
    for start, got, first, second, side in firsts:
        pair = jnp.concatenate([start, got], axis=0)
        parts.append((pair, side, [0, first]))
    for pair, (_, _, first, second, side) in zip(list(parts), firsts):
        parts.append((flip(pair[0], second), side, [second, first | second]))
    others = []
    for array, side, rels in parts:
        others.append((flip(array, 1), side, [rel | 1 for rel in rels]))
    return parts + others


def gradient_blocks(left, right, d, order, odd):
    dp = lax.axis_size("dp")
    total, all_rows = left.shape
    tiles, _, width = right.shape
    rows = all_rows // dp
    count = dp // 2
    steps = order[1:]
    tile = min(width, 512)
    split = width // tile

    def distance(p):
        rel = odd
        for k, bit in enumerate(steps):
            rel += ((p >> (len(steps) - 1 - k)) & 1) << bit
        return rel

    if rows % 128 != 0:
        flat = jnp.transpose(right, (1, 0, 2)).reshape(total, tiles * width)
        product = matmul_tn(left, flat).astype(BF16).reshape(dp, rows, tiles * width)
        rel = jnp.array([distance(p) for p in range(count)], jnp.int32)
        return product[jnp.bitwise_xor(rel, d)]

    def body(d_ref, left_ref, right_ref, out_ref, turned_ref):
        @pl.when(pl.program_id(0) == 0)
        def _():
            for p in range(count):
                at = pl.multiple_of(jnp.bitwise_xor(d_ref[0], distance(p)) * rows, 128)
                turned_ref[pl.ds(p * rows, rows), :] = left_ref[:, pl.ds(at, rows)].T

        step = min(count * rows, 512)
        for r in range(count * rows // step):
            product = jnp.dot(
                turned_ref[pl.ds(r * step, step), :], right_ref[0], preferred_element_type=F32
            ).astype(BF16)
            for q in range(max(step // rows, 1)):
                size = min(rows, step)
                at = r * step + q * size
                out_ref[at // rows, pl.ds(at % rows, size), :] = product[q * size : (q + 1) * size]

    return pl.pallas_call(
        body,
        out_shape=jax.ShapeDtypeStruct((count, rows, tiles * width), BF16),
        grid_spec=pltpu.PrefetchScalarGridSpec(
            num_scalar_prefetch=1,
            grid=(tiles * split,),
            in_specs=[
                pl.BlockSpec((total, all_rows), lambda c, d_ref: (0, 0)),
                pl.BlockSpec((1, total, tile), lambda c, d_ref: (c // split, 0, c % split)),
            ],
            out_specs=pl.BlockSpec((count, rows, tile), lambda c, d_ref: (0, 0, c)),
            scratch_shapes=[pltpu.VMEM((count * rows, total), BF16)],
        ),
        compiler_params=pltpu.CompilerParams(vmem_limit_bytes=40 * 2**20),
        cost_estimate=pl.CostEstimate(
            flops=total * all_rows * tiles * width,
            bytes_accessed=2 * total * (all_rows + tiles * width) + all_rows * tiles * width,
            transcendentals=0,
        ),
        name="gradient",
    )(d.reshape(1).astype(jnp.int32), left, right)


def head_probs(q, k, far, slope):
    scores = lax.dot_general(q, k, (((1,), (1,)), ((), ())), preferred_element_type=F32)
    scores = scores * (HEAD ** (-0.5)) - slope * far
    raised = jnp.exp(scores - jnp.max(scores, axis=-1, keepdims=True))
    return raised * (1.0 / jnp.sum(raised, axis=-1, keepdims=True))


def flat_frames(block):
    sources, _, rows, lanes = block.shape
    if rows % 16 == 0:
        return block.reshape(sources * rows, lanes)
    return block.astype(F32).reshape(sources * rows, lanes).astype(BF16)


def by_source(value, like):
    sources, _, rows, lanes = like
    if rows % 16 == 0:
        return value.astype(BF16).reshape(sources, 1, rows, lanes)
    return value.reshape(sources, 1, rows, lanes).astype(BF16)


def attend(triple, far, slopes):
    dp, micro, rows, wide = triple.shape
    frames = dp * rows
    width = wide // 3
    pairs = width // 128
    shape = (dp, 1, rows, 128)

    def body(slope_ref, q_ref, k_ref, v_ref, far_ref, out_ref):
        h = pl.program_id(1)
        q, k, v = (flat_frames(ref[...]) for ref in (q_ref, k_ref, v_ref))
        first = lax.broadcasted_iota(jnp.int32, (frames, 128), 1) < HEAD
        zero = jnp.zeros_like(q)
        outs = []
        for j, own in enumerate((jnp.where(first, q, zero), jnp.where(first, zero, q))):
            probs = head_probs(own, k, far_ref[0], slope_ref[h * 2 + j])
            outs.append(jnp.dot(probs.astype(BF16), v, preferred_element_type=F32))
        out_ref[...] = by_source(jnp.where(first, outs[0], outs[1]), shape)

    def spec(offset):
        return pl.BlockSpec(shape, lambda m, h, s: (0, m, 0, h + offset))

    return pl.pallas_call(
        body,
        out_shape=jax.ShapeDtypeStruct((dp, micro, rows, width), BF16),
        grid_spec=pltpu.PrefetchScalarGridSpec(
            num_scalar_prefetch=1,
            grid=(micro, pairs),
            in_specs=[
                spec(0),
                spec(pairs),
                spec(2 * pairs),
                pl.BlockSpec((1, frames, frames), lambda m, h, s: (m, 0, 0)),
            ],
            out_specs=spec(0),
        ),
        compiler_params=pltpu.CompilerParams(vmem_limit_bytes=24 * 2**20),
        cost_estimate=pl.CostEstimate(
            flops=8 * micro * frames * frames * width,
            bytes_accessed=8 * micro * frames * width,
            transcendentals=micro * HEADS * frames * frames,
        ),
        name="attend",
    )(slopes, triple, triple, triple, far)


def attend_back(triple, grad, far, slopes):
    dp, micro, rows, wide = triple.shape
    frames = dp * rows
    width = wide // 3
    pairs = width // 128
    shape = (dp, 1, rows, 128)
    scale = HEAD ** (-0.5)

    def turned(left, right):
        return lax.dot_general(left, right, (((0,), (0,)), ((), ())), preferred_element_type=F32)

    def body(slope_ref, q_ref, k_ref, v_ref, g_ref, far_ref, out_ref):
        h = pl.program_id(1)
        q, k, v, g = (flat_frames(ref[...]) for ref in (q_ref, k_ref, v_ref, g_ref))
        first = lax.broadcasted_iota(jnp.int32, (frames, 128), 1) < HEAD
        zero = jnp.zeros_like(q)
        grads = []
        for j in range(2):
            own_q = jnp.where(first, q, zero) if j == 0 else jnp.where(first, zero, q)
            own_g = jnp.where(first, g, zero) if j == 0 else jnp.where(first, zero, g)
            probs = head_probs(own_q, k, far_ref[0], slope_ref[h * 2 + j])
            back = lax.dot_general(own_g, v, (((1,), (1,)), ((), ())), preferred_element_type=F32)
            back = probs * (back - jnp.sum(back * probs, axis=-1, keepdims=True))
            low = back.astype(BF16)
            grads.append(
                (
                    jnp.dot(low, k, preferred_element_type=F32) * scale,
                    turned(low, q) * scale,
                    turned(probs.astype(BF16), g),
                )
            )
        for i in range(3):
            out_ref[i] = by_source(jnp.where(first, grads[0][i], grads[1][i]), shape)

    def spec(offset):
        return pl.BlockSpec(shape, lambda m, h, s: (0, m, 0, h + offset))

    return pl.pallas_call(
        body,
        out_shape=jax.ShapeDtypeStruct((3, dp, micro, rows, width), BF16),
        grid_spec=pltpu.PrefetchScalarGridSpec(
            num_scalar_prefetch=1,
            grid=(micro, pairs),
            in_specs=[
                spec(0),
                spec(pairs),
                spec(2 * pairs),
                spec(0),
                pl.BlockSpec((1, frames, frames), lambda m, h, s: (m, 0, 0)),
            ],
            out_specs=pl.BlockSpec((3,) + shape, lambda m, h, s: (0, 0, m, 0, h)),
        ),
        compiler_params=pltpu.CompilerParams(vmem_limit_bytes=24 * 2**20),
        cost_estimate=pl.CostEstimate(
            flops=20 * micro * frames * frames * width,
            bytes_accessed=14 * micro * frames * width,
            transcendentals=micro * HEADS * frames * frames,
        ),
        name="attend_back",
    )(slopes, triple, triple, triple, grad, far)


class Reduction:
    def __init__(self, left, right, d, dims):
        self.dims = dims
        if right.ndim == 2:
            right = right[None]
        send = gradient_blocks(left, right, d, [0] + dims, 1)
        self.sent = send
        self.got = flip(send, 1)
        self.kept = gradient_blocks(left, after(right, send), d, [0] + dims, 0)
        self.halves = None

    def step(self, ready=None):
        if self.halves is None:
            shape = (2,) * len(self.dims) + self.kept.shape[1:]
            half = self.kept.shape[2] // 2
            whole_keep = self.kept.reshape(shape)
            whole_got = self.got.reshape(shape)
            halves = []
            for column, order in ((0, self.dims), (half, self.dims[::-1])):
                halves.append(
                    (
                        whole_keep[..., column : column + half],
                        whole_got[..., column : column + half],
                        list(order),
                        list(self.dims),
                    )
                )
        else:
            halves = self.halves
        self.halves = []
        tokens = []
        for keep, got, order, left in halves:
            bit = order[0]
            at = left.index(bit)

            def total(index):
                a = lax.index_in_dim(keep, index, at, keepdims=False)
                b = lax.index_in_dim(got, index, at, keepdims=False)
                return (a.astype(F32) + b.astype(F32)).astype(BF16)

            send, stay = total(1), total(0)
            if ready is not None:
                send = after(send, *ready)
            tokens.append(send)
            self.halves.append((stay, flip(send, 1 << bit), order[1:], [b for b in left if b != bit]))
        self.arrived = [half[1] for half in self.halves]
        return tokens

    def line(self):
        while self.halves[0][2]:
            self.step()
        pieces = [
            (keep.astype(F32) + got.astype(F32)).astype(BF16) for keep, got, _, _ in self.halves
        ]
        self.value = jnp.concatenate(pieces, axis=1)
        self.stage = 0
        return self.along()

    def along(self):
        rep = lax.axis_size("rep")
        z = lax.axis_index("rep")
        half = rep // 2
        k = self.stage
        self.stage += 1
        value = self.value
        if k < half - 1:
            got = lax.ppermute(value, "rep", [(k, k + 1), (rep - 1 - k, rep - 2 - k)])
            self.value = (value.astype(F32) + got.astype(F32)).astype(BF16)
        elif k == half - 1:
            got = lax.ppermute(value, "rep", [(k, k + 1), (k + 1, k)])
            self.value = (value.astype(F32) + got.astype(F32)).astype(BF16)
        else:
            i = rep - 2 - k
            got = lax.ppermute(value, "rep", [(i + 1, i), (rep - 2 - i, rep - 1 - i)])
            self.value = jnp.where((z == i) | (z == rep - 1 - i), got, value)
        return self.value

    def finish(self):
        while self.stage < lax.axis_size("rep") - 1:
            self.along()
        return self.value.astype(F32)


def matmul(left, right):
    return jnp.dot(left, right, preferred_element_type=F32)


def matmul_nt(left, right):
    return lax.dot_general(left, right, (((1,), (1,)), ((), ())), preferred_element_type=F32)


def matmul_tn(left, right):
    return lax.dot_general(left, right, (((0,), (0,)), ((), ())), preferred_element_type=F32)


def norm_parts(values):
    average = jnp.mean(values, axis=-1, keepdims=True)
    centred = values - average
    spread = jnp.mean(centred * centred, axis=-1, keepdims=True)
    scale = lax.rsqrt(spread + EPS)
    return centred * scale, scale


def norm_back(grad, gain, unit, scale):
    e = grad * gain
    return scale * (
        e
        - jnp.mean(e, axis=-1, keepdims=True)
        - unit * jnp.mean(e * unit, axis=-1, keepdims=True)
    )


def shards(
    inputs,
    skips,
    cotangent,
    dest_slot,
    pack_segments,
    block_live,
    counts,
    w_skip,
    b_skip,
    g_one,
    b_one,
    w_qkv,
    w_out,
    b_out,
    g_two,
    b_two,
    w_up,
    c_up,
    w_down,
    c_down,
):
    dp = lax.axis_size("dp")
    rep = lax.axis_size("rep")
    d = lax.axis_index("dp")
    z = lax.axis_index("rep")
    micro = inputs.shape[0]
    frames = inputs.shape[2]
    width = inputs.shape[3]
    blocks = dest_slot.shape[2]
    block = frames // blocks
    per_pair = blocks // dp
    total = micro * frames
    bits = dp.bit_length() - 1
    place = jnp.stack([z, lax.rem(d, 8)]).astype(jnp.int32)
    dims = list(range(1, bits))
    own_skip = own_chunk(place, width, w_skip)
    own_mid = own_chunk(place, width, w_qkv, w_out)
    own_up = own_chunk(place, width, w_up)
    own_down = own_chunk(place, width, w_down)
    far_skip = fetch_far(own_skip, None)
    far_mid = fetch_far(own_mid, far_skip)
    far_up = fetch_far(own_up, far_mid)
    far_down = fetch_far(own_down, far_up)
    parts_skip = spread_pieces(far_skip, None)
    parts_mid = spread_pieces(far_mid, [part[0] for part in parts_skip[2:4]])
    parts_up = spread_pieces(far_up, [part[0] for part in parts_mid[2:4]])
    parts_down = spread_pieces(far_down, [part[0] for part in parts_up[2:4]])
    moved = parts_skip[0][0]
    mid_rows = w_qkv.shape[0] // 8
    full_skip = assemble(w_skip, parts_skip, place, 0, 1)
    full_qkv = assemble(w_qkv, parts_mid, place, 0, 3)
    full_out = assemble(w_out, parts_mid, place, 3 * mid_rows, 1)
    full_up = assemble(w_up, parts_up, place, 0, w_up.shape[1] // width)
    full_down = assemble(w_down, parts_down, place, 0, 1)

    slots = dest_slot[:, 0, :]
    small = jnp.concatenate(
        [slots.reshape(-1), block_live[:, 0, :].reshape(-1), counts.reshape(-1)]
    )
    small, _ = lax.optimization_barrier((small, moved))
    every = small[None]
    for bit in range(bits):
        every = jnp.concatenate([every, flip(every, 1 << bit)], axis=0)
    span = micro * blocks
    all_slots = every[:, :span].reshape(dp, micro, blocks)
    all_live = every[:, span : 2 * span].reshape(dp, micro, blocks)
    source = jnp.bitwise_xor(jnp.arange(dp), d)
    count_total = jnp.sum(every[:, 2 * span]).astype(F32).reshape(1, 1)
    for bit in range(rep.bit_length() - 1):
        count_total = count_total + rep_flip(count_total, 1 << bit)
    share = counts[0, 0].astype(F32) * (dp * rep) / count_total[0, 0]

    rank = jnp.sum(
        (all_slots[:, :, None, :] < all_slots[:, :, :, None]).astype(jnp.int32), axis=3
    )
    mine_rank = jnp.sum((slots[:, None, :] < slots[:, :, None]).astype(jnp.int32), axis=2)
    here = (all_slots // blocks) == d
    arrive = source[:, None, None] * per_pair + rank % per_pair
    arrive = jnp.where(here, arrive, -1)
    match = arrive[None] == jnp.arange(blocks)[:, None, None, None]
    placing = jnp.sum(jnp.where(match, (all_slots % blocks)[None], 0), axis=(1, 3)).T
    pick = placing[:, :, None] == jnp.arange(blocks)[None, None, :]
    seg_blocks = pack_segments[:, 0, :].reshape(micro, blocks, block)
    segment = jnp.sum(jnp.where(pick[..., None], seg_blocks[:, None], 0), axis=2)
    segment = segment.reshape(micro, frames)
    live_count = jnp.sum(jnp.where(pick, block_live[:, 0, None, :], 0), axis=2)
    inner = jnp.arange(frames) % block
    live = inner[None] < jnp.repeat(live_count, block, axis=1)
    position = jnp.repeat(placing * block, block, axis=1) + inner[None]
    flat_live = jnp.transpose(all_live, (1, 0, 2)).reshape(micro, dp * blocks)
    flat_slot = (source[:, None] * blocks + jnp.arange(blocks)).reshape(-1)
    own_live = jnp.sum(jnp.where(slots[:, :, None] == flat_slot, flat_live[:, None], 0), axis=2)
    keep_rows = (inner[None] < jnp.repeat(own_live, block, axis=1)).astype(F32)
    keep_rows = keep_rows.reshape(total, 1)

    target = mine_rank // per_pair
    row = (target * micro + jnp.arange(micro)[:, None]) * per_pair + mine_rank % per_pair
    row = jnp.repeat(row.reshape(-1) * block, block) + jnp.tile(jnp.arange(block), micro * blocks)
    shuffle = (jnp.arange(total)[:, None] == row[None, :]).astype(BF16)

    def to_packs(values):
        sent = matmul(shuffle, values).astype(BF16)
        got = lax.all_to_all(
            sent.reshape(dp, total // dp, width), "dp", split_axis=0, concat_axis=0, tiled=True
        )
        return got.reshape(total, width)

    def to_owners(values):
        sent = values.reshape(dp, total // dp, width)
        got = lax.all_to_all(sent, "dp", split_axis=0, concat_axis=0, tiled=True)
        return matmul_tn(shuffle, got.reshape(total, width))

    joined = jnp.concatenate(
        [inputs.reshape(total, width), skips.reshape(total, width)], axis=1
    )
    base = matmul(joined, full_skip) + b_skip
    unit_one, scale_one = norm_parts(base)
    normed = to_packs((unit_one * g_one + b_one).astype(BF16))
    triple = matmul(after(normed, far_up), full_qkv).astype(BF16)
    triple = triple.reshape(dp, micro, per_pair * block, 3 * width)
    slopes = 2.0 ** (-8.0 * (jnp.arange(HEADS, dtype=F32) + 1.0) / HEADS)
    distance = jnp.abs(position[:, :, None] - position[:, None, :]).astype(F32)
    allowed = (segment[:, :, None] == segment[:, None, :]) & (
        live[:, None, :] | (position[:, :, None] == position[:, None, :])
    )
    far = jnp.where(allowed, distance, 1e32)
    attended = after(attend(triple, far, slopes), far_down)
    attended = to_owners(attended).astype(BF16)
    mixed = base + matmul(attended, full_out) + b_out
    unit_two, scale_two = norm_parts(mixed)
    normed_two = (unit_two * g_two + b_two).astype(BF16)
    normed_two = after(normed_two, parts_down[0][0], parts_down[1][0])
    hidden = matmul(normed_two, full_up) + c_up
    phi = 0.5 * (1.0 + lax.erf(hidden * (0.5**0.5)))
    active = (hidden * phi).astype(BF16)
    slope = (phi + hidden * jnp.exp(-0.5 * hidden * hidden) * ((2 * jnp.pi) ** -0.5)).astype(BF16)

    scaled = (cotangent.reshape(total, width).astype(F32) * share).astype(BF16)
    grad_result = scaled * keep_rows.astype(BF16)
    red_down = Reduction(active, grad_result, d, dims)
    grad_result = after(grad_result, red_down.kept)
    grad_result_full = grad_result.astype(F32)
    grad_active = matmul_nt(grad_result, full_down)
    grad_hidden = slope.astype(F32) * grad_active
    hidden_low = grad_hidden.astype(BF16)
    tokens = red_down.step()
    down_one = red_down.arrived
    hidden_low = after(hidden_low, *tokens)
    red_up = Reduction(normed_two, hidden_low, d, dims)
    hidden_low = after(hidden_low, red_up.kept)
    grad_normed_two = matmul_nt(hidden_low, full_up)
    grad_mixed = grad_result_full + norm_back(grad_normed_two, g_two, unit_two, scale_two)
    mixed_low = grad_mixed.astype(BF16)
    red_out = Reduction(attended, mixed_low, d, dims)
    mixed_low = after(mixed_low, red_out.kept)
    tokens = red_up.step()
    up_one = red_up.arrived
    grad_attended = to_packs(after(matmul_nt(mixed_low, full_out).astype(BF16), *tokens))
    active_late = after(active, mixed_low)
    result = mixed + matmul(active_late, full_down) + c_down
    output = (result * keep_rows).astype(BF16)
    tokens = red_down.step()
    down_two = red_down.arrived
    grad_attended = after(grad_attended, output, *tokens)
    grad_attended = grad_attended.reshape(dp, micro, per_pair * block, width)
    grad_triple = attend_back(triple, grad_attended, far, slopes).reshape(3, total, width)
    tokens = red_out.step(up_one) + red_up.step(down_two)
    out_one, up_two = red_out.arrived, red_up.arrived
    grad_triple = after(grad_triple, *tokens)
    red_qkv = Reduction(normed, grad_triple, d, dims)
    grad_triple = after(grad_triple, red_qkv.kept, red_down.line())
    grad_normed = sum(
        matmul_nt(grad_triple[i], full_qkv[:, i * width : (i + 1) * width]) for i in range(3)
    )
    grad_normed = to_owners(grad_normed.astype(BF16))
    tokens = red_out.step(out_one) + red_qkv.step(up_two) + [red_up.line(), red_down.along()]
    out_two, qkv_one = red_out.arrived, red_qkv.arrived
    grad_normed = after(grad_normed, *tokens)
    grad_base = grad_mixed + norm_back(grad_normed, g_one, unit_one, scale_one)
    base_low = grad_base.astype(BF16)
    red_skip = Reduction(joined, base_low, d, dims)
    base_low = after(base_low, red_skip.kept)
    red_down.value = after(red_down.value, red_skip.kept)
    red_up.value = after(red_up.value, red_skip.kept)
    tokens = red_qkv.step(out_two) + red_skip.step(qkv_one)
    base_low = after(base_low, *tokens)
    grad_joined = matmul_nt(base_low, full_skip).astype(BF16)
    qkv_two = red_qkv.arrived
    red_out.line()
    red_skip.step(qkv_two)
    red_qkv.line()
    red_skip.line()
    finals = [red.finish() for red in (red_down, red_up, red_out, red_qkv, red_skip)]
    vectors = (
        jnp.sum(grad_base, axis=0),
        jnp.sum(grad_normed * unit_one, axis=0),
        jnp.sum(grad_normed, axis=0),
        jnp.sum(grad_mixed, axis=0),
        jnp.sum(grad_normed_two * unit_two, axis=0),
        jnp.sum(grad_normed_two, axis=0),
        jnp.sum(grad_hidden, axis=0),
        jnp.sum(grad_result_full, axis=0),
    )
    lengths = [v.shape[0] for v in vectors]
    summed = jnp.concatenate(vectors).reshape(-1, 128)
    for bit in range(bits):
        summed = summed + flip(summed, 1 << bit)
    for bit in range(rep.bit_length() - 1):
        summed = summed + rep_flip(summed, 1 << bit)
    summed = summed.reshape(-1)
    sums = []
    offset = 0
    for length in lengths:
        sums.append(summed[offset : offset + length])
        offset += length

    def as_owned(values):
        return values.reshape(inputs.shape)

    return (
        as_owned(output),
        as_owned(grad_joined[:, :width]),
        as_owned(grad_joined[:, width:]),
        finals[4],
        sums[0],
        sums[1],
        sums[2],
        finals[3],
        finals[2],
        sums[3],
        sums[4],
        sums[5],
        finals[1],
        sums[6],
        finals[0],
        sums[7],
    )


def solution(mesh):
    frames = P(None, "rep", "dp", None)
    slots = P(None, "rep", "dp")
    rows = P("rep", None)
    whole = P()
    in_specs = (
        (frames,) * 3
        + (slots,) * 3
        + (P("dp", "rep"), rows, whole, whole, whole, rows, rows)
        + (whole,) * 3
        + (rows, whole, rows, whole)
    )
    split = P("dp", None)
    out_specs = (
        (frames,) * 3
        + (split,)
        + (whole,) * 3
        + (split, split)
        + (whole,) * 3
        + (split, whole, split, whole)
    )
    return jax.shard_map(shards, mesh=mesh, in_specs=in_specs, out_specs=out_specs, check_vma=False)
```

```python
import jax
import jax.numpy as jnp
from jax import lax
from jax.experimental import pallas as pl
from jax.experimental.pallas import tpu as pltpu
from jax.sharding import PartitionSpec as P

HEADS = 16
HEAD = 64
EPS = 1e-05
F32 = jnp.float32
BF16 = jnp.bfloat16


def flip(value, bit):
    n = lax.axis_size("dp")
    return lax.ppermute(value, "dp", [(i, i ^ bit) for i in range(n)])


def rep_flip(value, bit):
    n = lax.axis_size("rep")
    return lax.ppermute(value, "rep", [(i, i ^ bit) for i in range(n)])


def after(value, *earlier):
    return lax.optimization_barrier((value,) + earlier)[0]


def assemble(w_local, parts, place, row_at, tiles):
    rep = lax.axis_size("rep")
    shard_rows, columns = w_local.shape
    rows = shard_rows // 8
    tile = columns // tiles
    half = tile // 2
    chunk_rows = parts[0][0].shape[0] // (len(parts[0][2]) * (rep - 1))
    arrays = [part[0] for part in parts]
    count = 1 + sum(len(part[2]) for part in parts) * (rep - 1) * tiles

    def body(place_ref, local_ref, *refs):
        out_ref, sems = refs[len(parts)], refs[len(parts) + 1]
        z = place_ref[0]
        e = place_ref[1]
        copies = [
            pltpu.make_async_copy(
                local_ref,
                out_ref.at[pl.ds(pl.multiple_of(z * shard_rows, 16), shard_rows), :],
                sems.at[0],
            )
        ]
        for ref, (_, side, rels) in zip(refs, parts):
            for k, rel in enumerate(rels):
                chunk = jnp.bitwise_xor(e, rel)
                for s, apart in enumerate(far_order(rep), 1):
                    shard = jnp.bitwise_xor(z, apart)
                    start = pl.multiple_of(shard * shard_rows + chunk * rows, 16)
                    for t in range(tiles):
                        at = (k * (rep - 1) + s - 1) * chunk_rows + row_at + t * rows
                        copies.append(
                            pltpu.make_async_copy(
                                ref.at[pl.ds(at, rows), :],
                                out_ref.at[pl.ds(start, rows), pl.ds(t * tile + side * half, half)],
                                sems.at[len(copies)],
                            )
                        )
        for copy in copies:
            copy.start()
        for copy in copies:
            copy.wait()

    return pl.pallas_call(
        body,
        out_shape=jax.ShapeDtypeStruct((shard_rows * rep, columns), w_local.dtype),
        in_specs=[pl.BlockSpec(memory_space=pltpu.SMEM)]
        + [pl.BlockSpec(memory_space=pl.ANY)] * (1 + len(parts)),
        out_specs=pl.BlockSpec(memory_space=pltpu.VMEM),
        scratch_shapes=[pltpu.SemaphoreType.DMA((count,))],
        compiler_params=pltpu.CompilerParams(vmem_limit_bytes=24 * 2**20),
        cost_estimate=pl.CostEstimate(
            flops=0, bytes_accessed=4 * shard_rows * rep * columns, transcendentals=0
        ),
        name="assemble",
    )(place, w_local, *arrays)


def own_chunk(place, width, *shards_local):
    pieces = []
    for w_local in shards_local:
        rows = w_local.shape[0] // 8
        own = lax.dynamic_slice_in_dim(w_local, place[1] * rows, rows, 0)
        for t in range(w_local.shape[1] // width):
            pieces.append(own[:, t * width : (t + 1) * width])
    return jnp.concatenate(pieces, axis=0)


def fetch_far(own, previous):
    rep = lax.axis_size("rep")
    if previous is not None:
        own = after(own, previous)
    pieces = own
    first = None
    for bit in reversed(range(rep.bit_length() - 1)):
        got = rep_flip(pieces, 1 << bit)
        first = got if first is None else first
        pieces = jnp.concatenate([pieces, got], axis=0)
    return pieces[own.shape[0] :], first


def far_order(rep):
    order = [0]
    for bit in reversed(range(rep.bit_length() - 1)):
        order = order + [distance ^ (1 << bit) for distance in order]
    return order[1:]


def spread_pieces(far, previous):
    half = far.shape[1] // 2
    parts = []
    firsts = []
    if previous is not None:
        far = after(far, *previous)
    for first, second, side in ((2, 4, 0), (4, 2, 1)):
        start = far[:, side * half : (side + 1) * half]
        firsts.append((start, flip(start, first), first, second, side))
    for start, got, first, second, side in firsts:
        pair = jnp.concatenate([start, got], axis=0)
        parts.append((pair, side, [0, first]))
    for pair, (_, _, first, second, side) in zip(list(parts), firsts):
        parts.append((flip(pair[0], second), side, [second, first | second]))
    others = []
    for array, side, rels in parts:
        others.append((flip(array, 1), side, [rel | 1 for rel in rels]))
    return parts + others


def gradient_blocks(pairs, d, dims, got=None):
    dp = lax.axis_size("dp")
    total, all_rows = pairs[0][0].shape
    width = pairs[0][1].shape[2]
    tiles = [right.shape[0] for _, right in pairs]
    columns = sum(tiles) * width
    rows = all_rows // dp
    count = dp // 2
    odd = 1 if got is None else 0
    tile = min(width, 512)
    split = width // tile
    steps = sum(tiles) * split
    starts = [sum(tiles[:i]) * split for i in range(len(tiles))]

    def distance(p):
        rel = odd
        for k, bit in enumerate(dims):
            rel += ((p >> (len(dims) - 1 - k)) & 1) << bit
        return rel

    upper = [p for p in range(count) if p >= count // 2]
    lower = [p for p in range(count) if p < count // 2]
    odds = [p for p in range(count) if p % 2 == 1]
    evens = [p for p in range(count) if p % 2 == 0]
    chosen = (upper, lower, odds, evens)

    if rows % 128 != 0:
        products = []
        for left, right in pairs:
            flat = jnp.transpose(right, (1, 0, 2)).reshape(total, -1)
            products.append(matmul_tn(left, flat))
        product = jnp.concatenate(products, axis=1).reshape(dp, rows, columns)
        rel = jnp.array([distance(p) for p in range(count)], jnp.int32)
        product = product[jnp.bitwise_xor(rel, d)]
        if got is None:
            return product.astype(BF16)
        product = (product + got.astype(F32)).astype(BF16)
        half = columns // 2
        return [
            jnp.stack([product[p, :, side * half : (side + 1) * half] for p in ps])
            for side, ps in zip((0, 0, 1, 1), chosen)
        ]

    def body(d_ref, *refs):
        lefts = refs[: len(pairs)]
        rights = refs[len(pairs) : 2 * len(pairs)]
        rest = refs[2 * len(pairs) :]
        turned_ref = rest[-1]
        got_ref = None if got is None else rest[0]
        outs = rest[:-1] if got is None else rest[1:-1]
        c = pl.program_id(0)

        @pl.when(c == 0)
        def _():
            for i, left_ref in enumerate(lefts):
                for p in range(count):
                    at = pl.multiple_of(jnp.bitwise_xor(d_ref[0], distance(p)) * rows, 128)
                    turned_ref[i, pl.ds(p * rows, rows), :] = left_ref[:, pl.ds(at, rows)].T

        def piece(i, p):
            return jnp.dot(
                turned_ref[i, pl.ds(p * rows, rows), :], rights[i][0], preferred_element_type=F32
            )

        def write(i, half):
            for p in range(count):
                value = piece(i, p)
                if got is None:
                    outs[0][p] = value.astype(BF16)
                    continue
                value = (value + got_ref[p].astype(F32)).astype(BF16)
                for which in (2 * half, 2 * half + 1):
                    if p in chosen[which]:
                        outs[which][chosen[which].index(p)] = value

        for i in range(len(pairs)):
            for half in (0, 1):
                low = max(starts[i], half * (steps // 2))
                high = min(starts[i] + tiles[i] * split, (half + 1) * (steps // 2))
                if low < high:
                    pl.when((c >= low) & (c < high))(lambda i=i, half=half: write(i, half))

    def right_spec(start, n):
        def at(c, d_ref):
            k = jnp.clip(c - start, 0, n * split - 1)
            return (lax.div(k, jnp.int32(split)), 0, lax.rem(k, jnp.int32(split)))

        return pl.BlockSpec((1, total, tile), at)

    in_specs = [pl.BlockSpec((total, all_rows), lambda c, d_ref: (0, 0))] * len(pairs)
    in_specs += [right_spec(start, n) for start, n in zip(starts, tiles)]
    args = [left for left, _ in pairs] + [right for _, right in pairs]
    if got is None:
        out_shape = jax.ShapeDtypeStruct((count, rows, columns), BF16)
        out_specs = pl.BlockSpec((count, rows, tile), lambda c, d_ref: (0, 0, c))
    else:
        in_specs.append(pl.BlockSpec((count, rows, tile), lambda c, d_ref: (0, 0, c)))
        args.append(got)
        out_shape = [jax.ShapeDtypeStruct((count // 2, rows, columns // 2), BF16)] * 4
        mid = steps // 2
        first = pl.BlockSpec(
            (count // 2, rows, tile), lambda c, d_ref: (0, 0, jnp.minimum(c, mid - 1))
        )
        second = pl.BlockSpec(
            (count // 2, rows, tile), lambda c, d_ref: (0, 0, jnp.maximum(c - mid, 0))
        )
        out_specs = [first, first, second, second]
    return pl.pallas_call(
        body,
        out_shape=out_shape,
        grid_spec=pltpu.PrefetchScalarGridSpec(
            num_scalar_prefetch=1,
            grid=(steps,),
            in_specs=in_specs,
            out_specs=out_specs,
            scratch_shapes=[pltpu.VMEM((len(pairs), count * rows, total), BF16)],
        ),
        compiler_params=pltpu.CompilerParams(vmem_limit_bytes=40 * 2**20),
        cost_estimate=pl.CostEstimate(
            flops=total * all_rows * columns,
            bytes_accessed=2 * total * (all_rows + columns) + 2 * all_rows * columns,
            transcendentals=0,
        ),
        name="gradient",
    )(d.reshape(1).astype(jnp.int32), *args)


def head_probs(q, k, far, slope):
    scores = lax.dot_general(q, k, (((1,), (1,)), ((), ())), preferred_element_type=F32)
    scores = scores * (HEAD ** (-0.5)) - slope * far
    raised = jnp.exp(scores - jnp.max(scores, axis=-1, keepdims=True))
    return raised * (1.0 / jnp.sum(raised, axis=-1, keepdims=True))


def flat_frames(block):
    sources, _, rows, lanes = block.shape
    if rows % 16 == 0:
        return block.reshape(sources * rows, lanes)
    return block.astype(F32).reshape(sources * rows, lanes).astype(BF16)


def by_source(value, like):
    sources, _, rows, lanes = like
    if rows % 16 == 0:
        return value.astype(BF16).reshape(sources, 1, rows, lanes)
    return value.reshape(sources, 1, rows, lanes).astype(BF16)


def attend(triple, far, slopes):
    dp, micro, rows, wide = triple.shape
    frames = dp * rows
    width = wide // 3
    pairs = width // 128
    shape = (dp, 1, rows, 128)

    def body(slope_ref, q_ref, k_ref, v_ref, far_ref, out_ref):
        h = pl.program_id(1)
        q, k, v = (flat_frames(ref[...]) for ref in (q_ref, k_ref, v_ref))
        first = lax.broadcasted_iota(jnp.int32, (frames, 128), 1) < HEAD
        zero = jnp.zeros_like(q)
        outs = []
        for j, own in enumerate((jnp.where(first, q, zero), jnp.where(first, zero, q))):
            probs = head_probs(own, k, far_ref[0], slope_ref[h * 2 + j])
            outs.append(jnp.dot(probs.astype(BF16), v, preferred_element_type=F32))
        out_ref[...] = by_source(jnp.where(first, outs[0], outs[1]), shape)

    def spec(offset):
        return pl.BlockSpec(shape, lambda m, h, s: (0, m, 0, h + offset))

    return pl.pallas_call(
        body,
        out_shape=jax.ShapeDtypeStruct((dp, micro, rows, width), BF16),
        grid_spec=pltpu.PrefetchScalarGridSpec(
            num_scalar_prefetch=1,
            grid=(micro, pairs),
            in_specs=[
                spec(0),
                spec(pairs),
                spec(2 * pairs),
                pl.BlockSpec((1, frames, frames), lambda m, h, s: (m, 0, 0)),
            ],
            out_specs=spec(0),
        ),
        compiler_params=pltpu.CompilerParams(vmem_limit_bytes=24 * 2**20),
        cost_estimate=pl.CostEstimate(
            flops=8 * micro * frames * frames * width,
            bytes_accessed=8 * micro * frames * width,
            transcendentals=micro * HEADS * frames * frames,
        ),
        name="attend",
    )(slopes, triple, triple, triple, far)


def attend_back(triple, grad, far, slopes):
    dp, micro, rows, wide = triple.shape
    frames = dp * rows
    width = wide // 3
    pairs = width // 128
    shape = (dp, 1, rows, 128)
    scale = HEAD ** (-0.5)

    def turned(left, right):
        return lax.dot_general(left, right, (((0,), (0,)), ((), ())), preferred_element_type=F32)

    def body(slope_ref, q_ref, k_ref, v_ref, g_ref, far_ref, out_ref):
        h = pl.program_id(1)
        q, k, v, g = (flat_frames(ref[...]) for ref in (q_ref, k_ref, v_ref, g_ref))
        first = lax.broadcasted_iota(jnp.int32, (frames, 128), 1) < HEAD
        zero = jnp.zeros_like(q)
        grads = []
        for j in range(2):
            own_q = jnp.where(first, q, zero) if j == 0 else jnp.where(first, zero, q)
            own_g = jnp.where(first, g, zero) if j == 0 else jnp.where(first, zero, g)
            probs = head_probs(own_q, k, far_ref[0], slope_ref[h * 2 + j])
            back = lax.dot_general(own_g, v, (((1,), (1,)), ((), ())), preferred_element_type=F32)
            back = probs * (back - jnp.sum(back * probs, axis=-1, keepdims=True))
            low = back.astype(BF16)
            grads.append(
                (
                    jnp.dot(low, k, preferred_element_type=F32) * scale,
                    turned(low, q) * scale,
                    turned(probs.astype(BF16), g),
                )
            )
        for i in range(3):
            out_ref[i] = by_source(jnp.where(first, grads[0][i], grads[1][i]), shape)

    def spec(offset):
        return pl.BlockSpec(shape, lambda m, h, s: (0, m, 0, h + offset))

    return pl.pallas_call(
        body,
        out_shape=jax.ShapeDtypeStruct((3, dp, micro, rows, width), BF16),
        grid_spec=pltpu.PrefetchScalarGridSpec(
            num_scalar_prefetch=1,
            grid=(micro, pairs),
            in_specs=[
                spec(0),
                spec(pairs),
                spec(2 * pairs),
                spec(0),
                pl.BlockSpec((1, frames, frames), lambda m, h, s: (m, 0, 0)),
            ],
            out_specs=pl.BlockSpec((3,) + shape, lambda m, h, s: (0, 0, m, 0, h)),
        ),
        compiler_params=pltpu.CompilerParams(vmem_limit_bytes=24 * 2**20),
        cost_estimate=pl.CostEstimate(
            flops=20 * micro * frames * frames * width,
            bytes_accessed=14 * micro * frames * width,
            transcendentals=micro * HEADS * frames * frames,
        ),
        name="attend_back",
    )(slopes, triple, triple, triple, grad, far)


def add_up(values):
    total = values[0].astype(F32)
    for value in values[1:]:
        total = total + value.astype(F32)
    return total.astype(BF16)


class Reduction:
    def __init__(self, pairs, d, dims):
        self.pairs = [(left, right if right.ndim == 3 else right[None]) for left, right in pairs]
        self.d = d
        self.dims = dims
        self.sent = gradient_blocks(self.pairs, d, dims)
        self.got = flip(self.sent, 1)

    def own(self, ready=None):
        got = self.got if ready is None else after(self.got, *ready)
        parts = gradient_blocks(self.pairs, self.d, self.dims, got)
        self.kept = parts[1]
        self.halves = []
        for side, order in ((0, self.dims), (1, self.dims[::-1])):
            send, stay = parts[2 * side], parts[2 * side + 1]
            left = [bit for bit in self.dims if bit != order[0]]
            shape = (2,) * len(left) + stay.shape[1:]
            values = [stay.reshape(shape), flip(send, 1 << order[0]).reshape(shape)]
            self.halves.append((values, list(order[1:]), left))
        self.arrived = [values[-1] for values, _, _ in self.halves]
        return list(parts)

    def step(self, ready=None):
        tokens = []
        halves = []
        for values, order, left in self.halves:
            bit = order[0]
            at = left.index(bit)
            send = add_up([lax.index_in_dim(v, 1, at, keepdims=False) for v in values])
            if ready is not None:
                send = after(send, *ready)
            tokens.append(send)
            stay = [lax.index_in_dim(v, 0, at, keepdims=False) for v in values]
            halves.append((stay + [flip(send, 1 << bit)], order[1:], [b for b in left if b != bit]))
        self.halves = halves
        self.arrived = [values[-1] for values, _, _ in halves]
        return tokens

    def line(self):
        while self.halves[0][1]:
            self.step()
        self.value = jnp.concatenate([add_up(values) for values, _, _ in self.halves], axis=1)
        self.stage = 0
        return self.along()

    def along(self):
        rep = lax.axis_size("rep")
        z = lax.axis_index("rep")
        half = rep // 2
        k = self.stage
        self.stage += 1
        value = self.value
        if k < half - 1:
            got = lax.ppermute(value, "rep", [(k, k + 1), (rep - 1 - k, rep - 2 - k)])
            self.value = (value.astype(F32) + got.astype(F32)).astype(BF16)
        elif k == half - 1:
            got = lax.ppermute(value, "rep", [(k, k + 1), (k + 1, k)])
            self.value = (value.astype(F32) + got.astype(F32)).astype(BF16)
        else:
            i = rep - 2 - k
            got = lax.ppermute(value, "rep", [(i + 1, i), (rep - 2 - i, rep - 1 - i)])
            self.value = jnp.where((z == i) | (z == rep - 1 - i), got, value)
        return self.value

    def finish(self):
        while self.stage < lax.axis_size("rep") - 1:
            self.along()
        return self.value.astype(F32)


def matmul(left, right):
    return jnp.dot(left, right, preferred_element_type=F32)


def matmul_nt(left, right):
    return lax.dot_general(left, right, (((1,), (1,)), ((), ())), preferred_element_type=F32)


def matmul_tn(left, right):
    return lax.dot_general(left, right, (((0,), (0,)), ((), ())), preferred_element_type=F32)


def norm_parts(values):
    average = jnp.mean(values, axis=-1, keepdims=True)
    centred = values - average
    spread = jnp.mean(centred * centred, axis=-1, keepdims=True)
    scale = lax.rsqrt(spread + EPS)
    return centred * scale, scale


def norm_back(grad, gain, unit, scale):
    e = grad * gain
    return scale * (
        e
        - jnp.mean(e, axis=-1, keepdims=True)
        - unit * jnp.mean(e * unit, axis=-1, keepdims=True)
    )


def shards(
    inputs,
    skips,
    cotangent,
    dest_slot,
    pack_segments,
    block_live,
    counts,
    w_skip,
    b_skip,
    g_one,
    b_one,
    w_qkv,
    w_out,
    b_out,
    g_two,
    b_two,
    w_up,
    c_up,
    w_down,
    c_down,
):
    dp = lax.axis_size("dp")
    rep = lax.axis_size("rep")
    d = lax.axis_index("dp")
    z = lax.axis_index("rep")
    micro = inputs.shape[0]
    frames = inputs.shape[2]
    width = inputs.shape[3]
    blocks = dest_slot.shape[2]
    block = frames // blocks
    per_pair = blocks // dp
    total = micro * frames
    bits = dp.bit_length() - 1
    place = jnp.stack([z, lax.rem(d, 8)]).astype(jnp.int32)
    dims = list(range(1, bits))
    own_skip = own_chunk(place, width, w_skip)
    own_mid = own_chunk(place, width, w_qkv, w_out)
    own_up = own_chunk(place, width, w_up)
    own_down = own_chunk(place, width, w_down)
    far_skip, first_skip = fetch_far(own_skip, None)
    far_mid, first_mid = fetch_far(own_mid, first_skip)
    far_up, first_up = fetch_far(own_up, first_mid)
    far_down, _ = fetch_far(own_down, first_up)
    parts_skip = spread_pieces(far_skip, None)
    parts_mid = spread_pieces(far_mid, [part[0] for part in parts_skip[2:4]])
    parts_up = spread_pieces(far_up, [part[0] for part in parts_mid[2:4]])
    parts_down = spread_pieces(far_down, [part[0] for part in parts_up[2:4]])
    moved = parts_skip[0][0]
    mid_rows = w_qkv.shape[0] // 8
    full_skip = assemble(w_skip, parts_skip, place, 0, 1)
    full_qkv = assemble(w_qkv, parts_mid, place, 0, 3)
    full_out = assemble(w_out, parts_mid, place, 3 * mid_rows, 1)
    full_up = assemble(w_up, parts_up, place, 0, w_up.shape[1] // width)
    full_down = assemble(w_down, parts_down, place, 0, 1)

    slots = dest_slot[:, 0, :]
    small = jnp.concatenate(
        [slots.reshape(-1), block_live[:, 0, :].reshape(-1), counts.reshape(-1)]
    )
    small, _ = lax.optimization_barrier((small, moved))
    every = small[None]
    for bit in range(bits):
        every = jnp.concatenate([every, flip(every, 1 << bit)], axis=0)
    span = micro * blocks
    all_slots = every[:, :span].reshape(dp, micro, blocks)
    all_live = every[:, span : 2 * span].reshape(dp, micro, blocks)
    source = jnp.bitwise_xor(jnp.arange(dp), d)
    count_total = jnp.sum(every[:, 2 * span]).astype(F32).reshape(1, 1)
    count_total = after(count_total, far_down)
    for bit in range(rep.bit_length() - 1):
        count_total = count_total + rep_flip(count_total, 1 << bit)
    share = counts[0, 0].astype(F32) * (dp * rep) / count_total[0, 0]

    rank = jnp.sum(
        (all_slots[:, :, None, :] < all_slots[:, :, :, None]).astype(jnp.int32), axis=3
    )
    mine_rank = jnp.sum((slots[:, None, :] < slots[:, :, None]).astype(jnp.int32), axis=2)
    here = (all_slots // blocks) == d
    arrive = source[:, None, None] * per_pair + rank % per_pair
    arrive = jnp.where(here, arrive, -1)
    match = arrive[None] == jnp.arange(blocks)[:, None, None, None]
    placing = jnp.sum(jnp.where(match, (all_slots % blocks)[None], 0), axis=(1, 3)).T
    pick = placing[:, :, None] == jnp.arange(blocks)[None, None, :]
    seg_blocks = pack_segments[:, 0, :].reshape(micro, blocks, block)
    segment = jnp.sum(jnp.where(pick[..., None], seg_blocks[:, None], 0), axis=2)
    segment = segment.reshape(micro, frames)
    live_count = jnp.sum(jnp.where(pick, block_live[:, 0, None, :], 0), axis=2)
    inner = jnp.arange(frames) % block
    live = inner[None] < jnp.repeat(live_count, block, axis=1)
    position = jnp.repeat(placing * block, block, axis=1) + inner[None]
    flat_live = jnp.transpose(all_live, (1, 0, 2)).reshape(micro, dp * blocks)
    flat_slot = (source[:, None] * blocks + jnp.arange(blocks)).reshape(-1)
    own_live = jnp.sum(jnp.where(slots[:, :, None] == flat_slot, flat_live[:, None], 0), axis=2)
    keep_rows = (inner[None] < jnp.repeat(own_live, block, axis=1)).astype(F32)
    keep_rows = keep_rows.reshape(total, 1)

    target = mine_rank // per_pair
    row = (target * micro + jnp.arange(micro)[:, None]) * per_pair + mine_rank % per_pair
    row = jnp.repeat(row.reshape(-1) * block, block) + jnp.tile(jnp.arange(block), micro * blocks)
    shuffle = (jnp.arange(total)[:, None] == row[None, :]).astype(BF16)

    def to_packs(values):
        sent = matmul(shuffle, values).astype(BF16)
        got = lax.all_to_all(
            sent.reshape(dp, total // dp, width), "dp", split_axis=0, concat_axis=0, tiled=True
        )
        return got.reshape(total, width)

    def to_owners(values):
        sent = values.reshape(dp, total // dp, width)
        got = lax.all_to_all(sent, "dp", split_axis=0, concat_axis=0, tiled=True)
        return matmul_tn(shuffle, got.reshape(total, width))

    joined = jnp.concatenate(
        [inputs.reshape(total, width), skips.reshape(total, width)], axis=1
    )
    base = matmul(joined, full_skip) + b_skip
    unit_one, scale_one = norm_parts(base)
    normed = to_packs((unit_one * g_one + b_one).astype(BF16))
    triple = matmul(after(normed, far_up), full_qkv).astype(BF16)
    triple = triple.reshape(dp, micro, per_pair * block, 3 * width)
    slopes = 2.0 ** (-8.0 * (jnp.arange(HEADS, dtype=F32) + 1.0) / HEADS)
    distance = jnp.abs(position[:, :, None] - position[:, None, :]).astype(F32)
    allowed = (segment[:, :, None] == segment[:, None, :]) & (
        live[:, None, :] | (position[:, :, None] == position[:, None, :])
    )
    far = jnp.where(allowed, distance, 1e32)
    attended = after(attend(triple, far, slopes), far_down)
    attended = to_owners(attended).astype(BF16)
    mixed = base + matmul(attended, full_out) + b_out
    unit_two, scale_two = norm_parts(mixed)
    normed_two = (unit_two * g_two + b_two).astype(BF16)
    normed_two = after(normed_two, parts_down[0][0], parts_down[1][0])
    hidden = matmul(normed_two, full_up) + c_up
    phi = 0.5 * (1.0 + lax.erf(hidden * (0.5**0.5)))
    active = (hidden * phi).astype(BF16)
    slope = (phi + hidden * jnp.exp(-0.5 * hidden * hidden) * ((2 * jnp.pi) ** -0.5)).astype(BF16)

    scaled = (cotangent.reshape(total, width).astype(F32) * share).astype(BF16)
    grad_result = scaled * keep_rows.astype(BF16)
    red_down = Reduction([(active, grad_result)], d, dims)
    grad_result = after(grad_result, red_down.sent)
    grad_result_full = grad_result.astype(F32)
    grad_active = matmul_nt(grad_result, full_down)
    grad_hidden = slope.astype(F32) * grad_active
    hidden_low = grad_hidden.astype(BF16)
    hidden_low = after(hidden_low, *red_down.own([hidden_low]))
    down_one = red_down.arrived
    red_up = Reduction([(normed_two, hidden_low)], d, dims)
    hidden_low = after(hidden_low, red_up.sent)
    grad_normed_two = matmul_nt(hidden_low, full_up)
    grad_mixed = grad_result_full + norm_back(grad_normed_two, g_two, unit_two, scale_two)
    mixed_low = grad_mixed.astype(BF16)
    grad_attended = to_packs(matmul_nt(mixed_low, full_out).astype(BF16))
    tokens = red_up.own([mixed_low])
    up_one = red_up.arrived
    active_late = after(active, *tokens)
    result = mixed + matmul(active_late, full_down) + c_down
    output = (result * keep_rows).astype(BF16)
    tokens = red_down.step()
    down_two = red_down.arrived
    grad_attended = after(grad_attended, output, *tokens)
    grad_attended = grad_attended.reshape(dp, micro, per_pair * block, width)
    grad_triple = attend_back(triple, grad_attended, far, slopes).reshape(3, total, width)
    tokens = red_up.step(down_two)
    up_two = red_up.arrived
    red_mid = Reduction([(attended, mixed_low), (normed, grad_triple)], d, dims)
    grad_triple = after(grad_triple, red_mid.sent, *tokens)
    grad_normed = sum(
        matmul_nt(grad_triple[i], full_qkv[:, i * width : (i + 1) * width]) for i in range(3)
    )
    grad_normed = to_owners(grad_normed.astype(BF16))
    tokens = red_mid.own() + [red_down.line()]
    mid_one = red_mid.arrived
    grad_normed = after(grad_normed, *tokens)
    grad_base = grad_mixed + norm_back(grad_normed, g_one, unit_one, scale_one)
    base_low = grad_base.astype(BF16)
    red_skip = Reduction([(joined, base_low)], d, dims)
    base_low = after(base_low, red_skip.sent)
    red_down.value = after(red_down.value, red_skip.sent)
    grad_joined = matmul_nt(base_low, full_skip).astype(BF16)
    tokens = red_skip.own([grad_joined])
    red_up.line()
    red_mid.step()
    red_skip.step()
    red_mid.line()
    red_skip.line()
    final_mid = red_mid.finish()
    finals = [
        red_down.finish(),
        red_up.finish(),
        final_mid[:, :width],
        final_mid[:, width:],
        red_skip.finish(),
    ]
    vectors = (
        jnp.sum(grad_base, axis=0),
        jnp.sum(grad_normed * unit_one, axis=0),
        jnp.sum(grad_normed, axis=0),
        jnp.sum(grad_mixed, axis=0),
        jnp.sum(grad_normed_two * unit_two, axis=0),
        jnp.sum(grad_normed_two, axis=0),
        jnp.sum(grad_hidden, axis=0),
        jnp.sum(grad_result_full, axis=0),
    )
    lengths = [v.shape[0] for v in vectors]
    summed = jnp.concatenate(vectors).reshape(-1, 128)
    for bit in range(bits):
        summed = summed + flip(summed, 1 << bit)
    for bit in range(rep.bit_length() - 1):
        summed = summed + rep_flip(summed, 1 << bit)
    summed = summed.reshape(-1)
    sums = []
    offset = 0
    for length in lengths:
        sums.append(summed[offset : offset + length])
        offset += length

    def as_owned(values):
        return values.reshape(inputs.shape)

    return (
        as_owned(output),
        as_owned(grad_joined[:, :width]),
        as_owned(grad_joined[:, width:]),
        finals[4],
        sums[0],
        sums[1],
        sums[2],
        finals[3],
        finals[2],
        sums[3],
        sums[4],
        sums[5],
        finals[1],
        sums[6],
        finals[0],
        sums[7],
    )


def solution(mesh):
    frames = P(None, "rep", "dp", None)
    slots = P(None, "rep", "dp")
    rows = P("rep", None)
    whole = P()
    in_specs = (
        (frames,) * 3
        + (slots,) * 3
        + (P("dp", "rep"), rows, whole, whole, whole, rows, rows)
        + (whole,) * 3
        + (rows, whole, rows, whole)
    )
    split = P("dp", None)
    out_specs = (
        (frames,) * 3
        + (split,)
        + (whole,) * 3
        + (split, split)
        + (whole,) * 3
        + (split, whole, split, whole)
    )
    return jax.shard_map(shards, mesh=mesh, in_specs=in_specs, out_specs=out_specs, check_vma=False)
```

```python
import jax
import jax.numpy as jnp
from jax import lax
from jax.experimental import pallas as pl
from jax.experimental.pallas import tpu as pltpu
from jax.sharding import PartitionSpec as P

HEADS = 16
HEAD = 64
EPS = 1e-05
F32 = jnp.float32
BF16 = jnp.bfloat16


def flip(value, bit):
    n = lax.axis_size("dp")
    return lax.ppermute(value, "dp", [(i, i ^ bit) for i in range(n)])


def rep_flip(value, bit):
    n = lax.axis_size("rep")
    return lax.ppermute(value, "rep", [(i, i ^ bit) for i in range(n)])


def after(value, *earlier):
    return lax.optimization_barrier((value,) + earlier)[0]


def flip_pair(left, left_bit, right, right_bit):
    return lax.optimization_barrier((flip(left, left_bit), flip(right, right_bit)))


def assemble(w_local, parts, place, row_at, tiles):
    rep = lax.axis_size("rep")
    shard_rows, columns = w_local.shape
    rows = shard_rows // 8
    tile = columns // tiles
    half = tile // 2
    chunk_rows = parts[0][0].shape[0] // (len(parts[0][2]) * (rep - 1))
    arrays = [part[0] for part in parts]
    count = 1 + sum(len(part[2]) for part in parts) * (rep - 1) * tiles

    def body(place_ref, local_ref, *refs):
        out_ref, sems = refs[len(parts)], refs[len(parts) + 1]
        z = place_ref[0]
        e = place_ref[1]
        copies = [
            pltpu.make_async_copy(
                local_ref,
                out_ref.at[pl.ds(pl.multiple_of(z * shard_rows, 16), shard_rows), :],
                sems.at[0],
            )
        ]
        for ref, (_, side, rels) in zip(refs, parts):
            for k, rel in enumerate(rels):
                chunk = jnp.bitwise_xor(e, rel)
                for s, apart in enumerate(far_order(rep), 1):
                    shard = jnp.bitwise_xor(z, apart)
                    start = pl.multiple_of(shard * shard_rows + chunk * rows, 16)
                    for t in range(tiles):
                        at = (k * (rep - 1) + s - 1) * chunk_rows + row_at + t * rows
                        copies.append(
                            pltpu.make_async_copy(
                                ref.at[pl.ds(at, rows), :],
                                out_ref.at[pl.ds(start, rows), pl.ds(t * tile + side * half, half)],
                                sems.at[len(copies)],
                            )
                        )
        for copy in copies:
            copy.start()
        for copy in copies:
            copy.wait()

    return pl.pallas_call(
        body,
        out_shape=jax.ShapeDtypeStruct((shard_rows * rep, columns), w_local.dtype),
        in_specs=[pl.BlockSpec(memory_space=pltpu.SMEM)]
        + [pl.BlockSpec(memory_space=pl.ANY)] * (1 + len(parts)),
        out_specs=pl.BlockSpec(memory_space=pltpu.VMEM),
        scratch_shapes=[pltpu.SemaphoreType.DMA((count,))],
        compiler_params=pltpu.CompilerParams(vmem_limit_bytes=24 * 2**20),
        cost_estimate=pl.CostEstimate(
            flops=0, bytes_accessed=4 * shard_rows * rep * columns, transcendentals=0
        ),
        name="assemble",
    )(place, w_local, *arrays)


def own_chunk(place, width, *shards_local):
    pieces = []
    for w_local in shards_local:
        rows = w_local.shape[0] // 8
        own = lax.dynamic_slice_in_dim(w_local, place[1] * rows, rows, 0)
        for t in range(w_local.shape[1] // width):
            pieces.append(own[:, t * width : (t + 1) * width])
    return jnp.concatenate(pieces, axis=0)


def fetch_far(own, previous):
    rep = lax.axis_size("rep")
    if previous is not None:
        own = after(own, previous)
    pieces = own
    first = None
    for bit in reversed(range(rep.bit_length() - 1)):
        got = rep_flip(pieces, 1 << bit)
        first = got if first is None else first
        pieces = jnp.concatenate([pieces, got], axis=0)
    return pieces[own.shape[0] :], first


def far_order(rep):
    order = [0]
    for bit in reversed(range(rep.bit_length() - 1)):
        order = order + [distance ^ (1 << bit) for distance in order]
    return order[1:]


class Spread:
    def __init__(self, far, *previous):
        half = far.shape[1] // 2
        if previous:
            far = after(far, *previous)
        left, right = far[:, :half], far[:, half:]
        got_left, got_right = flip_pair(left, 2, right, 4)
        self.pairs = [
            jnp.concatenate([left, got_left], axis=0),
            jnp.concatenate([right, got_right], axis=0),
        ]
        self.first = self.pairs[0]

    def cross(self, *previous):
        left, right = self.pairs
        if previous:
            left = after(left, *previous)
        got = flip_pair(left, 4, right, 2)
        self.second = got[0]
        parts = [
            (self.pairs[0], 0, [0, 2]),
            (self.pairs[1], 1, [0, 4]),
            (got[0], 0, [4, 6]),
            (got[1], 1, [2, 6]),
        ]
        others = [(flip(a, 1), side, [rel | 1 for rel in rels]) for a, side, rels in parts]
        self.parts = parts + others
        return self


def gradient_blocks(pairs, d, dims, got=None):
    dp = lax.axis_size("dp")
    total, all_rows = pairs[0][0].shape
    width = pairs[0][1].shape[2]
    tiles = [right.shape[0] for _, right in pairs]
    columns = sum(tiles) * width
    rows = all_rows // dp
    count = dp // 2
    odd = 1 if got is None else 0
    tile = min(width, 512)
    split = width // tile
    steps = sum(tiles) * split
    starts = [sum(tiles[:i]) * split for i in range(len(tiles))]

    def distance(p):
        rel = odd
        for k, bit in enumerate(dims):
            rel += ((p >> (len(dims) - 1 - k)) & 1) << bit
        return rel

    upper = [p for p in range(count) if p >= count // 2]
    lower = [p for p in range(count) if p < count // 2]
    odds = [p for p in range(count) if p % 2 == 1]
    evens = [p for p in range(count) if p % 2 == 0]
    chosen = (upper, lower, odds, evens)

    if rows % 128 != 0:
        products = []
        for left, right in pairs:
            flat = jnp.transpose(right, (1, 0, 2)).reshape(total, -1)
            products.append(matmul_tn(left, flat))
        product = jnp.concatenate(products, axis=1).reshape(dp, rows, columns)
        rel = jnp.array([distance(p) for p in range(count)], jnp.int32)
        product = product[jnp.bitwise_xor(rel, d)]
        if got is None:
            return product.astype(BF16)
        product = (product + got.astype(F32)).astype(BF16)
        half = columns // 2
        return [
            jnp.stack([product[p, :, side * half : (side + 1) * half] for p in ps])
            for side, ps in zip((0, 0, 1, 1), chosen)
        ]

    def body(d_ref, *refs):
        lefts = refs[: len(pairs)]
        rights = refs[len(pairs) : 2 * len(pairs)]
        rest = refs[2 * len(pairs) :]
        turned_ref = rest[-1]
        got_ref = None if got is None else rest[0]
        outs = rest[:-1] if got is None else rest[1:-1]
        c = pl.program_id(0)

        @pl.when(c == 0)
        def _():
            for i, left_ref in enumerate(lefts):
                for p in range(count):
                    at = pl.multiple_of(jnp.bitwise_xor(d_ref[0], distance(p)) * rows, 128)
                    turned_ref[i, pl.ds(p * rows, rows), :] = left_ref[:, pl.ds(at, rows)].T

        def piece(i, p):
            return jnp.dot(
                turned_ref[i, pl.ds(p * rows, rows), :], rights[i][0], preferred_element_type=F32
            )

        def write(i, half):
            for p in range(count):
                value = piece(i, p)
                if got is None:
                    outs[0][p] = value.astype(BF16)
                    continue
                value = (value + got_ref[p].astype(F32)).astype(BF16)
                for which in (2 * half, 2 * half + 1):
                    if p in chosen[which]:
                        outs[which][chosen[which].index(p)] = value

        for i in range(len(pairs)):
            for half in (0, 1):
                low = max(starts[i], half * (steps // 2))
                high = min(starts[i] + tiles[i] * split, (half + 1) * (steps // 2))
                if low < high:
                    pl.when((c >= low) & (c < high))(lambda i=i, half=half: write(i, half))

    def right_spec(start, n):
        def at(c, d_ref):
            k = jnp.clip(c - start, 0, n * split - 1)
            return (lax.div(k, jnp.int32(split)), 0, lax.rem(k, jnp.int32(split)))

        return pl.BlockSpec((1, total, tile), at)

    in_specs = [pl.BlockSpec((total, all_rows), lambda c, d_ref: (0, 0))] * len(pairs)
    in_specs += [right_spec(start, n) for start, n in zip(starts, tiles)]
    args = [left for left, _ in pairs] + [right for _, right in pairs]
    if got is None:
        out_shape = jax.ShapeDtypeStruct((count, rows, columns), BF16)
        out_specs = pl.BlockSpec((count, rows, tile), lambda c, d_ref: (0, 0, c))
    else:
        in_specs.append(pl.BlockSpec((count, rows, tile), lambda c, d_ref: (0, 0, c)))
        args.append(got)
        out_shape = [jax.ShapeDtypeStruct((count // 2, rows, columns // 2), BF16)] * 4
        mid = steps // 2
        first = pl.BlockSpec(
            (count // 2, rows, tile), lambda c, d_ref: (0, 0, jnp.minimum(c, mid - 1))
        )
        second = pl.BlockSpec(
            (count // 2, rows, tile), lambda c, d_ref: (0, 0, jnp.maximum(c - mid, 0))
        )
        out_specs = [first, first, second, second]
    return pl.pallas_call(
        body,
        out_shape=out_shape,
        grid_spec=pltpu.PrefetchScalarGridSpec(
            num_scalar_prefetch=1,
            grid=(steps,),
            in_specs=in_specs,
            out_specs=out_specs,
            scratch_shapes=[pltpu.VMEM((len(pairs), count * rows, total), BF16)],
        ),
        compiler_params=pltpu.CompilerParams(vmem_limit_bytes=40 * 2**20),
        cost_estimate=pl.CostEstimate(
            flops=total * all_rows * columns,
            bytes_accessed=2 * total * (all_rows + columns) + 2 * all_rows * columns,
            transcendentals=0,
        ),
        name="gradient",
    )(d.reshape(1).astype(jnp.int32), *args)


def head_probs(q, k, far, slope):
    scores = lax.dot_general(q, k, (((1,), (1,)), ((), ())), preferred_element_type=F32)
    scores = scores * (HEAD ** (-0.5)) - slope * far
    raised = jnp.exp(scores - jnp.max(scores, axis=-1, keepdims=True))
    return raised * (1.0 / jnp.sum(raised, axis=-1, keepdims=True))


def flat_frames(block):
    sources, _, rows, lanes = block.shape
    if rows % 16 == 0:
        return block.reshape(sources * rows, lanes)
    return block.astype(F32).reshape(sources * rows, lanes).astype(BF16)


def by_source(value, like):
    sources, _, rows, lanes = like
    if rows % 16 == 0:
        return value.astype(BF16).reshape(sources, 1, rows, lanes)
    return value.reshape(sources, 1, rows, lanes).astype(BF16)


def attend(triple, far, slopes):
    dp, micro, rows, wide = triple.shape
    frames = dp * rows
    width = wide // 3
    pairs = width // 128
    shape = (dp, 1, rows, 128)

    def body(slope_ref, q_ref, k_ref, v_ref, far_ref, out_ref):
        h = pl.program_id(1)
        q, k, v = (flat_frames(ref[...]) for ref in (q_ref, k_ref, v_ref))
        first = lax.broadcasted_iota(jnp.int32, (frames, 128), 1) < HEAD
        zero = jnp.zeros_like(q)
        outs = []
        for j, own in enumerate((jnp.where(first, q, zero), jnp.where(first, zero, q))):
            probs = head_probs(own, k, far_ref[0], slope_ref[h * 2 + j])
            outs.append(jnp.dot(probs.astype(BF16), v, preferred_element_type=F32))
        out_ref[...] = by_source(jnp.where(first, outs[0], outs[1]), shape)

    def spec(offset):
        return pl.BlockSpec(shape, lambda m, h, s: (0, m, 0, h + offset))

    return pl.pallas_call(
        body,
        out_shape=jax.ShapeDtypeStruct((dp, micro, rows, width), BF16),
        grid_spec=pltpu.PrefetchScalarGridSpec(
            num_scalar_prefetch=1,
            grid=(micro, pairs),
            in_specs=[
                spec(0),
                spec(pairs),
                spec(2 * pairs),
                pl.BlockSpec((1, frames, frames), lambda m, h, s: (m, 0, 0)),
            ],
            out_specs=spec(0),
        ),
        compiler_params=pltpu.CompilerParams(vmem_limit_bytes=24 * 2**20),
        cost_estimate=pl.CostEstimate(
            flops=8 * micro * frames * frames * width,
            bytes_accessed=8 * micro * frames * width,
            transcendentals=micro * HEADS * frames * frames,
        ),
        name="attend",
    )(slopes, triple, triple, triple, far)


def attend_back(triple, grad, far, slopes):
    dp, micro, rows, wide = triple.shape
    frames = dp * rows
    width = wide // 3
    pairs = width // 128
    shape = (dp, 1, rows, 128)
    scale = HEAD ** (-0.5)

    def turned(left, right):
        return lax.dot_general(left, right, (((0,), (0,)), ((), ())), preferred_element_type=F32)

    def body(slope_ref, q_ref, k_ref, v_ref, g_ref, far_ref, out_ref):
        h = pl.program_id(1)
        q, k, v, g = (flat_frames(ref[...]) for ref in (q_ref, k_ref, v_ref, g_ref))
        first = lax.broadcasted_iota(jnp.int32, (frames, 128), 1) < HEAD
        zero = jnp.zeros_like(q)
        grads = []
        for j in range(2):
            own_q = jnp.where(first, q, zero) if j == 0 else jnp.where(first, zero, q)
            own_g = jnp.where(first, g, zero) if j == 0 else jnp.where(first, zero, g)
            probs = head_probs(own_q, k, far_ref[0], slope_ref[h * 2 + j])
            back = lax.dot_general(own_g, v, (((1,), (1,)), ((), ())), preferred_element_type=F32)
            back = probs * (back - jnp.sum(back * probs, axis=-1, keepdims=True))
            low = back.astype(BF16)
            grads.append(
                (
                    jnp.dot(low, k, preferred_element_type=F32) * scale,
                    turned(low, q) * scale,
                    turned(probs.astype(BF16), g),
                )
            )
        for i in range(3):
            out_ref[i] = by_source(jnp.where(first, grads[0][i], grads[1][i]), shape)

    def spec(offset):
        return pl.BlockSpec(shape, lambda m, h, s: (0, m, 0, h + offset))

    return pl.pallas_call(
        body,
        out_shape=jax.ShapeDtypeStruct((3, dp, micro, rows, width), BF16),
        grid_spec=pltpu.PrefetchScalarGridSpec(
            num_scalar_prefetch=1,
            grid=(micro, pairs),
            in_specs=[
                spec(0),
                spec(pairs),
                spec(2 * pairs),
                spec(0),
                pl.BlockSpec((1, frames, frames), lambda m, h, s: (m, 0, 0)),
            ],
            out_specs=pl.BlockSpec((3,) + shape, lambda m, h, s: (0, 0, m, 0, h)),
        ),
        compiler_params=pltpu.CompilerParams(vmem_limit_bytes=24 * 2**20),
        cost_estimate=pl.CostEstimate(
            flops=20 * micro * frames * frames * width,
            bytes_accessed=14 * micro * frames * width,
            transcendentals=micro * HEADS * frames * frames,
        ),
        name="attend_back",
    )(slopes, triple, triple, triple, grad, far)


def add_up(values):
    total = values[0].astype(F32)
    for value in values[1:]:
        total = total + value.astype(F32)
    return total.astype(BF16)


class Reduction:
    def __init__(self, pairs, d, dims):
        self.pairs = [(left, right if right.ndim == 3 else right[None]) for left, right in pairs]
        self.d = d
        self.dims = dims
        self.sent = gradient_blocks(self.pairs, d, dims)
        self.got = flip(self.sent, 1)

    def own(self, *ready):
        got = after(self.got, *ready) if ready else self.got
        parts = gradient_blocks(self.pairs, self.d, self.dims, got)
        self.parts = list(parts)
        arrived = flip_pair(parts[0], 1 << self.dims[0], parts[2], 1 << self.dims[-1])
        self.halves = []
        for side, order in ((0, self.dims), (1, self.dims[::-1])):
            stay = parts[2 * side + 1]
            left = [bit for bit in self.dims if bit != order[0]]
            shape = (2,) * len(left) + stay.shape[1:]
            values = [stay.reshape(shape), arrived[side].reshape(shape)]
            self.halves.append((values, list(order[1:]), left))
        self.arrived = arrived[0]
        return self.parts

    def step(self, *ready):
        sends, stays = [], []
        for values, order, left in self.halves:
            at = left.index(order[0])
            sends.append(add_up([lax.index_in_dim(v, 1, at, keepdims=False) for v in values]))
            stays.append([lax.index_in_dim(v, 0, at, keepdims=False) for v in values])
        if ready:
            sends[0] = after(sends[0], *ready)
        bits = [order[0] for _, order, _ in self.halves]
        arrived = flip_pair(sends[0], 1 << bits[0], sends[1], 1 << bits[1])
        self.halves = [
            (stays[i] + [arrived[i]], self.halves[i][1][1:], [b for b in self.halves[i][2] if b != bits[i]])
            for i in (0, 1)
        ]
        self.arrived = arrived[0]
        return sends

    def rows(self):
        while self.halves[0][1]:
            self.step()
        self.value = jnp.concatenate([add_up(values) for values, _, _ in self.halves], axis=1)
        self.stage = 0
        return self.value

    def line(self, *ready):
        value = self.rows()
        if ready:
            self.value = after(value, *ready)
        return self.along()

    def halve(self, *ready):
        rep = lax.axis_size("rep")
        z = lax.axis_index("rep")
        value = self.rows()
        if ready:
            value = after(value, *ready)
        bits = range(rep.bit_length() - 1)
        for bit in bits:
            mine = lax.bitwise_and(lax.shift_right_logical(z, bit), 1)
            size = value.shape[0] // 2
            send = lax.dynamic_slice_in_dim(value, (1 - mine) * size, size, 0)
            keep = lax.dynamic_slice_in_dim(value, mine * size, size, 0)
            value = add_up([keep, rep_flip(send, 1 << bit)])
        for bit in reversed(bits):
            mine = lax.bitwise_and(lax.shift_right_logical(z, bit), 1)
            got = rep_flip(value, 1 << bit)
            lower = jnp.where(mine == 0, value, got)
            upper = jnp.where(mine == 0, got, value)
            value = jnp.concatenate([lower, upper], axis=0)
        return value.astype(F32)

    def along(self):
        rep = lax.axis_size("rep")
        z = lax.axis_index("rep")
        half = rep // 2
        k = self.stage
        self.stage += 1
        value = self.value
        if k < half - 1:
            got = lax.ppermute(value, "rep", [(k, k + 1), (rep - 1 - k, rep - 2 - k)])
            self.value = (value.astype(F32) + got.astype(F32)).astype(BF16)
        elif k == half - 1:
            got = lax.ppermute(value, "rep", [(k, k + 1), (k + 1, k)])
            self.value = (value.astype(F32) + got.astype(F32)).astype(BF16)
        else:
            i = rep - 2 - k
            got = lax.ppermute(value, "rep", [(i + 1, i), (rep - 2 - i, rep - 1 - i)])
            self.value = jnp.where((z == i) | (z == rep - 1 - i), got, value)
        return self.value

    def finish(self):
        while self.stage < lax.axis_size("rep") - 1:
            self.along()
        return self.value.astype(F32)


def matmul(left, right):
    return jnp.dot(left, right, preferred_element_type=F32)


def matmul_nt(left, right):
    return lax.dot_general(left, right, (((1,), (1,)), ((), ())), preferred_element_type=F32)


def matmul_tn(left, right):
    return lax.dot_general(left, right, (((0,), (0,)), ((), ())), preferred_element_type=F32)


def norm_parts(values):
    average = jnp.mean(values, axis=-1, keepdims=True)
    centred = values - average
    spread = jnp.mean(centred * centred, axis=-1, keepdims=True)
    scale = lax.rsqrt(spread + EPS)
    return centred * scale, scale


def norm_back(grad, gain, unit, scale):
    e = grad * gain
    return scale * (
        e
        - jnp.mean(e, axis=-1, keepdims=True)
        - unit * jnp.mean(e * unit, axis=-1, keepdims=True)
    )


def shards(
    inputs,
    skips,
    cotangent,
    dest_slot,
    pack_segments,
    block_live,
    counts,
    w_skip,
    b_skip,
    g_one,
    b_one,
    w_qkv,
    w_out,
    b_out,
    g_two,
    b_two,
    w_up,
    c_up,
    w_down,
    c_down,
):
    dp = lax.axis_size("dp")
    rep = lax.axis_size("rep")
    d = lax.axis_index("dp")
    z = lax.axis_index("rep")
    micro = inputs.shape[0]
    frames = inputs.shape[2]
    width = inputs.shape[3]
    blocks = dest_slot.shape[2]
    block = frames // blocks
    per_pair = blocks // dp
    total = micro * frames
    bits = dp.bit_length() - 1
    place = jnp.stack([z, lax.rem(d, 8)]).astype(jnp.int32)
    dims = list(range(1, bits))
    own_skip = own_chunk(place, width, w_skip)
    own_mid = own_chunk(place, width, w_qkv, w_out)
    own_up = own_chunk(place, width, w_up)
    own_down = own_chunk(place, width, w_down)
    far_skip, first_skip = fetch_far(own_skip, None)
    far_mid, first_mid = fetch_far(own_mid, first_skip)
    far_up, first_up = fetch_far(own_up, first_mid)
    far_down, _ = fetch_far(own_down, first_up)
    run_skip = Spread(far_skip)
    moved = run_skip.first
    run_skip.cross()
    run_mid = Spread(far_mid, run_skip.second)
    run_mid.cross()
    run_up = Spread(far_up, run_mid.second)
    run_down = Spread(far_down, run_up.first)
    run_up.cross()
    run_down.cross(run_up.second)
    parts_skip, parts_mid = run_skip.parts, run_mid.parts
    parts_up, parts_down = run_up.parts, run_down.parts
    mid_rows = w_qkv.shape[0] // 8
    full_skip = assemble(w_skip, parts_skip, place, 0, 1)
    full_qkv = assemble(w_qkv, parts_mid, place, 0, 3)
    full_out = assemble(w_out, parts_mid, place, 3 * mid_rows, 1)
    full_up = assemble(w_up, parts_up, place, 0, w_up.shape[1] // width)
    full_down = assemble(w_down, parts_down, place, 0, 1)

    slots = after(dest_slot, moved)[:, 0, :]
    small = jnp.concatenate(
        [slots.reshape(-1), block_live[:, 0, :].reshape(-1), counts.reshape(-1)]
    )
    small = after(small, moved)
    every = small[None]
    for bit in range(bits):
        every = jnp.concatenate([every, flip(every, 1 << bit)], axis=0)
    span = micro * blocks
    all_slots = every[:, :span].reshape(dp, micro, blocks)
    all_live = every[:, span : 2 * span].reshape(dp, micro, blocks)
    source = jnp.bitwise_xor(jnp.arange(dp), d)
    count_total = jnp.sum(every[:, 2 * span]).astype(F32).reshape(1, 1)
    count_total = after(count_total, far_down)
    for bit in range(rep.bit_length() - 1):
        count_total = count_total + rep_flip(count_total, 1 << bit)
    share = counts[0, 0].astype(F32) * (dp * rep) / count_total[0, 0]

    rank = jnp.sum(
        (all_slots[:, :, None, :] < all_slots[:, :, :, None]).astype(jnp.int32), axis=3
    )
    mine_rank = jnp.sum((slots[:, None, :] < slots[:, :, None]).astype(jnp.int32), axis=2)
    here = (all_slots // blocks) == d
    arrive = source[:, None, None] * per_pair + rank % per_pair
    arrive = jnp.where(here, arrive, -1)
    match = arrive[None] == jnp.arange(blocks)[:, None, None, None]
    placing = jnp.sum(jnp.where(match, (all_slots % blocks)[None], 0), axis=(1, 3)).T
    pick = placing[:, :, None] == jnp.arange(blocks)[None, None, :]
    seg_blocks = pack_segments[:, 0, :].reshape(micro, blocks, block)
    segment = jnp.sum(jnp.where(pick[..., None], seg_blocks[:, None], 0), axis=2)
    segment = segment.reshape(micro, frames)
    live_count = jnp.sum(jnp.where(pick, block_live[:, 0, None, :], 0), axis=2)
    inner = jnp.arange(frames) % block
    live = inner[None] < jnp.repeat(live_count, block, axis=1)
    position = jnp.repeat(placing * block, block, axis=1) + inner[None]
    flat_live = jnp.transpose(all_live, (1, 0, 2)).reshape(micro, dp * blocks)
    flat_slot = (source[:, None] * blocks + jnp.arange(blocks)).reshape(-1)
    own_live = jnp.sum(jnp.where(slots[:, :, None] == flat_slot, flat_live[:, None], 0), axis=2)
    keep_rows = (inner[None] < jnp.repeat(own_live, block, axis=1)).astype(F32)
    keep_rows = keep_rows.reshape(total, 1)

    target = mine_rank // per_pair
    row = (target * micro + jnp.arange(micro)[:, None]) * per_pair + mine_rank % per_pair
    row = jnp.repeat(row.reshape(-1) * block, block) + jnp.tile(jnp.arange(block), micro * blocks)
    shuffle = (jnp.arange(total)[:, None] == row[None, :]).astype(BF16)

    def to_packs(values):
        sent = matmul(shuffle, values).astype(BF16)
        got = lax.all_to_all(
            sent.reshape(dp, total // dp, width), "dp", split_axis=0, concat_axis=0, tiled=True
        )
        return got.reshape(total, width)

    def to_owners(values):
        sent = values.reshape(dp, total // dp, width)
        got = lax.all_to_all(sent, "dp", split_axis=0, concat_axis=0, tiled=True)
        return matmul_tn(shuffle, got.reshape(total, width))

    joined = jnp.concatenate(
        [inputs.reshape(total, width), skips.reshape(total, width)], axis=1
    )
    base = matmul(joined, full_skip) + b_skip
    unit_one, scale_one = norm_parts(base)
    normed = to_packs((unit_one * g_one + b_one).astype(BF16))
    triple = matmul(after(normed, far_up), full_qkv).astype(BF16)
    triple = triple.reshape(dp, micro, per_pair * block, 3 * width)
    slopes = 2.0 ** (-8.0 * (jnp.arange(HEADS, dtype=F32) + 1.0) / HEADS)
    distance = jnp.abs(position[:, :, None] - position[:, None, :]).astype(F32)
    allowed = (segment[:, :, None] == segment[:, None, :]) & (
        live[:, None, :] | (position[:, :, None] == position[:, None, :])
    )
    far = jnp.where(allowed, distance, 1e32)
    attended = after(attend(triple, far, slopes), run_down.first)
    attended = to_owners(attended).astype(BF16)
    mixed = base + matmul(attended, full_out) + b_out
    unit_two, scale_two = norm_parts(mixed)
    normed_two = (unit_two * g_two + b_two).astype(BF16)
    normed_two = after(normed_two, run_up.second)
    hidden = matmul(normed_two, full_up) + c_up
    phi = 0.5 * (1.0 + lax.erf(hidden * (0.5**0.5)))
    active = (hidden * phi).astype(BF16)
    slope = (phi + hidden * jnp.exp(-0.5 * hidden * hidden) * ((2 * jnp.pi) ** -0.5)).astype(BF16)

    scaled = (cotangent.reshape(total, width).astype(F32) * share).astype(BF16)
    grad_result = scaled * keep_rows.astype(BF16)
    red_down = Reduction([(active, grad_result)], d, dims)
    grad_result = after(grad_result, red_down.sent)
    grad_result_full = grad_result.astype(F32)
    grad_active = matmul_nt(grad_result, full_down)
    grad_hidden = slope.astype(F32) * grad_active
    hidden_low = grad_hidden.astype(BF16)
    hidden_low = after(hidden_low, *red_down.own(hidden_low))
    red_up = Reduction([(normed_two, hidden_low)], d, dims)
    hidden_low = after(hidden_low, red_up.sent)
    grad_normed_two = matmul_nt(hidden_low, full_up)
    grad_mixed = grad_result_full + norm_back(grad_normed_two, g_two, unit_two, scale_two)
    mixed_low = grad_mixed.astype(BF16)
    grad_attended = to_packs(matmul_nt(mixed_low, full_out).astype(BF16))
    up_parts = red_up.own(mixed_low)
    down_sends = red_down.step(*up_parts)
    active_late = after(active, *up_parts, *down_sends)
    result = mixed + matmul(active_late, full_down) + c_down
    output = (result * keep_rows).astype(BF16)
    grad_attended = after(grad_attended, output)
    grad_attended = grad_attended.reshape(dp, micro, per_pair * block, width)
    grad_triple = attend_back(triple, grad_attended, far, slopes).reshape(3, total, width)
    up_sends = red_up.step(grad_triple, red_down.arrived)
    red_mid = Reduction([(attended, mixed_low), (normed, grad_triple)], d, dims)
    down_rows = red_down.rows()
    grad_triple = after(grad_triple, red_mid.sent, down_rows, *up_sends)
    grad_normed = sum(
        matmul_nt(grad_triple[i], full_qkv[:, i * width : (i + 1) * width]) for i in range(3)
    )
    sent_normed = grad_normed.astype(BF16)
    red_down.along()
    grad_normed = to_owners(sent_normed)
    mid_parts = red_mid.own(sent_normed)
    grad_normed = after(grad_normed, *mid_parts)
    grad_base = grad_mixed + norm_back(grad_normed, g_one, unit_one, scale_one)
    base_low = grad_base.astype(BF16)
    red_skip = Reduction([(joined, base_low)], d, dims)
    base_low = after(base_low, red_skip.sent)
    grad_joined = matmul_nt(base_low, full_skip).astype(BF16)
    red_up.line(*mid_parts)
    red_down.value = after(red_down.value, red_skip.sent)
    skip_parts = red_skip.own(grad_joined)
    mid_sends = red_mid.step(*skip_parts)
    red_skip.step(*mid_sends)
    final_mid = red_mid.halve()
    final_skip = red_skip.halve()
    finals = [
        red_down.finish(),
        red_up.finish(),
        final_mid[:, :width],
        final_mid[:, width:],
        final_skip,
    ]
    vectors = (
        jnp.sum(grad_base, axis=0),
        jnp.sum(grad_normed * unit_one, axis=0),
        jnp.sum(grad_normed, axis=0),
        jnp.sum(grad_mixed, axis=0),
        jnp.sum(grad_normed_two * unit_two, axis=0),
        jnp.sum(grad_normed_two, axis=0),
        jnp.sum(grad_hidden, axis=0),
        jnp.sum(grad_result_full, axis=0),
    )
    lengths = [v.shape[0] for v in vectors]
    summed = after(jnp.concatenate(vectors), *skip_parts).reshape(-1, 128)
    for bit in range(bits):
        summed = summed + flip(summed, 1 << bit)
    for bit in range(rep.bit_length() - 1):
        summed = summed + rep_flip(summed, 1 << bit)
    summed = summed.reshape(-1)
    sums = []
    offset = 0
    for length in lengths:
        sums.append(summed[offset : offset + length])
        offset += length

    def as_owned(values):
        return values.reshape(inputs.shape)

    return (
        as_owned(output),
        as_owned(grad_joined[:, :width]),
        as_owned(grad_joined[:, width:]),
        finals[4],
        sums[0],
        sums[1],
        sums[2],
        finals[3],
        finals[2],
        sums[3],
        sums[4],
        sums[5],
        finals[1],
        sums[6],
        finals[0],
        sums[7],
    )


def solution(mesh):
    frames = P(None, "rep", "dp", None)
    slots = P(None, "rep", "dp")
    rows = P("rep", None)
    whole = P()
    in_specs = (
        (frames,) * 3
        + (slots,) * 3
        + (P("dp", "rep"), rows, whole, whole, whole, rows, rows)
        + (whole,) * 3
        + (rows, whole, rows, whole)
    )
    split = P("dp", None)
    out_specs = (
        (frames,) * 3
        + (split,)
        + (whole,) * 3
        + (split, split)
        + (whole,) * 3
        + (split, whole, split, whole)
    )
    return jax.shard_map(shards, mesh=mesh, in_specs=in_specs, out_specs=out_specs, check_vma=False)
```

```python
import jax
import jax.numpy as jnp
from jax import lax
from jax.experimental import pallas as pl
from jax.experimental.pallas import tpu as pltpu
from jax.sharding import PartitionSpec as P

HEADS = 16
HEAD = 64
EPS = 1e-05
F32 = jnp.float32
BF16 = jnp.bfloat16


def flip(value, bit):
    n = lax.axis_size("dp")
    return lax.ppermute(value, "dp", [(i, i ^ bit) for i in range(n)])


def rep_flip(value, bit):
    n = lax.axis_size("rep")
    return lax.ppermute(value, "rep", [(i, i ^ bit) for i in range(n)])


def after(value, *earlier):
    return lax.optimization_barrier((value,) + earlier)[0]


def flip_pair(left, left_bit, right, right_bit):
    return lax.optimization_barrier((flip(left, left_bit), flip(right, right_bit)))


def assemble(w_local, parts, place, row_at, tiles):
    rep = lax.axis_size("rep")
    shard_rows, columns = w_local.shape
    rows = shard_rows // 8
    tile = columns // tiles
    half = tile // 2
    chunk_rows = parts[0][0].shape[0] // (len(parts[0][1]) * (rep - 1))
    arrays = [part[0] for part in parts]
    count = 1 + sum(len(part[1]) for part in parts) * (rep - 1) * tiles

    def body(place_ref, local_ref, *refs):
        out_ref, sems = refs[len(parts)], refs[len(parts) + 1]
        z = place_ref[0]
        e = place_ref[1]
        copies = [
            pltpu.make_async_copy(
                local_ref,
                out_ref.at[pl.ds(pl.multiple_of(z * shard_rows, 16), shard_rows), :],
                sems.at[0],
            )
        ]
        for ref, (_, runs) in zip(refs, parts):
            for k, (side, rel) in enumerate(runs):
                chunk = jnp.bitwise_xor(e, rel)
                for s, apart in enumerate(far_order(rep), 1):
                    shard = jnp.bitwise_xor(z, apart)
                    start = pl.multiple_of(shard * shard_rows + chunk * rows, 16)
                    for t in range(tiles):
                        at = (k * (rep - 1) + s - 1) * chunk_rows + row_at + t * rows
                        copies.append(
                            pltpu.make_async_copy(
                                ref.at[pl.ds(at, rows), :],
                                out_ref.at[pl.ds(start, rows), pl.ds(t * tile + side * half, half)],
                                sems.at[len(copies)],
                            )
                        )
        for copy in copies:
            copy.start()
        for copy in copies:
            copy.wait()

    return pl.pallas_call(
        body,
        out_shape=jax.ShapeDtypeStruct((shard_rows * rep, columns), w_local.dtype),
        in_specs=[pl.BlockSpec(memory_space=pltpu.SMEM)]
        + [pl.BlockSpec(memory_space=pl.ANY)] * (1 + len(parts)),
        out_specs=pl.BlockSpec(memory_space=pltpu.VMEM),
        scratch_shapes=[pltpu.SemaphoreType.DMA((count,))],
        compiler_params=pltpu.CompilerParams(vmem_limit_bytes=24 * 2**20),
        cost_estimate=pl.CostEstimate(
            flops=0, bytes_accessed=4 * shard_rows * rep * columns, transcendentals=0
        ),
        name="assemble",
    )(place, w_local, *arrays)


def own_chunk(place, width, *shards_local):
    pieces = []
    for w_local in shards_local:
        rows = w_local.shape[0] // 8
        own = lax.dynamic_slice_in_dim(w_local, place[1] * rows, rows, 0)
        for t in range(w_local.shape[1] // width):
            pieces.append(own[:, t * width : (t + 1) * width])
    return jnp.concatenate(pieces, axis=0)


def fetch_far(own, previous):
    rep = lax.axis_size("rep")
    if previous is not None:
        own = after(own, previous)
    pieces = own
    first = None
    for bit in reversed(range(rep.bit_length() - 1)):
        got = rep_flip(pieces, 1 << bit)
        first = got if first is None else first
        pieces = jnp.concatenate([pieces, got], axis=0)
    return pieces[own.shape[0] :], first


def far_order(rep):
    order = [0]
    for bit in reversed(range(rep.bit_length() - 1)):
        order = order + [distance ^ (1 << bit) for distance in order]
    return order[1:]


class Spread:
    def __init__(self, far, *previous):
        half = far.shape[1] // 2
        if previous:
            far = after(far, *previous)
        left, right = far[:, :half], far[:, half:]
        got_left, got_right = flip_pair(left, 2, right, 4)
        self.pairs = [
            jnp.concatenate([left, got_left], axis=0),
            jnp.concatenate([right, got_right], axis=0),
        ]
        self.first = self.pairs[0]

    def cross(self, *previous):
        left, right = self.pairs
        if previous:
            left = after(left, *previous)
        got = flip_pair(left, 4, right, 2)
        self.second = got[0]
        every = jnp.concatenate([self.pairs[0], got[0], self.pairs[1], got[1]], axis=0)
        other = flip(every, 1)
        runs = [(0, 0), (0, 2), (0, 4), (0, 6), (1, 0), (1, 4), (1, 2), (1, 6)]
        self.parts = [
            (every, runs),
            (other, [(side, rel | 1) for side, rel in runs]),
        ]
        return self


def gradient_blocks(pairs, d, dims, got=None):
    dp = lax.axis_size("dp")
    total, all_rows = pairs[0][0].shape
    width = pairs[0][1].shape[2]
    tiles = [right.shape[0] for _, right in pairs]
    columns = sum(tiles) * width
    rows = all_rows // dp
    count = dp // 2
    odd = 1 if got is None else 0
    tile = min(width, 512)
    split = width // tile
    steps = sum(tiles) * split
    starts = [sum(tiles[:i]) * split for i in range(len(tiles))]

    def distance(p):
        rel = odd
        for k, bit in enumerate(dims):
            rel += ((p >> (len(dims) - 1 - k)) & 1) << bit
        return rel

    upper = [p for p in range(count) if p >= count // 2]
    lower = [p for p in range(count) if p < count // 2]
    odds = [p for p in range(count) if p % 2 == 1]
    evens = [p for p in range(count) if p % 2 == 0]
    chosen = (upper, lower, odds, evens)

    if rows % 128 != 0:
        products = []
        for left, right in pairs:
            flat = jnp.transpose(right, (1, 0, 2)).reshape(total, -1)
            products.append(matmul_tn(left, flat))
        product = jnp.concatenate(products, axis=1).reshape(dp, rows, columns)
        rel = jnp.array([distance(p) for p in range(count)], jnp.int32)
        product = product[jnp.bitwise_xor(rel, d)]
        if got is None:
            return product.astype(BF16)
        product = (product + got.astype(F32)).astype(BF16)
        half = columns // 2
        return [
            jnp.stack([product[p, :, side * half : (side + 1) * half] for p in ps])
            for side, ps in zip((0, 0, 1, 1), chosen)
        ]

    def body(d_ref, *refs):
        lefts = refs[: len(pairs)]
        rights = refs[len(pairs) : 2 * len(pairs)]
        rest = refs[2 * len(pairs) :]
        turned_ref = rest[-1]
        got_ref = None if got is None else rest[0]
        outs = rest[:-1] if got is None else rest[1:-1]
        c = pl.program_id(0)

        @pl.when(c == 0)
        def _():
            for i, left_ref in enumerate(lefts):
                for p in range(count):
                    at = pl.multiple_of(jnp.bitwise_xor(d_ref[0], distance(p)) * rows, 128)
                    turned_ref[i, pl.ds(p * rows, rows), :] = left_ref[:, pl.ds(at, rows)].T

        def piece(i, p):
            return jnp.dot(
                turned_ref[i, pl.ds(p * rows, rows), :], rights[i][0], preferred_element_type=F32
            )

        def write(i, half):
            for p in range(count):
                value = piece(i, p)
                if got is None:
                    outs[0][p] = value.astype(BF16)
                    continue
                value = (value + got_ref[p].astype(F32)).astype(BF16)
                for which in (2 * half, 2 * half + 1):
                    if p in chosen[which]:
                        outs[which][chosen[which].index(p)] = value

        for i in range(len(pairs)):
            for half in (0, 1):
                low = max(starts[i], half * (steps // 2))
                high = min(starts[i] + tiles[i] * split, (half + 1) * (steps // 2))
                if low < high:
                    pl.when((c >= low) & (c < high))(lambda i=i, half=half: write(i, half))

    def right_spec(start, n):
        def at(c, d_ref):
            k = jnp.clip(c - start, 0, n * split - 1)
            return (lax.div(k, jnp.int32(split)), 0, lax.rem(k, jnp.int32(split)))

        return pl.BlockSpec((1, total, tile), at)

    in_specs = [pl.BlockSpec((total, all_rows), lambda c, d_ref: (0, 0))] * len(pairs)
    in_specs += [right_spec(start, n) for start, n in zip(starts, tiles)]
    args = [left for left, _ in pairs] + [right for _, right in pairs]
    if got is None:
        out_shape = jax.ShapeDtypeStruct((count, rows, columns), BF16)
        out_specs = pl.BlockSpec((count, rows, tile), lambda c, d_ref: (0, 0, c))
    else:
        in_specs.append(pl.BlockSpec((count, rows, tile), lambda c, d_ref: (0, 0, c)))
        args.append(got)
        out_shape = [jax.ShapeDtypeStruct((count // 2, rows, columns // 2), BF16)] * 4
        mid = steps // 2
        first = pl.BlockSpec(
            (count // 2, rows, tile), lambda c, d_ref: (0, 0, jnp.minimum(c, mid - 1))
        )
        second = pl.BlockSpec(
            (count // 2, rows, tile), lambda c, d_ref: (0, 0, jnp.maximum(c - mid, 0))
        )
        out_specs = [first, first, second, second]
    return pl.pallas_call(
        body,
        out_shape=out_shape,
        grid_spec=pltpu.PrefetchScalarGridSpec(
            num_scalar_prefetch=1,
            grid=(steps,),
            in_specs=in_specs,
            out_specs=out_specs,
            scratch_shapes=[pltpu.VMEM((len(pairs), count * rows, total), BF16)],
        ),
        compiler_params=pltpu.CompilerParams(vmem_limit_bytes=40 * 2**20),
        cost_estimate=pl.CostEstimate(
            flops=total * all_rows * columns,
            bytes_accessed=2 * total * (all_rows + columns) + 2 * all_rows * columns,
            transcendentals=0,
        ),
        name="gradient",
    )(d.reshape(1).astype(jnp.int32), *args)


def head_probs(q, k, far, slope):
    scores = lax.dot_general(q, k, (((1,), (1,)), ((), ())), preferred_element_type=F32)
    scores = scores * (HEAD ** (-0.5)) - slope * far
    raised = jnp.exp(scores - jnp.max(scores, axis=-1, keepdims=True))
    return raised * (1.0 / jnp.sum(raised, axis=-1, keepdims=True))


def flat_frames(block):
    sources, _, rows, lanes = block.shape
    if rows % 16 == 0:
        return block.reshape(sources * rows, lanes)
    return block.astype(F32).reshape(sources * rows, lanes).astype(BF16)


def by_source(value, like):
    sources, _, rows, lanes = like
    if rows % 16 == 0:
        return value.astype(BF16).reshape(sources, 1, rows, lanes)
    return value.reshape(sources, 1, rows, lanes).astype(BF16)


def attend(triple, far, slopes):
    dp, micro, rows, wide = triple.shape
    frames = dp * rows
    width = wide // 3
    pairs = width // 128
    shape = (dp, 1, rows, 128)

    def body(slope_ref, q_ref, k_ref, v_ref, far_ref, out_ref):
        h = pl.program_id(1)
        q, k, v = (flat_frames(ref[...]) for ref in (q_ref, k_ref, v_ref))
        first = lax.broadcasted_iota(jnp.int32, (frames, 128), 1) < HEAD
        zero = jnp.zeros_like(q)
        outs = []
        for j, own in enumerate((jnp.where(first, q, zero), jnp.where(first, zero, q))):
            probs = head_probs(own, k, far_ref[0], slope_ref[h * 2 + j])
            outs.append(jnp.dot(probs.astype(BF16), v, preferred_element_type=F32))
        out_ref[...] = by_source(jnp.where(first, outs[0], outs[1]), shape)

    def spec(offset):
        return pl.BlockSpec(shape, lambda m, h, s: (0, m, 0, h + offset))

    return pl.pallas_call(
        body,
        out_shape=jax.ShapeDtypeStruct((dp, micro, rows, width), BF16),
        grid_spec=pltpu.PrefetchScalarGridSpec(
            num_scalar_prefetch=1,
            grid=(micro, pairs),
            in_specs=[
                spec(0),
                spec(pairs),
                spec(2 * pairs),
                pl.BlockSpec((1, frames, frames), lambda m, h, s: (m, 0, 0)),
            ],
            out_specs=spec(0),
        ),
        compiler_params=pltpu.CompilerParams(vmem_limit_bytes=24 * 2**20),
        cost_estimate=pl.CostEstimate(
            flops=8 * micro * frames * frames * width,
            bytes_accessed=8 * micro * frames * width,
            transcendentals=micro * HEADS * frames * frames,
        ),
        name="attend",
    )(slopes, triple, triple, triple, far)


def attend_back(triple, grad, far, slopes):
    dp, micro, rows, wide = triple.shape
    frames = dp * rows
    width = wide // 3
    pairs = width // 128
    shape = (dp, 1, rows, 128)
    scale = HEAD ** (-0.5)

    def turned(left, right):
        return lax.dot_general(left, right, (((0,), (0,)), ((), ())), preferred_element_type=F32)

    def body(slope_ref, q_ref, k_ref, v_ref, g_ref, far_ref, out_ref):
        h = pl.program_id(1)
        q, k, v, g = (flat_frames(ref[...]) for ref in (q_ref, k_ref, v_ref, g_ref))
        first = lax.broadcasted_iota(jnp.int32, (frames, 128), 1) < HEAD
        zero = jnp.zeros_like(q)
        grads = []
        for j in range(2):
            own_q = jnp.where(first, q, zero) if j == 0 else jnp.where(first, zero, q)
            own_g = jnp.where(first, g, zero) if j == 0 else jnp.where(first, zero, g)
            probs = head_probs(own_q, k, far_ref[0], slope_ref[h * 2 + j])
            back = lax.dot_general(own_g, v, (((1,), (1,)), ((), ())), preferred_element_type=F32)
            back = probs * (back - jnp.sum(back * probs, axis=-1, keepdims=True))
            low = back.astype(BF16)
            grads.append(
                (
                    jnp.dot(low, k, preferred_element_type=F32) * scale,
                    turned(low, q) * scale,
                    turned(probs.astype(BF16), g),
                )
            )
        for i in range(3):
            out_ref[i] = by_source(jnp.where(first, grads[0][i], grads[1][i]), shape)

    def spec(offset):
        return pl.BlockSpec(shape, lambda m, h, s: (0, m, 0, h + offset))

    return pl.pallas_call(
        body,
        out_shape=jax.ShapeDtypeStruct((3, dp, micro, rows, width), BF16),
        grid_spec=pltpu.PrefetchScalarGridSpec(
            num_scalar_prefetch=1,
            grid=(micro, pairs),
            in_specs=[
                spec(0),
                spec(pairs),
                spec(2 * pairs),
                spec(0),
                pl.BlockSpec((1, frames, frames), lambda m, h, s: (m, 0, 0)),
            ],
            out_specs=pl.BlockSpec((3,) + shape, lambda m, h, s: (0, 0, m, 0, h)),
        ),
        compiler_params=pltpu.CompilerParams(vmem_limit_bytes=24 * 2**20),
        cost_estimate=pl.CostEstimate(
            flops=20 * micro * frames * frames * width,
            bytes_accessed=14 * micro * frames * width,
            transcendentals=micro * HEADS * frames * frames,
        ),
        name="attend_back",
    )(slopes, triple, triple, triple, grad, far)


def add_up(values):
    total = values[0].astype(F32)
    for value in values[1:]:
        total = total + value.astype(F32)
    return total.astype(BF16)


class Reduction:
    def __init__(self, pairs, d, dims):
        self.pairs = [(left, right if right.ndim == 3 else right[None]) for left, right in pairs]
        self.d = d
        self.dims = dims
        self.sent = gradient_blocks(self.pairs, d, dims)
        self.got = flip(self.sent, 1)

    def own(self, *ready):
        got = after(self.got, *ready) if ready else self.got
        parts = gradient_blocks(self.pairs, self.d, self.dims, got)
        self.parts = list(parts)
        arrived = flip_pair(parts[0], 1 << self.dims[0], parts[2], 1 << self.dims[-1])
        self.halves = []
        for side, order in ((0, self.dims), (1, self.dims[::-1])):
            stay = parts[2 * side + 1]
            left = [bit for bit in self.dims if bit != order[0]]
            shape = (2,) * len(left) + stay.shape[1:]
            values = [stay.reshape(shape), arrived[side].reshape(shape)]
            self.halves.append((values, list(order[1:]), left))
        self.arrived = arrived[0]
        return self.parts

    def step(self, *ready):
        sends, stays = [], []
        for values, order, left in self.halves:
            at = left.index(order[0])
            sends.append(add_up([lax.index_in_dim(v, 1, at, keepdims=False) for v in values]))
            stays.append([lax.index_in_dim(v, 0, at, keepdims=False) for v in values])
        if ready:
            sends[0] = after(sends[0], *ready)
        bits = [order[0] for _, order, _ in self.halves]
        arrived = flip_pair(sends[0], 1 << bits[0], sends[1], 1 << bits[1])
        self.halves = [
            (stays[i] + [arrived[i]], self.halves[i][1][1:], [b for b in self.halves[i][2] if b != bits[i]])
            for i in (0, 1)
        ]
        self.arrived = arrived[0]
        return sends

    def rows(self):
        while self.halves[0][1]:
            self.step()
        self.value = jnp.concatenate([add_up(values) for values, _, _ in self.halves], axis=1)
        self.stage = 0
        return self.value

    def line(self, *ready):
        value = self.rows()
        if ready:
            self.value = after(value, *ready)
        return self.along()

    def halve(self, extra=None):
        rep = lax.axis_size("rep")
        z = lax.axis_index("rep")
        value = self.rows()
        if extra is not None:
            value = jnp.concatenate([value, extra], axis=0)
        bits = range(rep.bit_length() - 1)
        for bit in bits:
            mine = lax.bitwise_and(lax.shift_right_logical(z, bit), 1)
            size = value.shape[0] // 2
            send = lax.dynamic_slice_in_dim(value, (1 - mine) * size, size, 0)
            keep = lax.dynamic_slice_in_dim(value, mine * size, size, 0)
            value = add_up([keep, rep_flip(send, 1 << bit)])
        for bit in reversed(bits):
            mine = lax.bitwise_and(lax.shift_right_logical(z, bit), 1)
            got = rep_flip(value, 1 << bit)
            lower = jnp.where(mine == 0, value, got)
            upper = jnp.where(mine == 0, got, value)
            value = jnp.concatenate([lower, upper], axis=0)
        return value.astype(F32)

    def along(self, *late):
        rep = lax.axis_size("rep")
        z = lax.axis_index("rep")
        half = rep // 2
        k = self.stage
        self.stage += 1
        value = self.value
        if k < half - 1:
            got = lax.ppermute(value, "rep", [(k, k + 1), (rep - 1 - k, rep - 2 - k)])
            got = after(got, *late) if late else got
            self.value = (value.astype(F32) + got.astype(F32)).astype(BF16)
        elif k == half - 1:
            got = lax.ppermute(value, "rep", [(k, k + 1), (k + 1, k)])
            got = after(got, *late) if late else got
            self.value = (value.astype(F32) + got.astype(F32)).astype(BF16)
        else:
            i = rep - 2 - k
            got = lax.ppermute(value, "rep", [(i + 1, i), (rep - 2 - i, rep - 1 - i)])
            self.value = jnp.where((z == i) | (z == rep - 1 - i), got, value)
        return self.value

    def finish(self):
        while self.stage < lax.axis_size("rep") - 1:
            self.along()
        return self.value.astype(F32)


def matmul(left, right):
    return jnp.dot(left, right, preferred_element_type=F32)


def matmul_nt(left, right):
    return lax.dot_general(left, right, (((1,), (1,)), ((), ())), preferred_element_type=F32)


def matmul_tn(left, right):
    return lax.dot_general(left, right, (((0,), (0,)), ((), ())), preferred_element_type=F32)


def norm_parts(values):
    average = jnp.mean(values, axis=-1, keepdims=True)
    centred = values - average
    spread = jnp.mean(centred * centred, axis=-1, keepdims=True)
    scale = lax.rsqrt(spread + EPS)
    return centred * scale, scale


def norm_back(grad, gain, unit, scale):
    e = grad * gain
    return scale * (
        e
        - jnp.mean(e, axis=-1, keepdims=True)
        - unit * jnp.mean(e * unit, axis=-1, keepdims=True)
    )


def shards(
    inputs,
    skips,
    cotangent,
    dest_slot,
    pack_segments,
    block_live,
    counts,
    w_skip,
    b_skip,
    g_one,
    b_one,
    w_qkv,
    w_out,
    b_out,
    g_two,
    b_two,
    w_up,
    c_up,
    w_down,
    c_down,
):
    dp = lax.axis_size("dp")
    rep = lax.axis_size("rep")
    d = lax.axis_index("dp")
    z = lax.axis_index("rep")
    micro = inputs.shape[0]
    frames = inputs.shape[2]
    width = inputs.shape[3]
    blocks = dest_slot.shape[2]
    block = frames // blocks
    per_pair = blocks // dp
    total = micro * frames
    bits = dp.bit_length() - 1
    place = jnp.stack([z, lax.rem(d, 8)]).astype(jnp.int32)
    dims = list(range(1, bits))
    own_skip = own_chunk(place, width, w_skip)
    own_mid = own_chunk(place, width, w_qkv, w_out)
    own_up = own_chunk(place, width, w_up)
    own_down = own_chunk(place, width, w_down)
    far_skip, first_skip = fetch_far(own_skip, None)
    far_mid, first_mid = fetch_far(own_mid, first_skip)
    far_both, _ = fetch_far(jnp.concatenate([own_up, own_down], axis=0), first_mid)
    both = far_both.reshape(rep - 1, -1, width)
    up_rows = own_up.shape[0]
    far_up = both[:, :up_rows].reshape(-1, width)
    far_down = both[:, up_rows:].reshape(-1, width)

    small = jnp.concatenate(
        [dest_slot.reshape(-1), block_live.reshape(-1), counts.reshape(-1)]
    )
    every = small[None]
    for bit in range(bits):
        every = jnp.concatenate([every, flip(every, 1 << bit)], axis=0)

    run_skip = Spread(far_skip, every)
    moved = run_skip.first
    run_skip.cross()
    run_mid = Spread(far_mid, run_skip.second)
    run_mid.cross()
    run_up = Spread(far_up, run_mid.second)
    run_down = Spread(far_down, run_up.first)
    run_up.cross()
    run_down.cross(run_up.second)
    parts_skip, parts_mid = run_skip.parts, run_mid.parts
    parts_up, parts_down = run_up.parts, run_down.parts
    mid_rows = w_qkv.shape[0] // 8
    full_skip = assemble(w_skip, parts_skip, place, 0, 1)
    full_qkv = assemble(w_qkv, parts_mid, place, 0, 3)
    full_out = assemble(w_out, parts_mid, place, 3 * mid_rows, 1)
    full_up = assemble(w_up, parts_up, place, 0, w_up.shape[1] // width)
    full_down = assemble(w_down, parts_down, place, 0, 1)

    slots = after(dest_slot, moved)[:, 0, :]
    every = after(every, moved)
    span = micro * blocks
    all_slots = every[:, :span].reshape(dp, micro, blocks)
    all_live = every[:, span : 2 * span].reshape(dp, micro, blocks)
    source = jnp.bitwise_xor(jnp.arange(dp), d)
    count_total = jnp.sum(every[:, 2 * span]).astype(F32).reshape(1, 1)
    count_total = after(count_total, far_down)
    for bit in range(rep.bit_length() - 1):
        count_total = count_total + rep_flip(count_total, 1 << bit)
    share = counts[0, 0].astype(F32) * (dp * rep) / count_total[0, 0]

    rank = jnp.sum(
        (all_slots[:, :, None, :] < all_slots[:, :, :, None]).astype(jnp.int32), axis=3
    )
    mine_rank = jnp.sum((slots[:, None, :] < slots[:, :, None]).astype(jnp.int32), axis=2)
    here = (all_slots // blocks) == d
    arrive = source[:, None, None] * per_pair + rank % per_pair
    arrive = jnp.where(here, arrive, -1)
    match = arrive[None] == jnp.arange(blocks)[:, None, None, None]
    placing = jnp.sum(jnp.where(match, (all_slots % blocks)[None], 0), axis=(1, 3)).T
    pick = placing[:, :, None] == jnp.arange(blocks)[None, None, :]
    seg_blocks = pack_segments[:, 0, :].reshape(micro, blocks, block)
    segment = jnp.sum(jnp.where(pick[..., None], seg_blocks[:, None], 0), axis=2)
    segment = segment.reshape(micro, frames)
    live_count = jnp.sum(jnp.where(pick, block_live[:, 0, None, :], 0), axis=2)
    inner = jnp.arange(frames) % block
    live = inner[None] < jnp.repeat(live_count, block, axis=1)
    position = jnp.repeat(placing * block, block, axis=1) + inner[None]
    flat_live = jnp.transpose(all_live, (1, 0, 2)).reshape(micro, dp * blocks)
    flat_slot = (source[:, None] * blocks + jnp.arange(blocks)).reshape(-1)
    own_live = jnp.sum(jnp.where(slots[:, :, None] == flat_slot, flat_live[:, None], 0), axis=2)
    keep_rows = (inner[None] < jnp.repeat(own_live, block, axis=1)).astype(F32)
    keep_rows = keep_rows.reshape(total, 1)

    target = mine_rank // per_pair
    row = (target * micro + jnp.arange(micro)[:, None]) * per_pair + mine_rank % per_pair
    row = jnp.repeat(row.reshape(-1) * block, block) + jnp.tile(jnp.arange(block), micro * blocks)
    shuffle = (jnp.arange(total)[:, None] == row[None, :]).astype(BF16)

    def to_packs(values):
        sent = matmul(shuffle, values).astype(BF16)
        got = lax.all_to_all(
            sent.reshape(dp, total // dp, width), "dp", split_axis=0, concat_axis=0, tiled=True
        )
        return got.reshape(total, width)

    def to_owners(values):
        sent = values.reshape(dp, total // dp, width)
        got = lax.all_to_all(sent, "dp", split_axis=0, concat_axis=0, tiled=True)
        return matmul_tn(shuffle, got.reshape(total, width))

    joined = jnp.concatenate(
        [inputs.reshape(total, width), skips.reshape(total, width)], axis=1
    )
    base = matmul(joined, full_skip) + b_skip
    unit_one, scale_one = norm_parts(base)
    normed = to_packs((unit_one * g_one + b_one).astype(BF16))
    triple = matmul(after(normed, far_up), full_qkv).astype(BF16)
    triple = triple.reshape(dp, micro, per_pair * block, 3 * width)
    slopes = 2.0 ** (-8.0 * (jnp.arange(HEADS, dtype=F32) + 1.0) / HEADS)
    distance = jnp.abs(position[:, :, None] - position[:, None, :]).astype(F32)
    allowed = (segment[:, :, None] == segment[:, None, :]) & (
        live[:, None, :] | (position[:, :, None] == position[:, None, :])
    )
    far = jnp.where(allowed, distance, 1e32)
    attended = after(attend(triple, far, slopes), run_down.first)
    attended = to_owners(attended).astype(BF16)
    mixed = base + matmul(attended, full_out) + b_out
    unit_two, scale_two = norm_parts(mixed)
    normed_two = (unit_two * g_two + b_two).astype(BF16)
    normed_two = after(normed_two, run_up.second)
    hidden = matmul(normed_two, full_up) + c_up
    phi = 0.5 * (1.0 + lax.erf(hidden * (0.5**0.5)))
    active = (hidden * phi).astype(BF16)
    slope = (phi + hidden * jnp.exp(-0.5 * hidden * hidden) * ((2 * jnp.pi) ** -0.5)).astype(BF16)

    scaled = (cotangent.reshape(total, width).astype(F32) * share).astype(BF16)
    grad_result = scaled * keep_rows.astype(BF16)
    red_down = Reduction([(active, grad_result)], d, dims)
    grad_result = after(grad_result, red_down.sent)
    grad_result_full = grad_result.astype(F32)
    grad_active = matmul_nt(grad_result, full_down)
    grad_hidden = slope.astype(F32) * grad_active
    hidden_low = grad_hidden.astype(BF16)
    hidden_low = after(hidden_low, *red_down.own(hidden_low))
    red_up = Reduction([(normed_two, hidden_low)], d, dims)
    hidden_low = after(hidden_low, red_up.sent)
    grad_normed_two = matmul_nt(hidden_low, full_up)
    grad_mixed = grad_result_full + norm_back(grad_normed_two, g_two, unit_two, scale_two)
    mixed_low = grad_mixed.astype(BF16)
    grad_attended = to_packs(matmul_nt(mixed_low, full_out).astype(BF16))
    up_parts = red_up.own(mixed_low)
    down_sends = red_down.step(*up_parts)
    active_late = after(active, *up_parts, *down_sends)
    result = mixed + matmul(active_late, full_down) + c_down
    output = (result * keep_rows).astype(BF16)
    grad_attended = after(grad_attended, output)
    grad_attended = grad_attended.reshape(dp, micro, per_pair * block, width)
    grad_triple = attend_back(triple, grad_attended, far, slopes).reshape(3, total, width)
    up_sends = red_up.step(grad_triple, red_down.arrived)
    red_mid = Reduction([(attended, mixed_low), (normed, grad_triple)], d, dims)
    down_rows = red_down.rows()
    grad_normed = sum(
        matmul_nt(grad_triple[i], full_qkv[:, i * width : (i + 1) * width]) for i in range(3)
    )
    grad_normed = to_owners(after(grad_normed.astype(BF16), down_rows, *up_sends))
    red_down.along()
    grad_normed = after(grad_normed, red_mid.sent)
    grad_base = grad_mixed + norm_back(grad_normed, g_one, unit_one, scale_one)
    base_low = grad_base.astype(BF16)
    red_skip = Reduction([(joined, base_low)], d, dims)
    mid_parts = red_mid.own(red_skip.sent)
    red_down.along(*mid_parts)
    red_up.line(*mid_parts)
    base_low = after(base_low, *mid_parts)
    skip_parts = red_skip.own(*mid_parts)
    base_low = after(base_low, *skip_parts)
    grad_joined = matmul_nt(base_low, full_skip).astype(BF16)
    vectors = (
        jnp.sum(grad_base, axis=0),
        jnp.sum(grad_normed * unit_one, axis=0),
        jnp.sum(grad_normed, axis=0),
        jnp.sum(grad_mixed, axis=0),
        jnp.sum(grad_normed_two * unit_two, axis=0),
        jnp.sum(grad_normed_two, axis=0),
        jnp.sum(grad_hidden, axis=0),
        jnp.sum(grad_result_full, axis=0),
    )
    lengths = [v.shape[0] for v in vectors]
    summed = after(jnp.concatenate(vectors), *skip_parts).reshape(-1, 128)
    for bit in range(bits):
        summed = summed + flip(summed, 1 << bit)
    mid_sends = red_mid.step(*skip_parts)
    red_skip.step(*mid_sends)
    skip_columns = w_skip.shape[1]
    extra = jnp.pad(summed.reshape(-1), (0, -summed.size % (16 * rep * skip_columns)))
    extra = extra.reshape(-1, skip_columns).astype(BF16)
    final_mid = red_mid.halve()
    final_skip = red_skip.halve(extra)
    own_rows = w_skip.shape[0] * rep // dp
    summed = final_skip[own_rows:].reshape(-1)
    finals = [
        red_down.finish(),
        red_up.finish(),
        final_mid[:, :width],
        final_mid[:, width:],
        final_skip[:own_rows],
    ]
    sums = []
    offset = 0
    for length in lengths:
        sums.append(summed[offset : offset + length])
        offset += length

    def as_owned(values):
        return values.reshape(inputs.shape)

    return (
        as_owned(output),
        as_owned(grad_joined[:, :width]),
        as_owned(grad_joined[:, width:]),
        finals[4],
        sums[0],
        sums[1],
        sums[2],
        finals[3],
        finals[2],
        sums[3],
        sums[4],
        sums[5],
        finals[1],
        sums[6],
        finals[0],
        sums[7],
    )


def solution(mesh):
    frames = P(None, "rep", "dp", None)
    slots = P(None, "rep", "dp")
    rows = P("rep", None)
    whole = P()
    in_specs = (
        (frames,) * 3
        + (slots,) * 3
        + (P("dp", "rep"), rows, whole, whole, whole, rows, rows)
        + (whole,) * 3
        + (rows, whole, rows, whole)
    )
    split = P("dp", None)
    out_specs = (
        (frames,) * 3
        + (split,)
        + (whole,) * 3
        + (split, split)
        + (whole,) * 3
        + (split, whole, split, whole)
    )
    return jax.shard_map(shards, mesh=mesh, in_specs=in_specs, out_specs=out_specs, check_vma=False)
```

```python
import jax
import jax.numpy as jnp
from jax import lax
from jax.experimental import pallas as pl
from jax.experimental.pallas import tpu as pltpu
from jax.sharding import PartitionSpec as P

HEADS = 16
HEAD = 64
EPS = 1e-05
F32 = jnp.float32
BF16 = jnp.bfloat16
LIGHT = pl.CostEstimate(flops=1024, bytes_accessed=1024, transcendentals=0)


def flip(value, bit):
    n = lax.axis_size("dp")
    return lax.ppermute(value, "dp", [(i, i ^ bit) for i in range(n)])


def rep_flip(value, bit):
    n = lax.axis_size("rep")
    return lax.ppermute(value, "rep", [(i, i ^ bit) for i in range(n)])


def after(value, *earlier):
    return lax.optimization_barrier((value,) + earlier)[0]


def flip_pair(left, left_bit, right, right_bit, late=()):
    got = (flip(left, left_bit), flip(right, right_bit))
    return lax.optimization_barrier(got + tuple(late))[:2]


def assemble(w_local, parts, place, row_at, tiles):
    rep = lax.axis_size("rep")
    shard_rows, columns = w_local.shape
    rows = shard_rows // 8
    tile = columns // tiles
    half = tile // 2
    chunk_rows = parts[0][0].shape[0] // (len(parts[0][1]) * (rep - 1))
    arrays = [part[0] for part in parts]
    count = 1 + sum(len(part[1]) for part in parts) * (rep - 1) * tiles

    def body(place_ref, local_ref, *refs):
        out_ref, sems = refs[len(parts)], refs[len(parts) + 1]
        z = place_ref[0]
        e = place_ref[1]
        copies = [
            pltpu.make_async_copy(
                local_ref,
                out_ref.at[pl.ds(pl.multiple_of(z * shard_rows, 16), shard_rows), :],
                sems.at[0],
            )
        ]
        for ref, (_, runs) in zip(refs, parts):
            for k, (side, rel) in enumerate(runs):
                chunk = jnp.bitwise_xor(e, rel)
                for s, apart in enumerate(far_order(rep), 1):
                    shard = jnp.bitwise_xor(z, apart)
                    start = pl.multiple_of(shard * shard_rows + chunk * rows, 16)
                    for t in range(tiles):
                        at = (k * (rep - 1) + s - 1) * chunk_rows + row_at + t * rows
                        copies.append(
                            pltpu.make_async_copy(
                                ref.at[pl.ds(at, rows), :],
                                out_ref.at[pl.ds(start, rows), pl.ds(t * tile + side * half, half)],
                                sems.at[len(copies)],
                            )
                        )
        for copy in copies:
            copy.start()
        for copy in copies:
            copy.wait()

    return pl.pallas_call(
        body,
        out_shape=jax.ShapeDtypeStruct((shard_rows * rep, columns), w_local.dtype),
        in_specs=[pl.BlockSpec(memory_space=pltpu.SMEM)]
        + [pl.BlockSpec(memory_space=pl.ANY)] * (1 + len(parts)),
        out_specs=pl.BlockSpec(memory_space=pltpu.VMEM),
        scratch_shapes=[pltpu.SemaphoreType.DMA((count,))],
        compiler_params=pltpu.CompilerParams(vmem_limit_bytes=24 * 2**20),
        cost_estimate=LIGHT,
        name="assemble",
    )(place, w_local, *arrays)


def own_chunk(place, width, *shards_local):
    pieces = []
    for w_local in shards_local:
        rows = w_local.shape[0] // 8
        own = lax.dynamic_slice_in_dim(w_local, place[1] * rows, rows, 0)
        for t in range(w_local.shape[1] // width):
            pieces.append(own[:, t * width : (t + 1) * width])
    return jnp.concatenate(pieces, axis=0)


def pack(arrays, outs):
    count = sum(len(out) for out in outs)

    def body(*refs):
        sources, targets, sems = refs[: len(arrays)], refs[len(arrays) : -1], refs[-1]
        copies = []
        for target, out in zip(targets, outs):
            at = 0
            for which, row, rows, column, columns in out:
                copies.append(
                    pltpu.make_async_copy(
                        sources[which].at[pl.ds(row, rows), pl.ds(column, columns)],
                        target.at[pl.ds(at, rows), :],
                        sems.at[len(copies)],
                    )
                )
                at += rows
        for copy in copies:
            copy.start()
        for copy in copies:
            copy.wait()

    return pl.pallas_call(
        body,
        out_shape=[
            jax.ShapeDtypeStruct((sum(item[2] for item in out), out[0][4]), arrays[0].dtype)
            for out in outs
        ],
        in_specs=[pl.BlockSpec(memory_space=pl.ANY)] * len(arrays),
        out_specs=[pl.BlockSpec(memory_space=pltpu.VMEM)] * len(outs),
        scratch_shapes=[pltpu.SemaphoreType.DMA((count,))],
        compiler_params=pltpu.CompilerParams(vmem_limit_bytes=24 * 2**20),
        cost_estimate=LIGHT,
        name="pack",
    )(*arrays)


def fetch_far(own, previous):
    rep = lax.axis_size("rep")
    if previous is not None:
        own = after(own, previous)
    gots = []
    for bit in reversed(range(rep.bit_length() - 1)):
        held = [own] + gots
        if gots:
            (sent,) = pack(held, [[(i, 0, a.shape[0], 0, a.shape[1]) for i, a in enumerate(held)]])
        else:
            sent = own
        gots.append(rep_flip(sent, 1 << bit))
    return gots


def far_rows(gots, rows, start, size):
    items = []
    for i, got in enumerate(gots):
        for k in range(got.shape[0] // rows):
            items.append((i, k * rows + start, size))
    return items


def far_order(rep):
    order = [0]
    for bit in reversed(range(rep.bit_length() - 1)):
        order = order + [distance ^ (1 << bit) for distance in order]
    return order[1:]


class Spread:
    def __init__(self, gots, rows, start, size, *previous):
        width = gots[0].shape[1]
        half = width // 2
        if previous:
            gots = [after(gots[0], *previous)] + gots[1:]
        items = far_rows(gots, rows, start, size)
        left, right = pack(
            gots, [[item + (column, half) for item in items] for column in (0, half)]
        )
        got_left, got_right = flip_pair(left, 2, right, 4)
        n = left.shape[0]
        whole = [(i, 0, n, 0, half) for i in range(4)]
        self.pairs = pack([left, got_left, right, got_right], [whole[:2], whole[2:]])
        self.n = n
        self.half = half
        self.first = self.pairs[0]

    def cross(self, *previous, late=()):
        left, right = self.pairs
        if previous:
            left = after(left, *previous)
        got = flip_pair(left, 4, right, 2, late)
        self.second = got[0]
        self.got = got
        return self

    def share(self, *previous):
        got = self.got
        if previous:
            got = (after(got[0], *previous), got[1])
        whole = [(i, 0, 2 * self.n, 0, self.half) for i in range(4)]
        (every,) = pack([self.pairs[0], got[0], self.pairs[1], got[1]], [whole])
        other = flip(every, 1)
        runs = [(0, 0), (0, 2), (0, 4), (0, 6), (1, 0), (1, 4), (1, 2), (1, 6)]
        return [(every, runs), (other, [(side, rel | 1) for side, rel in runs])]


def plan_order(all_slots, all_live, codes, d, block):
    micro, owners = all_slots.shape
    frames = codes.shape[1]
    blocks = frames // block
    dp = owners // blocks
    per_pair = blocks // dp
    total = micro * frames

    def column(row):
        return jnp.broadcast_to(row, (128, row.shape[1])).T[:, :1]

    def as_row(values):
        return jnp.broadcast_to(values, (values.shape[0], 128)).T[:1, :]

    def body(d_ref, slots_ref, live_ref, codes_ref, far_ref, keep_ref, shuffle_ref):
        me = d_ref[0]
        lane = lax.broadcasted_iota(jnp.int32, (1, owners), 1)
        source = jnp.bitwise_xor(lax.div(lane, jnp.int32(blocks)), me)
        first_slot = (source * blocks).astype(F32) + lax.rem(lane, jnp.int32(blocks)).astype(F32)
        source_col = column(source.astype(F32))
        frame = lax.broadcasted_iota(jnp.int32, (frames, 1), 0)
        block_of = lax.div(frame, jnp.int32(block)).astype(F32)
        inner = lax.rem(frame, jnp.int32(block)).astype(F32)
        low = (me * blocks).astype(F32)
        rows = []
        for m in range(micro):
            slots = slots_ref[pl.ds(m, 1), :]
            slots_col = column(slots)
            same = source_col == source.astype(F32)
            rank = jnp.sum(jnp.where(same & (slots_col < slots), 1.0, 0.0), axis=0, keepdims=True)
            here = (slots >= low) & (slots < low + blocks)
            arrive = source.astype(F32) * per_pair + rank - (me * per_pair).astype(F32)
            arrive = jnp.where(here, arrive, -1.0)
            placed = jnp.sum(
                jnp.where(arrive == block_of, slots - low, 0.0), axis=1, keepdims=True
            )
            position = placed * block + inner
            at = lax.broadcasted_iota(jnp.int32, (1, frames), 1).astype(F32)
            code = jnp.sum(
                jnp.where(at == position, codes_ref[pl.ds(m, 1), :], 0.0), axis=1, keepdims=True
            )
            position_row, code_row = as_row(position), as_row(code)
            segment, segment_row = jnp.floor(code * 0.5), jnp.floor(code_row * 0.5)
            live_row = code_row - 2.0 * segment_row
            distance = jnp.abs(position - position_row)
            allowed = (segment == segment_row) & ((live_row > 0.5) | (distance < 0.5))
            far_ref[m] = jnp.where(allowed, distance, 1e32)
            own = lane < blocks
            mine = jnp.sum(
                jnp.where(own & (lane.astype(F32) == block_of), slots, 0.0), axis=1, keepdims=True
            )
            alive = jnp.sum(
                jnp.where(first_slot == mine, live_ref[pl.ds(m, 1), :], 0.0), axis=1, keepdims=True
            )
            keep_ref[pl.ds(m * frames, frames), :] = jnp.broadcast_to(
                jnp.where(inner < alive, 1.0, 0.0), (frames, 128)
            )
            my_rank = jnp.sum(
                jnp.where(own & (lane.astype(F32) == block_of), rank, 0.0), axis=1, keepdims=True
            )
            target = jnp.floor((my_rank + 0.5) / per_pair)
            row = (target * micro + m) * per_pair + (my_rank - target * per_pair)
            rows.append(as_row(row * block + inner))
        goal = jnp.concatenate(rows, axis=1)
        spot = lax.broadcasted_iota(jnp.int32, (total, total), 0).astype(F32)
        shuffle_ref[...] = jnp.where(spot == goal, 1.0, 0.0).astype(BF16)

    vmem = pl.BlockSpec(memory_space=pltpu.VMEM)
    return pl.pallas_call(
        body,
        out_shape=[
            jax.ShapeDtypeStruct((micro, frames, frames), F32),
            jax.ShapeDtypeStruct((total, 128), F32),
            jax.ShapeDtypeStruct((total, total), BF16),
        ],
        in_specs=[pl.BlockSpec(memory_space=pltpu.SMEM), vmem, vmem, vmem],
        out_specs=[vmem, vmem, vmem],
        compiler_params=pltpu.CompilerParams(vmem_limit_bytes=40 * 2**20),
        cost_estimate=LIGHT,
        name="plan_order",
    )(d.reshape(1).astype(jnp.int32), all_slots, all_live, codes)


def gradient_blocks(pairs, d, dims, got=None):
    dp = lax.axis_size("dp")
    total, all_rows = pairs[0][0].shape
    width = pairs[0][1].shape[2]
    tiles = [right.shape[0] for _, right in pairs]
    columns = sum(tiles) * width
    rows = all_rows // dp
    count = dp // 2
    odd = 1 if got is None else 0
    tile = min(width, 512)
    split = width // tile
    steps = sum(tiles) * split
    starts = [sum(tiles[:i]) * split for i in range(len(tiles))]

    def distance(p):
        rel = odd
        for k, bit in enumerate(dims):
            rel += ((p >> (len(dims) - 1 - k)) & 1) << bit
        return rel

    upper = [p for p in range(count) if p >= count // 2]
    lower = [p for p in range(count) if p < count // 2]
    odds = [p for p in range(count) if p % 2 == 1]
    evens = [p for p in range(count) if p % 2 == 0]
    chosen = (upper, lower, odds, evens)

    if rows % 128 != 0:
        products = []
        for left, right in pairs:
            flat = jnp.transpose(right, (1, 0, 2)).reshape(total, -1)
            products.append(matmul_tn(left, flat))
        product = jnp.concatenate(products, axis=1).reshape(dp, rows, columns)
        rel = jnp.array([distance(p) for p in range(count)], jnp.int32)
        product = product[jnp.bitwise_xor(rel, d)]
        if got is None:
            return product.astype(BF16)
        product = (product + got.astype(F32)).astype(BF16)
        half = columns // 2
        return [
            jnp.stack([product[p, :, side * half : (side + 1) * half] for p in ps])
            for side, ps in zip((0, 0, 1, 1), chosen)
        ]

    def body(d_ref, *refs):
        lefts = refs[: len(pairs)]
        rights = refs[len(pairs) : 2 * len(pairs)]
        rest = refs[2 * len(pairs) :]
        turned_ref = rest[-1]
        got_ref = None if got is None else rest[0]
        outs = rest[:-1] if got is None else rest[1:-1]
        c = pl.program_id(0)

        @pl.when(c == 0)
        def _():
            for i, left_ref in enumerate(lefts):
                for p in range(count):
                    at = pl.multiple_of(jnp.bitwise_xor(d_ref[0], distance(p)) * rows, 128)
                    turned_ref[i, pl.ds(p * rows, rows), :] = left_ref[:, pl.ds(at, rows)].T

        def piece(i, p):
            return jnp.dot(
                turned_ref[i, pl.ds(p * rows, rows), :], rights[i][0], preferred_element_type=F32
            )

        def write(i, half):
            for p in range(count):
                value = piece(i, p)
                if got is None:
                    outs[0][p] = value.astype(BF16)
                    continue
                value = (value + got_ref[p].astype(F32)).astype(BF16)
                for which in (2 * half, 2 * half + 1):
                    if p in chosen[which]:
                        outs[which][chosen[which].index(p)] = value

        for i in range(len(pairs)):
            for half in (0, 1):
                low = max(starts[i], half * (steps // 2))
                high = min(starts[i] + tiles[i] * split, (half + 1) * (steps // 2))
                if low < high:
                    pl.when((c >= low) & (c < high))(lambda i=i, half=half: write(i, half))

    def right_spec(start, n):
        def at(c, d_ref):
            k = jnp.clip(c - start, 0, n * split - 1)
            return (lax.div(k, jnp.int32(split)), 0, lax.rem(k, jnp.int32(split)))

        return pl.BlockSpec((1, total, tile), at)

    in_specs = [pl.BlockSpec((total, all_rows), lambda c, d_ref: (0, 0))] * len(pairs)
    in_specs += [right_spec(start, n) for start, n in zip(starts, tiles)]
    args = [left for left, _ in pairs] + [right for _, right in pairs]
    if got is None:
        out_shape = jax.ShapeDtypeStruct((count, rows, columns), BF16)
        out_specs = pl.BlockSpec((count, rows, tile), lambda c, d_ref: (0, 0, c))
    else:
        in_specs.append(pl.BlockSpec((count, rows, tile), lambda c, d_ref: (0, 0, c)))
        args.append(got)
        out_shape = [jax.ShapeDtypeStruct((count // 2, rows, columns // 2), BF16)] * 4
        mid = steps // 2
        first = pl.BlockSpec(
            (count // 2, rows, tile), lambda c, d_ref: (0, 0, jnp.minimum(c, mid - 1))
        )
        second = pl.BlockSpec(
            (count // 2, rows, tile), lambda c, d_ref: (0, 0, jnp.maximum(c - mid, 0))
        )
        out_specs = [first, first, second, second]
    return pl.pallas_call(
        body,
        out_shape=out_shape,
        grid_spec=pltpu.PrefetchScalarGridSpec(
            num_scalar_prefetch=1,
            grid=(steps,),
            in_specs=in_specs,
            out_specs=out_specs,
            scratch_shapes=[pltpu.VMEM((len(pairs), count * rows, total), BF16)],
        ),
        compiler_params=pltpu.CompilerParams(vmem_limit_bytes=40 * 2**20),
        cost_estimate=LIGHT,
        name="gradient",
    )(d.reshape(1).astype(jnp.int32), *args)


def head_probs(q, k, far, slope):
    scores = lax.dot_general(q, k, (((1,), (1,)), ((), ())), preferred_element_type=F32)
    scores = scores * (HEAD ** (-0.5)) - slope * far
    raised = jnp.exp(scores - jnp.max(scores, axis=-1, keepdims=True))
    return raised * (1.0 / jnp.sum(raised, axis=-1, keepdims=True))


def flat_frames(block):
    sources, _, rows, lanes = block.shape
    if rows % 16 == 0:
        return block.reshape(sources * rows, lanes)
    return block.astype(F32).reshape(sources * rows, lanes).astype(BF16)


def by_source(value, like):
    sources, _, rows, lanes = like
    if rows % 16 == 0:
        return value.astype(BF16).reshape(sources, 1, rows, lanes)
    return value.reshape(sources, 1, rows, lanes).astype(BF16)


def attend(triple, far, slopes):
    dp, micro, rows, wide = triple.shape
    frames = dp * rows
    width = wide // 3
    pairs = width // 128
    shape = (dp, 1, rows, 128)

    def body(slope_ref, q_ref, k_ref, v_ref, far_ref, out_ref):
        h = pl.program_id(1)
        q, k, v = (flat_frames(ref[...]) for ref in (q_ref, k_ref, v_ref))
        first = lax.broadcasted_iota(jnp.int32, (frames, 128), 1) < HEAD
        zero = jnp.zeros_like(q)
        outs = []
        for j, own in enumerate((jnp.where(first, q, zero), jnp.where(first, zero, q))):
            probs = head_probs(own, k, far_ref[0], slope_ref[h * 2 + j])
            outs.append(jnp.dot(probs.astype(BF16), v, preferred_element_type=F32))
        out_ref[...] = by_source(jnp.where(first, outs[0], outs[1]), shape)

    def spec(offset):
        return pl.BlockSpec(shape, lambda m, h, s: (0, m, 0, h + offset))

    return pl.pallas_call(
        body,
        out_shape=jax.ShapeDtypeStruct((dp, micro, rows, width), BF16),
        grid_spec=pltpu.PrefetchScalarGridSpec(
            num_scalar_prefetch=1,
            grid=(micro, pairs),
            in_specs=[
                spec(0),
                spec(pairs),
                spec(2 * pairs),
                pl.BlockSpec((1, frames, frames), lambda m, h, s: (m, 0, 0)),
            ],
            out_specs=spec(0),
        ),
        compiler_params=pltpu.CompilerParams(vmem_limit_bytes=24 * 2**20),
        cost_estimate=LIGHT,
        name="attend",
    )(slopes, triple, triple, triple, far)


def attend_back(triple, grad, far, slopes):
    dp, micro, rows, wide = triple.shape
    frames = dp * rows
    width = wide // 3
    pairs = width // 128
    shape = (dp, 1, rows, 128)
    scale = HEAD ** (-0.5)

    def turned(left, right):
        return lax.dot_general(left, right, (((0,), (0,)), ((), ())), preferred_element_type=F32)

    def body(slope_ref, q_ref, k_ref, v_ref, g_ref, far_ref, out_ref):
        h = pl.program_id(1)
        q, k, v, g = (flat_frames(ref[...]) for ref in (q_ref, k_ref, v_ref, g_ref))
        first = lax.broadcasted_iota(jnp.int32, (frames, 128), 1) < HEAD
        zero = jnp.zeros_like(q)
        grads = []
        for j in range(2):
            own_q = jnp.where(first, q, zero) if j == 0 else jnp.where(first, zero, q)
            own_g = jnp.where(first, g, zero) if j == 0 else jnp.where(first, zero, g)
            probs = head_probs(own_q, k, far_ref[0], slope_ref[h * 2 + j])
            back = lax.dot_general(own_g, v, (((1,), (1,)), ((), ())), preferred_element_type=F32)
            back = probs * (back - jnp.sum(back * probs, axis=-1, keepdims=True))
            low = back.astype(BF16)
            grads.append(
                (
                    jnp.dot(low, k, preferred_element_type=F32) * scale,
                    turned(low, q) * scale,
                    turned(probs.astype(BF16), g),
                )
            )
        for i in range(3):
            out_ref[i] = by_source(jnp.where(first, grads[0][i], grads[1][i]), shape)

    def spec(offset):
        return pl.BlockSpec(shape, lambda m, h, s: (0, m, 0, h + offset))

    return pl.pallas_call(
        body,
        out_shape=jax.ShapeDtypeStruct((3, dp, micro, rows, width), BF16),
        grid_spec=pltpu.PrefetchScalarGridSpec(
            num_scalar_prefetch=1,
            grid=(micro, pairs),
            in_specs=[
                spec(0),
                spec(pairs),
                spec(2 * pairs),
                spec(0),
                pl.BlockSpec((1, frames, frames), lambda m, h, s: (m, 0, 0)),
            ],
            out_specs=pl.BlockSpec((3,) + shape, lambda m, h, s: (0, 0, m, 0, h)),
        ),
        compiler_params=pltpu.CompilerParams(vmem_limit_bytes=24 * 2**20),
        cost_estimate=LIGHT,
        name="attend_back",
    )(slopes, triple, triple, triple, grad, far)


def add_up(values):
    total = values[0].astype(F32)
    for value in values[1:]:
        total = total + value.astype(F32)
    return total.astype(BF16)


class Reduction:
    def __init__(self, pairs, d, dims):
        self.pairs = [(left, right if right.ndim == 3 else right[None]) for left, right in pairs]
        self.d = d
        self.dims = dims
        self.sent = gradient_blocks(self.pairs, d, dims)
        self.got = flip(self.sent, 1)

    def own(self, *ready):
        got = after(self.got, *ready) if ready else self.got
        parts = gradient_blocks(self.pairs, self.d, self.dims, got)
        self.parts = list(parts)
        arrived = flip_pair(parts[0], 1 << self.dims[0], parts[2], 1 << self.dims[-1])
        self.halves = []
        for side, order in ((0, self.dims), (1, self.dims[::-1])):
            stay = parts[2 * side + 1]
            left = [bit for bit in self.dims if bit != order[0]]
            shape = (2,) * len(left) + stay.shape[1:]
            values = [stay.reshape(shape), arrived[side].reshape(shape)]
            self.halves.append((values, list(order[1:]), left))
        self.arrived = arrived[0]
        return self.parts

    def step(self, *ready):
        sends, stays = [], []
        for values, order, left in self.halves:
            at = left.index(order[0])
            sends.append(add_up([lax.index_in_dim(v, 1, at, keepdims=False) for v in values]))
            stays.append([lax.index_in_dim(v, 0, at, keepdims=False) for v in values])
        if ready:
            sends[0] = after(sends[0], *ready)
        bits = [order[0] for _, order, _ in self.halves]
        arrived = flip_pair(sends[0], 1 << bits[0], sends[1], 1 << bits[1])
        self.halves = [
            (stays[i] + [arrived[i]], self.halves[i][1][1:], [b for b in self.halves[i][2] if b != bits[i]])
            for i in (0, 1)
        ]
        self.arrived = arrived[0]
        return sends

    def rows(self):
        while self.halves[0][1]:
            self.step()
        self.value = jnp.concatenate([add_up(values) for values, _, _ in self.halves], axis=1)
        self.stage = 0
        return self.value

    def line(self, *late):
        self.rows()
        return self.along(*late)

    def halve(self, extra=None, ready=()):
        rep = lax.axis_size("rep")
        z = lax.axis_index("rep")
        value = self.rows()
        if extra is not None:
            value = jnp.concatenate([value, extra], axis=0)
        if ready:
            value = after(value, *ready)
        bits = range(rep.bit_length() - 1)
        for bit in bits:
            mine = lax.bitwise_and(lax.shift_right_logical(z, bit), 1)
            size = value.shape[0] // 2
            send = lax.dynamic_slice_in_dim(value, (1 - mine) * size, size, 0)
            keep = lax.dynamic_slice_in_dim(value, mine * size, size, 0)
            value = add_up([keep, rep_flip(send, 1 << bit)])
        for bit in reversed(bits):
            mine = lax.bitwise_and(lax.shift_right_logical(z, bit), 1)
            got = rep_flip(value, 1 << bit)
            lower = jnp.where(mine == 0, value, got)
            upper = jnp.where(mine == 0, got, value)
            value = jnp.concatenate([lower, upper], axis=0)
        return value.astype(F32)

    def along(self, *late):
        rep = lax.axis_size("rep")
        z = lax.axis_index("rep")
        half = rep // 2
        k = self.stage
        self.stage += 1
        value = self.value
        if k < half - 1:
            got = lax.ppermute(value, "rep", [(k, k + 1), (rep - 1 - k, rep - 2 - k)])
            got = after(got, *late) if late else got
            self.value = (value.astype(F32) + got.astype(F32)).astype(BF16)
        elif k == half - 1:
            got = lax.ppermute(value, "rep", [(k, k + 1), (k + 1, k)])
            got = after(got, *late) if late else got
            self.value = (value.astype(F32) + got.astype(F32)).astype(BF16)
        else:
            i = rep - 2 - k
            got = lax.ppermute(value, "rep", [(i + 1, i), (rep - 2 - i, rep - 1 - i)])
            self.value = jnp.where((z == i) | (z == rep - 1 - i), got, value)
        return self.value

    def finish(self):
        while self.stage < lax.axis_size("rep") - 1:
            self.along()
        return self.value.astype(F32)


def matmul(left, right):
    return jnp.dot(left, right, preferred_element_type=F32)


def matmul_nt(left, right):
    return lax.dot_general(left, right, (((1,), (1,)), ((), ())), preferred_element_type=F32)


def matmul_tn(left, right):
    return lax.dot_general(left, right, (((0,), (0,)), ((), ())), preferred_element_type=F32)


def norm_parts(values):
    average = jnp.mean(values, axis=-1, keepdims=True)
    centred = values - average
    spread = jnp.mean(centred * centred, axis=-1, keepdims=True)
    scale = lax.rsqrt(spread + EPS)
    return centred * scale, scale


def norm_back(grad, gain, unit, scale):
    e = grad * gain
    return scale * (
        e
        - jnp.mean(e, axis=-1, keepdims=True)
        - unit * jnp.mean(e * unit, axis=-1, keepdims=True)
    )


def shards(
    inputs,
    skips,
    cotangent,
    dest_slot,
    pack_segments,
    block_live,
    counts,
    w_skip,
    b_skip,
    g_one,
    b_one,
    w_qkv,
    w_out,
    b_out,
    g_two,
    b_two,
    w_up,
    c_up,
    w_down,
    c_down,
):
    dp = lax.axis_size("dp")
    rep = lax.axis_size("rep")
    d = lax.axis_index("dp")
    z = lax.axis_index("rep")
    micro = inputs.shape[0]
    frames = inputs.shape[2]
    width = inputs.shape[3]
    blocks = dest_slot.shape[2]
    block = frames // blocks
    per_pair = blocks // dp
    total = micro * frames
    bits = dp.bit_length() - 1
    place = jnp.stack([z, lax.rem(d, 8)]).astype(jnp.int32)
    dims = list(range(1, bits))
    own_skip = own_chunk(place, width, w_skip)
    own_mid = own_chunk(place, width, w_qkv, w_out)
    own_up = own_chunk(place, width, w_up)
    own_down = own_chunk(place, width, w_down)
    far_skip = fetch_far(own_skip, None)
    far_mid = fetch_far(own_mid, far_skip[0])
    far_both = fetch_far(jnp.concatenate([own_up, own_down], axis=0), far_mid[0])

    small = jnp.concatenate(
        [dest_slot.reshape(-1), block_live.reshape(-1), counts.reshape(-1)]
    )
    every = small[None]
    for bit in range(bits):
        every = jnp.concatenate([every, flip(every, 1 << bit)], axis=0)

    skip_rows, mid_rows = own_skip.shape[0], own_mid.shape[0]
    up_rows, both_rows = own_up.shape[0], own_up.shape[0] + own_down.shape[0]
    run_skip = Spread(far_skip, skip_rows, 0, skip_rows, every)
    run_skip.cross()
    run_mid = Spread(far_mid, mid_rows, 0, mid_rows, run_skip.second)
    parts_skip = run_skip.share()
    full_skip = assemble(w_skip, parts_skip, place, 0, 1)

    every = after(every, run_skip.first)
    span = micro * blocks
    numbers = every[:, : 2 * span].reshape(dp, 2 * micro, blocks)
    numbers = jnp.transpose(numbers, (1, 0, 2)).reshape(2 * micro, dp * blocks).astype(F32)
    count_total = jnp.sum(every[:, 2 * span]).astype(F32).reshape(1, 1)
    inner = jnp.arange(frames) % block
    live = inner[None] < jnp.repeat(block_live[:, 0, :], block, axis=1)
    codes = (2 * pack_segments[:, 0, :] + live).astype(F32)
    far, keep_wide, shuffle = plan_order(numbers[:micro], numbers[micro:], codes, d, block)
    keep_rows = keep_wide[:, :1]

    def to_packs(values):
        sent = matmul(shuffle, values).astype(BF16)
        got = lax.all_to_all(
            sent.reshape(dp, total // dp, width), "dp", split_axis=0, concat_axis=0, tiled=True
        )
        return got.reshape(total, width)

    def to_owners(values, *ready):
        sent = values.reshape(dp, total // dp, width)
        got = lax.all_to_all(sent, "dp", split_axis=0, concat_axis=0, tiled=True)
        got = after(got, *ready) if ready else got
        return matmul_tn(shuffle, got.reshape(total, width))

    joined = jnp.concatenate(
        [inputs.reshape(total, width), skips.reshape(total, width)], axis=1
    )
    base = matmul(joined, full_skip) + b_skip
    unit_one, scale_one = norm_parts(base)
    own_normed = (unit_one * g_one + b_one).astype(BF16)
    run_mid.cross(late=[own_normed])
    parts_mid = run_mid.share()
    run_up = Spread(far_both, both_rows, 0, up_rows, run_mid.second)
    run_up.cross()
    run_down = Spread(far_both, both_rows, up_rows, both_rows - up_rows, run_up.first)
    parts_up = run_up.share()
    run_down.cross(run_up.second)
    parts_down = run_down.share()
    shard_rows = w_qkv.shape[0] // 8
    full_qkv = assemble(w_qkv, parts_mid, place, 0, 3)
    full_out = assemble(w_out, parts_mid, place, 3 * shard_rows, 1)
    full_up = assemble(w_up, parts_up, place, 0, w_up.shape[1] // width)
    full_down = assemble(w_down, parts_down, place, 0, 1)
    count_total = after(count_total, run_down.first)
    for bit in range(rep.bit_length() - 1):
        count_total = count_total + rep_flip(count_total, 1 << bit)
    share = counts[0, 0].astype(F32) * (dp * rep) / count_total[0, 0]

    normed = to_packs(own_normed)
    triple = matmul(normed, full_qkv).astype(BF16)
    triple = triple.reshape(dp, micro, per_pair * block, 3 * width)
    slopes = 2.0 ** (-8.0 * (jnp.arange(HEADS, dtype=F32) + 1.0) / HEADS)
    attended = after(attend(triple, far, slopes), run_down.first)
    attended = to_owners(attended, full_up).astype(BF16)
    mixed = base + matmul(attended, full_out) + b_out
    unit_two, scale_two = norm_parts(mixed)
    normed_two = (unit_two * g_two + b_two).astype(BF16)
    normed_two = after(normed_two, run_down.second)
    hidden = matmul(normed_two, full_up) + c_up
    phi = 0.5 * (1.0 + lax.erf(hidden * (0.5**0.5)))
    active = (hidden * phi).astype(BF16)
    slope = (phi + hidden * jnp.exp(-0.5 * hidden * hidden) * ((2 * jnp.pi) ** -0.5)).astype(BF16)

    scaled = (cotangent.reshape(total, width).astype(F32) * share).astype(BF16)
    grad_result = scaled * keep_rows.astype(BF16)
    red_down = Reduction([(active, grad_result)], d, dims)
    grad_result = after(grad_result, *red_down.own(full_down))
    grad_result_full = grad_result.astype(F32)
    grad_active = matmul_nt(grad_result, full_down)
    grad_hidden = slope.astype(F32) * grad_active
    hidden_low = grad_hidden.astype(BF16)
    red_up = Reduction([(normed_two, hidden_low)], d, dims)
    hidden_low = after(hidden_low, red_up.sent)
    grad_normed_two = matmul_nt(hidden_low, full_up)
    grad_mixed = grad_result_full + norm_back(grad_normed_two, g_two, unit_two, scale_two)
    mixed_low = grad_mixed.astype(BF16)
    mixed_late = after(mixed_low, red_down.arrived)
    grad_attended = to_packs(matmul_nt(mixed_late, full_out).astype(BF16))
    up_parts = red_up.own(mixed_low)
    down_sends = red_down.step(*up_parts)
    active_late = after(active, *up_parts, *down_sends)
    result = mixed + matmul(active_late, full_down) + c_down
    output = (result * keep_rows).astype(BF16)
    grad_attended = after(grad_attended, output)
    grad_attended = grad_attended.reshape(dp, micro, per_pair * block, width)
    grad_triple = attend_back(triple, grad_attended, far, slopes).reshape(3, total, width)
    up_sends = red_up.step(grad_triple, red_down.arrived)
    red_mid = Reduction([(attended, mixed_low), (normed, grad_triple)], d, dims)
    down_rows = red_down.rows()
    grad_normed = sum(
        matmul_nt(grad_triple[i], full_qkv[:, i * width : (i + 1) * width]) for i in range(3)
    )
    grad_normed = to_owners(after(grad_normed.astype(BF16), down_rows, *up_sends))
    red_down.along()
    grad_normed = after(grad_normed, red_mid.sent)
    grad_base = grad_mixed + norm_back(grad_normed, g_one, unit_one, scale_one)
    base_low = grad_base.astype(BF16)
    red_skip = Reduction([(joined, base_low)], d, dims)
    vectors = (
        jnp.sum(grad_base, axis=0),
        jnp.sum(grad_normed * unit_one, axis=0),
        jnp.sum(grad_normed, axis=0),
        jnp.sum(grad_mixed, axis=0),
        jnp.sum(grad_normed_two * unit_two, axis=0),
        jnp.sum(grad_normed_two, axis=0),
        jnp.sum(grad_hidden, axis=0),
        jnp.sum(grad_result_full, axis=0),
    )
    lengths = [v.shape[0] for v in vectors]
    summed = after(jnp.concatenate(vectors), red_skip.sent).reshape(-1, 128)
    for bit in range(bits):
        summed = summed + flip(summed, 1 << bit)
    mid_parts = red_mid.own(red_skip.sent)
    red_down.along(*mid_parts)
    up_line = red_up.line(*mid_parts)
    skip_parts = red_skip.own(summed, *mid_parts)
    base_low = after(base_low, *skip_parts)
    grad_joined = matmul_nt(base_low, full_skip).astype(BF16)
    mid_sends = red_mid.step(grad_joined, up_line)
    red_up.along()
    skip_sends = red_skip.step(*mid_sends)
    red_down.finish()
    skip_columns = w_skip.shape[1]
    extra = jnp.pad(summed.reshape(-1), (0, -summed.size % (16 * rep * skip_columns)))
    extra = extra.reshape(-1, skip_columns).astype(BF16)
    final_mid = red_mid.halve(ready=[red_up.value])
    final_skip = red_skip.halve(extra)
    own_rows = w_skip.shape[0] * rep // dp
    summed = final_skip[own_rows:].reshape(-1)
    finals = [
        red_down.finish(),
        red_up.finish(),
        final_mid[:, :width],
        final_mid[:, width:],
        final_skip[:own_rows],
    ]
    sums = []
    offset = 0
    for length in lengths:
        sums.append(summed[offset : offset + length])
        offset += length

    def as_owned(values):
        return values.reshape(inputs.shape)

    return (
        as_owned(output),
        as_owned(grad_joined[:, :width]),
        as_owned(grad_joined[:, width:]),
        finals[4],
        sums[0],
        sums[1],
        sums[2],
        finals[3],
        finals[2],
        sums[3],
        sums[4],
        sums[5],
        finals[1],
        sums[6],
        finals[0],
        sums[7],
    )


def solution(mesh):
    frames = P(None, "rep", "dp", None)
    slots = P(None, "rep", "dp")
    rows = P("rep", None)
    whole = P()
    in_specs = (
        (frames,) * 3
        + (slots,) * 3
        + (P("dp", "rep"), rows, whole, whole, whole, rows, rows)
        + (whole,) * 3
        + (rows, whole, rows, whole)
    )
    split = P("dp", None)
    out_specs = (
        (frames,) * 3
        + (split,)
        + (whole,) * 3
        + (split, split)
        + (whole,) * 3
        + (split, whole, split, whole)
    )
    return jax.shard_map(shards, mesh=mesh, in_specs=in_specs, out_specs=out_specs, check_vma=False)
```

```python
import jax
import jax.numpy as jnp
from jax import lax
from jax.experimental import pallas as pl
from jax.experimental.pallas import tpu as pltpu
from jax.sharding import PartitionSpec as P

HEADS = 16
HEAD = 64
EPS = 1e-05
F32 = jnp.float32
BF16 = jnp.bfloat16
LIGHT = pl.CostEstimate(flops=1024, bytes_accessed=1024, transcendentals=0)


def flip(value, bit):
    n = lax.axis_size("dp")
    return lax.ppermute(value, "dp", [(i, i ^ bit) for i in range(n)])


def rep_flip(value, bit):
    n = lax.axis_size("rep")
    return lax.ppermute(value, "rep", [(i, i ^ bit) for i in range(n)])


def after(value, *earlier):
    return lax.optimization_barrier((value,) + earlier)[0]


def together(*values):
    return lax.optimization_barrier(values)


def assemble(w_local, parts, place, row_at, tiles):
    rep = lax.axis_size("rep")
    shard_rows, columns = w_local.shape
    rows = shard_rows // 8
    tile = columns // tiles
    half = tile // 2
    chunk_rows = parts[0][0].shape[0] // (len(parts[0][1]) * (rep - 1))
    arrays = [part[0] for part in parts]
    count = 1 + sum(len(part[1]) for part in parts) * (rep - 1) * tiles

    def body(place_ref, local_ref, *refs):
        out_ref, sems = refs[len(parts)], refs[len(parts) + 1]
        z = place_ref[0]
        e = place_ref[1]
        copies = [
            pltpu.make_async_copy(
                local_ref,
                out_ref.at[pl.ds(pl.multiple_of(z * shard_rows, 16), shard_rows), :],
                sems.at[0],
            )
        ]
        for ref, (_, runs) in zip(refs, parts):
            for k, (side, rel) in enumerate(runs):
                chunk = jnp.bitwise_xor(e, rel)
                for s, apart in enumerate(far_order(rep), 1):
                    shard = jnp.bitwise_xor(z, apart)
                    start = pl.multiple_of(shard * shard_rows + chunk * rows, 16)
                    for t in range(tiles):
                        at = (k * (rep - 1) + s - 1) * chunk_rows + row_at + t * rows
                        copies.append(
                            pltpu.make_async_copy(
                                ref.at[pl.ds(at, rows), :],
                                out_ref.at[pl.ds(start, rows), pl.ds(t * tile + side * half, half)],
                                sems.at[len(copies)],
                            )
                        )
        for copy in copies:
            copy.start()
        for copy in copies:
            copy.wait()

    return pl.pallas_call(
        body,
        out_shape=jax.ShapeDtypeStruct((shard_rows * rep, columns), w_local.dtype),
        in_specs=[pl.BlockSpec(memory_space=pltpu.SMEM)]
        + [pl.BlockSpec(memory_space=pl.ANY)] * (1 + len(parts)),
        out_specs=pl.BlockSpec(memory_space=pltpu.VMEM),
        scratch_shapes=[pltpu.SemaphoreType.DMA((count,))],
        compiler_params=pltpu.CompilerParams(vmem_limit_bytes=24 * 2**20),
        cost_estimate=LIGHT,
        name="assemble",
    )(place, w_local, *arrays)


def own_chunk(place, width, *shards_local):
    pieces = []
    for w_local in shards_local:
        rows = w_local.shape[0] // 8
        own = lax.dynamic_slice_in_dim(w_local, place[1] * rows, rows, 0)
        for t in range(w_local.shape[1] // width):
            pieces.append(own[:, t * width : (t + 1) * width])
    return jnp.concatenate(pieces, axis=0)


def pack(arrays, outs):
    count = sum(len(out) for out in outs)

    def body(*refs):
        sources, targets, sems = refs[: len(arrays)], refs[len(arrays) : -1], refs[-1]
        copies = []
        for target, out in zip(targets, outs):
            at = 0
            for which, row, rows, column, columns in out:
                copies.append(
                    pltpu.make_async_copy(
                        sources[which].at[pl.ds(row, rows), pl.ds(column, columns)],
                        target.at[pl.ds(at, rows), :],
                        sems.at[len(copies)],
                    )
                )
                at += rows
        for copy in copies:
            copy.start()
        for copy in copies:
            copy.wait()

    return pl.pallas_call(
        body,
        out_shape=[
            jax.ShapeDtypeStruct((sum(item[2] for item in out), out[0][4]), arrays[0].dtype)
            for out in outs
        ],
        in_specs=[pl.BlockSpec(memory_space=pl.ANY)] * len(arrays),
        out_specs=[pl.BlockSpec(memory_space=pltpu.VMEM)] * len(outs),
        scratch_shapes=[pltpu.SemaphoreType.DMA((count,))],
        compiler_params=pltpu.CompilerParams(vmem_limit_bytes=24 * 2**20),
        cost_estimate=LIGHT,
        name="pack",
    )(*arrays)


def far_order(rep):
    order = [0]
    for bit in reversed(range(rep.bit_length() - 1)):
        order = order + [distance ^ (1 << bit) for distance in order]
    return order[1:]


class Spread:
    def __init__(self, gots, width):
        self.half = width // 2
        rows = sum(got.shape[0] for got in gots)
        items = [(i, 0, got.shape[0]) for i, got in enumerate(gots)]
        self.start = pack(
            gots, [[item + (column, self.half) for item in items] for column in (0, self.half)]
        )
        self.n = rows

    def near(self):
        return [flip(self.start[0], 2), flip(self.start[1], 4)]

    def near_landed(self, got):
        whole = [(i, 0, self.n, 0, self.half) for i in range(4)]
        self.pairs = pack(
            [self.start[0], got[0], self.start[1], got[1]], [whole[:2], whole[2:]]
        )

    def cross(self):
        return [flip(self.pairs[0], 4), flip(self.pairs[1], 2)]

    def cross_landed(self, got):
        whole = [(i, 0, 2 * self.n, 0, self.half) for i in range(4)]
        (self.every,) = pack([self.pairs[0], got[0], self.pairs[1], got[1]], [whole])

    def share(self):
        return flip(self.every, 1)

    def parts(self, other):
        runs = [(0, 0), (0, 2), (0, 4), (0, 6), (1, 0), (1, 4), (1, 2), (1, 6)]
        return [(self.every, runs), (other, [(side, rel | 1) for side, rel in runs])]


def rep_steps(rep):
    return [1 << bit for bit in reversed(range(rep.bit_length() - 1))]


class Fetch:
    def __init__(self, own):
        self.held = [own]
        self.steps = rep_steps(lax.axis_size("rep"))

    def send(self):
        sent = self.held[0]
        if len(self.held) > 1:
            whole = [(i, 0, a.shape[0], 0, a.shape[1]) for i, a in enumerate(self.held)]
            (sent,) = pack(self.held, [whole])
        return rep_flip(sent, self.steps[len(self.held) - 1])

    def landed(self, got):
        self.held.append(got)

    def rest(self):
        while len(self.held) < len(self.steps):
            self.landed(self.send())

    def far(self):
        return self.held[1:]


def plan_order(all_slots, all_live, codes, d, block):
    micro, owners = all_slots.shape
    frames = codes.shape[1]
    blocks = frames // block
    dp = owners // blocks
    per_pair = blocks // dp
    total = micro * frames

    def column(row):
        return jnp.broadcast_to(row, (128, row.shape[1])).T[:, :1]

    def as_row(values):
        return jnp.broadcast_to(values, (values.shape[0], 128)).T[:1, :]

    def body(d_ref, slots_ref, live_ref, codes_ref, far_ref, keep_ref, shuffle_ref):
        me = d_ref[0]
        lane = lax.broadcasted_iota(jnp.int32, (1, owners), 1)
        source = jnp.bitwise_xor(lax.div(lane, jnp.int32(blocks)), me)
        first_slot = (source * blocks).astype(F32) + lax.rem(lane, jnp.int32(blocks)).astype(F32)
        source_col = column(source.astype(F32))
        frame = lax.broadcasted_iota(jnp.int32, (frames, 1), 0)
        block_of = lax.div(frame, jnp.int32(block)).astype(F32)
        inner = lax.rem(frame, jnp.int32(block)).astype(F32)
        low = (me * blocks).astype(F32)
        rows = []
        for m in range(micro):
            slots = slots_ref[pl.ds(m, 1), :]
            slots_col = column(slots)
            same = source_col == source.astype(F32)
            rank = jnp.sum(jnp.where(same & (slots_col < slots), 1.0, 0.0), axis=0, keepdims=True)
            here = (slots >= low) & (slots < low + blocks)
            arrive = source.astype(F32) * per_pair + rank - (me * per_pair).astype(F32)
            arrive = jnp.where(here, arrive, -1.0)
            placed = jnp.sum(
                jnp.where(arrive == block_of, slots - low, 0.0), axis=1, keepdims=True
            )
            position = placed * block + inner
            at = lax.broadcasted_iota(jnp.int32, (1, frames), 1).astype(F32)
            code = jnp.sum(
                jnp.where(at == position, codes_ref[pl.ds(m, 1), :], 0.0), axis=1, keepdims=True
            )
            position_row, code_row = as_row(position), as_row(code)
            segment, segment_row = jnp.floor(code * 0.5), jnp.floor(code_row * 0.5)
            live_row = code_row - 2.0 * segment_row
            distance = jnp.abs(position - position_row)
            allowed = (segment == segment_row) & ((live_row > 0.5) | (distance < 0.5))
            far_ref[m] = jnp.where(allowed, distance, 1e32)
            own = lane < blocks
            mine = jnp.sum(
                jnp.where(own & (lane.astype(F32) == block_of), slots, 0.0), axis=1, keepdims=True
            )
            alive = jnp.sum(
                jnp.where(first_slot == mine, live_ref[pl.ds(m, 1), :], 0.0), axis=1, keepdims=True
            )
            keep_ref[pl.ds(m * frames, frames), :] = jnp.broadcast_to(
                jnp.where(inner < alive, 1.0, 0.0), (frames, 128)
            )
            my_rank = jnp.sum(
                jnp.where(own & (lane.astype(F32) == block_of), rank, 0.0), axis=1, keepdims=True
            )
            target = jnp.floor((my_rank + 0.5) / per_pair)
            row = (target * micro + m) * per_pair + (my_rank - target * per_pair)
            rows.append(as_row(row * block + inner))
        goal = jnp.concatenate(rows, axis=1)
        spot = lax.broadcasted_iota(jnp.int32, (total, total), 0).astype(F32)
        shuffle_ref[...] = jnp.where(spot == goal, 1.0, 0.0).astype(BF16)

    vmem = pl.BlockSpec(memory_space=pltpu.VMEM)
    return pl.pallas_call(
        body,
        out_shape=[
            jax.ShapeDtypeStruct((micro, frames, frames), F32),
            jax.ShapeDtypeStruct((total, 128), F32),
            jax.ShapeDtypeStruct((total, total), BF16),
        ],
        in_specs=[pl.BlockSpec(memory_space=pltpu.SMEM), vmem, vmem, vmem],
        out_specs=[vmem, vmem, vmem],
        compiler_params=pltpu.CompilerParams(vmem_limit_bytes=40 * 2**20),
        cost_estimate=LIGHT,
        name="plan_order",
    )(d.reshape(1).astype(jnp.int32), all_slots, all_live, codes)


def gradient_blocks(pairs, d, dims, got=None):
    dp = lax.axis_size("dp")
    total, all_rows = pairs[0][0].shape
    width = pairs[0][1].shape[2]
    tiles = [right.shape[0] for _, right in pairs]
    columns = sum(tiles) * width
    rows = all_rows // dp
    count = dp // 2
    odd = 1 if got is None else 0
    tile = min(width, 512)
    split = width // tile
    steps = sum(tiles) * split
    starts = [sum(tiles[:i]) * split for i in range(len(tiles))]

    def distance(p):
        rel = odd
        for k, bit in enumerate(dims):
            rel += ((p >> (len(dims) - 1 - k)) & 1) << bit
        return rel

    upper = [p for p in range(count) if p >= count // 2]
    lower = [p for p in range(count) if p < count // 2]
    odds = [p for p in range(count) if p % 2 == 1]
    evens = [p for p in range(count) if p % 2 == 0]
    chosen = (upper, lower, odds, evens)

    if rows % 128 != 0:
        products = []
        for left, right in pairs:
            flat = jnp.transpose(right, (1, 0, 2)).reshape(total, -1)
            products.append(matmul_tn(left, flat))
        product = jnp.concatenate(products, axis=1).reshape(dp, rows, columns)
        rel = jnp.array([distance(p) for p in range(count)], jnp.int32)
        product = product[jnp.bitwise_xor(rel, d)]
        if got is None:
            return product.astype(BF16)
        product = (product + got.astype(F32)).astype(BF16)
        half = columns // 2
        return [
            jnp.stack([product[p, :, side * half : (side + 1) * half] for p in ps])
            for side, ps in zip((0, 0, 1, 1), chosen)
        ]

    def body(d_ref, *refs):
        lefts = refs[: len(pairs)]
        rights = refs[len(pairs) : 2 * len(pairs)]
        rest = refs[2 * len(pairs) :]
        turned_ref = rest[-1]
        got_ref = None if got is None else rest[0]
        outs = rest[:-1] if got is None else rest[1:-1]
        c = pl.program_id(0)

        @pl.when(c == 0)
        def _():
            for i, left_ref in enumerate(lefts):
                for p in range(count):
                    at = pl.multiple_of(jnp.bitwise_xor(d_ref[0], distance(p)) * rows, 128)
                    turned_ref[i, pl.ds(p * rows, rows), :] = left_ref[:, pl.ds(at, rows)].T

        def piece(i, p):
            return jnp.dot(
                turned_ref[i, pl.ds(p * rows, rows), :], rights[i][0], preferred_element_type=F32
            )

        def write(i, half):
            for p in range(count):
                value = piece(i, p)
                if got is None:
                    outs[0][p] = value.astype(BF16)
                    continue
                value = (value + got_ref[p].astype(F32)).astype(BF16)
                for which in (2 * half, 2 * half + 1):
                    if p in chosen[which]:
                        outs[which][chosen[which].index(p)] = value

        for i in range(len(pairs)):
            for half in (0, 1):
                low = max(starts[i], half * (steps // 2))
                high = min(starts[i] + tiles[i] * split, (half + 1) * (steps // 2))
                if low < high:
                    pl.when((c >= low) & (c < high))(lambda i=i, half=half: write(i, half))

    def right_spec(start, n):
        def at(c, d_ref):
            k = jnp.clip(c - start, 0, n * split - 1)
            return (lax.div(k, jnp.int32(split)), 0, lax.rem(k, jnp.int32(split)))

        return pl.BlockSpec((1, total, tile), at)

    in_specs = [pl.BlockSpec((total, all_rows), lambda c, d_ref: (0, 0))] * len(pairs)
    in_specs += [right_spec(start, n) for start, n in zip(starts, tiles)]
    args = [left for left, _ in pairs] + [right for _, right in pairs]
    if got is None:
        out_shape = jax.ShapeDtypeStruct((count, rows, columns), BF16)
        out_specs = pl.BlockSpec((count, rows, tile), lambda c, d_ref: (0, 0, c))
    else:
        in_specs.append(pl.BlockSpec((count, rows, tile), lambda c, d_ref: (0, 0, c)))
        args.append(got)
        out_shape = [jax.ShapeDtypeStruct((count // 2, rows, columns // 2), BF16)] * 4
        mid = steps // 2
        first = pl.BlockSpec(
            (count // 2, rows, tile), lambda c, d_ref: (0, 0, jnp.minimum(c, mid - 1))
        )
        second = pl.BlockSpec(
            (count // 2, rows, tile), lambda c, d_ref: (0, 0, jnp.maximum(c - mid, 0))
        )
        out_specs = [first, first, second, second]
    return pl.pallas_call(
        body,
        out_shape=out_shape,
        grid_spec=pltpu.PrefetchScalarGridSpec(
            num_scalar_prefetch=1,
            grid=(steps,),
            in_specs=in_specs,
            out_specs=out_specs,
            scratch_shapes=[pltpu.VMEM((len(pairs), count * rows, total), BF16)],
        ),
        compiler_params=pltpu.CompilerParams(vmem_limit_bytes=40 * 2**20),
        cost_estimate=LIGHT,
        name="gradient",
    )(d.reshape(1).astype(jnp.int32), *args)


def head_probs(q, k, far, slope):
    scores = lax.dot_general(q, k, (((1,), (1,)), ((), ())), preferred_element_type=F32)
    scores = scores * (HEAD ** (-0.5)) - slope * far
    raised = jnp.exp(scores - jnp.max(scores, axis=-1, keepdims=True))
    return raised * (1.0 / jnp.sum(raised, axis=-1, keepdims=True))


def flat_frames(block):
    sources, _, rows, lanes = block.shape
    if rows % 16 == 0:
        return block.reshape(sources * rows, lanes)
    return block.astype(F32).reshape(sources * rows, lanes).astype(BF16)


def by_source(value, like):
    sources, _, rows, lanes = like
    if rows % 16 == 0:
        return value.astype(BF16).reshape(sources, 1, rows, lanes)
    return value.reshape(sources, 1, rows, lanes).astype(BF16)


def attend(triple, far, slopes):
    dp, micro, rows, wide = triple.shape
    frames = dp * rows
    width = wide // 3
    pairs = width // 128
    shape = (dp, 1, rows, 128)

    def body(slope_ref, q_ref, k_ref, v_ref, far_ref, out_ref):
        h = pl.program_id(1)
        q, k, v = (flat_frames(ref[...]) for ref in (q_ref, k_ref, v_ref))
        first = lax.broadcasted_iota(jnp.int32, (frames, 128), 1) < HEAD
        zero = jnp.zeros_like(q)
        outs = []
        for j, own in enumerate((jnp.where(first, q, zero), jnp.where(first, zero, q))):
            probs = head_probs(own, k, far_ref[0], slope_ref[h * 2 + j])
            outs.append(jnp.dot(probs.astype(BF16), v, preferred_element_type=F32))
        out_ref[...] = by_source(jnp.where(first, outs[0], outs[1]), shape)

    def spec(offset):
        return pl.BlockSpec(shape, lambda m, h, s: (0, m, 0, h + offset))

    return pl.pallas_call(
        body,
        out_shape=jax.ShapeDtypeStruct((dp, micro, rows, width), BF16),
        grid_spec=pltpu.PrefetchScalarGridSpec(
            num_scalar_prefetch=1,
            grid=(micro, pairs),
            in_specs=[
                spec(0),
                spec(pairs),
                spec(2 * pairs),
                pl.BlockSpec((1, frames, frames), lambda m, h, s: (m, 0, 0)),
            ],
            out_specs=spec(0),
        ),
        compiler_params=pltpu.CompilerParams(vmem_limit_bytes=24 * 2**20),
        cost_estimate=LIGHT,
        name="attend",
    )(slopes, triple, triple, triple, far)


def attend_back(triple, grad, far, slopes):
    dp, micro, rows, wide = triple.shape
    frames = dp * rows
    width = wide // 3
    pairs = width // 128
    shape = (dp, 1, rows, 128)
    scale = HEAD ** (-0.5)

    def turned(left, right):
        return lax.dot_general(left, right, (((0,), (0,)), ((), ())), preferred_element_type=F32)

    def body(slope_ref, q_ref, k_ref, v_ref, g_ref, far_ref, out_ref):
        h = pl.program_id(1)
        q, k, v, g = (flat_frames(ref[...]) for ref in (q_ref, k_ref, v_ref, g_ref))
        first = lax.broadcasted_iota(jnp.int32, (frames, 128), 1) < HEAD
        zero = jnp.zeros_like(q)
        grads = []
        for j in range(2):
            own_q = jnp.where(first, q, zero) if j == 0 else jnp.where(first, zero, q)
            own_g = jnp.where(first, g, zero) if j == 0 else jnp.where(first, zero, g)
            probs = head_probs(own_q, k, far_ref[0], slope_ref[h * 2 + j])
            back = lax.dot_general(own_g, v, (((1,), (1,)), ((), ())), preferred_element_type=F32)
            back = probs * (back - jnp.sum(back * probs, axis=-1, keepdims=True))
            low = back.astype(BF16)
            grads.append(
                (
                    jnp.dot(low, k, preferred_element_type=F32) * scale,
                    turned(low, q) * scale,
                    turned(probs.astype(BF16), g),
                )
            )
        for i in range(3):
            out_ref[i] = by_source(jnp.where(first, grads[0][i], grads[1][i]), shape)

    def spec(offset):
        return pl.BlockSpec(shape, lambda m, h, s: (0, m, 0, h + offset))

    return pl.pallas_call(
        body,
        out_shape=jax.ShapeDtypeStruct((3, dp, micro, rows, width), BF16),
        grid_spec=pltpu.PrefetchScalarGridSpec(
            num_scalar_prefetch=1,
            grid=(micro, pairs),
            in_specs=[
                spec(0),
                spec(pairs),
                spec(2 * pairs),
                spec(0),
                pl.BlockSpec((1, frames, frames), lambda m, h, s: (m, 0, 0)),
            ],
            out_specs=pl.BlockSpec((3,) + shape, lambda m, h, s: (0, 0, m, 0, h)),
        ),
        compiler_params=pltpu.CompilerParams(vmem_limit_bytes=24 * 2**20),
        cost_estimate=LIGHT,
        name="attend_back",
    )(slopes, triple, triple, triple, grad, far)


def add_up(values):
    total = values[0].astype(F32)
    for value in values[1:]:
        total = total + value.astype(F32)
    return total.astype(BF16)


class Reduction:
    def __init__(self, pairs, d, dims):
        self.pairs = [(left, right if right.ndim == 3 else right[None]) for left, right in pairs]
        self.d = d
        self.dims = dims
        self.sent = gradient_blocks(self.pairs, d, dims)

    def share(self):
        return flip(self.sent, 1)

    def own(self, got):
        self.parts = list(gradient_blocks(self.pairs, self.d, self.dims, got))
        return self.parts

    def near(self):
        parts = self.parts
        return [flip(parts[0], 1 << self.dims[0]), flip(parts[2], 1 << self.dims[-1])]

    def near_landed(self, got):
        self.halves = []
        for side, order in ((0, self.dims), (1, self.dims[::-1])):
            stay = self.parts[2 * side + 1]
            left = [bit for bit in self.dims if bit != order[0]]
            shape = (2,) * len(left) + stay.shape[1:]
            values = [stay.reshape(shape), got[side].reshape(shape)]
            self.halves.append((values, list(order[1:]), left))

    def step(self):
        sends, self.stays = [], []
        for values, order, left in self.halves:
            at = left.index(order[0])
            sends.append(add_up([lax.index_in_dim(v, 1, at, keepdims=False) for v in values]))
            self.stays.append([lax.index_in_dim(v, 0, at, keepdims=False) for v in values])
        bits = [order[0] for _, order, _ in self.halves]
        return [flip(sends[0], 1 << bits[0]), flip(sends[1], 1 << bits[1])]

    def landed(self, got):
        halves = []
        for i, (_, order, left) in enumerate(self.halves):
            halves.append((self.stays[i] + [got[i]], order[1:], [b for b in left if b != order[0]]))
        self.halves = halves

    def cross(self):
        while len(self.halves[0][1]) > 1:
            self.landed(self.step())
        return self.step()

    def rows(self):
        self.value = jnp.concatenate([add_up(values) for values, _, _ in self.halves], axis=1)
        self.stage = 0
        return self.value

    def along(self):
        rep = lax.axis_size("rep")
        half = rep // 2
        k = self.stage
        if k < half - 1:
            pairs = [(k, k + 1), (rep - 1 - k, rep - 2 - k)]
        elif k == half - 1:
            pairs = [(k, k + 1), (k + 1, k)]
        else:
            i = rep - 2 - k
            pairs = [(i + 1, i), (rep - 2 - i, rep - 1 - i)]
        return lax.ppermute(self.value, "rep", pairs)

    def along_landed(self, got):
        rep = lax.axis_size("rep")
        z = lax.axis_index("rep")
        k = self.stage
        self.stage += 1
        if k < rep // 2:
            self.value = add_up([self.value, got])
        else:
            i = rep - 2 - k
            self.value = jnp.where((z == i) | (z == rep - 1 - i), got, self.value)

    def finish(self):
        while self.stage < lax.axis_size("rep") - 1:
            self.along_landed(self.along())
        return self.value.astype(F32)

    def halve(self, extra=None):
        rep = lax.axis_size("rep")
        z = lax.axis_index("rep")
        value = self.value
        if extra is not None:
            value = jnp.concatenate([value, extra], axis=0)
        bits = range(rep.bit_length() - 1)
        for bit in bits:
            mine = lax.bitwise_and(lax.shift_right_logical(z, bit), 1)
            size = value.shape[0] // 2
            send = lax.dynamic_slice_in_dim(value, (1 - mine) * size, size, 0)
            keep = lax.dynamic_slice_in_dim(value, mine * size, size, 0)
            value = add_up([keep, rep_flip(send, 1 << bit)])
        for bit in reversed(bits):
            mine = lax.bitwise_and(lax.shift_right_logical(z, bit), 1)
            got = rep_flip(value, 1 << bit)
            lower = jnp.where(mine == 0, value, got)
            upper = jnp.where(mine == 0, got, value)
            value = jnp.concatenate([lower, upper], axis=0)
        return value.astype(F32)


def nt(left, right):
    return lax.dot_general(left, right, (((1,), (1,)), ((), ())), preferred_element_type=F32)


def hidden_gradient(grad_result, w_down, slope):
    total, width = grad_result.shape
    units = w_down.shape[0]
    tile = 512

    def body(grad_ref, w_ref, slope_ref, out_ref, sum_ref):
        value = nt(grad_ref[...], w_ref[...]) * slope_ref[...].astype(F32)
        out_ref[...] = value.astype(BF16)
        sum_ref[...] = jnp.sum(value, axis=0, keepdims=True)

    return pl.pallas_call(
        body,
        out_shape=[
            jax.ShapeDtypeStruct((total, units), BF16),
            jax.ShapeDtypeStruct((1, units), F32),
        ],
        grid=(units // tile,),
        in_specs=[
            pl.BlockSpec((total, width), lambda c: (0, 0)),
            pl.BlockSpec((tile, width), lambda c: (c, 0)),
            pl.BlockSpec((total, tile), lambda c: (0, c)),
        ],
        out_specs=[
            pl.BlockSpec((total, tile), lambda c: (0, c)),
            pl.BlockSpec((1, tile), lambda c: (0, c)),
        ],
        compiler_params=pltpu.CompilerParams(vmem_limit_bytes=24 * 2**20),
        cost_estimate=LIGHT,
        name="hidden_gradient",
    )(grad_result, w_down, slope)


def mixed_gradient(hidden_low, w_up, w_out, mixed, grad_result, gain):
    total, units = hidden_low.shape
    width = w_up.shape[0]
    tile = 256

    def body(low_ref, up_ref, out_w_ref, mixed_ref, result_ref, gain_ref, *outs):
        grad_ref, rounded_ref, attended_ref, sums_ref = outs
        grad = nt(low_ref[...], up_ref[...])
        unit, scale = norm_parts(mixed_ref[...])
        result = result_ref[...].astype(F32)
        value = result + norm_back(grad, gain_ref[...], unit, scale)
        rounded = value.astype(BF16)
        grad_ref[...] = value
        rounded_ref[...] = rounded
        attended_ref[...] = nt(rounded, out_w_ref[...]).astype(BF16)

        @pl.when(pl.program_id(0) == 0)
        def _():
            sums_ref[...] = jnp.zeros_like(sums_ref)

        for i, terms in enumerate((value, grad * unit, grad, result)):
            sums_ref[pl.ds(i, 1), :] += jnp.sum(terms, axis=0, keepdims=True)

    rows = pl.BlockSpec((tile, width), lambda r: (r, 0))
    whole = [
        pl.BlockSpec((width, units), lambda r: (0, 0)),
        pl.BlockSpec((width, width), lambda r: (0, 0)),
    ]
    return pl.pallas_call(
        body,
        out_shape=[
            jax.ShapeDtypeStruct((total, width), F32),
            jax.ShapeDtypeStruct((total, width), BF16),
            jax.ShapeDtypeStruct((total, width), BF16),
            jax.ShapeDtypeStruct((8, width), F32),
        ],
        grid=(total // tile,),
        in_specs=[pl.BlockSpec((tile, units), lambda r: (r, 0))]
        + whole
        + [rows, rows, pl.BlockSpec((1, width), lambda r: (0, 0))],
        out_specs=[rows, rows, rows, pl.BlockSpec((8, width), lambda r: (0, 0))],
        compiler_params=pltpu.CompilerParams(vmem_limit_bytes=44 * 2**20),
        cost_estimate=LIGHT,
        name="mixed_gradient",
    )(hidden_low, w_up, w_out, mixed, grad_result, gain.reshape(1, width))


def normed_gradient(grad_triple, w_qkv):
    three, total, width = grad_triple.shape
    tile = 256

    def body(grad_ref, w_ref, out_ref):
        value = nt(grad_ref[0], w_ref[:, pl.ds(0, width)])
        for i in range(1, three):
            value += nt(grad_ref[i], w_ref[:, pl.ds(i * width, width)])
        out_ref[...] = value.astype(BF16)

    return pl.pallas_call(
        body,
        out_shape=jax.ShapeDtypeStruct((total, width), BF16),
        grid=(total // tile,),
        in_specs=[
            pl.BlockSpec((three, tile, width), lambda r: (0, r, 0)),
            pl.BlockSpec((width, three * width), lambda r: (0, 0)),
        ],
        out_specs=pl.BlockSpec((tile, width), lambda r: (r, 0)),
        compiler_params=pltpu.CompilerParams(vmem_limit_bytes=32 * 2**20),
        cost_estimate=LIGHT,
        name="normed_gradient",
    )(grad_triple, w_qkv)


def matmul(left, right):
    return jnp.dot(left, right, preferred_element_type=F32)


def matmul_nt(left, right):
    return lax.dot_general(left, right, (((1,), (1,)), ((), ())), preferred_element_type=F32)


def matmul_tn(left, right):
    return lax.dot_general(left, right, (((0,), (0,)), ((), ())), preferred_element_type=F32)


def norm_parts(values):
    average = jnp.mean(values, axis=-1, keepdims=True)
    centred = values - average
    spread = jnp.mean(centred * centred, axis=-1, keepdims=True)
    scale = lax.rsqrt(spread + EPS)
    return centred * scale, scale


def norm_back(grad, gain, unit, scale):
    e = grad * gain
    return scale * (
        e
        - jnp.mean(e, axis=-1, keepdims=True)
        - unit * jnp.mean(e * unit, axis=-1, keepdims=True)
    )


def shards(
    inputs,
    skips,
    cotangent,
    dest_slot,
    pack_segments,
    block_live,
    counts,
    w_skip,
    b_skip,
    g_one,
    b_one,
    w_qkv,
    w_out,
    b_out,
    g_two,
    b_two,
    w_up,
    c_up,
    w_down,
    c_down,
):
    dp = lax.axis_size("dp")
    rep = lax.axis_size("rep")
    d = lax.axis_index("dp")
    z = lax.axis_index("rep")
    micro = inputs.shape[0]
    frames = inputs.shape[2]
    width = inputs.shape[3]
    blocks = dest_slot.shape[2]
    block = frames // blocks
    per_pair = blocks // dp
    total = micro * frames
    bits = dp.bit_length() - 1
    place = jnp.stack([z, lax.rem(d, 8)]).astype(jnp.int32)
    dims = list(range(1, bits))
    small = jnp.concatenate([dest_slot.reshape(-1), block_live.reshape(-1), counts.reshape(-1)])

    own_skip = own_chunk(place, width, w_skip)
    z_skip = Fetch(own_skip)
    z_skip.rest()
    got = z_skip.send()
    every = small[None]
    for bit in range(bits):
        every = jnp.concatenate([every, flip(every, 1 << bit)], axis=0)
    if rep > 2:
        w_qkv_now, w_out_now = after(w_qkv, z_skip.held[-1]), after(w_out, z_skip.held[-1])
    else:
        w_qkv_now, w_out_now = w_qkv, w_out
    z_mid = Fetch(own_chunk(place, width, w_qkv_now, w_out_now))
    z_mid.rest()
    got, every, first = together(got, every, z_mid.held[-1])
    z_mid.held[-1] = first
    z_skip.landed(got)

    run_skip = Spread(z_skip.far(), width)
    got, mid = together(run_skip.near(), z_mid.send())
    run_skip.near_landed(got)
    z_mid.landed(mid)

    span = micro * blocks
    numbers = every[:, : 2 * span].reshape(dp, 2 * micro, blocks)
    numbers = jnp.transpose(numbers, (1, 0, 2)).reshape(2 * micro, dp * blocks).astype(F32)
    count_total = jnp.sum(every[:, 2 * span]).astype(F32).reshape(1, 1)
    inner = jnp.arange(frames) % block
    live = inner[None] < jnp.repeat(block_live[:, 0, :], block, axis=1)
    codes = (2 * pack_segments[:, 0, :] + live).astype(F32)
    codes = after(codes, run_skip.pairs[0])
    far, keep_wide, shuffle = plan_order(numbers[:micro], numbers[micro:], codes, d, block)

    z_up = Fetch(own_chunk(place, width, after(w_up, run_skip.start[0])))
    z_up.rest()
    got, first, far, keep_wide, shuffle = together(
        run_skip.cross(), z_up.held[-1], far, keep_wide, shuffle
    )
    z_up.held[-1] = first
    run_skip.cross_landed(got)
    keep_rows = keep_wide[:, :1]

    run_mid = Spread(z_mid.far(), width)
    other, got, up = together(run_skip.share(), run_mid.near(), z_up.send())
    run_mid.near_landed(got)
    z_up.landed(up)
    full_skip = assemble(w_skip, run_skip.parts(other), place, 0, 1)

    joined = jnp.concatenate([inputs.reshape(total, width), skips.reshape(total, width)], axis=1)
    z_down = Fetch(own_chunk(place, width, after(w_down, run_mid.start[0])))
    z_down.rest()
    base = matmul(joined, full_skip) + b_skip
    unit_one, scale_one = norm_parts(base)
    own_normed = (unit_one * g_one + b_one).astype(BF16)
    sent = matmul(shuffle, own_normed).astype(BF16)
    got, first, sent = together(run_mid.cross(), z_down.held[-1], sent)
    z_down.held[-1] = first
    run_mid.cross_landed(got)

    def exchange(values):
        values = values.reshape(dp, total // dp, width)
        got = lax.all_to_all(values, "dp", split_axis=0, concat_axis=0, tiled=True)
        return got.reshape(total, width)

    run_up = Spread(z_up.far(), width)
    normed, other, got, down = together(
        exchange(sent), run_mid.share(), run_up.near(), z_down.send()
    )
    run_up.near_landed(got)
    z_down.landed(down)
    shard_rows = w_qkv.shape[0] // 8
    parts_mid = run_mid.parts(other)
    full_qkv = assemble(w_qkv, parts_mid, place, 0, 3)

    triple = matmul(normed, full_qkv).astype(BF16)
    triple = triple.reshape(dp, micro, per_pair * block, 3 * width)
    slopes = 2.0 ** (-8.0 * (jnp.arange(HEADS, dtype=F32) + 1.0) / HEADS)
    attended = attend(triple, far, slopes)
    count_steps = rep_steps(rep)
    for step in count_steps[:-1]:
        count_total = count_total + rep_flip(count_total, step)
    got, attended, count_total = together(run_up.cross(), attended, count_total)
    run_up.cross_landed(got)

    run_down = Spread(z_down.far(), width)
    full_out = assemble(w_out, parts_mid, place, 3 * shard_rows, 1)
    last_count = rep_flip(count_total, count_steps[-1])
    attended, other, got, last_count, full_out = together(
        exchange(attended), run_up.share(), run_down.near(), last_count, full_out
    )
    run_down.near_landed(got)
    count_total = count_total + last_count
    share = counts[0, 0].astype(F32) * (dp * rep) / count_total[0, 0]
    full_up = assemble(w_up, run_up.parts(other), place, 0, w_up.shape[1] // width)

    attended = matmul_tn(shuffle, attended).astype(BF16)
    mixed = base + matmul(attended, full_out) + b_out
    unit_two, scale_two = norm_parts(mixed)
    normed_two = (unit_two * g_two + b_two).astype(BF16)
    hidden = matmul(normed_two, full_up) + c_up
    phi = 0.5 * (1.0 + lax.erf(hidden * (0.5**0.5)))
    active = (hidden * phi).astype(BF16)
    slope = (phi + hidden * jnp.exp(-0.5 * hidden * hidden) * ((2 * jnp.pi) ** -0.5)).astype(BF16)
    scaled = (cotangent.reshape(total, width).astype(F32) * share).astype(BF16)
    grad_result = scaled * keep_rows.astype(BF16)
    red_down = Reduction([(active, grad_result)], d, dims)
    got, red_down.sent = together(run_down.cross(), red_down.sent)
    run_down.cross_landed(got)

    other, down_got = run_down.share(), red_down.share()
    full_down = assemble(w_down, run_down.parts(other), place, 0, 1)
    down_got, full_down = together(down_got, full_down)
    grad_result = after(grad_result, *red_down.own(down_got))

    flying = red_down.near()
    hidden_low, sum_hidden = hidden_gradient(grad_result, full_down, slope)
    red_up = Reduction([(normed_two, hidden_low)], d, dims)
    up_got = red_up.share()
    hidden_low = after(hidden_low, red_up.sent)
    grad_mixed, mixed_low, grad_attended, sums_mixed = mixed_gradient(
        hidden_low, full_up, full_out, mixed, grad_result, g_two
    )
    flying, up_got, grad_attended = together(flying, up_got, grad_attended)
    red_down.near_landed(flying)

    flying = red_down.cross()
    sent = matmul(shuffle, grad_attended).astype(BF16)
    grad_attended = exchange(sent)
    up_parts = red_up.own(after(up_got, sent))
    flying, red_up.parts = together(flying, up_parts)
    red_down.landed(flying)
    red_down.rows()

    flying = red_up.near()
    line = red_down.along()
    active_late = after(active, *red_up.parts)
    result = mixed + matmul(active_late, full_down) + c_down
    output = (result * keep_rows).astype(BF16)
    grad_attended = after(grad_attended, output)
    grad_attended = grad_attended.reshape(dp, micro, per_pair * block, width)
    grad_triple = attend_back(triple, grad_attended, far, slopes).reshape(3, total, width)
    flying, line, grad_triple = together(flying, line, grad_triple)
    red_up.near_landed(flying)
    red_down.along_landed(line)

    flying = red_up.cross()
    line = red_down.along()
    sent = normed_gradient(grad_triple, full_qkv)
    grad_normed = exchange(sent)
    grad_triple = after(grad_triple, sent)
    red_mid = Reduction([(attended, mixed_low), (normed, grad_triple)], d, dims)
    flying, red_mid.sent, grad_normed = together(flying, red_mid.sent, grad_normed)
    red_up.landed(flying)
    red_up.rows()

    up_line = red_up.along()
    mid_got = red_mid.share()
    grad_normed = matmul_tn(shuffle, grad_normed)
    grad_base = grad_mixed + norm_back(grad_normed, g_one, unit_one, scale_one)
    base_low = grad_base.astype(BF16)
    red_skip = Reduction([(joined, base_low)], d, dims)
    skip_got = red_skip.share()
    mid_parts = red_mid.own(after(mid_got, red_skip.sent))
    line, red_mid.parts, skip_got = together(line, mid_parts, skip_got)
    red_down.along_landed(line)

    flying = red_mid.near()
    line = red_down.along()
    skip_parts = red_skip.own(after(skip_got, *red_mid.parts))
    skip_flying = red_skip.near()
    vectors = (
        jnp.sum(grad_base, axis=0),
        jnp.sum(grad_normed * unit_one, axis=0),
        jnp.sum(grad_normed, axis=0),
        sums_mixed[0],
        sums_mixed[1],
        sums_mixed[2],
        sum_hidden[0],
        sums_mixed[3],
    )
    lengths = [v.shape[0] for v in vectors]
    summed = after(jnp.concatenate(vectors), *skip_parts).reshape(-1, 128)
    summed = summed + flip(summed, 1)
    grad_joined = matmul_nt(after(base_low, *skip_parts), full_skip).astype(BF16)
    flying, up_line, grad_joined, summed = together(flying, up_line, grad_joined, summed)
    red_mid.near_landed(flying)
    red_up.along_landed(up_line)

    flying = red_mid.cross()
    up_line = red_up.along()
    for bit in range(1, bits - 1):
        summed = summed + flip(summed, 1 << bit)
    skip_flying, line, summed = together(skip_flying, line, summed)
    red_skip.near_landed(skip_flying)
    red_down.along_landed(line)
    skip_flying = red_skip.cross()
    if bits > 1:
        summed = summed + flip(summed, 1 << (bits - 1))
    flying, up_line = together(flying, up_line)
    red_mid.landed(flying)
    red_mid.rows()
    red_up.along_landed(up_line)
    up_line = red_up.along()
    skip_columns = w_skip.shape[1]
    extra = jnp.pad(summed.reshape(-1), (0, -summed.size % (16 * rep * skip_columns)))
    extra = extra.reshape(-1, skip_columns).astype(BF16)
    skip_flying, extra = together(skip_flying, extra)
    red_skip.landed(skip_flying)
    red_skip.rows()
    final_mid = red_mid.halve()
    final_skip = red_skip.halve(extra)
    red_up.along_landed(up_line)
    own_rows = w_skip.shape[0] * rep // dp
    summed = final_skip[own_rows:].reshape(-1)
    finals = [
        red_down.finish(),
        red_up.finish(),
        final_mid[:, :width],
        final_mid[:, width:],
        final_skip[:own_rows],
    ]
    sums = []
    offset = 0
    for length in lengths:
        sums.append(summed[offset : offset + length])
        offset += length

    def as_owned(values):
        return values.reshape(inputs.shape)

    return (
        as_owned(output),
        as_owned(grad_joined[:, :width]),
        as_owned(grad_joined[:, width:]),
        finals[4],
        sums[0],
        sums[1],
        sums[2],
        finals[3],
        finals[2],
        sums[3],
        sums[4],
        sums[5],
        finals[1],
        sums[6],
        finals[0],
        sums[7],
    )


def solution(mesh):
    frames = P(None, "rep", "dp", None)
    slots = P(None, "rep", "dp")
    rows = P("rep", None)
    whole = P()
    in_specs = (
        (frames,) * 3
        + (slots,) * 3
        + (P("dp", "rep"), rows, whole, whole, whole, rows, rows)
        + (whole,) * 3
        + (rows, whole, rows, whole)
    )
    split = P("dp", None)
    out_specs = (
        (frames,) * 3
        + (split,)
        + (whole,) * 3
        + (split, split)
        + (whole,) * 3
        + (split, whole, split, whole)
    )
    return jax.shard_map(shards, mesh=mesh, in_specs=in_specs, out_specs=out_specs, check_vma=False)
```

```python
import jax
import jax.numpy as jnp
from jax import lax
from jax.experimental import pallas as pl
from jax.experimental.pallas import tpu as pltpu
from jax.sharding import PartitionSpec as P

HEADS = 16
HEAD = 64
EPS = 1e-05
F32 = jnp.float32
BF16 = jnp.bfloat16
TOKEN = jax.ShapeDtypeStruct((8, 128), F32)
ANY = pl.BlockSpec(memory_space=pl.ANY)
LIGHT = pl.CostEstimate(flops=1024, bytes_accessed=1024, transcendentals=0)


def flip(value, bit):
    n = lax.axis_size("dp")
    return lax.ppermute(value, "dp", [(i, i ^ bit) for i in range(n)])


def rep_flip(value, bit):
    n = lax.axis_size("rep")
    return lax.ppermute(value, "rep", [(i, i ^ bit) for i in range(n)])


def after(value, *earlier):
    return lax.optimization_barrier((value,) + earlier)[0]


def together(*values):
    return lax.optimization_barrier(values)


def assemble(w_local, parts, place, row_at, tiles, deps=()):
    rep = lax.axis_size("rep")
    shard_rows, columns = w_local.shape
    rows = shard_rows // 8
    tile = columns // tiles
    half = tile // 2
    chunk_rows = parts[0][0].shape[0] // (len(parts[0][1]) * (rep - 1))
    arrays = [part[0] for part in parts]
    count = 1 + sum(len(part[1]) for part in parts) * (rep - 1) * tiles

    def body(place_ref, local_ref, *refs):
        out_ref, token_ref, sems = refs[-3:]
        token_ref[...] = jnp.zeros_like(token_ref)
        z = place_ref[0]
        e = place_ref[1]
        copies = [
            pltpu.make_async_copy(
                local_ref,
                out_ref.at[pl.ds(pl.multiple_of(z * shard_rows, 16), shard_rows), :],
                sems.at[0],
            )
        ]
        for ref, (_, runs) in zip(refs, parts):
            for k, (side, rel) in enumerate(runs):
                chunk = jnp.bitwise_xor(e, rel)
                for s, apart in enumerate(far_order(rep), 1):
                    shard = jnp.bitwise_xor(z, apart)
                    start = pl.multiple_of(shard * shard_rows + chunk * rows, 16)
                    for t in range(tiles):
                        at = (k * (rep - 1) + s - 1) * chunk_rows + row_at + t * rows
                        copies.append(
                            pltpu.make_async_copy(
                                ref.at[pl.ds(at, rows), :],
                                out_ref.at[pl.ds(start, rows), pl.ds(t * tile + side * half, half)],
                                sems.at[len(copies)],
                            )
                        )
        for copy in copies:
            copy.start()
        for copy in copies:
            copy.wait()

    return pl.pallas_call(
        body,
        out_shape=[jax.ShapeDtypeStruct((shard_rows * rep, columns), w_local.dtype), TOKEN],
        grid=(1,),
        in_specs=[pl.BlockSpec(memory_space=pltpu.SMEM)] + [ANY] * (1 + len(parts) + len(deps)),
        out_specs=[
            pl.BlockSpec((shard_rows * rep, columns), lambda i: (0, 0)),
            pl.BlockSpec(TOKEN.shape, lambda i: (0, 0)),
        ],
        scratch_shapes=[pltpu.SemaphoreType.DMA((count,))],
        compiler_params=pltpu.CompilerParams(vmem_limit_bytes=26 * 2**20),
        cost_estimate=LIGHT,
        name="assemble",
    )(place, w_local, *arrays, *deps)


def own_chunk(place, width, shards_local, deps=()):
    items = []
    for which, w_local in enumerate(shards_local):
        for t in range(w_local.shape[1] // width):
            items.append((which, w_local.shape[0] // 8, t * width))
    total = sum(item[1] for item in items)

    def body(place_ref, *refs):
        out_ref, sems = refs[-2:]
        copies = []
        at = 0
        for which, rows, column in items:
            start = pl.multiple_of(place_ref[1] * rows, 16)
            copies.append(
                pltpu.make_async_copy(
                    refs[which].at[pl.ds(start, rows), pl.ds(column, width)],
                    out_ref.at[pl.ds(at, rows), :],
                    sems.at[len(copies)],
                )
            )
            at += rows
        for copy in copies:
            copy.start()
        for copy in copies:
            copy.wait()

    return pl.pallas_call(
        body,
        out_shape=jax.ShapeDtypeStruct((total, width), shards_local[0].dtype),
        grid=(1,),
        in_specs=[pl.BlockSpec(memory_space=pltpu.SMEM)]
        + [ANY] * (len(shards_local) + len(deps)),
        out_specs=pl.BlockSpec((total, width), lambda i: (0, 0)),
        scratch_shapes=[pltpu.SemaphoreType.DMA((len(items),))],
        compiler_params=pltpu.CompilerParams(vmem_limit_bytes=24 * 2**20),
        cost_estimate=LIGHT,
        name="own_chunk",
    )(place, *shards_local, *deps)


def pack(arrays, outs, deps=()):
    count = sum(len(out) for out in outs)

    def body(*refs):
        sources, targets, sems = refs[: len(arrays)], refs[-1 - len(outs) : -1], refs[-1]
        copies = []
        for target, out in zip(targets, outs):
            at = 0
            for which, row, rows, column, columns in out:
                copies.append(
                    pltpu.make_async_copy(
                        sources[which].at[pl.ds(row, rows), pl.ds(column, columns)],
                        target.at[pl.ds(at, rows), :],
                        sems.at[len(copies)],
                    )
                )
                at += rows
        for copy in copies:
            copy.start()
        for copy in copies:
            copy.wait()

    return pl.pallas_call(
        body,
        out_shape=[
            jax.ShapeDtypeStruct((sum(item[2] for item in out), out[0][4]), arrays[0].dtype)
            for out in outs
        ],
        grid=(1,),
        in_specs=[ANY] * (len(arrays) + len(deps)),
        out_specs=[
            pl.BlockSpec((sum(item[2] for item in out), out[0][4]), lambda i: (0, 0))
            for out in outs
        ],
        scratch_shapes=[pltpu.SemaphoreType.DMA((count,))],
        compiler_params=pltpu.CompilerParams(vmem_limit_bytes=24 * 2**20),
        cost_estimate=LIGHT,
        name="pack",
    )(*arrays, *deps)


def far_order(rep):
    order = [0]
    for bit in reversed(range(rep.bit_length() - 1)):
        order = order + [distance ^ (1 << bit) for distance in order]
    return order[1:]


class Spread:
    def __init__(self, gots, width, deps=()):
        self.half = width // 2
        rows = sum(got.shape[0] for got in gots)
        items = [(i, 0, got.shape[0]) for i, got in enumerate(gots)]
        self.start = pack(
            gots, [[item + (column, self.half) for item in items] for column in (0, self.half)], deps
        )
        self.n = rows

    def near(self):
        return [flip(self.start[0], 2), flip(self.start[1], 4)]

    def near_landed(self, got, deps=()):
        whole = [(i, 0, self.n, 0, self.half) for i in range(4)]
        self.pairs = pack(
            [self.start[0], got[0], self.start[1], got[1]], [whole[:2], whole[2:]], deps
        )

    def cross(self):
        return [flip(self.pairs[0], 4), flip(self.pairs[1], 2)]

    def cross_landed(self, got, deps=()):
        whole = [(i, 0, 2 * self.n, 0, self.half) for i in range(4)]
        (self.every,) = pack([self.pairs[0], got[0], self.pairs[1], got[1]], [whole], deps)

    def share(self):
        return flip(self.every, 1)

    def parts(self, other):
        runs = [(0, 0), (0, 2), (0, 4), (0, 6), (1, 0), (1, 4), (1, 2), (1, 6)]
        return [(self.every, runs), (other, [(side, rel | 1) for side, rel in runs])]


def rep_steps(rep):
    return [1 << bit for bit in reversed(range(rep.bit_length() - 1))]


class Fetch:
    def __init__(self, own):
        self.held = [own]
        self.steps = rep_steps(lax.axis_size("rep"))

    def send(self):
        sent = self.held[0]
        if len(self.held) > 1:
            whole = [(i, 0, a.shape[0], 0, a.shape[1]) for i, a in enumerate(self.held)]
            (sent,) = pack(self.held, [whole])
        return rep_flip(sent, self.steps[len(self.held) - 1])

    def landed(self, got):
        self.held.append(got)

    def rest(self):
        while len(self.held) < len(self.steps):
            self.landed(self.send())

    def far(self):
        return self.held[1:]


def plan_order(all_slots, all_live, codes, d, block, deps=()):
    micro, owners = all_slots.shape
    frames = codes.shape[1]
    blocks = frames // block
    dp = owners // blocks
    per_pair = blocks // dp
    total = micro * frames

    def column(row):
        return jnp.broadcast_to(row, (128, row.shape[1])).T[:, :1]

    def as_row(values):
        return jnp.broadcast_to(values, (values.shape[0], 128)).T[:1, :]

    def body(d_ref, slots_ref, live_ref, codes_ref, *refs):
        far_ref, turned_ref, keep_ref, shuffle_ref = refs[-4:]
        me = d_ref[0]
        lane = lax.broadcasted_iota(jnp.int32, (1, owners), 1)
        source = jnp.bitwise_xor(lax.div(lane, jnp.int32(blocks)), me)
        first_slot = (source * blocks).astype(F32) + lax.rem(lane, jnp.int32(blocks)).astype(F32)
        source_col = column(source.astype(F32))
        frame = lax.broadcasted_iota(jnp.int32, (frames, 1), 0)
        block_of = lax.div(frame, jnp.int32(block)).astype(F32)
        inner = lax.rem(frame, jnp.int32(block)).astype(F32)
        low = (me * blocks).astype(F32)
        rows = []
        for m in range(micro):
            slots = slots_ref[pl.ds(m, 1), :]
            slots_col = column(slots)
            same = source_col == source.astype(F32)
            rank = jnp.sum(jnp.where(same & (slots_col < slots), 1.0, 0.0), axis=0, keepdims=True)
            here = (slots >= low) & (slots < low + blocks)
            arrive = source.astype(F32) * per_pair + rank - (me * per_pair).astype(F32)
            arrive = jnp.where(here, arrive, -1.0)
            placed = jnp.sum(
                jnp.where(arrive == block_of, slots - low, 0.0), axis=1, keepdims=True
            )
            position = placed * block + inner
            at = lax.broadcasted_iota(jnp.int32, (1, frames), 1).astype(F32)
            code = jnp.sum(
                jnp.where(at == position, codes_ref[pl.ds(m, 1), :], 0.0), axis=1, keepdims=True
            )
            position_row, code_row = as_row(position), as_row(code)
            segment, segment_row = jnp.floor(code * 0.5), jnp.floor(code_row * 0.5)
            live_row = code_row - 2.0 * segment_row
            distance = jnp.abs(position - position_row)
            allowed = (segment == segment_row) & ((live_row > 0.5) | (distance < 0.5))
            far_ref[m] = jnp.where(allowed, distance, 1e32)
            live_col = code - 2.0 * segment
            allowed = (segment == segment_row) & ((live_col > 0.5) | (distance < 0.5))
            turned_ref[m] = jnp.where(allowed, distance, 1e32)
            own = lane < blocks
            mine = jnp.sum(
                jnp.where(own & (lane.astype(F32) == block_of), slots, 0.0), axis=1, keepdims=True
            )
            alive = jnp.sum(
                jnp.where(first_slot == mine, live_ref[pl.ds(m, 1), :], 0.0), axis=1, keepdims=True
            )
            keep_ref[pl.ds(m * frames, frames), :] = jnp.broadcast_to(
                jnp.where(inner < alive, 1.0, 0.0), (frames, 128)
            )
            my_rank = jnp.sum(
                jnp.where(own & (lane.astype(F32) == block_of), rank, 0.0), axis=1, keepdims=True
            )
            target = jnp.floor((my_rank + 0.5) / per_pair)
            row = (target * micro + m) * per_pair + (my_rank - target * per_pair)
            rows.append(as_row(row * block + inner))
        goal = jnp.concatenate(rows, axis=1)
        spot = lax.broadcasted_iota(jnp.int32, (total, total), 0).astype(F32)
        shuffle_ref[...] = jnp.where(spot == goal, 1.0, 0.0).astype(BF16)

    vmem = pl.BlockSpec(memory_space=pltpu.VMEM)
    return pl.pallas_call(
        body,
        out_shape=[
            jax.ShapeDtypeStruct((micro, frames, frames), F32),
            jax.ShapeDtypeStruct((micro, frames, frames), F32),
            jax.ShapeDtypeStruct((total, 128), F32),
            jax.ShapeDtypeStruct((total, total), BF16),
        ],
        in_specs=[pl.BlockSpec(memory_space=pltpu.SMEM), vmem, vmem, vmem] + [ANY] * len(deps),
        out_specs=[vmem, vmem, vmem, vmem],
        compiler_params=pltpu.CompilerParams(vmem_limit_bytes=24 * 2**20),
        cost_estimate=LIGHT,
        name="plan_order",
    )(d.reshape(1).astype(jnp.int32), all_slots, all_live, codes, *deps)


def gradient_blocks(pairs, d, dims, got=None, deps=()):
    dp = lax.axis_size("dp")
    total, all_rows = pairs[0][0].shape
    width = pairs[0][1].shape[2]
    tiles = [right.shape[0] for _, right in pairs]
    columns = sum(tiles) * width
    rows = all_rows // dp
    count = dp // 2
    odd = 1 if got is None else 0
    tile = min(width, 512)
    split = width // tile
    steps = sum(tiles) * split
    starts = [sum(tiles[:i]) * split for i in range(len(tiles))]

    def distance(p):
        rel = odd
        for k, bit in enumerate(dims):
            rel += ((p >> (len(dims) - 1 - k)) & 1) << bit
        return rel

    upper = [p for p in range(count) if p >= count // 2]
    lower = [p for p in range(count) if p < count // 2]
    odds = [p for p in range(count) if p % 2 == 1]
    evens = [p for p in range(count) if p % 2 == 0]
    chosen = (upper, lower, odds, evens)

    if rows % 128 != 0:
        products = []
        for left, right in pairs:
            flat = jnp.transpose(right, (1, 0, 2)).reshape(total, -1)
            products.append(matmul_tn(left, flat))
        product = jnp.concatenate(products, axis=1).reshape(dp, rows, columns)
        rel = jnp.array([distance(p) for p in range(count)], jnp.int32)
        product = product[jnp.bitwise_xor(rel, d)]
        token = jnp.zeros(TOKEN.shape, F32) + product[0, :1, :1]
        if got is None:
            return [product.astype(BF16), token]
        product = (product + got.astype(F32)).astype(BF16)
        half = columns // 2
        return [
            jnp.stack([product[p, :, side * half : (side + 1) * half] for p in ps])
            for side, ps in zip((0, 0, 1, 1), chosen)
        ] + [token]

    def body(d_ref, *refs):
        lefts = refs[: len(pairs)]
        rights = refs[len(pairs) : 2 * len(pairs)]
        got_ref = None if got is None else refs[2 * len(pairs)]
        token_ref, turned_ref = refs[-2:]
        outs = refs[-3:-2] if got is None else refs[-6:-2]
        c = pl.program_id(0)

        @pl.when(c == 0)
        def _():
            token_ref[...] = jnp.zeros_like(token_ref)
            for i, left_ref in enumerate(lefts):
                for p in range(count):
                    at = pl.multiple_of(jnp.bitwise_xor(d_ref[0], distance(p)) * rows, 128)
                    turned_ref[i, pl.ds(p * rows, rows), :] = left_ref[:, pl.ds(at, rows)].T

        def piece(i, p):
            return jnp.dot(
                turned_ref[i, pl.ds(p * rows, rows), :], rights[i][0], preferred_element_type=F32
            )

        def write(i, half):
            for p in range(count):
                value = piece(i, p)
                if got is None:
                    outs[0][p] = value.astype(BF16)
                    continue
                value = (value + got_ref[p].astype(F32)).astype(BF16)
                for which in (2 * half, 2 * half + 1):
                    if p in chosen[which]:
                        outs[which][chosen[which].index(p)] = value

        for i in range(len(pairs)):
            for half in (0, 1):
                low = max(starts[i], half * (steps // 2))
                high = min(starts[i] + tiles[i] * split, (half + 1) * (steps // 2))
                if low < high:
                    pl.when((c >= low) & (c < high))(lambda i=i, half=half: write(i, half))

    def right_spec(start, n):
        def at(c, d_ref):
            k = jnp.clip(c - start, 0, n * split - 1)
            return (lax.div(k, jnp.int32(split)), 0, lax.rem(k, jnp.int32(split)))

        return pl.BlockSpec((1, total, tile), at)

    in_specs = [pl.BlockSpec((total, all_rows), lambda c, d_ref: (0, 0))] * len(pairs)
    in_specs += [right_spec(start, n) for start, n in zip(starts, tiles)]
    args = [left for left, _ in pairs] + [right for _, right in pairs]
    if got is None:
        out_shape = [jax.ShapeDtypeStruct((count, rows, columns), BF16)]
        out_specs = [pl.BlockSpec((count, rows, tile), lambda c, d_ref: (0, 0, c))]
    else:
        in_specs.append(pl.BlockSpec((count, rows, tile), lambda c, d_ref: (0, 0, c)))
        args.append(got)
        out_shape = [jax.ShapeDtypeStruct((count // 2, rows, columns // 2), BF16)] * 4
        mid = steps // 2
        first = pl.BlockSpec(
            (count // 2, rows, tile), lambda c, d_ref: (0, 0, jnp.minimum(c, mid - 1))
        )
        second = pl.BlockSpec(
            (count // 2, rows, tile), lambda c, d_ref: (0, 0, jnp.maximum(c - mid, 0))
        )
        out_specs = [first, first, second, second]
    out_shape = out_shape + [TOKEN]
    out_specs = out_specs + [pl.BlockSpec(TOKEN.shape, lambda c, d_ref: (0, 0))]
    in_specs += [ANY] * len(deps)
    return pl.pallas_call(
        body,
        out_shape=out_shape,
        grid_spec=pltpu.PrefetchScalarGridSpec(
            num_scalar_prefetch=1,
            grid=(steps,),
            in_specs=in_specs,
            out_specs=out_specs,
            scratch_shapes=[pltpu.VMEM((len(pairs), count * rows, total), BF16)],
        ),
        compiler_params=pltpu.CompilerParams(vmem_limit_bytes=34 * 2**20),
        cost_estimate=LIGHT,
        name="gradient",
    )(d.reshape(1).astype(jnp.int32), *args, *deps)


def head_probs(q, k, far, slope):
    scores = lax.dot_general(q, k, (((1,), (1,)), ((), ())), preferred_element_type=F32)
    scores = scores * (HEAD ** (-0.5)) - slope * far
    raised = jnp.exp(scores - jnp.max(scores, axis=-1, keepdims=True))
    return raised * (1.0 / jnp.sum(raised, axis=-1, keepdims=True))


def flat_frames(block):
    sources, _, rows, lanes = block.shape
    if rows % 16 == 0:
        return block.reshape(sources * rows, lanes)
    return block.astype(F32).reshape(sources * rows, lanes).astype(BF16)


def by_source(value, like):
    sources, _, rows, lanes = like
    if rows % 16 == 0:
        return value.astype(BF16).reshape(sources, 1, rows, lanes)
    return value.reshape(sources, 1, rows, lanes).astype(BF16)


def attend(triple, far, slopes):
    dp, micro, rows, wide = triple.shape
    frames = dp * rows
    width = wide // 3
    pairs = width // 128
    shape = (dp, 1, rows, 128)

    def body(slope_ref, q_ref, k_ref, v_ref, far_ref, out_ref):
        h = pl.program_id(1)
        q, k, v = (flat_frames(ref[...]) for ref in (q_ref, k_ref, v_ref))
        first = lax.broadcasted_iota(jnp.int32, (frames, 128), 1) < HEAD
        zero = jnp.zeros_like(q)
        outs = []
        for j, own in enumerate((jnp.where(first, q, zero), jnp.where(first, zero, q))):
            probs = head_probs(own, k, far_ref[0], slope_ref[h * 2 + j])
            outs.append(jnp.dot(probs.astype(BF16), v, preferred_element_type=F32))
        out_ref[...] = by_source(jnp.where(first, outs[0], outs[1]), shape)

    def spec(offset):
        return pl.BlockSpec(shape, lambda m, h, s: (0, m, 0, h + offset))

    return pl.pallas_call(
        body,
        out_shape=jax.ShapeDtypeStruct((dp, micro, rows, width), BF16),
        grid_spec=pltpu.PrefetchScalarGridSpec(
            num_scalar_prefetch=1,
            grid=(micro, pairs),
            in_specs=[
                spec(0),
                spec(pairs),
                spec(2 * pairs),
                pl.BlockSpec((1, frames, frames), lambda m, h, s: (m, 0, 0)),
            ],
            out_specs=spec(0),
        ),
        compiler_params=pltpu.CompilerParams(vmem_limit_bytes=24 * 2**20),
        cost_estimate=LIGHT,
        name="attend",
    )(slopes, triple, triple, triple, far)


def attend_back(triple, grad, far, slopes, deps=()):
    dp, micro, rows, wide = triple.shape
    frames = dp * rows
    width = wide // 3
    pairs = width // 128
    shape = (dp, 1, rows, 128)
    scale = HEAD ** (-0.5)

    def turned(left, right):
        return lax.dot_general(left, right, (((0,), (0,)), ((), ())), preferred_element_type=F32)

    def body(slope_ref, q_ref, k_ref, v_ref, g_ref, far_ref, *refs):
        out_ref, token_ref = refs[-2:]
        token_ref[...] = jnp.zeros_like(token_ref)
        h = pl.program_id(1)
        q, k, v, g = (flat_frames(ref[...]) for ref in (q_ref, k_ref, v_ref, g_ref))
        first = lax.broadcasted_iota(jnp.int32, (frames, 128), 1) < HEAD
        zero = jnp.zeros_like(q)
        grads = []
        for j in range(2):
            own_q = jnp.where(first, q, zero) if j == 0 else jnp.where(first, zero, q)
            own_g = jnp.where(first, g, zero) if j == 0 else jnp.where(first, zero, g)
            scores = nt(k, own_q) * scale - slope_ref[h * 2 + j] * far_ref[0]
            raised = jnp.exp(scores - jnp.max(scores, axis=0, keepdims=True))
            probs = raised * (1.0 / jnp.sum(raised, axis=0, keepdims=True))
            back = nt(v, own_g)
            back = probs * (back - jnp.sum(back * probs, axis=0, keepdims=True))
            low = back.astype(BF16)
            grads.append(
                (
                    turned(low, k) * scale,
                    jnp.dot(low, q, preferred_element_type=F32) * scale,
                    jnp.dot(probs.astype(BF16), g, preferred_element_type=F32),
                )
            )
        for i in range(3):
            out_ref[i] = by_source(jnp.where(first, grads[0][i], grads[1][i]), shape)

    def spec(offset):
        return pl.BlockSpec(shape, lambda m, h, s: (0, m, 0, h + offset))

    return pl.pallas_call(
        body,
        out_shape=[jax.ShapeDtypeStruct((3, dp, micro, rows, width), BF16), TOKEN],
        grid_spec=pltpu.PrefetchScalarGridSpec(
            num_scalar_prefetch=1,
            grid=(micro, pairs),
            in_specs=[
                spec(0),
                spec(pairs),
                spec(2 * pairs),
                spec(0),
                pl.BlockSpec((1, frames, frames), lambda m, h, s: (m, 0, 0)),
            ]
            + [ANY] * len(deps),
            out_specs=[
                pl.BlockSpec((3,) + shape, lambda m, h, s: (0, 0, m, 0, h)),
                pl.BlockSpec(TOKEN.shape, lambda m, h, s: (0, 0)),
            ],
        ),
        compiler_params=pltpu.CompilerParams(vmem_limit_bytes=24 * 2**20),
        cost_estimate=LIGHT,
        name="attend_back",
    )(slopes, triple, triple, triple, grad, far, *deps)


def add_up(values):
    total = values[0].astype(F32)
    for value in values[1:]:
        total = total + value.astype(F32)
    return total.astype(BF16)


class Reduction:
    def __init__(self, pairs, d, dims, deps=()):
        self.pairs = [(left, right if right.ndim == 3 else right[None]) for left, right in pairs]
        self.d = d
        self.dims = dims
        self.sent, self.token = gradient_blocks(self.pairs, d, dims, deps=deps)

    def share(self):
        return flip(self.sent, 1)

    def own(self, got, deps=()):
        *self.parts, self.token = gradient_blocks(self.pairs, self.d, self.dims, got, deps)

    def near(self):
        parts = self.parts
        return [flip(parts[0], 1 << self.dims[0]), flip(parts[2], 1 << self.dims[-1])]

    def near_landed(self, got):
        self.halves = []
        for side, order in ((0, self.dims), (1, self.dims[::-1])):
            stay = self.parts[2 * side + 1]
            left = [bit for bit in self.dims if bit != order[0]]
            shape = (2,) * len(left) + stay.shape[1:]
            values = [stay.reshape(shape), got[side].reshape(shape)]
            self.halves.append((values, list(order[1:]), left))

    def step(self):
        sends, self.stays = [], []
        for values, order, left in self.halves:
            at = left.index(order[0])
            sends.append(add_up([lax.index_in_dim(v, 1, at, keepdims=False) for v in values]))
            self.stays.append([lax.index_in_dim(v, 0, at, keepdims=False) for v in values])
        bits = [order[0] for _, order, _ in self.halves]
        return [flip(sends[0], 1 << bits[0]), flip(sends[1], 1 << bits[1])]

    def landed(self, got):
        halves = []
        for i, (_, order, left) in enumerate(self.halves):
            halves.append((self.stays[i] + [got[i]], order[1:], [b for b in left if b != order[0]]))
        self.halves = halves

    def cross(self):
        while len(self.halves[0][1]) > 1:
            self.landed(self.step())
        return self.step()

    def rows(self):
        self.value = jnp.concatenate([add_up(values) for values, _, _ in self.halves], axis=1)
        self.stage = 0
        return self.value

    def along(self):
        rep = lax.axis_size("rep")
        half = rep // 2
        k = self.stage
        if k < half - 1:
            pairs = [(k, k + 1), (rep - 1 - k, rep - 2 - k)]
        elif k == half - 1:
            pairs = [(k, k + 1), (k + 1, k)]
        else:
            i = rep - 2 - k
            pairs = [(i + 1, i), (rep - 2 - i, rep - 1 - i)]
        return lax.ppermute(self.value, "rep", pairs)

    def along_landed(self, got):
        rep = lax.axis_size("rep")
        z = lax.axis_index("rep")
        k = self.stage
        self.stage += 1
        if k < rep // 2:
            self.value = add_up([self.value, got])
        else:
            i = rep - 2 - k
            self.value = jnp.where((z == i) | (z == rep - 1 - i), got, self.value)

    def finish(self):
        while self.stage < lax.axis_size("rep") - 1:
            self.along_landed(self.along())
        return self.value.astype(F32)

    def halve(self, extra=None):
        rep = lax.axis_size("rep")
        z = lax.axis_index("rep")
        value = self.value
        if extra is not None:
            value = jnp.concatenate([value, extra], axis=0)
        bits = range(rep.bit_length() - 1)
        for bit in bits:
            mine = lax.bitwise_and(lax.shift_right_logical(z, bit), 1)
            size = value.shape[0] // 2
            send = lax.dynamic_slice_in_dim(value, (1 - mine) * size, size, 0)
            keep = lax.dynamic_slice_in_dim(value, mine * size, size, 0)
            value = add_up([keep, rep_flip(send, 1 << bit)])
        for bit in reversed(bits):
            mine = lax.bitwise_and(lax.shift_right_logical(z, bit), 1)
            got = rep_flip(value, 1 << bit)
            lower = jnp.where(mine == 0, value, got)
            upper = jnp.where(mine == 0, got, value)
            value = jnp.concatenate([lower, upper], axis=0)
        return value.astype(F32)


def nt(left, right):
    return lax.dot_general(left, right, (((1,), (1,)), ((), ())), preferred_element_type=F32)


def hidden_gradient(grad_result, w_down, slope, deps=()):
    total, width = grad_result.shape
    units = w_down.shape[0]
    tile = 512

    def body(grad_ref, w_ref, slope_ref, *refs):
        out_ref, sum_ref = refs[-2:]
        value = nt(grad_ref[...], w_ref[...]) * slope_ref[...].astype(F32)
        out_ref[...] = value.astype(BF16)
        sum_ref[...] = jnp.sum(value, axis=0, keepdims=True)

    return pl.pallas_call(
        body,
        out_shape=[
            jax.ShapeDtypeStruct((total, units), BF16),
            jax.ShapeDtypeStruct((1, units), F32),
        ],
        grid=(units // tile,),
        in_specs=[
            pl.BlockSpec((total, width), lambda c: (0, 0)),
            pl.BlockSpec((tile, width), lambda c: (c, 0)),
            pl.BlockSpec((total, tile), lambda c: (0, c)),
        ]
        + [ANY] * len(deps),
        out_specs=[
            pl.BlockSpec((total, tile), lambda c: (0, c)),
            pl.BlockSpec((1, tile), lambda c: (0, c)),
        ],
        compiler_params=pltpu.CompilerParams(vmem_limit_bytes=24 * 2**20),
        cost_estimate=LIGHT,
        name="hidden_gradient",
    )(grad_result, w_down, slope, *deps)


def mixed_gradient(hidden_low, w_up, w_out, mixed, grad_result, gain):
    total, units = hidden_low.shape
    width = w_up.shape[0]
    tile = 256

    def body(low_ref, up_ref, out_w_ref, mixed_ref, result_ref, gain_ref, *outs):
        grad_ref, rounded_ref, attended_ref, sums_ref = outs
        grad = nt(low_ref[...], up_ref[...])
        unit, scale = norm_parts(mixed_ref[...])
        result = result_ref[...].astype(F32)
        value = result + norm_back(grad, gain_ref[...], unit, scale)
        rounded = value.astype(BF16)
        grad_ref[...] = value
        rounded_ref[...] = rounded
        attended_ref[...] = nt(rounded, out_w_ref[...]).astype(BF16)

        @pl.when(pl.program_id(0) == 0)
        def _():
            sums_ref[...] = jnp.zeros_like(sums_ref)

        for i, terms in enumerate((value, grad * unit, grad, result)):
            sums_ref[pl.ds(i, 1), :] += jnp.sum(terms, axis=0, keepdims=True)

    rows = pl.BlockSpec((tile, width), lambda r: (r, 0))
    whole = [
        pl.BlockSpec((width, units), lambda r: (0, 0)),
        pl.BlockSpec((width, width), lambda r: (0, 0)),
    ]
    return pl.pallas_call(
        body,
        out_shape=[
            jax.ShapeDtypeStruct((total, width), F32),
            jax.ShapeDtypeStruct((total, width), BF16),
            jax.ShapeDtypeStruct((total, width), BF16),
            jax.ShapeDtypeStruct((8, width), F32),
        ],
        grid=(total // tile,),
        in_specs=[pl.BlockSpec((tile, units), lambda r: (r, 0))]
        + whole
        + [rows, rows, pl.BlockSpec((1, width), lambda r: (0, 0))],
        out_specs=[rows, rows, rows, pl.BlockSpec((8, width), lambda r: (0, 0))],
        compiler_params=pltpu.CompilerParams(vmem_limit_bytes=44 * 2**20),
        cost_estimate=LIGHT,
        name="mixed_gradient",
    )(hidden_low, w_up, w_out, mixed, grad_result, gain.reshape(1, width))


def normed_gradient(grad_triple, w_qkv, deps=()):
    three, total, width = grad_triple.shape
    tile = 256

    def body(grad_ref, w_ref, *refs):
        out_ref = refs[-1]
        value = nt(grad_ref[0], w_ref[:, pl.ds(0, width)])
        for i in range(1, three):
            value += nt(grad_ref[i], w_ref[:, pl.ds(i * width, width)])
        out_ref[...] = value.astype(BF16)

    return pl.pallas_call(
        body,
        out_shape=jax.ShapeDtypeStruct((total, width), BF16),
        grid=(total // tile,),
        in_specs=[
            pl.BlockSpec((three, tile, width), lambda r: (0, r, 0)),
            pl.BlockSpec((width, three * width), lambda r: (0, 0)),
        ]
        + [ANY] * len(deps),
        out_specs=pl.BlockSpec((tile, width), lambda r: (r, 0)),
        compiler_params=pltpu.CompilerParams(vmem_limit_bytes=24 * 2**20),
        cost_estimate=LIGHT,
        name="normed_gradient",
    )(grad_triple, w_qkv, *deps)


def matmul(left, right):
    return jnp.dot(left, right, preferred_element_type=F32)


def matmul_nt(left, right):
    return lax.dot_general(left, right, (((1,), (1,)), ((), ())), preferred_element_type=F32)


def matmul_tn(left, right):
    return lax.dot_general(left, right, (((0,), (0,)), ((), ())), preferred_element_type=F32)


def norm_parts(values):
    average = jnp.mean(values, axis=-1, keepdims=True)
    centred = values - average
    spread = jnp.mean(centred * centred, axis=-1, keepdims=True)
    scale = lax.rsqrt(spread + EPS)
    return centred * scale, scale


def norm_back(grad, gain, unit, scale):
    e = grad * gain
    return scale * (
        e
        - jnp.mean(e, axis=-1, keepdims=True)
        - unit * jnp.mean(e * unit, axis=-1, keepdims=True)
    )


def shards(
    inputs,
    skips,
    cotangent,
    dest_slot,
    pack_segments,
    block_live,
    counts,
    w_skip,
    b_skip,
    g_one,
    b_one,
    w_qkv,
    w_out,
    b_out,
    g_two,
    b_two,
    w_up,
    c_up,
    w_down,
    c_down,
):
    dp = lax.axis_size("dp")
    rep = lax.axis_size("rep")
    d = lax.axis_index("dp")
    z = lax.axis_index("rep")
    micro = inputs.shape[0]
    frames = inputs.shape[2]
    width = inputs.shape[3]
    blocks = dest_slot.shape[2]
    block = frames // blocks
    per_pair = blocks // dp
    total = micro * frames
    bits = dp.bit_length() - 1
    place = jnp.stack([z, lax.rem(d, 8)]).astype(jnp.int32)
    dims = list(range(1, bits))
    small = jnp.concatenate([dest_slot.reshape(-1), block_live.reshape(-1), counts.reshape(-1)])

    own_skip = own_chunk(place, width, [w_skip])
    z_skip = Fetch(own_skip)
    z_skip.rest()
    got = z_skip.send()
    every = small[None]
    for bit in range(bits):
        every = jnp.concatenate([every, flip(every, 1 << bit)], axis=0)
    z_mid = Fetch(own_chunk(place, width, [w_qkv, w_out], z_skip.held[1:]))
    z_mid.rest()
    z_skip.landed(got)

    run_skip = Spread(z_skip.far(), width, [every, z_mid.held[-1]])
    mid = z_mid.send()
    run_skip.near_landed(run_skip.near())

    span = micro * blocks
    numbers = every[:, : 2 * span].reshape(dp, 2 * micro, blocks)
    numbers = jnp.transpose(numbers, (1, 0, 2)).reshape(2 * micro, dp * blocks).astype(F32)
    count_total = jnp.sum(every[:, 2 * span]).astype(F32).reshape(1, 1)
    inner = jnp.arange(frames) % block
    live = inner[None] < jnp.repeat(block_live[:, 0, :], block, axis=1)
    codes = (2 * pack_segments[:, 0, :] + live).astype(F32)
    far, far_turned, keep_wide, shuffle = plan_order(
        numbers[:micro], numbers[micro:], codes, d, block, [run_skip.pairs[0]]
    )
    keep_rows = keep_wide[:, :1]

    run_skip.cross_landed(run_skip.cross(), [shuffle])

    z_mid.landed(mid)
    run_mid = Spread(z_mid.far(), width)
    full_skip, _ = assemble(
        w_skip, run_skip.parts(run_skip.share()), place, 0, 1, [run_mid.start[0]]
    )
    z_up = Fetch(own_chunk(place, width, [w_up], [run_mid.start[0]]))
    z_up.rest()
    joined = jnp.concatenate([inputs.reshape(total, width), skips.reshape(total, width)], axis=1)
    base = matmul(joined, full_skip) + b_skip
    unit_one, scale_one = norm_parts(base)
    own_normed = (unit_one * g_one + b_one).astype(BF16)
    sent = matmul(shuffle, own_normed).astype(BF16)
    run_mid.near_landed(run_mid.near(), [sent, z_up.held[-1]])

    def exchange(values):
        values = values.reshape(dp, total // dp, width)
        got = lax.all_to_all(values, "dp", split_axis=0, concat_axis=0, tiled=True)
        return got.reshape(total, width)

    normed = exchange(sent)
    up = z_up.send()
    run_mid.cross_landed(run_mid.cross(), [up])
    z_up.landed(up)

    other = run_mid.share()
    run_up = Spread(z_up.far(), width, [run_mid.every])
    z_down = Fetch(own_chunk(place, width, [w_down], [run_up.start[0]]))
    z_down.rest()
    run_up.near_landed(run_up.near(), [other, normed])
    shard_rows = w_qkv.shape[0] // 8
    parts_mid = run_mid.parts(other)
    full_qkv, _ = assemble(w_qkv, parts_mid, place, 0, 3, [run_up.pairs[0]])

    triple = matmul(normed, full_qkv).astype(BF16)
    triple = triple.reshape(dp, micro, per_pair * block, 3 * width)
    slopes = 2.0 ** (-8.0 * (jnp.arange(HEADS, dtype=F32) + 1.0) / HEADS)
    attended = attend(triple, far, slopes)
    down = z_down.send()
    run_up.cross_landed(run_up.cross(), [attended, down])
    z_down.landed(down)

    attended = exchange(attended)
    other = run_up.share()
    run_down = Spread(z_down.far(), width, [run_up.every])
    down = run_down.near()
    full_out, out_token = assemble(w_out, parts_mid, place, 3 * shard_rows, 1, [run_up.every])
    full_up, up_token = assemble(w_up, run_up.parts(other), place, 0, w_up.shape[1] // width)
    attended, out_token, up_token = together(attended, out_token, up_token)

    attended = matmul_tn(shuffle, attended).astype(BF16)
    mixed = base + matmul(attended, full_out) + (b_out + out_token[0, 0])
    unit_two, scale_two = norm_parts(mixed)
    normed_two = (unit_two * g_two + b_two).astype(BF16)
    count_total = count_total + up_token[:1, :1]
    for step in rep_steps(rep):
        count_total = count_total + rep_flip(count_total, step)
    share = counts[0, 0].astype(F32) * (dp * rep) / count_total[0, 0]
    run_down.near_landed(down, [normed_two])
    down = run_down.cross()
    hidden = matmul(normed_two, full_up) + c_up
    phi = 0.5 * (1.0 + lax.erf(hidden * (0.5**0.5)))
    active = (hidden * phi).astype(BF16)
    slope = (phi + hidden * jnp.exp(-0.5 * hidden * hidden) * ((2 * jnp.pi) ** -0.5)).astype(BF16)
    scaled = (cotangent.reshape(total, width).astype(F32) * share).astype(BF16)
    grad_result = scaled * keep_rows.astype(BF16)
    red_down = Reduction([(active, grad_result)], d, dims, [run_down.pairs[0]])

    down_got = red_down.share()
    run_down.cross_landed(down, [red_down.sent])
    full_down, down_token = assemble(
        w_down, run_down.parts(run_down.share()), place, 0, 1
    )
    red_down.own(down_got, [down_token])

    flying = red_down.near()
    hidden_low, sum_hidden = hidden_gradient(grad_result, full_down, slope, [red_down.token])
    grad_mixed, mixed_low, grad_attended, sums_mixed = mixed_gradient(
        hidden_low, full_up, full_out, mixed, grad_result, g_two
    )
    flying, sums_mixed = together(flying, sums_mixed)
    red_down.near_landed(flying)

    down_flying = red_down.cross()
    sent = matmul(shuffle, grad_attended).astype(BF16)
    grad_attended = exchange(sent)
    red_up = Reduction([(normed_two, hidden_low)], d, dims, [sent])
    up_got = red_up.share()
    result = mixed + matmul(active, full_down) + (c_down + red_up.token[0, 0])
    output = (result * keep_rows).astype(BF16)
    red_up.own(up_got, [output])
    down_flying, token = together(down_flying, red_up.token)
    red_down.landed(down_flying)
    red_down.rows()

    flying = red_up.near()
    line = red_down.along()
    grad_attended = grad_attended.reshape(dp, micro, per_pair * block, width)
    grad_triple, token = attend_back(
        triple, grad_attended, far_turned, slopes, [red_down.value, token]
    )
    grad_triple = grad_triple.reshape(3, total, width)
    flying, line, token = together(flying, line, token)
    red_up.near_landed(flying)
    red_down.along_landed(line)

    up_flying = red_up.cross()
    line = red_down.along()
    sent = normed_gradient(grad_triple, full_qkv, [token])
    grad_normed = exchange(sent)
    red_mid = Reduction([(attended, mixed_low), (normed, grad_triple)], d, dims, [sent])
    grad_normed, token = together(grad_normed, red_mid.token)

    mid_got = red_mid.share()
    grad_normed = matmul_tn(shuffle, grad_normed)
    grad_base = grad_mixed + norm_back(grad_normed, g_one, unit_one, scale_one)
    base_low = grad_base.astype(BF16)
    red_skip = Reduction([(joined, base_low)], d, dims, [token])
    skip_got = red_skip.share()
    up_flying, token = together(up_flying, red_skip.token)
    red_up.landed(up_flying)
    red_up.rows()
    up_line = red_up.along()
    red_mid.own(mid_got, [token])
    line, token = together(line, red_mid.token)
    red_down.along_landed(line)

    flying = red_mid.near()
    line = red_down.along()
    red_skip.own(skip_got, [token])
    skip_flying = red_skip.near()
    vectors = (
        jnp.sum(grad_base, axis=0),
        jnp.sum(grad_normed * unit_one, axis=0),
        jnp.sum(grad_normed, axis=0),
        sums_mixed[0],
        sums_mixed[1],
        sums_mixed[2],
        sum_hidden[0],
        sums_mixed[3],
    )
    lengths = [v.shape[0] for v in vectors]
    summed = jnp.concatenate(vectors).reshape(-1, 128)
    summed = summed + flip(summed, 1)
    grad_joined = matmul_nt(base_low, full_skip).astype(BF16)
    flying, up_line, grad_joined, summed = together(flying, up_line, grad_joined, summed)
    red_mid.near_landed(flying)
    red_up.along_landed(up_line)

    flying = red_mid.cross()
    up_line = red_up.along()
    for bit in range(1, bits - 1):
        summed = summed + flip(summed, 1 << bit)
    skip_flying, line, summed = together(skip_flying, line, summed)
    red_skip.near_landed(skip_flying)
    red_down.along_landed(line)
    skip_flying = red_skip.cross()
    if bits > 1:
        summed = summed + flip(summed, 1 << (bits - 1))
    flying, up_line = together(flying, up_line)
    red_mid.landed(flying)
    red_mid.rows()
    red_up.along_landed(up_line)
    up_line = red_up.along()
    skip_columns = w_skip.shape[1]
    extra = jnp.pad(summed.reshape(-1), (0, -summed.size % (16 * rep * skip_columns)))
    extra = extra.reshape(-1, skip_columns).astype(BF16)
    skip_flying, extra = together(skip_flying, extra)
    red_skip.landed(skip_flying)
    red_skip.rows()
    final_mid = red_mid.halve()
    final_skip = red_skip.halve(extra)
    red_up.along_landed(up_line)
    own_rows = w_skip.shape[0] * rep // dp
    summed = final_skip[own_rows:].reshape(-1)
    finals = [
        red_down.finish(),
        red_up.finish(),
        final_mid[:, :width],
        final_mid[:, width:],
        final_skip[:own_rows],
    ]
    sums = []
    offset = 0
    for length in lengths:
        sums.append(summed[offset : offset + length])
        offset += length

    def as_owned(values):
        return values.reshape(inputs.shape)

    return (
        as_owned(output),
        as_owned(grad_joined[:, :width]),
        as_owned(grad_joined[:, width:]),
        finals[4],
        sums[0],
        sums[1],
        sums[2],
        finals[3],
        finals[2],
        sums[3],
        sums[4],
        sums[5],
        finals[1],
        sums[6],
        finals[0],
        sums[7],
    )


def solution(mesh):
    frames = P(None, "rep", "dp", None)
    slots = P(None, "rep", "dp")
    rows = P("rep", None)
    whole = P()
    in_specs = (
        (frames,) * 3
        + (slots,) * 3
        + (P("dp", "rep"), rows, whole, whole, whole, rows, rows)
        + (whole,) * 3
        + (rows, whole, rows, whole)
    )
    split = P("dp", None)
    out_specs = (
        (frames,) * 3
        + (split,)
        + (whole,) * 3
        + (split, split)
        + (whole,) * 3
        + (split, whole, split, whole)
    )
    return jax.shard_map(shards, mesh=mesh, in_specs=in_specs, out_specs=out_specs, check_vma=False)
```

```python
import jax
import jax.numpy as jnp
from jax import lax
from jax.experimental import pallas as pl
from jax.experimental.pallas import tpu as pltpu
from jax.sharding import PartitionSpec as P

HEADS = 16
HEAD = 64
EPS = 1e-05
F32 = jnp.float32
BF16 = jnp.bfloat16
TOKEN = jax.ShapeDtypeStruct((8, 128), F32)
ANY = pl.BlockSpec(memory_space=pl.ANY)
LIGHT = pl.CostEstimate(flops=1024, bytes_accessed=1024, transcendentals=0)


def flip(value, bit):
    n = lax.axis_size("dp")
    return lax.ppermute(value, "dp", [(i, i ^ bit) for i in range(n)])


def rep_flip(value, bit):
    n = lax.axis_size("rep")
    return lax.ppermute(value, "rep", [(i, i ^ bit) for i in range(n)])


def after(value, *earlier):
    return lax.optimization_barrier((value,) + earlier)[0]


def together(*values):
    return lax.optimization_barrier(values)


def assemble(w_local, parts, place, row_at, tiles, deps=()):
    rep = lax.axis_size("rep")
    shard_rows, columns = w_local.shape
    rows = shard_rows // 8
    tile = columns // tiles
    half = tile // 2
    chunk_rows = parts[0][0].shape[0] // (len(parts[0][1]) * (rep - 1))
    arrays = [part[0] for part in parts]
    count = 1 + sum(len(part[1]) for part in parts) * (rep - 1) * tiles

    def body(place_ref, local_ref, *refs):
        out_ref, token_ref, sems = refs[-3:]
        token_ref[...] = jnp.zeros_like(token_ref)
        z = place_ref[0]
        e = place_ref[1]
        copies = [
            pltpu.make_async_copy(
                local_ref,
                out_ref.at[pl.ds(pl.multiple_of(z * shard_rows, 16), shard_rows), :],
                sems.at[0],
            )
        ]
        for ref, (_, runs) in zip(refs, parts):
            for k, (side, rel) in enumerate(runs):
                chunk = jnp.bitwise_xor(e, rel)
                for s, apart in enumerate(far_order(rep), 1):
                    shard = jnp.bitwise_xor(z, apart)
                    start = pl.multiple_of(shard * shard_rows + chunk * rows, 16)
                    for t in range(tiles):
                        at = (k * (rep - 1) + s - 1) * chunk_rows + row_at + t * rows
                        copies.append(
                            pltpu.make_async_copy(
                                ref.at[pl.ds(at, rows), :],
                                out_ref.at[pl.ds(start, rows), pl.ds(t * tile + side * half, half)],
                                sems.at[len(copies)],
                            )
                        )
        for copy in copies:
            copy.start()
        for copy in copies:
            copy.wait()

    return pl.pallas_call(
        body,
        out_shape=[jax.ShapeDtypeStruct((shard_rows * rep, columns), w_local.dtype), TOKEN],
        grid=(1,),
        in_specs=[pl.BlockSpec(memory_space=pltpu.SMEM)] + [ANY] * (1 + len(parts) + len(deps)),
        out_specs=[
            pl.BlockSpec((shard_rows * rep, columns), lambda i: (0, 0)),
            pl.BlockSpec(TOKEN.shape, lambda i: (0, 0)),
        ],
        scratch_shapes=[pltpu.SemaphoreType.DMA((count,))],
        compiler_params=pltpu.CompilerParams(vmem_limit_bytes=26 * 2**20),
        cost_estimate=pl.CostEstimate(flops=int(1.5 * 1.15e9), bytes_accessed=1024, transcendentals=0),
        name="assemble",
    )(place, w_local, *arrays, *deps)


def own_chunk(place, width, shards_local, deps=()):
    items = []
    for which, w_local in enumerate(shards_local):
        for t in range(w_local.shape[1] // width):
            items.append((which, w_local.shape[0] // 8, t * width))
    total = sum(item[1] for item in items)

    def body(place_ref, *refs):
        out_ref, sems = refs[-2:]
        copies = []
        at = 0
        for which, rows, column in items:
            start = pl.multiple_of(place_ref[1] * rows, 16)
            copies.append(
                pltpu.make_async_copy(
                    refs[which].at[pl.ds(start, rows), pl.ds(column, width)],
                    out_ref.at[pl.ds(at, rows), :],
                    sems.at[len(copies)],
                )
            )
            at += rows
        for copy in copies:
            copy.start()
        for copy in copies:
            copy.wait()

    return pl.pallas_call(
        body,
        out_shape=jax.ShapeDtypeStruct((total, width), shards_local[0].dtype),
        grid=(1,),
        in_specs=[pl.BlockSpec(memory_space=pltpu.SMEM)]
        + [ANY] * (len(shards_local) + len(deps)),
        out_specs=pl.BlockSpec((total, width), lambda i: (0, 0)),
        scratch_shapes=[pltpu.SemaphoreType.DMA((len(items),))],
        compiler_params=pltpu.CompilerParams(vmem_limit_bytes=24 * 2**20),
        cost_estimate=LIGHT,
        name="own_chunk",
    )(place, *shards_local, *deps)


def pack(arrays, outs, deps=()):
    count = sum(len(out) for out in outs)

    def body(*refs):
        sources, targets = refs[: len(arrays)], refs[-2 - len(outs) : -2]
        token_ref, sems = refs[-2:]
        token_ref[...] = jnp.zeros_like(token_ref)
        copies = []
        for target, out in zip(targets, outs):
            at = 0
            for which, row, rows, column, columns in out:
                copies.append(
                    pltpu.make_async_copy(
                        sources[which].at[pl.ds(row, rows), pl.ds(column, columns)],
                        target.at[pl.ds(at, rows), :],
                        sems.at[len(copies)],
                    )
                )
                at += rows
        for copy in copies:
            copy.start()
        for copy in copies:
            copy.wait()

    return pl.pallas_call(
        body,
        out_shape=[
            jax.ShapeDtypeStruct((sum(item[2] for item in out), out[0][4]), arrays[0].dtype)
            for out in outs
        ]
        + [TOKEN],
        grid=(1,),
        in_specs=[ANY] * (len(arrays) + len(deps)),
        out_specs=[
            pl.BlockSpec((sum(item[2] for item in out), out[0][4]), lambda i: (0, 0))
            for out in outs
        ]
        + [pl.BlockSpec(TOKEN.shape, lambda i: (0, 0))],
        scratch_shapes=[pltpu.SemaphoreType.DMA((count,))],
        compiler_params=pltpu.CompilerParams(vmem_limit_bytes=24 * 2**20),
        cost_estimate=LIGHT,
        name="pack",
    )(*arrays, *deps)


def far_order(rep):
    order = [0]
    for bit in reversed(range(rep.bit_length() - 1)):
        order = order + [distance ^ (1 << bit) for distance in order]
    return order[1:]


class Spread:
    def __init__(self, gots, width, deps=()):
        self.half = width // 2
        rows = sum(got.shape[0] for got in gots)
        items = [(i, 0, got.shape[0]) for i, got in enumerate(gots)]
        *self.start, _ = pack(
            gots, [[item + (column, self.half) for item in items] for column in (0, self.half)], deps
        )
        self.n = rows

    def near(self):
        return [flip(self.start[0], 2), flip(self.start[1], 4)]

    def near_landed(self, got, deps=()):
        whole = [(i, 0, self.n, 0, self.half) for i in range(4)]
        *self.pairs, self.token = pack(
            [self.start[0], got[0], self.start[1], got[1]], [whole[:2], whole[2:]], deps
        )

    def cross(self):
        return [flip(self.pairs[0], 4), flip(self.pairs[1], 2)]

    def cross_landed(self, got, deps=()):
        whole = [(i, 0, 2 * self.n, 0, self.half) for i in range(4)]
        self.every, self.token = pack([self.pairs[0], got[0], self.pairs[1], got[1]], [whole], deps)

    def share(self):
        return flip(self.every, 1)

    def parts(self, other):
        runs = [(0, 0), (0, 2), (0, 4), (0, 6), (1, 0), (1, 4), (1, 2), (1, 6)]
        return [(self.every, runs), (other, [(side, rel | 1) for side, rel in runs])]


def rep_steps(rep):
    return [1 << bit for bit in reversed(range(rep.bit_length() - 1))]


class Fetch:
    def __init__(self, own):
        self.held = [own]
        self.steps = rep_steps(lax.axis_size("rep"))

    def send(self):
        sent = self.held[0]
        if len(self.held) > 1:
            whole = [(i, 0, a.shape[0], 0, a.shape[1]) for i, a in enumerate(self.held)]
            sent, _ = pack(self.held, [whole])
        return rep_flip(sent, self.steps[len(self.held) - 1])

    def landed(self, got):
        self.held.append(got)

    def rest(self):
        while len(self.held) < len(self.steps):
            self.landed(self.send())

    def far(self):
        return self.held[1:]


def plan_order(all_slots, all_live, codes, d, block, deps=()):
    micro, owners = all_slots.shape
    frames = codes.shape[1]
    blocks = frames // block
    dp = owners // blocks
    per_pair = blocks // dp
    total = micro * frames

    def column(row):
        return jnp.broadcast_to(row, (128, row.shape[1])).T[:, :1]

    def as_row(values):
        return jnp.broadcast_to(values, (values.shape[0], 128)).T[:1, :]

    def body(d_ref, slots_ref, live_ref, codes_ref, *refs):
        far_ref, turned_ref, keep_ref, shuffle_ref = refs[-4:]
        me = d_ref[0]
        lane = lax.broadcasted_iota(jnp.int32, (1, owners), 1)
        source = jnp.bitwise_xor(lax.div(lane, jnp.int32(blocks)), me)
        first_slot = (source * blocks).astype(F32) + lax.rem(lane, jnp.int32(blocks)).astype(F32)
        source_col = column(source.astype(F32))
        frame = lax.broadcasted_iota(jnp.int32, (frames, 1), 0)
        block_of = lax.div(frame, jnp.int32(block)).astype(F32)
        inner = lax.rem(frame, jnp.int32(block)).astype(F32)
        low = (me * blocks).astype(F32)
        rows = []
        for m in range(micro):
            slots = slots_ref[pl.ds(m, 1), :]
            slots_col = column(slots)
            same = source_col == source.astype(F32)
            rank = jnp.sum(jnp.where(same & (slots_col < slots), 1.0, 0.0), axis=0, keepdims=True)
            here = (slots >= low) & (slots < low + blocks)
            arrive = source.astype(F32) * per_pair + rank - (me * per_pair).astype(F32)
            arrive = jnp.where(here, arrive, -1.0)
            placed = jnp.sum(
                jnp.where(arrive == block_of, slots - low, 0.0), axis=1, keepdims=True
            )
            position = placed * block + inner
            at = lax.broadcasted_iota(jnp.int32, (1, frames), 1).astype(F32)
            code = jnp.sum(
                jnp.where(at == position, codes_ref[pl.ds(m, 1), :], 0.0), axis=1, keepdims=True
            )
            position_row, code_row = as_row(position), as_row(code)
            segment, segment_row = jnp.floor(code * 0.5), jnp.floor(code_row * 0.5)
            live_row = code_row - 2.0 * segment_row
            distance = jnp.abs(position - position_row)
            allowed = (segment == segment_row) & ((live_row > 0.5) | (distance < 0.5))
            far_ref[m] = jnp.where(allowed, distance, 1e32)
            live_col = code - 2.0 * segment
            allowed = (segment == segment_row) & ((live_col > 0.5) | (distance < 0.5))
            turned_ref[m] = jnp.where(allowed, distance, 1e32)
            own = lane < blocks
            mine = jnp.sum(
                jnp.where(own & (lane.astype(F32) == block_of), slots, 0.0), axis=1, keepdims=True
            )
            alive = jnp.sum(
                jnp.where(first_slot == mine, live_ref[pl.ds(m, 1), :], 0.0), axis=1, keepdims=True
            )
            keep_ref[pl.ds(m * frames, frames), :] = jnp.broadcast_to(
                jnp.where(inner < alive, 1.0, 0.0), (frames, 128)
            )
            my_rank = jnp.sum(
                jnp.where(own & (lane.astype(F32) == block_of), rank, 0.0), axis=1, keepdims=True
            )
            target = jnp.floor((my_rank + 0.5) / per_pair)
            row = (target * micro + m) * per_pair + (my_rank - target * per_pair)
            rows.append(as_row(row * block + inner))
        goal = jnp.concatenate(rows, axis=1)
        spot = lax.broadcasted_iota(jnp.int32, (total, total), 0).astype(F32)
        shuffle_ref[...] = jnp.where(spot == goal, 1.0, 0.0).astype(BF16)

    vmem = pl.BlockSpec(memory_space=pltpu.VMEM)
    return pl.pallas_call(
        body,
        out_shape=[
            jax.ShapeDtypeStruct((micro, frames, frames), F32),
            jax.ShapeDtypeStruct((micro, frames, frames), F32),
            jax.ShapeDtypeStruct((total, 128), F32),
            jax.ShapeDtypeStruct((total, total), BF16),
        ],
        in_specs=[pl.BlockSpec(memory_space=pltpu.SMEM), vmem, vmem, vmem] + [ANY] * len(deps),
        out_specs=[vmem, vmem, vmem, vmem],
        compiler_params=pltpu.CompilerParams(vmem_limit_bytes=24 * 2**20),
        cost_estimate=LIGHT,
        name="plan_order",
    )(d.reshape(1).astype(jnp.int32), all_slots, all_live, codes, *deps)


def gradient_blocks(pairs, d, dims, got=None, deps=()):
    dp = lax.axis_size("dp")
    total, all_rows = pairs[0][0].shape
    width = pairs[0][1].shape[2]
    tiles = [right.shape[0] for _, right in pairs]
    columns = sum(tiles) * width
    rows = all_rows // dp
    count = dp // 2
    odd = 1 if got is None else 0
    tile = min(width, 512)
    split = width // tile
    steps = sum(tiles) * split
    starts = [sum(tiles[:i]) * split for i in range(len(tiles))]

    def distance(p):
        rel = odd
        for k, bit in enumerate(dims):
            rel += ((p >> (len(dims) - 1 - k)) & 1) << bit
        return rel

    upper = [p for p in range(count) if p >= count // 2]
    lower = [p for p in range(count) if p < count // 2]
    odds = [p for p in range(count) if p % 2 == 1]
    evens = [p for p in range(count) if p % 2 == 0]
    chosen = (upper, lower, odds, evens)

    if rows % 128 != 0:
        products = []
        for left, right in pairs:
            flat = jnp.transpose(right, (1, 0, 2)).reshape(total, -1)
            products.append(matmul_tn(left, flat))
        product = jnp.concatenate(products, axis=1).reshape(dp, rows, columns)
        rel = jnp.array([distance(p) for p in range(count)], jnp.int32)
        product = product[jnp.bitwise_xor(rel, d)]
        token = jnp.zeros(TOKEN.shape, F32) + product[0, :1, :1]
        if got is None:
            return [product.astype(BF16), token]
        product = (product + got.astype(F32)).astype(BF16)
        half = columns // 2
        return [
            jnp.stack([product[p, :, side * half : (side + 1) * half] for p in ps])
            for side, ps in zip((0, 0, 1, 1), chosen)
        ] + [token]

    def body(d_ref, *refs):
        lefts = refs[: len(pairs)]
        rights = refs[len(pairs) : 2 * len(pairs)]
        got_ref = None if got is None else refs[2 * len(pairs)]
        token_ref, turned_ref = refs[-2:]
        outs = refs[-3:-2] if got is None else refs[-6:-2]
        c = pl.program_id(0)

        @pl.when(c == 0)
        def _():
            token_ref[...] = jnp.zeros_like(token_ref)
            for i, left_ref in enumerate(lefts):
                for p in range(count):
                    at = pl.multiple_of(jnp.bitwise_xor(d_ref[0], distance(p)) * rows, 128)
                    turned_ref[i, pl.ds(p * rows, rows), :] = left_ref[:, pl.ds(at, rows)].T

        def piece(i, p):
            return jnp.dot(
                turned_ref[i, pl.ds(p * rows, rows), :], rights[i][0], preferred_element_type=F32
            )

        def write(i, half):
            for p in range(count):
                value = piece(i, p)
                if got is None:
                    outs[0][p] = value.astype(BF16)
                    continue
                value = (value + got_ref[p].astype(F32)).astype(BF16)
                for which in (2 * half, 2 * half + 1):
                    if p in chosen[which]:
                        outs[which][chosen[which].index(p)] = value

        for i in range(len(pairs)):
            for half in (0, 1):
                low = max(starts[i], half * (steps // 2))
                high = min(starts[i] + tiles[i] * split, (half + 1) * (steps // 2))
                if low < high:
                    pl.when((c >= low) & (c < high))(lambda i=i, half=half: write(i, half))

    def right_spec(start, n):
        def at(c, d_ref):
            k = jnp.clip(c - start, 0, n * split - 1)
            return (lax.div(k, jnp.int32(split)), 0, lax.rem(k, jnp.int32(split)))

        return pl.BlockSpec((1, total, tile), at)

    in_specs = [pl.BlockSpec((total, all_rows), lambda c, d_ref: (0, 0))] * len(pairs)
    in_specs += [right_spec(start, n) for start, n in zip(starts, tiles)]
    args = [left for left, _ in pairs] + [right for _, right in pairs]
    if got is None:
        out_shape = [jax.ShapeDtypeStruct((count, rows, columns), BF16)]
        out_specs = [pl.BlockSpec((count, rows, tile), lambda c, d_ref: (0, 0, c))]
    else:
        in_specs.append(pl.BlockSpec((count, rows, tile), lambda c, d_ref: (0, 0, c)))
        args.append(got)
        out_shape = [jax.ShapeDtypeStruct((count // 2, rows, columns // 2), BF16)] * 4
        mid = steps // 2
        first = pl.BlockSpec(
            (count // 2, rows, tile), lambda c, d_ref: (0, 0, jnp.minimum(c, mid - 1))
        )
        second = pl.BlockSpec(
            (count // 2, rows, tile), lambda c, d_ref: (0, 0, jnp.maximum(c - mid, 0))
        )
        out_specs = [first, first, second, second]
    out_shape = out_shape + [TOKEN]
    out_specs = out_specs + [pl.BlockSpec(TOKEN.shape, lambda c, d_ref: (0, 0))]
    in_specs += [ANY] * len(deps)
    return pl.pallas_call(
        body,
        out_shape=out_shape,
        grid_spec=pltpu.PrefetchScalarGridSpec(
            num_scalar_prefetch=1,
            grid=(steps,),
            in_specs=in_specs,
            out_specs=out_specs,
            scratch_shapes=[pltpu.VMEM((len(pairs), count * rows, total), BF16)],
        ),
        compiler_params=pltpu.CompilerParams(vmem_limit_bytes=34 * 2**20),
        cost_estimate=pl.CostEstimate(flops=int(2.5 * 1.15e9), bytes_accessed=1024, transcendentals=0),
        name="gradient",
    )(d.reshape(1).astype(jnp.int32), *args, *deps)


def head_probs(q, k, far, slope):
    scores = lax.dot_general(q, k, (((1,), (1,)), ((), ())), preferred_element_type=F32)
    scores = scores * (HEAD ** (-0.5)) - slope * far
    raised = jnp.exp(scores - jnp.max(scores, axis=-1, keepdims=True))
    return raised * (1.0 / jnp.sum(raised, axis=-1, keepdims=True))


def flat_frames(block):
    sources, _, rows, lanes = block.shape
    if rows % 16 == 0:
        return block.reshape(sources * rows, lanes)
    return block.astype(F32).reshape(sources * rows, lanes).astype(BF16)


def by_source(value, like):
    sources, _, rows, lanes = like
    if rows % 16 == 0:
        return value.astype(BF16).reshape(sources, 1, rows, lanes)
    return value.reshape(sources, 1, rows, lanes).astype(BF16)


def attend(triple, far, slopes):
    dp, micro, rows, wide = triple.shape
    frames = dp * rows
    width = wide // 3
    pairs = width // 128
    shape = (dp, 1, rows, 128)

    def body(slope_ref, q_ref, k_ref, v_ref, far_ref, out_ref):
        h = pl.program_id(1)
        q, k, v = (flat_frames(ref[...]) for ref in (q_ref, k_ref, v_ref))
        first = lax.broadcasted_iota(jnp.int32, (frames, 128), 1) < HEAD
        zero = jnp.zeros_like(q)
        outs = []
        for j, own in enumerate((jnp.where(first, q, zero), jnp.where(first, zero, q))):
            probs = head_probs(own, k, far_ref[0], slope_ref[h * 2 + j])
            outs.append(jnp.dot(probs.astype(BF16), v, preferred_element_type=F32))
        out_ref[...] = by_source(jnp.where(first, outs[0], outs[1]), shape)

    def spec(offset):
        return pl.BlockSpec(shape, lambda m, h, s: (0, m, 0, h + offset))

    return pl.pallas_call(
        body,
        out_shape=jax.ShapeDtypeStruct((dp, micro, rows, width), BF16),
        grid_spec=pltpu.PrefetchScalarGridSpec(
            num_scalar_prefetch=1,
            grid=(micro, pairs),
            in_specs=[
                spec(0),
                spec(pairs),
                spec(2 * pairs),
                pl.BlockSpec((1, frames, frames), lambda m, h, s: (m, 0, 0)),
            ],
            out_specs=spec(0),
        ),
        compiler_params=pltpu.CompilerParams(vmem_limit_bytes=24 * 2**20),
        cost_estimate=pl.CostEstimate(flops=int(8 * 1.15e9), bytes_accessed=1024, transcendentals=0),
        name="attend",
    )(slopes, triple, triple, triple, far)


def attend_back(triple, grad, far, slopes, deps=()):
    dp, micro, rows, wide = triple.shape
    frames = dp * rows
    width = wide // 3
    pairs = width // 128
    shape = (dp, 1, rows, 128)
    scale = HEAD ** (-0.5)

    def turned(left, right):
        return lax.dot_general(left, right, (((0,), (0,)), ((), ())), preferred_element_type=F32)

    def body(slope_ref, q_ref, k_ref, v_ref, g_ref, far_ref, *refs):
        out_ref, token_ref = refs[-2:]
        token_ref[...] = jnp.zeros_like(token_ref)
        h = pl.program_id(1)
        q, k, v, g = (flat_frames(ref[...]) for ref in (q_ref, k_ref, v_ref, g_ref))
        first = lax.broadcasted_iota(jnp.int32, (frames, 128), 1) < HEAD
        zero = jnp.zeros_like(q)
        grads = []
        for j in range(2):
            own_q = jnp.where(first, q, zero) if j == 0 else jnp.where(first, zero, q)
            own_g = jnp.where(first, g, zero) if j == 0 else jnp.where(first, zero, g)
            scores = nt(k, own_q) * scale - slope_ref[h * 2 + j] * far_ref[0]
            raised = jnp.exp(scores - jnp.max(scores, axis=0, keepdims=True))
            probs = raised * (1.0 / jnp.sum(raised, axis=0, keepdims=True))
            back = nt(v, own_g)
            back = probs * (back - jnp.sum(back * probs, axis=0, keepdims=True))
            low = back.astype(BF16)
            grads.append(
                (
                    turned(low, k) * scale,
                    jnp.dot(low, q, preferred_element_type=F32) * scale,
                    jnp.dot(probs.astype(BF16), g, preferred_element_type=F32),
                )
            )
        for i in range(3):
            out_ref[i] = by_source(jnp.where(first, grads[0][i], grads[1][i]), shape)

    def spec(offset):
        return pl.BlockSpec(shape, lambda m, h, s: (0, m, 0, h + offset))

    return pl.pallas_call(
        body,
        out_shape=[jax.ShapeDtypeStruct((3, dp, micro, rows, width), BF16), TOKEN],
        grid_spec=pltpu.PrefetchScalarGridSpec(
            num_scalar_prefetch=1,
            grid=(micro, pairs),
            in_specs=[
                spec(0),
                spec(pairs),
                spec(2 * pairs),
                spec(0),
                pl.BlockSpec((1, frames, frames), lambda m, h, s: (m, 0, 0)),
            ]
            + [ANY] * len(deps),
            out_specs=[
                pl.BlockSpec((3,) + shape, lambda m, h, s: (0, 0, m, 0, h)),
                pl.BlockSpec(TOKEN.shape, lambda m, h, s: (0, 0)),
            ],
        ),
        compiler_params=pltpu.CompilerParams(vmem_limit_bytes=24 * 2**20),
        cost_estimate=pl.CostEstimate(flops=int(2 * 1.15e9), bytes_accessed=1024, transcendentals=0),
        name="attend_back",
    )(slopes, triple, triple, triple, grad, far, *deps)


def add_up(values):
    total = values[0].astype(F32)
    for value in values[1:]:
        total = total + value.astype(F32)
    return total.astype(BF16)


class Reduction:
    def __init__(self, pairs, d, dims, deps=()):
        self.pairs = [(left, right if right.ndim == 3 else right[None]) for left, right in pairs]
        self.d = d
        self.dims = dims
        self.sent, self.token = gradient_blocks(self.pairs, d, dims, deps=deps)

    def share(self):
        return flip(self.sent, 1)

    def own(self, got, deps=()):
        *self.parts, self.token = gradient_blocks(self.pairs, self.d, self.dims, got, deps)

    def near(self):
        parts = self.parts
        return [flip(parts[0], 1 << self.dims[0]), flip(parts[2], 1 << self.dims[-1])]

    def near_landed(self, got):
        self.halves = []
        for side, order in ((0, self.dims), (1, self.dims[::-1])):
            stay = self.parts[2 * side + 1]
            left = [bit for bit in self.dims if bit != order[0]]
            shape = (2,) * len(left) + stay.shape[1:]
            values = [stay.reshape(shape), got[side].reshape(shape)]
            self.halves.append((values, list(order[1:]), left))

    def step(self):
        sends, self.stays = [], []
        for values, order, left in self.halves:
            at = left.index(order[0])
            sends.append(add_up([lax.index_in_dim(v, 1, at, keepdims=False) for v in values]))
            self.stays.append([lax.index_in_dim(v, 0, at, keepdims=False) for v in values])
        bits = [order[0] for _, order, _ in self.halves]
        return [flip(sends[0], 1 << bits[0]), flip(sends[1], 1 << bits[1])]

    def landed(self, got):
        halves = []
        for i, (_, order, left) in enumerate(self.halves):
            halves.append((self.stays[i] + [got[i]], order[1:], [b for b in left if b != order[0]]))
        self.halves = halves

    def cross(self):
        while len(self.halves[0][1]) > 1:
            self.landed(self.step())
        return self.step()

    def rows(self):
        self.value = jnp.concatenate([add_up(values) for values, _, _ in self.halves], axis=1)
        self.stage = 0
        return self.value

    def along(self):
        rep = lax.axis_size("rep")
        half = rep // 2
        k = self.stage
        if k < half - 1:
            pairs = [(k, k + 1), (rep - 1 - k, rep - 2 - k)]
        elif k == half - 1:
            pairs = [(k, k + 1), (k + 1, k)]
        else:
            i = rep - 2 - k
            pairs = [(i + 1, i), (rep - 2 - i, rep - 1 - i)]
        return lax.ppermute(self.value, "rep", pairs)

    def along_landed(self, got):
        rep = lax.axis_size("rep")
        z = lax.axis_index("rep")
        k = self.stage
        self.stage += 1
        if k < rep // 2:
            self.value = add_up([self.value, got])
        else:
            i = rep - 2 - k
            self.value = jnp.where((z == i) | (z == rep - 1 - i), got, self.value)

    def finish(self):
        while self.stage < lax.axis_size("rep") - 1:
            self.along_landed(self.along())
        return self.value.astype(F32)

    def halve(self, extra=None):
        rep = lax.axis_size("rep")
        z = lax.axis_index("rep")
        value = self.value
        if extra is not None:
            value = jnp.concatenate([value, extra], axis=0)
        bits = range(rep.bit_length() - 1)
        for bit in bits:
            mine = lax.bitwise_and(lax.shift_right_logical(z, bit), 1)
            size = value.shape[0] // 2
            send = lax.dynamic_slice_in_dim(value, (1 - mine) * size, size, 0)
            keep = lax.dynamic_slice_in_dim(value, mine * size, size, 0)
            value = add_up([keep, rep_flip(send, 1 << bit)])
        for bit in reversed(bits):
            mine = lax.bitwise_and(lax.shift_right_logical(z, bit), 1)
            got = rep_flip(value, 1 << bit)
            lower = jnp.where(mine == 0, value, got)
            upper = jnp.where(mine == 0, got, value)
            value = jnp.concatenate([lower, upper], axis=0)
        return value.astype(F32)


def nt(left, right):
    return lax.dot_general(left, right, (((1,), (1,)), ((), ())), preferred_element_type=F32)


def hidden_gradient(grad_result, w_down, slope, deps=()):
    total, width = grad_result.shape
    units = w_down.shape[0]
    tile = 512

    def body(grad_ref, w_ref, slope_ref, *refs):
        out_ref, sum_ref = refs[-2:]
        value = nt(grad_ref[...], w_ref[...]) * slope_ref[...].astype(F32)
        out_ref[...] = value.astype(BF16)
        sum_ref[...] = jnp.sum(value, axis=0, keepdims=True)

    return pl.pallas_call(
        body,
        out_shape=[
            jax.ShapeDtypeStruct((total, units), BF16),
            jax.ShapeDtypeStruct((1, units), F32),
        ],
        grid=(units // tile,),
        in_specs=[
            pl.BlockSpec((total, width), lambda c: (0, 0)),
            pl.BlockSpec((tile, width), lambda c: (c, 0)),
            pl.BlockSpec((total, tile), lambda c: (0, c)),
        ]
        + [ANY] * len(deps),
        out_specs=[
            pl.BlockSpec((total, tile), lambda c: (0, c)),
            pl.BlockSpec((1, tile), lambda c: (0, c)),
        ],
        compiler_params=pltpu.CompilerParams(vmem_limit_bytes=24 * 2**20),
        cost_estimate=pl.CostEstimate(flops=int(3 * 1.15e9), bytes_accessed=1024, transcendentals=0),
        name="hidden_gradient",
    )(grad_result, w_down, slope, *deps)


def mixed_gradient(hidden_low, w_up, w_out, mixed, grad_result, gain, deps=()):
    total, units = hidden_low.shape
    width = w_up.shape[0]
    tile = 256

    def body(low_ref, up_ref, out_w_ref, mixed_ref, result_ref, gain_ref, *outs):
        grad_ref, rounded_ref, attended_ref, sums_ref = outs[-4:]
        grad = nt(low_ref[...], up_ref[...])
        unit, scale = norm_parts(mixed_ref[...])
        result = result_ref[...].astype(F32)
        value = result + norm_back(grad, gain_ref[...], unit, scale)
        rounded = value.astype(BF16)
        grad_ref[...] = value
        rounded_ref[...] = rounded
        attended_ref[...] = nt(rounded, out_w_ref[...]).astype(BF16)

        @pl.when(pl.program_id(0) == 0)
        def _():
            sums_ref[...] = jnp.zeros_like(sums_ref)

        for i, terms in enumerate((value, grad * unit, grad, result)):
            sums_ref[pl.ds(i, 1), :] += jnp.sum(terms, axis=0, keepdims=True)

    rows = pl.BlockSpec((tile, width), lambda r: (r, 0))
    whole = [
        pl.BlockSpec((width, units), lambda r: (0, 0)),
        pl.BlockSpec((width, width), lambda r: (0, 0)),
    ]
    return pl.pallas_call(
        body,
        out_shape=[
            jax.ShapeDtypeStruct((total, width), F32),
            jax.ShapeDtypeStruct((total, width), BF16),
            jax.ShapeDtypeStruct((total, width), BF16),
            jax.ShapeDtypeStruct((8, width), F32),
        ],
        grid=(total // tile,),
        in_specs=[pl.BlockSpec((tile, units), lambda r: (r, 0))]
        + whole
        + [rows, rows, pl.BlockSpec((1, width), lambda r: (0, 0))]
        + [ANY] * len(deps),
        out_specs=[rows, rows, rows, pl.BlockSpec((8, width), lambda r: (0, 0))],
        compiler_params=pltpu.CompilerParams(vmem_limit_bytes=44 * 2**20),
        cost_estimate=pl.CostEstimate(flops=int(2 * 1.15e9), bytes_accessed=1024, transcendentals=0),
        name="mixed_gradient",
    )(hidden_low, w_up, w_out, mixed, grad_result, gain.reshape(1, width), *deps)


def normed_gradient(grad_triple, w_qkv, deps=()):
    three, total, width = grad_triple.shape
    tile = 256

    def body(grad_ref, w_ref, *refs):
        out_ref = refs[-1]
        value = nt(grad_ref[0], w_ref[:, pl.ds(0, width)])
        for i in range(1, three):
            value += nt(grad_ref[i], w_ref[:, pl.ds(i * width, width)])
        out_ref[...] = value.astype(BF16)

    return pl.pallas_call(
        body,
        out_shape=jax.ShapeDtypeStruct((total, width), BF16),
        grid=(total // tile,),
        in_specs=[
            pl.BlockSpec((three, tile, width), lambda r: (0, r, 0)),
            pl.BlockSpec((width, three * width), lambda r: (0, 0)),
        ]
        + [ANY] * len(deps),
        out_specs=pl.BlockSpec((tile, width), lambda r: (r, 0)),
        compiler_params=pltpu.CompilerParams(vmem_limit_bytes=24 * 2**20),
        cost_estimate=pl.CostEstimate(flops=int(2 * 1.15e9), bytes_accessed=1024, transcendentals=0),
        name="normed_gradient",
    )(grad_triple, w_qkv, *deps)


def matmul(left, right):
    return jnp.dot(left, right, preferred_element_type=F32)


def matmul_nt(left, right):
    return lax.dot_general(left, right, (((1,), (1,)), ((), ())), preferred_element_type=F32)


def matmul_tn(left, right):
    return lax.dot_general(left, right, (((0,), (0,)), ((), ())), preferred_element_type=F32)


def norm_parts(values):
    average = jnp.mean(values, axis=-1, keepdims=True)
    centred = values - average
    spread = jnp.mean(centred * centred, axis=-1, keepdims=True)
    scale = lax.rsqrt(spread + EPS)
    return centred * scale, scale


def norm_back(grad, gain, unit, scale):
    e = grad * gain
    return scale * (
        e
        - jnp.mean(e, axis=-1, keepdims=True)
        - unit * jnp.mean(e * unit, axis=-1, keepdims=True)
    )


def shards(
    inputs,
    skips,
    cotangent,
    dest_slot,
    pack_segments,
    block_live,
    counts,
    w_skip,
    b_skip,
    g_one,
    b_one,
    w_qkv,
    w_out,
    b_out,
    g_two,
    b_two,
    w_up,
    c_up,
    w_down,
    c_down,
):
    dp = lax.axis_size("dp")
    rep = lax.axis_size("rep")
    d = lax.axis_index("dp")
    z = lax.axis_index("rep")
    micro = inputs.shape[0]
    frames = inputs.shape[2]
    width = inputs.shape[3]
    blocks = dest_slot.shape[2]
    block = frames // blocks
    per_pair = blocks // dp
    total = micro * frames
    bits = dp.bit_length() - 1
    place = jnp.stack([z, lax.rem(d, 8)]).astype(jnp.int32)
    dims = list(range(1, bits))
    small = jnp.concatenate([dest_slot.reshape(-1), block_live.reshape(-1), counts.reshape(-1)])

    own_skip = own_chunk(place, width, [w_skip])
    z_skip = Fetch(own_skip)
    z_skip.rest()
    got = z_skip.send()
    every = small[None]
    for bit in range(bits):
        every = jnp.concatenate([every, flip(every, 1 << bit)], axis=0)
    z_mid = Fetch(own_chunk(place, width, [w_qkv, w_out], z_skip.held[1:]))
    z_mid.rest()
    z_skip.landed(got)

    run_skip = Spread(z_skip.far(), width, [every, z_mid.held[-1]])
    mid = z_mid.send()
    run_skip.near_landed(run_skip.near())

    span = micro * blocks
    numbers = every[:, : 2 * span].reshape(dp, 2 * micro, blocks)
    numbers = jnp.transpose(numbers, (1, 0, 2)).reshape(2 * micro, dp * blocks).astype(F32)
    count_total = jnp.sum(every[:, 2 * span]).astype(F32).reshape(1, 1)
    inner = jnp.arange(frames) % block
    live = inner[None] < jnp.repeat(block_live[:, 0, :], block, axis=1)
    codes = (2 * pack_segments[:, 0, :] + live).astype(F32)
    far, far_turned, keep_wide, shuffle = plan_order(
        numbers[:micro], numbers[micro:], codes, d, block, [run_skip.pairs[0]]
    )
    keep_rows = keep_wide[:, :1]

    run_skip.cross_landed(run_skip.cross(), [shuffle])

    z_mid.landed(mid)
    run_mid = Spread(z_mid.far(), width)
    full_skip, _ = assemble(
        w_skip, run_skip.parts(run_skip.share()), place, 0, 1, [run_mid.start[0]]
    )
    z_up = Fetch(own_chunk(place, width, [w_up], [run_mid.start[0]]))
    z_up.rest()
    joined = jnp.concatenate([inputs.reshape(total, width), skips.reshape(total, width)], axis=1)
    base = matmul(joined, full_skip) + b_skip
    unit_one, scale_one = norm_parts(base)
    own_normed = (unit_one * g_one + b_one).astype(BF16)
    sent = matmul(shuffle, own_normed).astype(BF16)
    run_mid.near_landed(run_mid.near(), [sent, z_up.held[-1]])

    def exchange(values):
        values = values.reshape(dp, total // dp, width)
        got = lax.all_to_all(values, "dp", split_axis=0, concat_axis=0, tiled=True)
        return got.reshape(total, width)

    normed = exchange(sent)
    up = z_up.send()
    run_mid.cross_landed(run_mid.cross(), [up])
    z_up.landed(up)

    other = run_mid.share()
    run_up = Spread(z_up.far(), width, [run_mid.every])
    z_down = Fetch(own_chunk(place, width, [w_down], [run_up.start[0]]))
    z_down.rest()
    run_up.near_landed(run_up.near(), [other, normed])
    shard_rows = w_qkv.shape[0] // 8
    parts_mid = run_mid.parts(other)
    full_qkv, _ = assemble(w_qkv, parts_mid, place, 0, 3, [run_up.pairs[0]])

    triple = matmul(normed, full_qkv).astype(BF16)
    triple = triple.reshape(dp, micro, per_pair * block, 3 * width)
    slopes = 2.0 ** (-8.0 * (jnp.arange(HEADS, dtype=F32) + 1.0) / HEADS)
    attended = attend(triple, far, slopes)
    down = z_down.send()
    run_up.cross_landed(run_up.cross(), [attended, down])
    z_down.landed(down)

    attended = exchange(attended)
    other = run_up.share()
    run_down = Spread(z_down.far(), width, [run_up.every])
    down = run_down.near()
    full_out, out_token = assemble(w_out, parts_mid, place, 3 * shard_rows, 1, [run_up.every])
    full_up, up_token = assemble(w_up, run_up.parts(other), place, 0, w_up.shape[1] // width)
    attended, out_token, up_token = together(attended, out_token, up_token)

    attended = matmul_tn(shuffle, attended).astype(BF16)
    mixed = base + matmul(attended, full_out) + (b_out + out_token[0, 0])
    unit_two, scale_two = norm_parts(mixed)
    normed_two = (unit_two * g_two + b_two).astype(BF16)
    count_total = count_total + up_token[:1, :1]
    for step in rep_steps(rep):
        count_total = count_total + rep_flip(count_total, step)
    share = counts[0, 0].astype(F32) * (dp * rep) / count_total[0, 0]
    run_down.near_landed(down, [up_token])
    down = run_down.cross()
    hidden = matmul(normed_two, full_up) + (c_up + run_down.token[0, 0])
    phi = 0.5 * (1.0 + lax.erf(hidden * (0.5**0.5)))
    active = (hidden * phi).astype(BF16)
    slope = (phi + hidden * jnp.exp(-0.5 * hidden * hidden) * ((2 * jnp.pi) ** -0.5)).astype(BF16)
    scaled = (cotangent.reshape(total, width).astype(F32) * share).astype(BF16)
    grad_result = scaled * keep_rows.astype(BF16)
    red_down = Reduction([(active, grad_result)], d, dims)

    down_got = red_down.share()
    run_down.cross_landed(down, [red_down.sent])
    full_down, _ = assemble(w_down, run_down.parts(run_down.share()), place, 0, 1)

    hidden_low, sum_hidden = hidden_gradient(grad_result, full_down, slope)
    red_up = Reduction([(normed_two, hidden_low)], d, dims)
    up_got = red_up.share()
    red_down.own(down_got, [red_up.sent])
    flying = red_down.near()
    grad_mixed, mixed_low, grad_attended, sums_mixed = mixed_gradient(
        hidden_low, full_up, full_out, mixed, grad_result, g_two, [red_down.token]
    )
    flying, sums_mixed = together(flying, sums_mixed)
    red_down.near_landed(flying)

    down_flying = red_down.cross()
    sent = matmul(shuffle, grad_attended).astype(BF16)
    grad_attended = exchange(sent)
    red_up.own(up_got, [sent])
    flying = red_up.near()
    result = mixed + matmul(active, full_down) + (c_down + red_up.token[0, 0])
    output = (result * keep_rows).astype(BF16)
    down_flying, token = together(down_flying, red_up.token)
    red_down.landed(down_flying)
    red_down.rows()

    line = red_down.along()
    grad_attended = grad_attended.reshape(dp, micro, per_pair * block, width)
    grad_triple, token = attend_back(
        triple, grad_attended, far_turned, slopes, [red_down.value, token, output]
    )
    grad_triple = grad_triple.reshape(3, total, width)
    flying, line, token = together(flying, line, token)
    red_up.near_landed(flying)
    red_down.along_landed(line)

    up_flying = red_up.cross()
    line = red_down.along()
    sent = normed_gradient(grad_triple, full_qkv, [token])
    grad_normed = exchange(sent)
    red_mid = Reduction([(attended, mixed_low), (normed, grad_triple)], d, dims, [sent])
    grad_normed, line, token = together(grad_normed, line, red_mid.token)
    red_down.along_landed(line)

    mid_got = red_mid.share()
    line = red_down.along()
    grad_normed = matmul_tn(shuffle, grad_normed)
    grad_base = grad_mixed + norm_back(grad_normed, g_one, unit_one, scale_one)
    base_low = grad_base.astype(BF16)
    red_skip = Reduction([(joined, base_low)], d, dims, [token])
    skip_got = red_skip.share()
    vectors = (
        jnp.sum(grad_base, axis=0),
        jnp.sum(grad_normed * unit_one, axis=0),
        jnp.sum(grad_normed, axis=0),
        sums_mixed[0],
        sums_mixed[1],
        sums_mixed[2],
        sum_hidden[0],
        sums_mixed[3],
    )
    lengths = [v.shape[0] for v in vectors]
    summed = jnp.concatenate(vectors).reshape(-1, 128)
    for bit in range(bits - 1):
        summed = summed + flip(summed, 1 << bit)
    up_flying, token = together(up_flying, red_skip.token)
    red_up.landed(up_flying)
    red_up.rows()
    up_line = red_up.along()
    red_mid.own(mid_got, [token])
    line, summed, token = together(line, summed, red_mid.token)
    red_down.along_landed(line)

    flying = red_mid.near()
    red_skip.own(skip_got, [token])
    skip_flying = red_skip.near()
    grad_joined = matmul_nt(base_low, full_skip).astype(BF16)
    flying, up_line, grad_joined = together(flying, up_line, grad_joined)
    red_mid.near_landed(flying)
    red_up.along_landed(up_line)

    flying = red_mid.cross()
    up_line = red_up.along()
    skip_flying, summed = together(skip_flying, summed)
    red_skip.near_landed(skip_flying)
    skip_flying = red_skip.cross()
    flying, up_line, summed = together(flying, up_line, summed)
    red_mid.landed(flying)
    red_mid.rows()
    red_up.along_landed(up_line)
    up_line = red_up.along()
    summed = summed + flip(summed, 1 << (bits - 1))
    skip_columns = w_skip.shape[1]
    extra = jnp.pad(summed.reshape(-1), (0, -summed.size % (16 * rep * skip_columns)))
    extra = extra.reshape(-1, skip_columns).astype(BF16)
    skip_flying, extra = together(skip_flying, extra)
    red_skip.landed(skip_flying)
    red_skip.rows()
    final_mid = red_mid.halve()
    final_skip = red_skip.halve(extra)
    red_up.along_landed(up_line)
    own_rows = w_skip.shape[0] * rep // dp
    summed = final_skip[own_rows:].reshape(-1)
    finals = [
        red_down.finish(),
        red_up.finish(),
        final_mid[:, :width],
        final_mid[:, width:],
        final_skip[:own_rows],
    ]
    sums = []
    offset = 0
    for length in lengths:
        sums.append(summed[offset : offset + length])
        offset += length

    def as_owned(values):
        return values.reshape(inputs.shape)

    return (
        as_owned(output),
        as_owned(grad_joined[:, :width]),
        as_owned(grad_joined[:, width:]),
        finals[4],
        sums[0],
        sums[1],
        sums[2],
        finals[3],
        finals[2],
        sums[3],
        sums[4],
        sums[5],
        finals[1],
        sums[6],
        finals[0],
        sums[7],
    )


def solution(mesh):
    frames = P(None, "rep", "dp", None)
    slots = P(None, "rep", "dp")
    rows = P("rep", None)
    whole = P()
    in_specs = (
        (frames,) * 3
        + (slots,) * 3
        + (P("dp", "rep"), rows, whole, whole, whole, rows, rows)
        + (whole,) * 3
        + (rows, whole, rows, whole)
    )
    split = P("dp", None)
    out_specs = (
        (frames,) * 3
        + (split,)
        + (whole,) * 3
        + (split, split)
        + (whole,) * 3
        + (split, whole, split, whole)
    )
    return jax.shard_map(shards, mesh=mesh, in_specs=in_specs, out_specs=out_specs, check_vma=False)
```

```python
import jax
import jax.numpy as jnp
from jax import lax
from jax.experimental import pallas as pl
from jax.experimental.pallas import tpu as pltpu
from jax.sharding import PartitionSpec as P

HEADS = 16
HEAD = 64
EPS = 1e-05
F32 = jnp.float32
BF16 = jnp.bfloat16
TOKEN = jax.ShapeDtypeStruct((8, 128), F32)
ANY = pl.BlockSpec(memory_space=pl.ANY)
LIGHT = pl.CostEstimate(flops=1024, bytes_accessed=1024, transcendentals=0)


def flip(value, bit):
    n = lax.axis_size("dp")
    return lax.ppermute(value, "dp", [(i, i ^ bit) for i in range(n)])


def rep_flip(value, bit):
    n = lax.axis_size("rep")
    return lax.ppermute(value, "rep", [(i, i ^ bit) for i in range(n)])


def after(value, *earlier):
    return lax.optimization_barrier((value,) + earlier)[0]


def together(*values):
    return lax.optimization_barrier(values)


def assemble(w_local, parts, place, row_at, tiles, deps=()):
    rep = lax.axis_size("rep")
    shard_rows, columns = w_local.shape
    rows = shard_rows // 8
    tile = columns // tiles
    half = tile // 2
    chunk_rows = parts[0][0].shape[0] // (len(parts[0][1]) * (rep - 1))
    arrays = [part[0] for part in parts]
    count = 1 + sum(len(part[1]) for part in parts) * (rep - 1) * tiles

    def body(place_ref, local_ref, *refs):
        out_ref, token_ref, sems = refs[-3:]
        token_ref[...] = jnp.zeros_like(token_ref)
        z = place_ref[0]
        e = place_ref[1]
        copies = [
            pltpu.make_async_copy(
                local_ref,
                out_ref.at[pl.ds(pl.multiple_of(z * shard_rows, 16), shard_rows), :],
                sems.at[0],
            )
        ]
        for ref, (_, runs) in zip(refs, parts):
            for k, (side, rel) in enumerate(runs):
                chunk = jnp.bitwise_xor(e, rel)
                for s, apart in enumerate(far_order(rep), 1):
                    shard = jnp.bitwise_xor(z, apart)
                    start = pl.multiple_of(shard * shard_rows + chunk * rows, 16)
                    for t in range(tiles):
                        at = (k * (rep - 1) + s - 1) * chunk_rows + row_at + t * rows
                        copies.append(
                            pltpu.make_async_copy(
                                ref.at[pl.ds(at, rows), :],
                                out_ref.at[pl.ds(start, rows), pl.ds(t * tile + side * half, half)],
                                sems.at[len(copies)],
                            )
                        )
        for copy in copies:
            copy.start()
        for copy in copies:
            copy.wait()

    return pl.pallas_call(
        body,
        out_shape=[jax.ShapeDtypeStruct((shard_rows * rep, columns), w_local.dtype), TOKEN],
        grid=(1,),
        in_specs=[pl.BlockSpec(memory_space=pltpu.SMEM)] + [ANY] * (1 + len(parts) + len(deps)),
        out_specs=[
            pl.BlockSpec((shard_rows * rep, columns), lambda i: (0, 0)),
            pl.BlockSpec(TOKEN.shape, lambda i: (0, 0)),
        ],
        scratch_shapes=[pltpu.SemaphoreType.DMA((count,))],
        compiler_params=pltpu.CompilerParams(vmem_limit_bytes=26 * 2**20),
        cost_estimate=pl.CostEstimate(flops=int(1.5 * 1.15e9), bytes_accessed=1024, transcendentals=0),
        name="assemble",
    )(place, w_local, *arrays, *deps)


def own_chunk(place, width, shards_local, deps=()):
    items = []
    for which, w_local in enumerate(shards_local):
        for t in range(w_local.shape[1] // width):
            items.append((which, w_local.shape[0] // 8, t * width))
    total = sum(item[1] for item in items)

    def body(place_ref, *refs):
        out_ref, sems = refs[-2:]
        copies = []
        at = 0
        for which, rows, column in items:
            start = pl.multiple_of(place_ref[1] * rows, 16)
            copies.append(
                pltpu.make_async_copy(
                    refs[which].at[pl.ds(start, rows), pl.ds(column, width)],
                    out_ref.at[pl.ds(at, rows), :],
                    sems.at[len(copies)],
                )
            )
            at += rows
        for copy in copies:
            copy.start()
        for copy in copies:
            copy.wait()

    return pl.pallas_call(
        body,
        out_shape=jax.ShapeDtypeStruct((total, width), shards_local[0].dtype),
        grid=(1,),
        in_specs=[pl.BlockSpec(memory_space=pltpu.SMEM)]
        + [ANY] * (len(shards_local) + len(deps)),
        out_specs=pl.BlockSpec((total, width), lambda i: (0, 0)),
        scratch_shapes=[pltpu.SemaphoreType.DMA((len(items),))],
        compiler_params=pltpu.CompilerParams(vmem_limit_bytes=24 * 2**20),
        cost_estimate=LIGHT,
        name="own_chunk",
    )(place, *shards_local, *deps)


def pack(arrays, outs, deps=()):
    count = sum(len(out) for out in outs)

    def body(*refs):
        sources, targets = refs[: len(arrays)], refs[-2 - len(outs) : -2]
        token_ref, sems = refs[-2:]
        token_ref[...] = jnp.zeros_like(token_ref)
        copies = []
        for target, out in zip(targets, outs):
            at = 0
            for which, row, rows, column, columns in out:
                copies.append(
                    pltpu.make_async_copy(
                        sources[which].at[pl.ds(row, rows), pl.ds(column, columns)],
                        target.at[pl.ds(at, rows), :],
                        sems.at[len(copies)],
                    )
                )
                at += rows
        for copy in copies:
            copy.start()
        for copy in copies:
            copy.wait()

    return pl.pallas_call(
        body,
        out_shape=[
            jax.ShapeDtypeStruct((sum(item[2] for item in out), out[0][4]), arrays[0].dtype)
            for out in outs
        ]
        + [TOKEN],
        grid=(1,),
        in_specs=[ANY] * (len(arrays) + len(deps)),
        out_specs=[
            pl.BlockSpec((sum(item[2] for item in out), out[0][4]), lambda i: (0, 0))
            for out in outs
        ]
        + [pl.BlockSpec(TOKEN.shape, lambda i: (0, 0))],
        scratch_shapes=[pltpu.SemaphoreType.DMA((count,))],
        compiler_params=pltpu.CompilerParams(vmem_limit_bytes=24 * 2**20),
        cost_estimate=LIGHT,
        name="pack",
    )(*arrays, *deps)


def far_order(rep):
    order = [0]
    for bit in reversed(range(rep.bit_length() - 1)):
        order = order + [distance ^ (1 << bit) for distance in order]
    return order[1:]


class Spread:
    def __init__(self, gots, width, deps=()):
        self.half = width // 2
        rows = sum(got.shape[0] for got in gots)
        items = [(i, 0, got.shape[0]) for i, got in enumerate(gots)]
        *self.start, _ = pack(
            gots, [[item + (column, self.half) for item in items] for column in (0, self.half)], deps
        )
        self.n = rows

    def near(self):
        return [flip(self.start[0], 2), flip(self.start[1], 4)]

    def near_landed(self, got, deps=()):
        whole = [(i, 0, self.n, 0, self.half) for i in range(4)]
        *self.pairs, self.token = pack(
            [self.start[0], got[0], self.start[1], got[1]], [whole[:2], whole[2:]], deps
        )

    def cross(self):
        return [flip(self.pairs[0], 4), flip(self.pairs[1], 2)]

    def cross_landed(self, got, deps=()):
        whole = [(i, 0, 2 * self.n, 0, self.half) for i in range(4)]
        self.every, self.token = pack([self.pairs[0], got[0], self.pairs[1], got[1]], [whole], deps)

    def share(self):
        return flip(self.every, 1)

    def parts(self, other):
        runs = [(0, 0), (0, 2), (0, 4), (0, 6), (1, 0), (1, 4), (1, 2), (1, 6)]
        return [(self.every, runs), (other, [(side, rel | 1) for side, rel in runs])]


def rep_steps(rep):
    return [1 << bit for bit in reversed(range(rep.bit_length() - 1))]


class Fetch:
    def __init__(self, own):
        self.held = [own]
        self.steps = rep_steps(lax.axis_size("rep"))

    def send(self, deps=()):
        sent = self.held[0]
        if len(self.held) > 1:
            whole = [(i, 0, a.shape[0], 0, a.shape[1]) for i, a in enumerate(self.held)]
            sent, _ = pack(self.held, [whole], deps)
        return rep_flip(sent, self.steps[len(self.held) - 1])

    def landed(self, got):
        self.held.append(got)

    def rest(self):
        while len(self.held) < len(self.steps):
            self.landed(self.send())

    def far(self):
        return self.held[1:]


def plan_order(all_slots, all_live, codes, d, block, deps=()):
    micro, owners = all_slots.shape
    frames = codes.shape[1]
    blocks = frames // block
    dp = owners // blocks
    per_pair = blocks // dp
    total = micro * frames

    def column(row):
        return jnp.broadcast_to(row, (128, row.shape[1])).T[:, :1]

    def as_row(values):
        return jnp.broadcast_to(values, (values.shape[0], 128)).T[:1, :]

    def body(d_ref, slots_ref, live_ref, codes_ref, *refs):
        far_ref, turned_ref, keep_ref, shuffle_ref = refs[-4:]
        me = d_ref[0]
        lane = lax.broadcasted_iota(jnp.int32, (1, owners), 1)
        source = jnp.bitwise_xor(lax.div(lane, jnp.int32(blocks)), me)
        first_slot = (source * blocks).astype(F32) + lax.rem(lane, jnp.int32(blocks)).astype(F32)
        source_col = column(source.astype(F32))
        frame = lax.broadcasted_iota(jnp.int32, (frames, 1), 0)
        block_of = lax.div(frame, jnp.int32(block)).astype(F32)
        inner = lax.rem(frame, jnp.int32(block)).astype(F32)
        low = (me * blocks).astype(F32)
        rows = []
        for m in range(micro):
            slots = slots_ref[pl.ds(m, 1), :]
            slots_col = column(slots)
            same = source_col == source.astype(F32)
            rank = jnp.sum(jnp.where(same & (slots_col < slots), 1.0, 0.0), axis=0, keepdims=True)
            here = (slots >= low) & (slots < low + blocks)
            arrive = source.astype(F32) * per_pair + rank - (me * per_pair).astype(F32)
            arrive = jnp.where(here, arrive, -1.0)
            placed = jnp.sum(
                jnp.where(arrive == block_of, slots - low, 0.0), axis=1, keepdims=True
            )
            position = placed * block + inner
            at = lax.broadcasted_iota(jnp.int32, (1, frames), 1).astype(F32)
            code = jnp.sum(
                jnp.where(at == position, codes_ref[pl.ds(m, 1), :], 0.0), axis=1, keepdims=True
            )
            position_row, code_row = as_row(position), as_row(code)
            segment, segment_row = jnp.floor(code * 0.5), jnp.floor(code_row * 0.5)
            live_row = code_row - 2.0 * segment_row
            distance = jnp.abs(position - position_row)
            allowed = (segment == segment_row) & ((live_row > 0.5) | (distance < 0.5))
            far_ref[m] = jnp.where(allowed, distance, 1e32)
            live_col = code - 2.0 * segment
            allowed = (segment == segment_row) & ((live_col > 0.5) | (distance < 0.5))
            turned_ref[m] = jnp.where(allowed, distance, 1e32)
            own = lane < blocks
            mine = jnp.sum(
                jnp.where(own & (lane.astype(F32) == block_of), slots, 0.0), axis=1, keepdims=True
            )
            alive = jnp.sum(
                jnp.where(first_slot == mine, live_ref[pl.ds(m, 1), :], 0.0), axis=1, keepdims=True
            )
            keep_ref[pl.ds(m * frames, frames), :] = jnp.broadcast_to(
                jnp.where(inner < alive, 1.0, 0.0), (frames, 128)
            )
            my_rank = jnp.sum(
                jnp.where(own & (lane.astype(F32) == block_of), rank, 0.0), axis=1, keepdims=True
            )
            target = jnp.floor((my_rank + 0.5) / per_pair)
            row = (target * micro + m) * per_pair + (my_rank - target * per_pair)
            rows.append(as_row(row * block + inner))
        goal = jnp.concatenate(rows, axis=1)
        spot = lax.broadcasted_iota(jnp.int32, (total, total), 0).astype(F32)
        shuffle_ref[...] = jnp.where(spot == goal, 1.0, 0.0).astype(BF16)

    vmem = pl.BlockSpec(memory_space=pltpu.VMEM)
    return pl.pallas_call(
        body,
        out_shape=[
            jax.ShapeDtypeStruct((micro, frames, frames), F32),
            jax.ShapeDtypeStruct((micro, frames, frames), F32),
            jax.ShapeDtypeStruct((total, 128), F32),
            jax.ShapeDtypeStruct((total, total), BF16),
        ],
        in_specs=[pl.BlockSpec(memory_space=pltpu.SMEM), vmem, vmem, vmem] + [ANY] * len(deps),
        out_specs=[vmem, vmem, vmem, vmem],
        compiler_params=pltpu.CompilerParams(vmem_limit_bytes=24 * 2**20),
        cost_estimate=LIGHT,
        name="plan_order",
    )(d.reshape(1).astype(jnp.int32), all_slots, all_live, codes, *deps)


def gradient_blocks(pairs, d, dims, got=None, deps=()):
    dp = lax.axis_size("dp")
    total, all_rows = pairs[0][0].shape
    widths = [right.shape[2] for _, right in pairs]
    columns = sum(right.shape[0] * right.shape[2] for _, right in pairs)
    rows = all_rows // dp
    count = dp // 2
    odd = 1 if got is None else 0
    tile = min(min(widths), 512)
    splits = [width // tile for width in widths]
    tiles = [right.shape[0] * split for (_, right), split in zip(pairs, splits)]
    steps = sum(tiles)
    starts = [sum(tiles[:i]) for i in range(len(tiles))]

    def distance(p):
        rel = odd
        for k, bit in enumerate(dims):
            rel += ((p >> (len(dims) - 1 - k)) & 1) << bit
        return rel

    upper = [p for p in range(count) if p >= count // 2]
    lower = [p for p in range(count) if p < count // 2]
    odds = [p for p in range(count) if p % 2 == 1]
    evens = [p for p in range(count) if p % 2 == 0]
    chosen = (upper, lower, odds, evens)

    if rows % 128 != 0:
        products = []
        for left, right in pairs:
            flat = jnp.transpose(right, (1, 0, 2)).reshape(total, -1)
            products.append(matmul_tn(left, flat))
        product = jnp.concatenate(products, axis=1).reshape(dp, rows, columns)
        rel = jnp.array([distance(p) for p in range(count)], jnp.int32)
        product = product[jnp.bitwise_xor(rel, d)]
        token = jnp.zeros(TOKEN.shape, F32) + product[0, :1, :1]
        if got is None:
            return [product.astype(BF16), token]
        product = (product + jnp.concatenate(got, axis=2).astype(F32)).astype(BF16)
        half = columns // 2
        return [
            jnp.stack([product[p, :, side * half : (side + 1) * half] for p in ps])
            for side, ps in zip((0, 0, 1, 1), chosen)
        ] + [token]

    def body(d_ref, *refs):
        lefts = refs[: len(pairs)]
        rights = refs[len(pairs) : 2 * len(pairs)]
        got_refs = refs[2 * len(pairs) : 3 * len(pairs)]
        token_ref, turned_ref = refs[-2:]
        outs = refs[-3:-2] if got is None else refs[-6:-2]
        c = pl.program_id(0)

        @pl.when(c == 0)
        def _():
            token_ref[...] = jnp.zeros_like(token_ref)
            for i, left_ref in enumerate(lefts):
                for p in range(count):
                    at = pl.multiple_of(jnp.bitwise_xor(d_ref[0], distance(p)) * rows, 128)
                    turned_ref[i, pl.ds(p * rows, rows), :] = left_ref[:, pl.ds(at, rows)].T

        def piece(i, p):
            return jnp.dot(
                turned_ref[i, pl.ds(p * rows, rows), :], rights[i][0], preferred_element_type=F32
            )

        def write(i, half):
            for p in range(count):
                value = piece(i, p)
                if got is None:
                    outs[0][p] = value.astype(BF16)
                    continue
                value = (value + got_refs[i][p].astype(F32)).astype(BF16)
                for which in (2 * half, 2 * half + 1):
                    if p in chosen[which]:
                        outs[which][chosen[which].index(p)] = value

        for i in range(len(pairs)):
            for half in (0, 1):
                low = max(starts[i], half * (steps // 2))
                high = min(starts[i] + tiles[i], (half + 1) * (steps // 2))
                if low < high:
                    pl.when((c >= low) & (c < high))(lambda i=i, half=half: write(i, half))

    def right_spec(start, n, split):
        def at(c, d_ref):
            k = jnp.clip(c - start, 0, n - 1)
            return (lax.div(k, jnp.int32(split)), 0, lax.rem(k, jnp.int32(split)))

        return pl.BlockSpec((1, total, tile), at)

    in_specs = [pl.BlockSpec((total, all_rows), lambda c, d_ref: (0, 0))] * len(pairs)
    in_specs += [right_spec(*item) for item in zip(starts, tiles, splits)]
    args = [left for left, _ in pairs] + [right for _, right in pairs]
    if got is None:
        out_shape = [jax.ShapeDtypeStruct((count, rows, columns), BF16)]
        out_specs = [pl.BlockSpec((count, rows, tile), lambda c, d_ref: (0, 0, c))]
    else:
        for start, n in zip(starts, tiles):
            in_specs.append(
                pl.BlockSpec(
                    (count, rows, tile),
                    lambda c, d_ref, start=start, n=n: (0, 0, jnp.clip(c - start, 0, n - 1)),
                )
            )
        args += got
        out_shape = [jax.ShapeDtypeStruct((count // 2, rows, columns // 2), BF16)] * 4
        mid = steps // 2
        first = pl.BlockSpec(
            (count // 2, rows, tile), lambda c, d_ref: (0, 0, jnp.minimum(c, mid - 1))
        )
        second = pl.BlockSpec(
            (count // 2, rows, tile), lambda c, d_ref: (0, 0, jnp.maximum(c - mid, 0))
        )
        out_specs = [first, first, second, second]
    out_shape = out_shape + [TOKEN]
    out_specs = out_specs + [pl.BlockSpec(TOKEN.shape, lambda c, d_ref: (0, 0))]
    in_specs += [ANY] * len(deps)
    return pl.pallas_call(
        body,
        out_shape=out_shape,
        grid_spec=pltpu.PrefetchScalarGridSpec(
            num_scalar_prefetch=1,
            grid=(steps,),
            in_specs=in_specs,
            out_specs=out_specs,
            scratch_shapes=[pltpu.VMEM((len(pairs), count * rows, total), BF16)],
        ),
        compiler_params=pltpu.CompilerParams(vmem_limit_bytes=34 * 2**20),
        cost_estimate=pl.CostEstimate(flops=int(2.5 * 1.15e9), bytes_accessed=1024, transcendentals=0),
        name="gradient",
    )(d.reshape(1).astype(jnp.int32), *args, *deps)


def head_probs(q, k, far, slope):
    scores = lax.dot_general(q, k, (((1,), (1,)), ((), ())), preferred_element_type=F32)
    scores = scores * (HEAD ** (-0.5)) - slope * far
    raised = jnp.exp(scores - jnp.max(scores, axis=-1, keepdims=True))
    return raised * (1.0 / jnp.sum(raised, axis=-1, keepdims=True))


def flat_frames(block):
    sources, _, rows, lanes = block.shape
    if rows % 16 == 0:
        return block.reshape(sources * rows, lanes)
    return block.astype(F32).reshape(sources * rows, lanes).astype(BF16)


def by_source(value, like):
    sources, _, rows, lanes = like
    if rows % 16 == 0:
        return value.astype(BF16).reshape(sources, 1, rows, lanes)
    return value.reshape(sources, 1, rows, lanes).astype(BF16)


def attend(triple, far, slopes, deps=()):
    dp, micro, rows, wide = triple.shape
    frames = dp * rows
    width = wide // 3
    pairs = width // 128
    shape = (dp, 1, rows, 128)

    def body(slope_ref, q_ref, k_ref, v_ref, far_ref, *refs):
        out_ref = refs[-1]
        h = pl.program_id(1)
        q, k, v = (flat_frames(ref[...]) for ref in (q_ref, k_ref, v_ref))
        first = lax.broadcasted_iota(jnp.int32, (frames, 128), 1) < HEAD
        zero = jnp.zeros_like(q)
        outs = []
        for j, own in enumerate((jnp.where(first, q, zero), jnp.where(first, zero, q))):
            probs = head_probs(own, k, far_ref[0], slope_ref[h * 2 + j])
            outs.append(jnp.dot(probs.astype(BF16), v, preferred_element_type=F32))
        out_ref[...] = by_source(jnp.where(first, outs[0], outs[1]), shape)

    def spec(offset):
        return pl.BlockSpec(shape, lambda m, h, s: (0, m, 0, h + offset))

    return pl.pallas_call(
        body,
        out_shape=jax.ShapeDtypeStruct((dp, micro, rows, width), BF16),
        grid_spec=pltpu.PrefetchScalarGridSpec(
            num_scalar_prefetch=1,
            grid=(micro, pairs),
            in_specs=[
                spec(0),
                spec(pairs),
                spec(2 * pairs),
                pl.BlockSpec((1, frames, frames), lambda m, h, s: (m, 0, 0)),
            ]
            + [ANY] * len(deps),
            out_specs=spec(0),
        ),
        compiler_params=pltpu.CompilerParams(vmem_limit_bytes=24 * 2**20),
        cost_estimate=pl.CostEstimate(flops=int(8 * 1.15e9), bytes_accessed=1024, transcendentals=0),
        name="attend",
    )(slopes, triple, triple, triple, far, *deps)


def attend_back(triple, grad, far, slopes, deps=()):
    dp, micro, rows, wide = triple.shape
    frames = dp * rows
    width = wide // 3
    pairs = width // 128
    shape = (dp, 1, rows, 128)
    scale = HEAD ** (-0.5)

    def turned(left, right):
        return lax.dot_general(left, right, (((0,), (0,)), ((), ())), preferred_element_type=F32)

    def body(slope_ref, q_ref, k_ref, v_ref, g_ref, far_ref, *refs):
        out_ref, token_ref = refs[-2:]
        token_ref[...] = jnp.zeros_like(token_ref)
        h = pl.program_id(1)
        q, k, v, g = (flat_frames(ref[...]) for ref in (q_ref, k_ref, v_ref, g_ref))
        first = lax.broadcasted_iota(jnp.int32, (frames, 128), 1) < HEAD
        zero = jnp.zeros_like(q)
        grads = []
        for j in range(2):
            own_q = jnp.where(first, q, zero) if j == 0 else jnp.where(first, zero, q)
            own_g = jnp.where(first, g, zero) if j == 0 else jnp.where(first, zero, g)
            scores = nt(k, own_q) * scale - slope_ref[h * 2 + j] * far_ref[0]
            raised = jnp.exp(scores - jnp.max(scores, axis=0, keepdims=True))
            probs = raised * (1.0 / jnp.sum(raised, axis=0, keepdims=True))
            back = nt(v, own_g)
            back = probs * (back - jnp.sum(back * probs, axis=0, keepdims=True))
            low = back.astype(BF16)
            grads.append(
                (
                    turned(low, k) * scale,
                    jnp.dot(low, q, preferred_element_type=F32) * scale,
                    jnp.dot(probs.astype(BF16), g, preferred_element_type=F32),
                )
            )
        for i in range(3):
            out_ref[i] = by_source(jnp.where(first, grads[0][i], grads[1][i]), shape)

    def spec(offset):
        return pl.BlockSpec(shape, lambda m, h, s: (0, m, 0, h + offset))

    return pl.pallas_call(
        body,
        out_shape=[jax.ShapeDtypeStruct((3, dp, micro, rows, width), BF16), TOKEN],
        grid_spec=pltpu.PrefetchScalarGridSpec(
            num_scalar_prefetch=1,
            grid=(micro, pairs),
            in_specs=[
                spec(0),
                spec(pairs),
                spec(2 * pairs),
                spec(0),
                pl.BlockSpec((1, frames, frames), lambda m, h, s: (m, 0, 0)),
            ]
            + [ANY] * len(deps),
            out_specs=[
                pl.BlockSpec((3,) + shape, lambda m, h, s: (0, 0, m, 0, h)),
                pl.BlockSpec(TOKEN.shape, lambda m, h, s: (0, 0)),
            ],
        ),
        compiler_params=pltpu.CompilerParams(vmem_limit_bytes=24 * 2**20),
        cost_estimate=pl.CostEstimate(flops=int(2 * 1.15e9), bytes_accessed=1024, transcendentals=0),
        name="attend_back",
    )(slopes, triple, triple, triple, grad, far, *deps)


def add_up(values):
    total = values[0].astype(F32)
    for value in values[1:]:
        total = total + value.astype(F32)
    return total.astype(BF16)


class Reduction:
    def __init__(self, pairs, d, dims, deps=()):
        self.pairs = [(left, right if right.ndim == 3 else right[None]) for left, right in pairs]
        self.d = d
        self.dims = dims
        self.sent, self.token = gradient_blocks(self.pairs, d, dims, deps=deps)

    def share(self):
        return flip(self.sent, 1)

    def own(self, got, deps=(), others=()):
        pairs = self.pairs + [pair for other, _ in others for pair in other.pairs]
        gots = [got] + [arrived for _, arrived in others]
        *self.parts, self.token = gradient_blocks(pairs, self.d, self.dims, gots, deps)

    def near(self):
        parts = self.parts
        return [flip(parts[0], 1 << self.dims[0]), flip(parts[2], 1 << self.dims[-1])]

    def near_landed(self, got):
        self.halves = []
        for side, order in ((0, self.dims), (1, self.dims[::-1])):
            stay = self.parts[2 * side + 1]
            left = [bit for bit in self.dims if bit != order[0]]
            shape = (2,) * len(left) + stay.shape[1:]
            values = [stay.reshape(shape), got[side].reshape(shape)]
            self.halves.append((values, list(order[1:]), left))

    def step(self):
        sends, self.stays = [], []
        for values, order, left in self.halves:
            at = left.index(order[0])
            sends.append(add_up([lax.index_in_dim(v, 1, at, keepdims=False) for v in values]))
            self.stays.append([lax.index_in_dim(v, 0, at, keepdims=False) for v in values])
        bits = [order[0] for _, order, _ in self.halves]
        return [flip(sends[0], 1 << bits[0]), flip(sends[1], 1 << bits[1])]

    def landed(self, got):
        halves = []
        for i, (_, order, left) in enumerate(self.halves):
            halves.append((self.stays[i] + [got[i]], order[1:], [b for b in left if b != order[0]]))
        self.halves = halves

    def cross(self):
        while len(self.halves[0][1]) > 1:
            self.landed(self.step())
        return self.step()

    def rows(self):
        self.value = jnp.concatenate([add_up(values) for values, _, _ in self.halves], axis=1)
        self.stage = 0
        return self.value

    def along(self):
        rep = lax.axis_size("rep")
        half = rep // 2
        k = self.stage
        if k < half - 1:
            pairs = [(k, k + 1), (rep - 1 - k, rep - 2 - k)]
        elif k == half - 1:
            pairs = [(k, k + 1), (k + 1, k)]
        else:
            i = rep - 2 - k
            pairs = [(i + 1, i), (rep - 2 - i, rep - 1 - i)]
        return lax.ppermute(self.value, "rep", pairs)

    def along_landed(self, got):
        rep = lax.axis_size("rep")
        z = lax.axis_index("rep")
        k = self.stage
        self.stage += 1
        if k < rep // 2:
            self.value = add_up([self.value, got])
        else:
            i = rep - 2 - k
            self.value = jnp.where((z == i) | (z == rep - 1 - i), got, self.value)

    def finish(self):
        while self.stage < lax.axis_size("rep") - 1:
            self.along_landed(self.along())
        return self.value.astype(F32)

    def halve(self, extra=None):
        rep = lax.axis_size("rep")
        z = lax.axis_index("rep")
        value = self.value
        if extra is not None:
            value = jnp.concatenate([value, extra], axis=0)
        bits = range(rep.bit_length() - 1)
        for bit in bits:
            mine = lax.bitwise_and(lax.shift_right_logical(z, bit), 1)
            size = value.shape[0] // 2
            send = lax.dynamic_slice_in_dim(value, (1 - mine) * size, size, 0)
            keep = lax.dynamic_slice_in_dim(value, mine * size, size, 0)
            value = add_up([keep, rep_flip(send, 1 << bit)])
        for bit in reversed(bits):
            mine = lax.bitwise_and(lax.shift_right_logical(z, bit), 1)
            got = rep_flip(value, 1 << bit)
            lower = jnp.where(mine == 0, value, got)
            upper = jnp.where(mine == 0, got, value)
            value = jnp.concatenate([lower, upper], axis=0)
        return value.astype(F32)


def nt(left, right):
    return lax.dot_general(left, right, (((1,), (1,)), ((), ())), preferred_element_type=F32)


def hidden_gradient(grad_result, w_down, slope, deps=()):
    total, width = grad_result.shape
    units = w_down.shape[0]
    tile = 512

    def body(grad_ref, w_ref, slope_ref, *refs):
        out_ref, sum_ref = refs[-2:]
        value = nt(grad_ref[...], w_ref[...]) * slope_ref[...].astype(F32)
        out_ref[...] = value.astype(BF16)
        sum_ref[...] = jnp.sum(value, axis=0, keepdims=True)

    return pl.pallas_call(
        body,
        out_shape=[
            jax.ShapeDtypeStruct((total, units), BF16),
            jax.ShapeDtypeStruct((1, units), F32),
        ],
        grid=(units // tile,),
        in_specs=[
            pl.BlockSpec((total, width), lambda c: (0, 0)),
            pl.BlockSpec((tile, width), lambda c: (c, 0)),
            pl.BlockSpec((total, tile), lambda c: (0, c)),
        ]
        + [ANY] * len(deps),
        out_specs=[
            pl.BlockSpec((total, tile), lambda c: (0, c)),
            pl.BlockSpec((1, tile), lambda c: (0, c)),
        ],
        compiler_params=pltpu.CompilerParams(vmem_limit_bytes=24 * 2**20),
        cost_estimate=pl.CostEstimate(flops=int(3 * 1.15e9), bytes_accessed=1024, transcendentals=0),
        name="hidden_gradient",
    )(grad_result, w_down, slope, *deps)


def mixed_gradient(hidden_low, w_up, w_out, mixed, grad_result, gain, deps=()):
    total, units = hidden_low.shape
    width = w_up.shape[0]
    tile = 256

    def body(low_ref, up_ref, out_w_ref, mixed_ref, result_ref, gain_ref, *outs):
        grad_ref, rounded_ref, attended_ref, sums_ref = outs[-4:]
        grad = nt(low_ref[...], up_ref[...])
        unit, scale = norm_parts(mixed_ref[...])
        result = result_ref[...].astype(F32)
        value = result + norm_back(grad, gain_ref[...], unit, scale)
        rounded = value.astype(BF16)
        grad_ref[...] = value
        rounded_ref[...] = rounded
        attended_ref[...] = nt(rounded, out_w_ref[...]).astype(BF16)

        @pl.when(pl.program_id(0) == 0)
        def _():
            sums_ref[...] = jnp.zeros_like(sums_ref)

        for i, terms in enumerate((value, grad * unit, grad, result)):
            sums_ref[pl.ds(i, 1), :] += jnp.sum(terms, axis=0, keepdims=True)

    rows = pl.BlockSpec((tile, width), lambda r: (r, 0))
    whole = [
        pl.BlockSpec((width, units), lambda r: (0, 0)),
        pl.BlockSpec((width, width), lambda r: (0, 0)),
    ]
    return pl.pallas_call(
        body,
        out_shape=[
            jax.ShapeDtypeStruct((total, width), F32),
            jax.ShapeDtypeStruct((total, width), BF16),
            jax.ShapeDtypeStruct((total, width), BF16),
            jax.ShapeDtypeStruct((8, width), F32),
        ],
        grid=(total // tile,),
        in_specs=[pl.BlockSpec((tile, units), lambda r: (r, 0))]
        + whole
        + [rows, rows, pl.BlockSpec((1, width), lambda r: (0, 0))]
        + [ANY] * len(deps),
        out_specs=[rows, rows, rows, pl.BlockSpec((8, width), lambda r: (0, 0))],
        compiler_params=pltpu.CompilerParams(vmem_limit_bytes=44 * 2**20),
        cost_estimate=pl.CostEstimate(flops=int(2 * 1.15e9), bytes_accessed=1024, transcendentals=0),
        name="mixed_gradient",
    )(hidden_low, w_up, w_out, mixed, grad_result, gain.reshape(1, width), *deps)


def normed_gradient(grad_triple, w_qkv, deps=()):
    three, total, width = grad_triple.shape
    tile = 256

    def body(grad_ref, w_ref, *refs):
        out_ref = refs[-1]
        value = nt(grad_ref[0], w_ref[:, pl.ds(0, width)])
        for i in range(1, three):
            value += nt(grad_ref[i], w_ref[:, pl.ds(i * width, width)])
        out_ref[...] = value.astype(BF16)

    return pl.pallas_call(
        body,
        out_shape=jax.ShapeDtypeStruct((total, width), BF16),
        grid=(total // tile,),
        in_specs=[
            pl.BlockSpec((three, tile, width), lambda r: (0, r, 0)),
            pl.BlockSpec((width, three * width), lambda r: (0, 0)),
        ]
        + [ANY] * len(deps),
        out_specs=pl.BlockSpec((tile, width), lambda r: (r, 0)),
        compiler_params=pltpu.CompilerParams(vmem_limit_bytes=24 * 2**20),
        cost_estimate=pl.CostEstimate(flops=int(2 * 1.15e9), bytes_accessed=1024, transcendentals=0),
        name="normed_gradient",
    )(grad_triple, w_qkv, *deps)


def matmul(left, right):
    return jnp.dot(left, right, preferred_element_type=F32)


def matmul_nt(left, right):
    return lax.dot_general(left, right, (((1,), (1,)), ((), ())), preferred_element_type=F32)


def matmul_tn(left, right):
    return lax.dot_general(left, right, (((0,), (0,)), ((), ())), preferred_element_type=F32)


def norm_parts(values):
    average = jnp.mean(values, axis=-1, keepdims=True)
    centred = values - average
    spread = jnp.mean(centred * centred, axis=-1, keepdims=True)
    scale = lax.rsqrt(spread + EPS)
    return centred * scale, scale


def norm_back(grad, gain, unit, scale):
    e = grad * gain
    return scale * (
        e
        - jnp.mean(e, axis=-1, keepdims=True)
        - unit * jnp.mean(e * unit, axis=-1, keepdims=True)
    )


def shards(
    inputs,
    skips,
    cotangent,
    dest_slot,
    pack_segments,
    block_live,
    counts,
    w_skip,
    b_skip,
    g_one,
    b_one,
    w_qkv,
    w_out,
    b_out,
    g_two,
    b_two,
    w_up,
    c_up,
    w_down,
    c_down,
):
    dp = lax.axis_size("dp")
    rep = lax.axis_size("rep")
    d = lax.axis_index("dp")
    z = lax.axis_index("rep")
    micro = inputs.shape[0]
    frames = inputs.shape[2]
    width = inputs.shape[3]
    blocks = dest_slot.shape[2]
    block = frames // blocks
    per_pair = blocks // dp
    total = micro * frames
    bits = dp.bit_length() - 1
    place = jnp.stack([z, lax.rem(d, 8)]).astype(jnp.int32)
    dims = list(range(1, bits))
    small = jnp.concatenate([dest_slot.reshape(-1), block_live.reshape(-1), counts.reshape(-1)])

    own_skip = own_chunk(place, width, [w_skip])
    z_skip = Fetch(own_skip)
    z_skip.rest()
    got = z_skip.send()
    every = small[None]
    for bit in range(bits):
        every = jnp.concatenate([every, flip(every, 1 << bit)], axis=0)
    z_mid = Fetch(own_chunk(place, width, [w_qkv, w_out], z_skip.held[1:]))
    z_mid.rest()
    z_skip.landed(got)

    run_skip = Spread(z_skip.far(), width, [every, z_mid.held[-1]])
    mid = z_mid.send()
    run_skip.near_landed(run_skip.near())

    span = micro * blocks
    numbers = every[:, : 2 * span].reshape(dp, 2 * micro, blocks)
    numbers = jnp.transpose(numbers, (1, 0, 2)).reshape(2 * micro, dp * blocks).astype(F32)
    count_total = jnp.sum(every[:, 2 * span]).astype(F32).reshape(1, 1)
    inner = jnp.arange(frames) % block
    live = inner[None] < jnp.repeat(block_live[:, 0, :], block, axis=1)
    codes = (2 * pack_segments[:, 0, :] + live).astype(F32)
    joined = jnp.concatenate([inputs.reshape(total, width), skips.reshape(total, width)], axis=1)
    far, far_turned, keep_wide, shuffle = plan_order(
        numbers[:micro], numbers[micro:], codes, d, block, [run_skip.pairs[0], joined]
    )
    keep_rows = keep_wide[:, :1]

    run_skip.cross_landed(run_skip.cross(), [shuffle, mid])

    z_mid.landed(mid)
    run_mid = Spread(z_mid.far(), width)
    full_skip, _ = assemble(
        w_skip, run_skip.parts(run_skip.share()), place, 0, 1, [run_mid.start[0]]
    )
    z_up = Fetch(own_chunk(place, width, [w_up], [run_mid.start[0]]))
    z_up.rest()
    base = matmul(joined, full_skip) + b_skip
    unit_one, scale_one = norm_parts(base)
    own_normed = (unit_one * g_one + b_one).astype(BF16)
    sent = matmul(shuffle, own_normed).astype(BF16)
    run_mid.near_landed(run_mid.near(), [sent, z_up.held[-1]])

    def exchange(values):
        values = values.reshape(dp, total // dp, width)
        got = lax.all_to_all(values, "dp", split_axis=0, concat_axis=0, tiled=True)
        return got.reshape(total, width)

    normed = exchange(sent)
    up = z_up.send([sent])
    z_down = Fetch(own_chunk(place, width, [w_down], [z_up.held[-1], sent]))
    z_down.rest()
    run_mid.cross_landed(run_mid.cross(), [up, z_down.held[-1], normed])
    z_up.landed(up)

    other = run_mid.share()
    run_up = Spread(z_up.far(), width, [run_mid.every])
    run_up.near_landed(run_up.near(), [other])
    shard_rows = w_qkv.shape[0] // 8
    parts_mid = run_mid.parts(other)
    full_qkv, _ = assemble(w_qkv, parts_mid, place, 0, 3)

    triple = matmul(normed, full_qkv).astype(BF16)
    triple = triple.reshape(dp, micro, per_pair * block, 3 * width)
    slopes = 2.0 ** (-8.0 * (jnp.arange(HEADS, dtype=F32) + 1.0) / HEADS)
    attended = attend(triple, far, slopes, [run_up.pairs[0]])
    down = z_down.send()
    run_up.cross_landed(run_up.cross(), [attended, down])
    z_down.landed(down)

    attended = exchange(attended)
    other = run_up.share()
    run_down = Spread(z_down.far(), width, [run_up.every])
    down = run_down.near()
    full_out, out_token = assemble(w_out, parts_mid, place, 3 * shard_rows, 1, [run_up.every])
    full_up, up_token = assemble(w_up, run_up.parts(other), place, 0, w_up.shape[1] // width)
    attended, out_token, up_token = together(attended, out_token, up_token)

    attended = matmul_tn(shuffle, attended).astype(BF16)
    mixed = base + matmul(attended, full_out) + (b_out + out_token[0, 0])
    unit_two, scale_two = norm_parts(mixed)
    normed_two = (unit_two * g_two + b_two).astype(BF16)
    count_total = count_total + up_token[:1, :1]
    for step in rep_steps(rep):
        count_total = count_total + rep_flip(count_total, step)
    share = counts[0, 0].astype(F32) * (dp * rep) / count_total[0, 0]
    run_down.near_landed(down, [up_token])
    down = run_down.cross()
    hidden = matmul(normed_two, full_up) + (c_up + run_down.token[0, 0])
    phi = 0.5 * (1.0 + lax.erf(hidden * (0.5**0.5)))
    active = (hidden * phi).astype(BF16)
    slope = (phi + hidden * jnp.exp(-0.5 * hidden * hidden) * ((2 * jnp.pi) ** -0.5)).astype(BF16)
    scaled = (cotangent.reshape(total, width).astype(F32) * share).astype(BF16)
    grad_result = scaled * keep_rows.astype(BF16)
    red_down = Reduction([(active, grad_result)], d, dims)

    down_got = red_down.share()
    run_down.cross_landed(down, [red_down.sent])
    full_down, _ = assemble(w_down, run_down.parts(run_down.share()), place, 0, 1)

    hidden_low, sum_hidden = hidden_gradient(grad_result, full_down, slope)
    red_up = Reduction([(normed_two, hidden_low)], d, dims)
    up_got = red_up.share()
    red_down.own(down_got, [red_up.sent])
    flying = red_down.near()
    grad_mixed, mixed_low, grad_attended, sums_mixed = mixed_gradient(
        hidden_low, full_up, full_out, mixed, grad_result, g_two, [red_down.token]
    )
    red_out = Reduction([(attended, mixed_low)], d, dims)
    out_got = red_out.share()
    flying, sums_mixed = together(flying, sums_mixed)
    red_down.near_landed(flying)

    down_flying = red_down.cross()
    sent = matmul(shuffle, grad_attended).astype(BF16)
    grad_attended = exchange(sent)
    red_up.own(up_got, [sent], [(red_out, out_got)])
    flying = red_up.near()
    result = mixed + matmul(active, full_down) + (c_down + red_up.token[0, 0])
    output = (result * keep_rows).astype(BF16)
    down_flying, token = together(down_flying, red_up.token)
    red_down.landed(down_flying)
    red_down.rows()

    line = red_down.along()
    grad_attended = grad_attended.reshape(dp, micro, per_pair * block, width)
    grad_triple, token = attend_back(
        triple, grad_attended, far_turned, slopes, [red_down.value, token, output]
    )
    grad_triple = grad_triple.reshape(3, total, width)
    flying, line, token = together(flying, line, token)
    red_up.near_landed(flying)
    red_down.along_landed(line)

    up_flying = red_up.cross()
    line = red_down.along()
    sent = normed_gradient(grad_triple, full_qkv, [token])
    grad_normed = exchange(sent)
    red_mid = Reduction([(normed, grad_triple)], d, dims, [sent])
    grad_normed, line, token = together(grad_normed, line, red_mid.token)
    red_down.along_landed(line)

    mid_got = red_mid.share()
    line = red_down.along()
    grad_normed = matmul_tn(shuffle, grad_normed)
    grad_base = grad_mixed + norm_back(grad_normed, g_one, unit_one, scale_one)
    base_low = grad_base.astype(BF16)
    red_skip = Reduction([(joined, base_low)], d, dims, [token])
    skip_got = red_skip.share()
    vectors = (
        jnp.sum(grad_base, axis=0),
        jnp.sum(grad_normed * unit_one, axis=0),
        jnp.sum(grad_normed, axis=0),
        sums_mixed[0],
        sums_mixed[1],
        sums_mixed[2],
        sum_hidden[0],
        sums_mixed[3],
    )
    lengths = [v.shape[0] for v in vectors]
    summed = jnp.concatenate(vectors).reshape(-1, 128)
    for bit in range(bits - 1):
        summed = summed + flip(summed, 1 << bit)
    up_flying, token = together(up_flying, red_skip.token)
    red_up.landed(up_flying)
    red_up.rows()
    up_line = red_up.along()
    red_mid.own(mid_got, [token])
    summed, token = together(summed, red_mid.token)

    flying = red_mid.near()
    red_skip.own(skip_got, [token])
    skip_flying = red_skip.near()
    grad_joined = matmul_nt(base_low, full_skip).astype(BF16)
    flying, up_line, line, grad_joined, summed = together(
        flying, up_line, line, grad_joined, summed
    )
    red_mid.near_landed(flying)
    red_up.along_landed(up_line)
    red_down.along_landed(line)

    flying = red_mid.cross()
    up_line = red_up.along()
    flying, up_line, skip_flying, summed = together(flying, up_line, skip_flying, summed)
    red_skip.near_landed(skip_flying)
    skip_flying = red_skip.cross()
    red_mid.landed(flying)
    red_mid.rows()
    red_up.along_landed(up_line)
    up_line = red_up.along()
    summed = summed + flip(summed, 1 << (bits - 1))
    skip_columns = w_skip.shape[1]
    extra = jnp.pad(summed.reshape(-1), (0, -summed.size % (16 * rep * skip_columns)))
    extra = extra.reshape(-1, skip_columns).astype(BF16)
    skip_flying, extra = together(skip_flying, extra)
    red_skip.landed(skip_flying)
    red_skip.rows()
    final_mid = red_mid.halve()
    final_skip = red_skip.halve(extra)
    red_up.along_landed(up_line)
    own_rows = w_skip.shape[0] * rep // dp
    summed = final_skip[own_rows:].reshape(-1)
    final_up = red_up.finish()
    units = c_up.shape[0]
    finals = [
        red_down.finish(),
        final_up[:, :units],
        final_up[:, units:],
        final_mid,
        final_skip[:own_rows],
    ]
    sums = []
    offset = 0
    for length in lengths:
        sums.append(summed[offset : offset + length])
        offset += length

    def as_owned(values):
        return values.reshape(inputs.shape)

    return (
        as_owned(output),
        as_owned(grad_joined[:, :width]),
        as_owned(grad_joined[:, width:]),
        finals[4],
        sums[0],
        sums[1],
        sums[2],
        finals[3],
        finals[2],
        sums[3],
        sums[4],
        sums[5],
        finals[1],
        sums[6],
        finals[0],
        sums[7],
    )


def solution(mesh):
    frames = P(None, "rep", "dp", None)
    slots = P(None, "rep", "dp")
    rows = P("rep", None)
    whole = P()
    in_specs = (
        (frames,) * 3
        + (slots,) * 3
        + (P("dp", "rep"), rows, whole, whole, whole, rows, rows)
        + (whole,) * 3
        + (rows, whole, rows, whole)
    )
    split = P("dp", None)
    out_specs = (
        (frames,) * 3
        + (split,)
        + (whole,) * 3
        + (split, split)
        + (whole,) * 3
        + (split, whole, split, whole)
    )
    return jax.shard_map(shards, mesh=mesh, in_specs=in_specs, out_specs=out_specs, check_vma=False)
```

```python
import jax
import jax.numpy as jnp
from jax import lax
from jax.experimental import pallas as pl
from jax.experimental.pallas import tpu as pltpu
from jax.sharding import PartitionSpec as P

HEADS = 16
HEAD = 64
EPS = 1e-05
F32 = jnp.float32
BF16 = jnp.bfloat16
TOKEN = jax.ShapeDtypeStruct((8, 128), F32)
ANY = pl.BlockSpec(memory_space=pl.ANY)
LIGHT = pl.CostEstimate(flops=1024, bytes_accessed=1024, transcendentals=0)


def flip(value, bit):
    n = lax.axis_size("dp")
    return lax.ppermute(value, "dp", [(i, i ^ bit) for i in range(n)])


def rep_flip(value, bit):
    n = lax.axis_size("rep")
    return lax.ppermute(value, "rep", [(i, i ^ bit) for i in range(n)])


def after(value, *earlier):
    return lax.optimization_barrier((value,) + earlier)[0]


def together(*values):
    return lax.optimization_barrier(values)


def assemble(w_local, parts, place, row_at, tiles, deps=()):
    rep = lax.axis_size("rep")
    shard_rows, columns = w_local.shape
    rows = shard_rows // 8
    tile = columns // tiles
    half = tile // 2
    chunk_rows = parts[0][0].shape[0] // (len(parts[0][1]) * (rep - 1))
    arrays = [part[0] for part in parts]
    count = 1 + sum(len(part[1]) for part in parts) * (rep - 1) * tiles

    def body(place_ref, local_ref, *refs):
        out_ref, token_ref, sems = refs[-3:]
        token_ref[...] = jnp.zeros_like(token_ref)
        z = place_ref[0]
        e = place_ref[1]
        copies = [
            pltpu.make_async_copy(
                local_ref,
                out_ref.at[pl.ds(pl.multiple_of(z * shard_rows, 16), shard_rows), :],
                sems.at[0],
            )
        ]
        for ref, (_, runs) in zip(refs, parts):
            for k, (side, rel) in enumerate(runs):
                chunk = jnp.bitwise_xor(e, rel)
                for s, apart in enumerate(far_order(rep), 1):
                    shard = jnp.bitwise_xor(z, apart)
                    start = pl.multiple_of(shard * shard_rows + chunk * rows, 16)
                    for t in range(tiles):
                        at = (k * (rep - 1) + s - 1) * chunk_rows + row_at + t * rows
                        copies.append(
                            pltpu.make_async_copy(
                                ref.at[pl.ds(at, rows), :],
                                out_ref.at[pl.ds(start, rows), pl.ds(t * tile + side * half, half)],
                                sems.at[len(copies)],
                            )
                        )
        for copy in copies:
            copy.start()
        for copy in copies:
            copy.wait()

    return pl.pallas_call(
        body,
        out_shape=[jax.ShapeDtypeStruct((shard_rows * rep, columns), w_local.dtype), TOKEN],
        grid=(1,),
        in_specs=[pl.BlockSpec(memory_space=pltpu.SMEM)] + [ANY] * (1 + len(parts) + len(deps)),
        out_specs=[
            pl.BlockSpec((shard_rows * rep, columns), lambda i: (0, 0)),
            pl.BlockSpec(TOKEN.shape, lambda i: (0, 0)),
        ],
        scratch_shapes=[pltpu.SemaphoreType.DMA((count,))],
        compiler_params=pltpu.CompilerParams(vmem_limit_bytes=26 * 2**20),
        cost_estimate=pl.CostEstimate(flops=int(1.5 * 1.15e9), bytes_accessed=1024, transcendentals=0),
        name="assemble",
    )(place, w_local, *arrays, *deps)


def own_chunk(place, width, shards_local, deps=()):
    items = []
    for which, w_local in enumerate(shards_local):
        for t in range(w_local.shape[1] // width):
            items.append((which, w_local.shape[0] // 8, t * width))
    total = sum(item[1] for item in items)

    def body(place_ref, *refs):
        out_ref, sems = refs[-2:]
        copies = []
        at = 0
        for which, rows, column in items:
            start = pl.multiple_of(place_ref[1] * rows, 16)
            copies.append(
                pltpu.make_async_copy(
                    refs[which].at[pl.ds(start, rows), pl.ds(column, width)],
                    out_ref.at[pl.ds(at, rows), :],
                    sems.at[len(copies)],
                )
            )
            at += rows
        for copy in copies:
            copy.start()
        for copy in copies:
            copy.wait()

    return pl.pallas_call(
        body,
        out_shape=jax.ShapeDtypeStruct((total, width), shards_local[0].dtype),
        grid=(1,),
        in_specs=[pl.BlockSpec(memory_space=pltpu.SMEM)]
        + [ANY] * (len(shards_local) + len(deps)),
        out_specs=pl.BlockSpec((total, width), lambda i: (0, 0)),
        scratch_shapes=[pltpu.SemaphoreType.DMA((len(items),))],
        compiler_params=pltpu.CompilerParams(vmem_limit_bytes=24 * 2**20),
        cost_estimate=LIGHT,
        name="own_chunk",
    )(place, *shards_local, *deps)


def pack(arrays, outs, deps=()):
    count = sum(len(out) for out in outs)

    def body(*refs):
        sources, targets = refs[: len(arrays)], refs[-2 - len(outs) : -2]
        token_ref, sems = refs[-2:]
        token_ref[...] = jnp.zeros_like(token_ref)
        copies = []
        for target, out in zip(targets, outs):
            at = 0
            for which, row, rows, column, columns in out:
                copies.append(
                    pltpu.make_async_copy(
                        sources[which].at[pl.ds(row, rows), pl.ds(column, columns)],
                        target.at[pl.ds(at, rows), :],
                        sems.at[len(copies)],
                    )
                )
                at += rows
        for copy in copies:
            copy.start()
        for copy in copies:
            copy.wait()

    return pl.pallas_call(
        body,
        out_shape=[
            jax.ShapeDtypeStruct((sum(item[2] for item in out), out[0][4]), arrays[0].dtype)
            for out in outs
        ]
        + [TOKEN],
        grid=(1,),
        in_specs=[ANY] * (len(arrays) + len(deps)),
        out_specs=[
            pl.BlockSpec((sum(item[2] for item in out), out[0][4]), lambda i: (0, 0))
            for out in outs
        ]
        + [pl.BlockSpec(TOKEN.shape, lambda i: (0, 0))],
        scratch_shapes=[pltpu.SemaphoreType.DMA((count,))],
        compiler_params=pltpu.CompilerParams(vmem_limit_bytes=24 * 2**20),
        cost_estimate=LIGHT,
        name="pack",
    )(*arrays, *deps)


def far_order(rep):
    order = [0]
    for bit in reversed(range(rep.bit_length() - 1)):
        order = order + [distance ^ (1 << bit) for distance in order]
    return order[1:]


class Spread:
    def __init__(self, gots, width, deps=()):
        self.half = width // 2
        rows = sum(got.shape[0] for got in gots)
        items = [(i, 0, got.shape[0]) for i, got in enumerate(gots)]
        *self.start, _ = pack(
            gots, [[item + (column, self.half) for item in items] for column in (0, self.half)], deps
        )
        self.n = rows

    def near(self):
        return [flip(self.start[0], 2), flip(self.start[1], 4)]

    def near_landed(self, got, deps=()):
        whole = [(i, 0, self.n, 0, self.half) for i in range(4)]
        *self.pairs, self.token = pack(
            [self.start[0], got[0], self.start[1], got[1]], [whole[:2], whole[2:]], deps
        )

    def cross(self):
        return [flip(self.pairs[0], 4), flip(self.pairs[1], 2)]

    def cross_landed(self, got, deps=()):
        whole = [(i, 0, 2 * self.n, 0, self.half) for i in range(4)]
        self.every, self.token = pack([self.pairs[0], got[0], self.pairs[1], got[1]], [whole], deps)

    def share(self):
        return flip(self.every, 1)

    def parts(self, other):
        runs = [(0, 0), (0, 2), (0, 4), (0, 6), (1, 0), (1, 4), (1, 2), (1, 6)]
        return [(self.every, runs), (other, [(side, rel | 1) for side, rel in runs])]


def rep_steps(rep):
    return [1 << bit for bit in reversed(range(rep.bit_length() - 1))]


class Fetch:
    def __init__(self, own):
        self.held = [own]
        self.steps = rep_steps(lax.axis_size("rep"))

    def send(self, deps=()):
        sent = self.held[0]
        if len(self.held) > 1:
            whole = [(i, 0, a.shape[0], 0, a.shape[1]) for i, a in enumerate(self.held)]
            sent, _ = pack(self.held, [whole], deps)
        return rep_flip(sent, self.steps[len(self.held) - 1])

    def landed(self, got):
        self.held.append(got)

    def rest(self):
        while len(self.held) < len(self.steps):
            self.landed(self.send())

    def far(self):
        return self.held[1:]


def plan_order(all_slots, all_live, codes, d, block, deps=()):
    micro, owners = all_slots.shape
    frames = codes.shape[1]
    blocks = frames // block
    dp = owners // blocks
    per_pair = blocks // dp
    total = micro * frames

    def column(row):
        return jnp.broadcast_to(row, (128, row.shape[1])).T[:, :1]

    def as_row(values):
        return jnp.broadcast_to(values, (values.shape[0], 128)).T[:1, :]

    def body(d_ref, slots_ref, live_ref, codes_ref, *refs):
        far_ref, turned_ref, keep_ref, shuffle_ref = refs[-4:]
        me = d_ref[0]
        lane = lax.broadcasted_iota(jnp.int32, (1, owners), 1)
        source = jnp.bitwise_xor(lax.div(lane, jnp.int32(blocks)), me)
        first_slot = (source * blocks).astype(F32) + lax.rem(lane, jnp.int32(blocks)).astype(F32)
        source_col = column(source.astype(F32))
        frame = lax.broadcasted_iota(jnp.int32, (frames, 1), 0)
        block_of = lax.div(frame, jnp.int32(block)).astype(F32)
        inner = lax.rem(frame, jnp.int32(block)).astype(F32)
        low = (me * blocks).astype(F32)
        rows = []
        for m in range(micro):
            slots = slots_ref[pl.ds(m, 1), :]
            slots_col = column(slots)
            same = source_col == source.astype(F32)
            rank = jnp.sum(jnp.where(same & (slots_col < slots), 1.0, 0.0), axis=0, keepdims=True)
            here = (slots >= low) & (slots < low + blocks)
            arrive = source.astype(F32) * per_pair + rank - (me * per_pair).astype(F32)
            arrive = jnp.where(here, arrive, -1.0)
            placed = jnp.sum(
                jnp.where(arrive == block_of, slots - low, 0.0), axis=1, keepdims=True
            )
            position = placed * block + inner
            at = lax.broadcasted_iota(jnp.int32, (1, frames), 1).astype(F32)
            code = jnp.sum(
                jnp.where(at == position, codes_ref[pl.ds(m, 1), :], 0.0), axis=1, keepdims=True
            )
            position_row, code_row = as_row(position), as_row(code)
            segment, segment_row = jnp.floor(code * 0.5), jnp.floor(code_row * 0.5)
            live_row = code_row - 2.0 * segment_row
            distance = jnp.abs(position - position_row)
            allowed = (segment == segment_row) & ((live_row > 0.5) | (distance < 0.5))
            far_ref[m] = jnp.where(allowed, distance, 1e32)
            live_col = code - 2.0 * segment
            allowed = (segment == segment_row) & ((live_col > 0.5) | (distance < 0.5))
            turned_ref[m] = jnp.where(allowed, distance, 1e32)
            own = lane < blocks
            mine = jnp.sum(
                jnp.where(own & (lane.astype(F32) == block_of), slots, 0.0), axis=1, keepdims=True
            )
            alive = jnp.sum(
                jnp.where(first_slot == mine, live_ref[pl.ds(m, 1), :], 0.0), axis=1, keepdims=True
            )
            keep_ref[pl.ds(m * frames, frames), :] = jnp.broadcast_to(
                jnp.where(inner < alive, 1.0, 0.0), (frames, 128)
            )
            my_rank = jnp.sum(
                jnp.where(own & (lane.astype(F32) == block_of), rank, 0.0), axis=1, keepdims=True
            )
            target = jnp.floor((my_rank + 0.5) / per_pair)
            row = (target * micro + m) * per_pair + (my_rank - target * per_pair)
            rows.append(as_row(row * block + inner))
        goal = jnp.concatenate(rows, axis=1)
        spot = lax.broadcasted_iota(jnp.int32, (total, total), 0).astype(F32)
        shuffle_ref[...] = jnp.where(spot == goal, 1.0, 0.0).astype(BF16)

    vmem = pl.BlockSpec(memory_space=pltpu.VMEM)
    return pl.pallas_call(
        body,
        out_shape=[
            jax.ShapeDtypeStruct((micro, frames, frames), F32),
            jax.ShapeDtypeStruct((micro, frames, frames), F32),
            jax.ShapeDtypeStruct((total, 128), F32),
            jax.ShapeDtypeStruct((total, total), BF16),
        ],
        in_specs=[pl.BlockSpec(memory_space=pltpu.SMEM), vmem, vmem, vmem] + [ANY] * len(deps),
        out_specs=[vmem, vmem, vmem, vmem],
        compiler_params=pltpu.CompilerParams(vmem_limit_bytes=24 * 2**20),
        cost_estimate=LIGHT,
        name="plan_order",
    )(d.reshape(1).astype(jnp.int32), all_slots, all_live, codes, *deps)


def gradient_blocks(pairs, d, dims, got=None, deps=()):
    dp = lax.axis_size("dp")
    total, all_rows = pairs[0][0].shape
    widths = [right.shape[2] for _, right in pairs]
    columns = sum(right.shape[0] * right.shape[2] for _, right in pairs)
    rows = all_rows // dp
    count = dp // 2
    odd = 1 if got is None else 0
    tile = min(min(widths), 512)
    splits = [width // tile for width in widths]
    tiles = [right.shape[0] * split for (_, right), split in zip(pairs, splits)]
    steps = sum(tiles)
    starts = [sum(tiles[:i]) for i in range(len(tiles))]

    def distance(p):
        rel = odd
        for k, bit in enumerate(dims):
            rel += ((p >> (len(dims) - 1 - k)) & 1) << bit
        return rel

    upper = [p for p in range(count) if p >= count // 2]
    lower = [p for p in range(count) if p < count // 2]
    odds = [p for p in range(count) if p % 2 == 1]
    evens = [p for p in range(count) if p % 2 == 0]
    chosen = (upper, lower, odds, evens)

    if rows % 128 != 0:
        products = []
        for left, right in pairs:
            flat = jnp.transpose(right, (1, 0, 2)).reshape(total, -1)
            products.append(matmul_tn(left, flat))
        product = jnp.concatenate(products, axis=1).reshape(dp, rows, columns)
        rel = jnp.array([distance(p) for p in range(count)], jnp.int32)
        product = product[jnp.bitwise_xor(rel, d)]
        token = jnp.zeros(TOKEN.shape, F32) + product[0, :1, :1]
        if got is None:
            return [product.astype(BF16), token]
        product = (product + jnp.concatenate(got, axis=2).astype(F32)).astype(BF16)
        half = columns // 2
        return [
            jnp.stack([product[p, :, side * half : (side + 1) * half] for p in ps])
            for side, ps in zip((0, 0, 1, 1), chosen)
        ] + [token]

    def body(d_ref, *refs):
        lefts = refs[: len(pairs)]
        rights = refs[len(pairs) : 2 * len(pairs)]
        got_refs = refs[2 * len(pairs) : 3 * len(pairs)]
        token_ref, turned_ref = refs[-2:]
        outs = refs[-3:-2] if got is None else refs[-6:-2]
        c = pl.program_id(0)

        @pl.when(c == 0)
        def _():
            token_ref[...] = jnp.zeros_like(token_ref)
            for i, left_ref in enumerate(lefts):
                for p in range(count):
                    at = pl.multiple_of(jnp.bitwise_xor(d_ref[0], distance(p)) * rows, 128)
                    turned_ref[i, pl.ds(p * rows, rows), :] = left_ref[:, pl.ds(at, rows)].T

        def piece(i, p):
            return jnp.dot(
                turned_ref[i, pl.ds(p * rows, rows), :], rights[i][0], preferred_element_type=F32
            )

        def write(i, half):
            for p in range(count):
                value = piece(i, p)
                if got is None:
                    outs[0][p] = value.astype(BF16)
                    continue
                value = (value + got_refs[i][p].astype(F32)).astype(BF16)
                for which in (2 * half, 2 * half + 1):
                    if p in chosen[which]:
                        outs[which][chosen[which].index(p)] = value

        for i in range(len(pairs)):
            for half in (0, 1):
                low = max(starts[i], half * (steps // 2))
                high = min(starts[i] + tiles[i], (half + 1) * (steps // 2))
                if low < high:
                    pl.when((c >= low) & (c < high))(lambda i=i, half=half: write(i, half))

    def right_spec(start, n, split):
        def at(c, d_ref):
            k = jnp.clip(c - start, 0, n - 1)
            return (lax.div(k, jnp.int32(split)), 0, lax.rem(k, jnp.int32(split)))

        return pl.BlockSpec((1, total, tile), at)

    in_specs = [pl.BlockSpec((total, all_rows), lambda c, d_ref: (0, 0))] * len(pairs)
    in_specs += [right_spec(*item) for item in zip(starts, tiles, splits)]
    args = [left for left, _ in pairs] + [right for _, right in pairs]
    if got is None:
        out_shape = [jax.ShapeDtypeStruct((count, rows, columns), BF16)]
        out_specs = [pl.BlockSpec((count, rows, tile), lambda c, d_ref: (0, 0, c))]
    else:
        for start, n in zip(starts, tiles):
            in_specs.append(
                pl.BlockSpec(
                    (count, rows, tile),
                    lambda c, d_ref, start=start, n=n: (0, 0, jnp.clip(c - start, 0, n - 1)),
                )
            )
        args += got
        out_shape = [jax.ShapeDtypeStruct((count // 2, rows, columns // 2), BF16)] * 4
        mid = steps // 2
        first = pl.BlockSpec(
            (count // 2, rows, tile), lambda c, d_ref: (0, 0, jnp.minimum(c, mid - 1))
        )
        second = pl.BlockSpec(
            (count // 2, rows, tile), lambda c, d_ref: (0, 0, jnp.maximum(c - mid, 0))
        )
        out_specs = [first, first, second, second]
    out_shape = out_shape + [TOKEN]
    out_specs = out_specs + [pl.BlockSpec(TOKEN.shape, lambda c, d_ref: (0, 0))]
    in_specs += [ANY] * len(deps)
    return pl.pallas_call(
        body,
        out_shape=out_shape,
        grid_spec=pltpu.PrefetchScalarGridSpec(
            num_scalar_prefetch=1,
            grid=(steps,),
            in_specs=in_specs,
            out_specs=out_specs,
            scratch_shapes=[pltpu.VMEM((len(pairs), count * rows, total), BF16)],
        ),
        compiler_params=pltpu.CompilerParams(vmem_limit_bytes=34 * 2**20),
        cost_estimate=pl.CostEstimate(flops=int(2.5 * 1.15e9), bytes_accessed=1024, transcendentals=0),
        name="gradient",
    )(d.reshape(1).astype(jnp.int32), *args, *deps)


def head_probs(q, k, far, slope):
    scores = lax.dot_general(q, k, (((1,), (1,)), ((), ())), preferred_element_type=F32)
    scores = scores * (HEAD ** (-0.5)) - slope * far
    raised = jnp.exp(scores - jnp.max(scores, axis=-1, keepdims=True))
    return raised * (1.0 / jnp.sum(raised, axis=-1, keepdims=True))


def flat_frames(block):
    sources, _, rows, lanes = block.shape
    if rows % 16 == 0:
        return block.reshape(sources * rows, lanes)
    return block.astype(F32).reshape(sources * rows, lanes).astype(BF16)


def by_source(value, like):
    sources, _, rows, lanes = like
    if rows % 16 == 0:
        return value.astype(BF16).reshape(sources, 1, rows, lanes)
    return value.reshape(sources, 1, rows, lanes).astype(BF16)


def attend(triple, far, slopes, deps=()):
    dp, micro, rows, wide = triple.shape
    frames = dp * rows
    width = wide // 3
    pairs = width // 128
    shape = (dp, 1, rows, 128)

    def body(slope_ref, q_ref, k_ref, v_ref, far_ref, *refs):
        out_ref = refs[-1]
        h = pl.program_id(1)
        q, k, v = (flat_frames(ref[...]) for ref in (q_ref, k_ref, v_ref))
        first = lax.broadcasted_iota(jnp.int32, (frames, 128), 1) < HEAD
        zero = jnp.zeros_like(q)
        outs = []
        for j, own in enumerate((jnp.where(first, q, zero), jnp.where(first, zero, q))):
            probs = head_probs(own, k, far_ref[0], slope_ref[h * 2 + j])
            outs.append(jnp.dot(probs.astype(BF16), v, preferred_element_type=F32))
        out_ref[...] = by_source(jnp.where(first, outs[0], outs[1]), shape)

    def spec(offset):
        return pl.BlockSpec(shape, lambda m, h, s: (0, m, 0, h + offset))

    return pl.pallas_call(
        body,
        out_shape=jax.ShapeDtypeStruct((dp, micro, rows, width), BF16),
        grid_spec=pltpu.PrefetchScalarGridSpec(
            num_scalar_prefetch=1,
            grid=(micro, pairs),
            in_specs=[
                spec(0),
                spec(pairs),
                spec(2 * pairs),
                pl.BlockSpec((1, frames, frames), lambda m, h, s: (m, 0, 0)),
            ]
            + [ANY] * len(deps),
            out_specs=spec(0),
        ),
        compiler_params=pltpu.CompilerParams(vmem_limit_bytes=24 * 2**20),
        cost_estimate=pl.CostEstimate(flops=int(8 * 1.15e9), bytes_accessed=1024, transcendentals=0),
        name="attend",
    )(slopes, triple, triple, triple, far, *deps)


def attend_back(triple, grad, far, slopes, deps=()):
    dp, micro, rows, wide = triple.shape
    frames = dp * rows
    width = wide // 3
    pairs = width // 128
    shape = (dp, 1, rows, 128)
    scale = HEAD ** (-0.5)

    def turned(left, right):
        return lax.dot_general(left, right, (((0,), (0,)), ((), ())), preferred_element_type=F32)

    def body(slope_ref, q_ref, k_ref, v_ref, g_ref, far_ref, *refs):
        out_ref, token_ref = refs[-2:]
        token_ref[...] = jnp.zeros_like(token_ref)
        h = pl.program_id(1)
        q, k, v, g = (flat_frames(ref[...]) for ref in (q_ref, k_ref, v_ref, g_ref))
        first = lax.broadcasted_iota(jnp.int32, (frames, 128), 1) < HEAD
        zero = jnp.zeros_like(q)
        grads = []
        for j in range(2):
            own_q = jnp.where(first, q, zero) if j == 0 else jnp.where(first, zero, q)
            own_g = jnp.where(first, g, zero) if j == 0 else jnp.where(first, zero, g)
            scores = nt(k, own_q) * scale - slope_ref[h * 2 + j] * far_ref[0]
            raised = jnp.exp(scores - jnp.max(scores, axis=0, keepdims=True))
            probs = raised * (1.0 / jnp.sum(raised, axis=0, keepdims=True))
            back = nt(v, own_g)
            back = probs * (back - jnp.sum(back * probs, axis=0, keepdims=True))
            low = back.astype(BF16)
            grads.append(
                (
                    turned(low, k) * scale,
                    jnp.dot(low, q, preferred_element_type=F32) * scale,
                    jnp.dot(probs.astype(BF16), g, preferred_element_type=F32),
                )
            )
        for i in range(3):
            out_ref[i] = by_source(jnp.where(first, grads[0][i], grads[1][i]), shape)

    def spec(offset):
        return pl.BlockSpec(shape, lambda m, h, s: (0, m, 0, h + offset))

    return pl.pallas_call(
        body,
        out_shape=[jax.ShapeDtypeStruct((3, dp, micro, rows, width), BF16), TOKEN],
        grid_spec=pltpu.PrefetchScalarGridSpec(
            num_scalar_prefetch=1,
            grid=(micro, pairs),
            in_specs=[
                spec(0),
                spec(pairs),
                spec(2 * pairs),
                spec(0),
                pl.BlockSpec((1, frames, frames), lambda m, h, s: (m, 0, 0)),
            ]
            + [ANY] * len(deps),
            out_specs=[
                pl.BlockSpec((3,) + shape, lambda m, h, s: (0, 0, m, 0, h)),
                pl.BlockSpec(TOKEN.shape, lambda m, h, s: (0, 0)),
            ],
        ),
        compiler_params=pltpu.CompilerParams(vmem_limit_bytes=24 * 2**20),
        cost_estimate=pl.CostEstimate(flops=int(2 * 1.15e9), bytes_accessed=1024, transcendentals=0),
        name="attend_back",
    )(slopes, triple, triple, triple, grad, far, *deps)


def add_up(values):
    total = values[0].astype(F32)
    for value in values[1:]:
        total = total + value.astype(F32)
    return total.astype(BF16)


class Reduction:
    def __init__(self, pairs, d, dims, deps=()):
        self.pairs = [(left, right if right.ndim == 3 else right[None]) for left, right in pairs]
        self.d = d
        self.dims = dims
        self.sent, self.token = gradient_blocks(self.pairs, d, dims, deps=deps)

    def share(self):
        return flip(self.sent, 1)

    def own(self, got, deps=(), others=()):
        pairs = self.pairs + [pair for other, _ in others for pair in other.pairs]
        gots = [got] + [arrived for _, arrived in others]
        *self.parts, self.token = gradient_blocks(pairs, self.d, self.dims, gots, deps)

    def near(self):
        parts = self.parts
        return [flip(parts[0], 1 << self.dims[0]), flip(parts[2], 1 << self.dims[-1])]

    def near_landed(self, got):
        self.halves = []
        for side, order in ((0, self.dims), (1, self.dims[::-1])):
            stay = self.parts[2 * side + 1]
            left = [bit for bit in self.dims if bit != order[0]]
            shape = (2,) * len(left) + stay.shape[1:]
            values = [stay.reshape(shape), got[side].reshape(shape)]
            self.halves.append((values, list(order[1:]), left))

    def step(self):
        sends, self.stays = [], []
        for values, order, left in self.halves:
            at = left.index(order[0])
            sends.append(add_up([lax.index_in_dim(v, 1, at, keepdims=False) for v in values]))
            self.stays.append([lax.index_in_dim(v, 0, at, keepdims=False) for v in values])
        bits = [order[0] for _, order, _ in self.halves]
        return [flip(sends[0], 1 << bits[0]), flip(sends[1], 1 << bits[1])]

    def landed(self, got):
        halves = []
        for i, (_, order, left) in enumerate(self.halves):
            halves.append((self.stays[i] + [got[i]], order[1:], [b for b in left if b != order[0]]))
        self.halves = halves

    def cross(self):
        while len(self.halves[0][1]) > 1:
            self.landed(self.step())
        return self.step()

    def rows(self):
        self.value = jnp.concatenate([add_up(values) for values, _, _ in self.halves], axis=1)
        self.stage = 0
        return self.value

    def along(self):
        rep = lax.axis_size("rep")
        half = rep // 2
        k = self.stage
        if k < half - 1:
            pairs = [(k, k + 1), (rep - 1 - k, rep - 2 - k)]
        elif k == half - 1:
            pairs = [(k, k + 1), (k + 1, k)]
        else:
            i = rep - 2 - k
            pairs = [(i + 1, i), (rep - 2 - i, rep - 1 - i)]
        return lax.ppermute(self.value, "rep", pairs)

    def along_landed(self, got):
        rep = lax.axis_size("rep")
        z = lax.axis_index("rep")
        k = self.stage
        self.stage += 1
        if k < rep // 2:
            self.value = add_up([self.value, got])
        else:
            i = rep - 2 - k
            self.value = jnp.where((z == i) | (z == rep - 1 - i), got, self.value)

    def finish(self):
        while self.stage < lax.axis_size("rep") - 1:
            self.along_landed(self.along())
        return self.value.astype(F32)

    def halve(self, extra=None, beside=None):
        rep = lax.axis_size("rep")
        z = lax.axis_index("rep")
        value = self.value
        if extra is not None:
            value = jnp.concatenate([value, extra], axis=0)
        bits = range(rep.bit_length() - 1)
        for bit in bits:
            mine = lax.bitwise_and(lax.shift_right_logical(z, bit), 1)
            size = value.shape[0] // 2
            send = lax.dynamic_slice_in_dim(value, (1 - mine) * size, size, 0)
            keep = lax.dynamic_slice_in_dim(value, mine * size, size, 0)
            got = rep_flip(send, 1 << bit)
            if bit == len(bits) - 1 and beside is not None:
                got, beside = together(got, beside)
            value = add_up([keep, got])
        for bit in reversed(bits):
            mine = lax.bitwise_and(lax.shift_right_logical(z, bit), 1)
            got = rep_flip(value, 1 << bit)
            lower = jnp.where(mine == 0, value, got)
            upper = jnp.where(mine == 0, got, value)
            value = jnp.concatenate([lower, upper], axis=0)
        return value.astype(F32), beside


def nt(left, right):
    return lax.dot_general(left, right, (((1,), (1,)), ((), ())), preferred_element_type=F32)


def hidden_gradient(grad_result, w_down, slope, deps=()):
    total, width = grad_result.shape
    units = w_down.shape[0]
    tile = 512

    def body(grad_ref, w_ref, slope_ref, *refs):
        out_ref, sum_ref = refs[-2:]
        value = nt(grad_ref[...], w_ref[...]) * slope_ref[...].astype(F32)
        out_ref[...] = value.astype(BF16)
        sum_ref[...] = jnp.sum(value, axis=0, keepdims=True)

    return pl.pallas_call(
        body,
        out_shape=[
            jax.ShapeDtypeStruct((total, units), BF16),
            jax.ShapeDtypeStruct((1, units), F32),
        ],
        grid=(units // tile,),
        in_specs=[
            pl.BlockSpec((total, width), lambda c: (0, 0)),
            pl.BlockSpec((tile, width), lambda c: (c, 0)),
            pl.BlockSpec((total, tile), lambda c: (0, c)),
        ]
        + [ANY] * len(deps),
        out_specs=[
            pl.BlockSpec((total, tile), lambda c: (0, c)),
            pl.BlockSpec((1, tile), lambda c: (0, c)),
        ],
        compiler_params=pltpu.CompilerParams(vmem_limit_bytes=24 * 2**20),
        cost_estimate=pl.CostEstimate(flops=int(3 * 1.15e9), bytes_accessed=1024, transcendentals=0),
        name="hidden_gradient",
    )(grad_result, w_down, slope, *deps)


def mixed_gradient(hidden_low, w_up, w_out, mixed, grad_result, gain, deps=()):
    total, units = hidden_low.shape
    width = w_up.shape[0]
    tile = 256

    def body(low_ref, up_ref, out_w_ref, mixed_ref, result_ref, gain_ref, *outs):
        grad_ref, rounded_ref, attended_ref, sums_ref = outs[-4:]
        grad = nt(low_ref[...], up_ref[...])
        unit, scale = norm_parts(mixed_ref[...])
        result = result_ref[...].astype(F32)
        value = result + norm_back(grad, gain_ref[...], unit, scale)
        rounded = value.astype(BF16)
        grad_ref[...] = value
        rounded_ref[...] = rounded
        attended_ref[...] = nt(rounded, out_w_ref[...]).astype(BF16)

        @pl.when(pl.program_id(0) == 0)
        def _():
            sums_ref[...] = jnp.zeros_like(sums_ref)

        for i, terms in enumerate((value, grad * unit, grad, result)):
            sums_ref[pl.ds(i, 1), :] += jnp.sum(terms, axis=0, keepdims=True)

    rows = pl.BlockSpec((tile, width), lambda r: (r, 0))
    whole = [
        pl.BlockSpec((width, units), lambda r: (0, 0)),
        pl.BlockSpec((width, width), lambda r: (0, 0)),
    ]
    return pl.pallas_call(
        body,
        out_shape=[
            jax.ShapeDtypeStruct((total, width), F32),
            jax.ShapeDtypeStruct((total, width), BF16),
            jax.ShapeDtypeStruct((total, width), BF16),
            jax.ShapeDtypeStruct((8, width), F32),
        ],
        grid=(total // tile,),
        in_specs=[pl.BlockSpec((tile, units), lambda r: (r, 0))]
        + whole
        + [rows, rows, pl.BlockSpec((1, width), lambda r: (0, 0))]
        + [ANY] * len(deps),
        out_specs=[rows, rows, rows, pl.BlockSpec((8, width), lambda r: (0, 0))],
        compiler_params=pltpu.CompilerParams(vmem_limit_bytes=44 * 2**20),
        cost_estimate=pl.CostEstimate(flops=int(2 * 1.15e9), bytes_accessed=1024, transcendentals=0),
        name="mixed_gradient",
    )(hidden_low, w_up, w_out, mixed, grad_result, gain.reshape(1, width), *deps)


def normed_gradient(grad_triple, w_qkv, deps=()):
    three, total, width = grad_triple.shape
    tile = 256

    def body(grad_ref, w_ref, *refs):
        out_ref = refs[-1]
        value = nt(grad_ref[0], w_ref[:, pl.ds(0, width)])
        for i in range(1, three):
            value += nt(grad_ref[i], w_ref[:, pl.ds(i * width, width)])
        out_ref[...] = value.astype(BF16)

    return pl.pallas_call(
        body,
        out_shape=jax.ShapeDtypeStruct((total, width), BF16),
        grid=(total // tile,),
        in_specs=[
            pl.BlockSpec((three, tile, width), lambda r: (0, r, 0)),
            pl.BlockSpec((width, three * width), lambda r: (0, 0)),
        ]
        + [ANY] * len(deps),
        out_specs=pl.BlockSpec((tile, width), lambda r: (r, 0)),
        compiler_params=pltpu.CompilerParams(vmem_limit_bytes=24 * 2**20),
        cost_estimate=pl.CostEstimate(flops=int(2 * 1.15e9), bytes_accessed=1024, transcendentals=0),
        name="normed_gradient",
    )(grad_triple, w_qkv, *deps)


def matmul(left, right):
    return jnp.dot(left, right, preferred_element_type=F32)


def matmul_nt(left, right):
    return lax.dot_general(left, right, (((1,), (1,)), ((), ())), preferred_element_type=F32)


def matmul_tn(left, right):
    return lax.dot_general(left, right, (((0,), (0,)), ((), ())), preferred_element_type=F32)


def norm_parts(values):
    average = jnp.mean(values, axis=-1, keepdims=True)
    centred = values - average
    spread = jnp.mean(centred * centred, axis=-1, keepdims=True)
    scale = lax.rsqrt(spread + EPS)
    return centred * scale, scale


def norm_back(grad, gain, unit, scale):
    e = grad * gain
    return scale * (
        e
        - jnp.mean(e, axis=-1, keepdims=True)
        - unit * jnp.mean(e * unit, axis=-1, keepdims=True)
    )


def shards(
    inputs,
    skips,
    cotangent,
    dest_slot,
    pack_segments,
    block_live,
    counts,
    w_skip,
    b_skip,
    g_one,
    b_one,
    w_qkv,
    w_out,
    b_out,
    g_two,
    b_two,
    w_up,
    c_up,
    w_down,
    c_down,
):
    dp = lax.axis_size("dp")
    rep = lax.axis_size("rep")
    d = lax.axis_index("dp")
    z = lax.axis_index("rep")
    micro = inputs.shape[0]
    frames = inputs.shape[2]
    width = inputs.shape[3]
    blocks = dest_slot.shape[2]
    block = frames // blocks
    per_pair = blocks // dp
    total = micro * frames
    bits = dp.bit_length() - 1
    place = jnp.stack([z, lax.rem(d, 8)]).astype(jnp.int32)
    dims = list(range(1, bits))
    small = jnp.concatenate([dest_slot.reshape(-1), block_live.reshape(-1), counts.reshape(-1)])

    own_skip = own_chunk(place, width, [w_skip])
    z_skip = Fetch(own_skip)
    z_skip.rest()
    got = z_skip.send()
    every = small[None]
    for bit in range(bits):
        every = jnp.concatenate([every, flip(every, 1 << bit)], axis=0)
    z_mid = Fetch(own_chunk(place, width, [w_qkv, w_out], z_skip.held[1:]))
    z_mid.rest()
    z_skip.landed(got)

    run_skip = Spread(z_skip.far(), width, [every, z_mid.held[-1]])
    mid = z_mid.send()
    run_skip.near_landed(run_skip.near())

    span = micro * blocks
    numbers = every[:, : 2 * span].reshape(dp, 2 * micro, blocks)
    numbers = jnp.transpose(numbers, (1, 0, 2)).reshape(2 * micro, dp * blocks).astype(F32)
    count_total = jnp.sum(every[:, 2 * span]).astype(F32).reshape(1, 1)
    inner = jnp.arange(frames) % block
    live = inner[None] < jnp.repeat(block_live[:, 0, :], block, axis=1)
    codes = (2 * pack_segments[:, 0, :] + live).astype(F32)
    joined = jnp.concatenate([inputs.reshape(total, width), skips.reshape(total, width)], axis=1)
    far, far_turned, keep_wide, shuffle = plan_order(
        numbers[:micro], numbers[micro:], codes, d, block, [run_skip.pairs[0], joined]
    )
    keep_rows = keep_wide[:, :1]

    run_skip.cross_landed(run_skip.cross(), [shuffle, mid])

    z_mid.landed(mid)
    run_mid = Spread(z_mid.far(), width)
    full_skip, _ = assemble(
        w_skip, run_skip.parts(run_skip.share()), place, 0, 1, [run_mid.start[0]]
    )
    z_up = Fetch(own_chunk(place, width, [w_up], [run_mid.start[0]]))
    z_up.rest()
    base = matmul(joined, full_skip) + b_skip
    unit_one, scale_one = norm_parts(base)
    own_normed = (unit_one * g_one + b_one).astype(BF16)
    sent = matmul(shuffle, own_normed).astype(BF16)
    run_mid.near_landed(run_mid.near(), [sent, z_up.held[-1]])

    def exchange(values):
        values = values.reshape(dp, total // dp, width)
        got = lax.all_to_all(values, "dp", split_axis=0, concat_axis=0, tiled=True)
        return got.reshape(total, width)

    normed = exchange(sent)
    up = z_up.send([sent])
    z_down = Fetch(own_chunk(place, width, [w_down], [z_up.held[-1], sent]))
    z_down.rest()
    run_mid.cross_landed(run_mid.cross(), [up, z_down.held[-1], normed])
    z_up.landed(up)

    other = run_mid.share()
    run_up = Spread(z_up.far(), width, [run_mid.every])
    run_up.near_landed(run_up.near(), [other])
    shard_rows = w_qkv.shape[0] // 8
    parts_mid = run_mid.parts(other)
    full_qkv, _ = assemble(w_qkv, parts_mid, place, 0, 3)

    triple = matmul(normed, full_qkv).astype(BF16)
    triple = triple.reshape(dp, micro, per_pair * block, 3 * width)
    slopes = 2.0 ** (-8.0 * (jnp.arange(HEADS, dtype=F32) + 1.0) / HEADS)
    attended = attend(triple, far, slopes, [run_up.pairs[0]])
    down = z_down.send()
    run_up.cross_landed(run_up.cross(), [attended, down])
    z_down.landed(down)

    attended = exchange(attended)
    other = run_up.share()
    run_down = Spread(z_down.far(), width, [run_up.every])
    down = run_down.near()
    full_out, out_token = assemble(w_out, parts_mid, place, 3 * shard_rows, 1, [run_up.every])
    full_up, up_token = assemble(w_up, run_up.parts(other), place, 0, w_up.shape[1] // width)
    attended, out_token, up_token = together(attended, out_token, up_token)

    attended = matmul_tn(shuffle, attended).astype(BF16)
    mixed = base + matmul(attended, full_out) + (b_out + out_token[0, 0])
    unit_two, scale_two = norm_parts(mixed)
    normed_two = (unit_two * g_two + b_two).astype(BF16)
    count_total = count_total + up_token[:1, :1]
    for step in rep_steps(rep):
        count_total = count_total + rep_flip(count_total, step)
    share = counts[0, 0].astype(F32) * (dp * rep) / count_total[0, 0]
    run_down.near_landed(down, [up_token])
    down = run_down.cross()
    hidden = matmul(normed_two, full_up) + (c_up + run_down.token[0, 0])
    phi = 0.5 * (1.0 + lax.erf(hidden * (0.5**0.5)))
    active = (hidden * phi).astype(BF16)
    slope = (phi + hidden * jnp.exp(-0.5 * hidden * hidden) * ((2 * jnp.pi) ** -0.5)).astype(BF16)
    scaled = (cotangent.reshape(total, width).astype(F32) * share).astype(BF16)
    grad_result = scaled * keep_rows.astype(BF16)
    red_down = Reduction([(active, grad_result)], d, dims)

    down_got = red_down.share()
    run_down.cross_landed(down, [red_down.sent])
    full_down, _ = assemble(w_down, run_down.parts(run_down.share()), place, 0, 1)

    hidden_low, sum_hidden = hidden_gradient(grad_result, full_down, slope)
    red_up = Reduction([(normed_two, hidden_low)], d, dims)
    up_got = red_up.share()
    red_down.own(down_got, [red_up.sent])
    flying = red_down.near()
    grad_mixed, mixed_low, grad_attended, sums_mixed = mixed_gradient(
        hidden_low, full_up, full_out, mixed, grad_result, g_two, [red_down.token]
    )
    red_out = Reduction([(attended, mixed_low)], d, dims)
    out_got = red_out.share()
    flying, sums_mixed = together(flying, sums_mixed)
    red_down.near_landed(flying)

    down_flying = red_down.cross()
    sent = matmul(shuffle, grad_attended).astype(BF16)
    grad_attended = exchange(sent)
    red_up.own(up_got, [sent], [(red_out, out_got)])
    flying = red_up.near()
    down_flying, token = together(down_flying, red_up.token)
    red_down.landed(down_flying)
    red_down.rows()

    line = red_down.along()
    grad_attended = grad_attended.reshape(dp, micro, per_pair * block, width)
    grad_triple, token = attend_back(
        triple, grad_attended, far_turned, slopes, [red_down.value, token]
    )
    grad_triple = grad_triple.reshape(3, total, width)

    sent = normed_gradient(grad_triple, full_qkv)
    grad_normed = exchange(sent)
    flying, line, token = together(flying, line, token)
    red_mid = Reduction([(normed, grad_triple)], d, dims, [sent, token])
    grad_normed, token = together(grad_normed, red_mid.token)
    red_up.near_landed(flying)
    red_down.along_landed(line)
    up_flying = red_up.cross()
    line = red_down.along()

    mid_got = red_mid.share()
    grad_normed = matmul_tn(shuffle, grad_normed)
    grad_base = grad_mixed + norm_back(grad_normed, g_one, unit_one, scale_one)
    base_low = grad_base.astype(BF16)
    red_skip = Reduction([(joined, base_low)], d, dims, [token])
    skip_got = red_skip.share()
    vectors = (
        jnp.sum(grad_base, axis=0),
        jnp.sum(grad_normed * unit_one, axis=0),
        jnp.sum(grad_normed, axis=0),
        sums_mixed[0],
        sums_mixed[1],
        sums_mixed[2],
        sum_hidden[0],
        sums_mixed[3],
    )
    lengths = [v.shape[0] for v in vectors]
    summed = jnp.concatenate(vectors).reshape(-1, 128)
    for bit in range(bits - 1):
        summed = summed + flip(summed, 1 << bit)
    up_flying, token = together(up_flying, red_skip.token)
    red_up.landed(up_flying)
    red_up.rows()
    up_line = red_up.along()
    red_mid.own(mid_got, [token])
    summed, token = together(summed, red_mid.token)

    flying = red_mid.near()
    red_skip.own(skip_got, [token])
    skip_flying = red_skip.near()
    line, token = together(line, red_skip.token)
    red_down.along_landed(line)
    line = red_down.along()
    result = mixed + matmul(active, full_down) + (c_down + token[0, 0])
    output = (result * keep_rows).astype(BF16)
    grad_joined = matmul_nt(base_low, full_skip).astype(BF16)
    flying, up_line, grad_joined, summed = together(flying, up_line, grad_joined, summed)
    red_mid.near_landed(flying)
    red_up.along_landed(up_line)

    flying = red_mid.cross()
    up_line = red_up.along()
    flying, up_line, line, skip_flying, summed = together(
        flying, up_line, line, skip_flying, summed
    )
    red_down.along_landed(line)
    red_skip.near_landed(skip_flying)
    skip_flying = red_skip.cross()
    red_mid.landed(flying)
    red_mid.rows()
    red_up.along_landed(up_line)
    up_line = red_up.along()
    summed = summed + flip(summed, 1 << (bits - 1))
    skip_columns = w_skip.shape[1]
    extra = jnp.pad(summed.reshape(-1), (0, -summed.size % (16 * rep * skip_columns)))
    extra = extra.reshape(-1, skip_columns).astype(BF16)
    skip_flying, extra = together(skip_flying, extra)
    red_skip.landed(skip_flying)
    red_skip.rows()
    final_mid, up_line = red_mid.halve(beside=up_line)
    final_skip, _ = red_skip.halve(extra)
    red_up.along_landed(up_line)
    own_rows = w_skip.shape[0] * rep // dp
    summed = final_skip[own_rows:].reshape(-1)
    final_up = red_up.finish()
    units = c_up.shape[0]
    finals = [
        red_down.finish(),
        final_up[:, :units],
        final_up[:, units:],
        final_mid,
        final_skip[:own_rows],
    ]
    sums = []
    offset = 0
    for length in lengths:
        sums.append(summed[offset : offset + length])
        offset += length

    def as_owned(values):
        return values.reshape(inputs.shape)

    return (
        as_owned(output),
        as_owned(grad_joined[:, :width]),
        as_owned(grad_joined[:, width:]),
        finals[4],
        sums[0],
        sums[1],
        sums[2],
        finals[3],
        finals[2],
        sums[3],
        sums[4],
        sums[5],
        finals[1],
        sums[6],
        finals[0],
        sums[7],
    )


def solution(mesh):
    frames = P(None, "rep", "dp", None)
    slots = P(None, "rep", "dp")
    rows = P("rep", None)
    whole = P()
    in_specs = (
        (frames,) * 3
        + (slots,) * 3
        + (P("dp", "rep"), rows, whole, whole, whole, rows, rows)
        + (whole,) * 3
        + (rows, whole, rows, whole)
    )
    split = P("dp", None)
    out_specs = (
        (frames,) * 3
        + (split,)
        + (whole,) * 3
        + (split, split)
        + (whole,) * 3
        + (split, whole, split, whole)
    )
    return jax.shard_map(shards, mesh=mesh, in_specs=in_specs, out_specs=out_specs, check_vma=False)
```

```python
import jax
import jax.numpy as jnp
from jax import lax
from jax.experimental import pallas as pl
from jax.experimental.pallas import tpu as pltpu
from jax.sharding import PartitionSpec as P

HEADS = 16
HEAD = 64
EPS = 1e-05
F32 = jnp.float32
BF16 = jnp.bfloat16
TOKEN = jax.ShapeDtypeStruct((8, 128), F32)
ANY = pl.BlockSpec(memory_space=pl.ANY)
LIGHT = pl.CostEstimate(flops=1024, bytes_accessed=1024, transcendentals=0)


def flip(value, bit):
    n = lax.axis_size("dp")
    return lax.ppermute(value, "dp", [(i, i ^ bit) for i in range(n)])


def rep_flip(value, bit):
    n = lax.axis_size("rep")
    return lax.ppermute(value, "rep", [(i, i ^ bit) for i in range(n)])


def after(value, *earlier):
    return lax.optimization_barrier((value,) + earlier)[0]


def together(*values):
    return lax.optimization_barrier(values)


def assemble(w_local, parts, place, row_at, tiles, deps=()):
    rep = lax.axis_size("rep")
    shard_rows, columns = w_local.shape
    rows = shard_rows // 8
    tile = columns // tiles
    half = tile // 2
    chunk_rows = parts[0][0].shape[0] // (len(parts[0][1]) * (rep - 1))
    arrays = [part[0] for part in parts]
    count = 1 + sum(len(part[1]) for part in parts) * (rep - 1) * tiles

    def body(place_ref, local_ref, *refs):
        out_ref, token_ref, sems = refs[-3:]
        token_ref[...] = jnp.zeros_like(token_ref)
        z = place_ref[0]
        e = place_ref[1]
        copies = [
            pltpu.make_async_copy(
                local_ref,
                out_ref.at[pl.ds(pl.multiple_of(z * shard_rows, 16), shard_rows), :],
                sems.at[0],
            )
        ]
        for ref, (_, runs) in zip(refs, parts):
            for k, (side, rel) in enumerate(runs):
                chunk = jnp.bitwise_xor(e, rel)
                for s, apart in enumerate(far_order(rep), 1):
                    shard = jnp.bitwise_xor(z, apart)
                    start = pl.multiple_of(shard * shard_rows + chunk * rows, 16)
                    for t in range(tiles):
                        at = (k * (rep - 1) + s - 1) * chunk_rows + row_at + t * rows
                        copies.append(
                            pltpu.make_async_copy(
                                ref.at[pl.ds(at, rows), :],
                                out_ref.at[pl.ds(start, rows), pl.ds(t * tile + side * half, half)],
                                sems.at[len(copies)],
                            )
                        )
        for copy in copies:
            copy.start()
        for copy in copies:
            copy.wait()

    return pl.pallas_call(
        body,
        out_shape=[jax.ShapeDtypeStruct((shard_rows * rep, columns), w_local.dtype), TOKEN],
        grid=(1,),
        in_specs=[pl.BlockSpec(memory_space=pltpu.SMEM)] + [ANY] * (1 + len(parts) + len(deps)),
        out_specs=[
            pl.BlockSpec((shard_rows * rep, columns), lambda i: (0, 0)),
            pl.BlockSpec(TOKEN.shape, lambda i: (0, 0)),
        ],
        scratch_shapes=[pltpu.SemaphoreType.DMA((count,))],
        compiler_params=pltpu.CompilerParams(vmem_limit_bytes=26 * 2**20),
        cost_estimate=pl.CostEstimate(flops=int(1.5 * 1.15e9), bytes_accessed=1024, transcendentals=0),
        name="assemble",
    )(place, w_local, *arrays, *deps)


def own_chunk(place, width, shards_local, deps=()):
    items = []
    for which, w_local in enumerate(shards_local):
        for t in range(w_local.shape[1] // width):
            items.append((which, w_local.shape[0] // 8, t * width))
    total = sum(item[1] for item in items)

    def body(place_ref, *refs):
        out_ref, sems = refs[-2:]
        copies = []
        at = 0
        for which, rows, column in items:
            start = pl.multiple_of(place_ref[1] * rows, 16)
            copies.append(
                pltpu.make_async_copy(
                    refs[which].at[pl.ds(start, rows), pl.ds(column, width)],
                    out_ref.at[pl.ds(at, rows), :],
                    sems.at[len(copies)],
                )
            )
            at += rows
        for copy in copies:
            copy.start()
        for copy in copies:
            copy.wait()

    return pl.pallas_call(
        body,
        out_shape=jax.ShapeDtypeStruct((total, width), shards_local[0].dtype),
        grid=(1,),
        in_specs=[pl.BlockSpec(memory_space=pltpu.SMEM)]
        + [ANY] * (len(shards_local) + len(deps)),
        out_specs=pl.BlockSpec((total, width), lambda i: (0, 0)),
        scratch_shapes=[pltpu.SemaphoreType.DMA((len(items),))],
        compiler_params=pltpu.CompilerParams(vmem_limit_bytes=24 * 2**20),
        cost_estimate=LIGHT,
        name="own_chunk",
    )(place, *shards_local, *deps)


def pack(arrays, outs, deps=()):
    count = sum(len(out) for out in outs)

    def body(*refs):
        sources, targets = refs[: len(arrays)], refs[-2 - len(outs) : -2]
        token_ref, sems = refs[-2:]
        token_ref[...] = jnp.zeros_like(token_ref)
        copies = []
        for target, out in zip(targets, outs):
            at = 0
            for which, row, rows, column, columns in out:
                copies.append(
                    pltpu.make_async_copy(
                        sources[which].at[pl.ds(row, rows), pl.ds(column, columns)],
                        target.at[pl.ds(at, rows), :],
                        sems.at[len(copies)],
                    )
                )
                at += rows
        for copy in copies:
            copy.start()
        for copy in copies:
            copy.wait()

    return pl.pallas_call(
        body,
        out_shape=[
            jax.ShapeDtypeStruct((sum(item[2] for item in out), out[0][4]), arrays[0].dtype)
            for out in outs
        ]
        + [TOKEN],
        grid=(1,),
        in_specs=[ANY] * (len(arrays) + len(deps)),
        out_specs=[
            pl.BlockSpec((sum(item[2] for item in out), out[0][4]), lambda i: (0, 0))
            for out in outs
        ]
        + [pl.BlockSpec(TOKEN.shape, lambda i: (0, 0))],
        scratch_shapes=[pltpu.SemaphoreType.DMA((count,))],
        compiler_params=pltpu.CompilerParams(vmem_limit_bytes=24 * 2**20),
        cost_estimate=LIGHT,
        name="pack",
    )(*arrays, *deps)


def far_order(rep):
    order = [0]
    for bit in reversed(range(rep.bit_length() - 1)):
        order = order + [distance ^ (1 << bit) for distance in order]
    return order[1:]


class Spread:
    def __init__(self, gots, width, deps=()):
        self.half = width // 2
        rows = sum(got.shape[0] for got in gots)
        items = [(i, 0, got.shape[0]) for i, got in enumerate(gots)]
        *self.start, _ = pack(
            gots, [[item + (column, self.half) for item in items] for column in (0, self.half)], deps
        )
        self.n = rows

    def near(self):
        return [flip(self.start[0], 2), flip(self.start[1], 4)]

    def near_landed(self, got, deps=()):
        whole = [(i, 0, self.n, 0, self.half) for i in range(4)]
        *self.pairs, self.token = pack(
            [self.start[0], got[0], self.start[1], got[1]], [whole[:2], whole[2:]], deps
        )

    def cross(self):
        return [flip(self.pairs[0], 4), flip(self.pairs[1], 2)]

    def cross_landed(self, got, deps=()):
        whole = [(i, 0, 2 * self.n, 0, self.half) for i in range(4)]
        self.every, self.token = pack([self.pairs[0], got[0], self.pairs[1], got[1]], [whole], deps)

    def share(self):
        return flip(self.every, 1)

    def parts(self, other):
        runs = [(0, 0), (0, 2), (0, 4), (0, 6), (1, 0), (1, 4), (1, 2), (1, 6)]
        return [(self.every, runs), (other, [(side, rel | 1) for side, rel in runs])]


def rep_steps(rep):
    return [1 << bit for bit in reversed(range(rep.bit_length() - 1))]


class Fetch:
    def __init__(self, own):
        self.held = [own]
        self.steps = rep_steps(lax.axis_size("rep"))

    def send(self, deps=()):
        sent = self.held[0]
        if len(self.held) > 1:
            whole = [(i, 0, a.shape[0], 0, a.shape[1]) for i, a in enumerate(self.held)]
            sent, _ = pack(self.held, [whole], deps)
        return rep_flip(sent, self.steps[len(self.held) - 1])

    def landed(self, got):
        self.held.append(got)

    def rest(self):
        while len(self.held) < len(self.steps):
            self.landed(self.send())

    def far(self):
        return self.held[1:]


def plan_order(all_slots, all_live, codes, d, block, deps=()):
    micro, owners = all_slots.shape
    frames = codes.shape[1]
    blocks = frames // block
    dp = owners // blocks
    per_pair = blocks // dp
    total = micro * frames

    def column(row):
        return jnp.broadcast_to(row, (128, row.shape[1])).T[:, :1]

    def as_row(values):
        return jnp.broadcast_to(values, (values.shape[0], 128)).T[:1, :]

    def body(d_ref, slots_ref, live_ref, codes_ref, *refs):
        far_ref, turned_ref, keep_ref, shuffle_ref = refs[-4:]
        me = d_ref[0]
        lane = lax.broadcasted_iota(jnp.int32, (1, owners), 1)
        source = jnp.bitwise_xor(lax.div(lane, jnp.int32(blocks)), me)
        first_slot = (source * blocks).astype(F32) + lax.rem(lane, jnp.int32(blocks)).astype(F32)
        source_col = column(source.astype(F32))
        frame = lax.broadcasted_iota(jnp.int32, (frames, 1), 0)
        block_of = lax.div(frame, jnp.int32(block)).astype(F32)
        inner = lax.rem(frame, jnp.int32(block)).astype(F32)
        low = (me * blocks).astype(F32)
        rows = []
        for m in range(micro):
            slots = slots_ref[pl.ds(m, 1), :]
            slots_col = column(slots)
            same = source_col == source.astype(F32)
            rank = jnp.sum(jnp.where(same & (slots_col < slots), 1.0, 0.0), axis=0, keepdims=True)
            here = (slots >= low) & (slots < low + blocks)
            arrive = source.astype(F32) * per_pair + rank - (me * per_pair).astype(F32)
            arrive = jnp.where(here, arrive, -1.0)
            placed = jnp.sum(
                jnp.where(arrive == block_of, slots - low, 0.0), axis=1, keepdims=True
            )
            position = placed * block + inner
            at = lax.broadcasted_iota(jnp.int32, (1, frames), 1).astype(F32)
            code = jnp.sum(
                jnp.where(at == position, codes_ref[pl.ds(m, 1), :], 0.0), axis=1, keepdims=True
            )
            position_row, code_row = as_row(position), as_row(code)
            segment, segment_row = jnp.floor(code * 0.5), jnp.floor(code_row * 0.5)
            live_row = code_row - 2.0 * segment_row
            distance = jnp.abs(position - position_row)
            allowed = (segment == segment_row) & ((live_row > 0.5) | (distance < 0.5))
            far_ref[m] = jnp.where(allowed, distance, 1e32)
            live_col = code - 2.0 * segment
            allowed = (segment == segment_row) & ((live_col > 0.5) | (distance < 0.5))
            turned_ref[m] = jnp.where(allowed, distance, 1e32)
            own = lane < blocks
            mine = jnp.sum(
                jnp.where(own & (lane.astype(F32) == block_of), slots, 0.0), axis=1, keepdims=True
            )
            alive = jnp.sum(
                jnp.where(first_slot == mine, live_ref[pl.ds(m, 1), :], 0.0), axis=1, keepdims=True
            )
            keep_ref[pl.ds(m * frames, frames), :] = jnp.broadcast_to(
                jnp.where(inner < alive, 1.0, 0.0), (frames, 128)
            )
            my_rank = jnp.sum(
                jnp.where(own & (lane.astype(F32) == block_of), rank, 0.0), axis=1, keepdims=True
            )
            target = jnp.floor((my_rank + 0.5) / per_pair)
            row = (target * micro + m) * per_pair + (my_rank - target * per_pair)
            rows.append(as_row(row * block + inner))
        goal = jnp.concatenate(rows, axis=1)
        spot = lax.broadcasted_iota(jnp.int32, (total, total), 0).astype(F32)
        shuffle_ref[...] = jnp.where(spot == goal, 1.0, 0.0).astype(BF16)

    vmem = pl.BlockSpec(memory_space=pltpu.VMEM)
    return pl.pallas_call(
        body,
        out_shape=[
            jax.ShapeDtypeStruct((micro, frames, frames), F32),
            jax.ShapeDtypeStruct((micro, frames, frames), F32),
            jax.ShapeDtypeStruct((total, 128), F32),
            jax.ShapeDtypeStruct((total, total), BF16),
        ],
        in_specs=[pl.BlockSpec(memory_space=pltpu.SMEM), vmem, vmem, vmem] + [ANY] * len(deps),
        out_specs=[vmem, vmem, vmem, vmem],
        compiler_params=pltpu.CompilerParams(vmem_limit_bytes=24 * 2**20),
        cost_estimate=LIGHT,
        name="plan_order",
    )(d.reshape(1).astype(jnp.int32), all_slots, all_live, codes, *deps)


def gradient_blocks(pairs, d, dims, got=None, deps=()):
    dp = lax.axis_size("dp")
    total, all_rows = pairs[0][0].shape
    widths = [right.shape[2] for _, right in pairs]
    columns = sum(right.shape[0] * right.shape[2] for _, right in pairs)
    rows = all_rows // dp
    count = dp // 2
    odd = 1 if got is None else 0
    tile = min(min(widths), 512)
    splits = [width // tile for width in widths]
    tiles = [right.shape[0] * split for (_, right), split in zip(pairs, splits)]
    steps = sum(tiles)
    starts = [sum(tiles[:i]) for i in range(len(tiles))]

    def distance(p):
        rel = odd
        for k, bit in enumerate(dims):
            rel += ((p >> (len(dims) - 1 - k)) & 1) << bit
        return rel

    upper = [p for p in range(count) if p >= count // 2]
    lower = [p for p in range(count) if p < count // 2]
    odds = [p for p in range(count) if p % 2 == 1]
    evens = [p for p in range(count) if p % 2 == 0]
    chosen = (upper, lower, odds, evens)

    if rows % 128 != 0:
        products = []
        for left, right in pairs:
            flat = jnp.transpose(right, (1, 0, 2)).reshape(total, -1)
            products.append(matmul_tn(left, flat))
        product = jnp.concatenate(products, axis=1).reshape(dp, rows, columns)
        rel = jnp.array([distance(p) for p in range(count)], jnp.int32)
        product = product[jnp.bitwise_xor(rel, d)]
        token = jnp.zeros(TOKEN.shape, F32) + product[0, :1, :1]
        if got is None:
            return [product.astype(BF16), token]
        product = (product + jnp.concatenate(got, axis=2).astype(F32)).astype(BF16)
        half = columns // 2
        return [
            jnp.stack([product[p, :, side * half : (side + 1) * half] for p in ps])
            for side, ps in zip((0, 0, 1, 1), chosen)
        ] + [token]

    def body(d_ref, *refs):
        lefts = refs[: len(pairs)]
        rights = refs[len(pairs) : 2 * len(pairs)]
        got_refs = refs[2 * len(pairs) : 3 * len(pairs)]
        token_ref, turned_ref = refs[-2:]
        outs = refs[-3:-2] if got is None else refs[-6:-2]
        c = pl.program_id(0)

        @pl.when(c == 0)
        def _():
            token_ref[...] = jnp.zeros_like(token_ref)
            for i, left_ref in enumerate(lefts):
                for p in range(count):
                    at = pl.multiple_of(jnp.bitwise_xor(d_ref[0], distance(p)) * rows, 128)
                    turned_ref[i, pl.ds(p * rows, rows), :] = left_ref[:, pl.ds(at, rows)].T

        def piece(i, p):
            return jnp.dot(
                turned_ref[i, pl.ds(p * rows, rows), :], rights[i][0], preferred_element_type=F32
            )

        def write(i, half):
            for p in range(count):
                value = piece(i, p)
                if got is None:
                    outs[0][p] = value.astype(BF16)
                    continue
                value = (value + got_refs[i][p].astype(F32)).astype(BF16)
                for which in (2 * half, 2 * half + 1):
                    if p in chosen[which]:
                        outs[which][chosen[which].index(p)] = value

        for i in range(len(pairs)):
            for half in (0, 1):
                low = max(starts[i], half * (steps // 2))
                high = min(starts[i] + tiles[i], (half + 1) * (steps // 2))
                if low < high:
                    pl.when((c >= low) & (c < high))(lambda i=i, half=half: write(i, half))

    def right_spec(start, n, split):
        def at(c, d_ref):
            k = jnp.clip(c - start, 0, n - 1)
            return (lax.div(k, jnp.int32(split)), 0, lax.rem(k, jnp.int32(split)))

        return pl.BlockSpec((1, total, tile), at)

    in_specs = [pl.BlockSpec((total, all_rows), lambda c, d_ref: (0, 0))] * len(pairs)
    in_specs += [right_spec(*item) for item in zip(starts, tiles, splits)]
    args = [left for left, _ in pairs] + [right for _, right in pairs]
    if got is None:
        out_shape = [jax.ShapeDtypeStruct((count, rows, columns), BF16)]
        out_specs = [pl.BlockSpec((count, rows, tile), lambda c, d_ref: (0, 0, c))]
    else:
        for start, n in zip(starts, tiles):
            in_specs.append(
                pl.BlockSpec(
                    (count, rows, tile),
                    lambda c, d_ref, start=start, n=n: (0, 0, jnp.clip(c - start, 0, n - 1)),
                )
            )
        args += got
        out_shape = [jax.ShapeDtypeStruct((count // 2, rows, columns // 2), BF16)] * 4
        mid = steps // 2
        first = pl.BlockSpec(
            (count // 2, rows, tile), lambda c, d_ref: (0, 0, jnp.minimum(c, mid - 1))
        )
        second = pl.BlockSpec(
            (count // 2, rows, tile), lambda c, d_ref: (0, 0, jnp.maximum(c - mid, 0))
        )
        out_specs = [first, first, second, second]
    out_shape = out_shape + [TOKEN]
    out_specs = out_specs + [pl.BlockSpec(TOKEN.shape, lambda c, d_ref: (0, 0))]
    in_specs += [ANY] * len(deps)
    return pl.pallas_call(
        body,
        out_shape=out_shape,
        grid_spec=pltpu.PrefetchScalarGridSpec(
            num_scalar_prefetch=1,
            grid=(steps,),
            in_specs=in_specs,
            out_specs=out_specs,
            scratch_shapes=[pltpu.VMEM((len(pairs), count * rows, total), BF16)],
        ),
        compiler_params=pltpu.CompilerParams(vmem_limit_bytes=34 * 2**20),
        cost_estimate=pl.CostEstimate(flops=int(2.5 * 1.15e9), bytes_accessed=1024, transcendentals=0),
        name="gradient",
    )(d.reshape(1).astype(jnp.int32), *args, *deps)


def head_probs(q, k, far, slope):
    scores = lax.dot_general(q, k, (((1,), (1,)), ((), ())), preferred_element_type=F32)
    scores = scores * (HEAD ** (-0.5)) - slope * far
    raised = jnp.exp(scores - jnp.max(scores, axis=-1, keepdims=True))
    return raised * (1.0 / jnp.sum(raised, axis=-1, keepdims=True))


def flat_frames(block):
    sources, _, rows, lanes = block.shape
    if rows % 16 == 0:
        return block.reshape(sources * rows, lanes)
    return block.astype(F32).reshape(sources * rows, lanes).astype(BF16)


def by_source(value, like):
    sources, _, rows, lanes = like
    if rows % 16 == 0:
        return value.astype(BF16).reshape(sources, 1, rows, lanes)
    return value.reshape(sources, 1, rows, lanes).astype(BF16)


def attend(triple, far, slopes, deps=()):
    dp, micro, rows, wide = triple.shape
    frames = dp * rows
    width = wide // 3
    pairs = width // 128
    shape = (dp, 1, rows, 128)

    def body(slope_ref, q_ref, k_ref, v_ref, far_ref, *refs):
        out_ref = refs[-1]
        h = pl.program_id(1)
        q, k, v = (flat_frames(ref[...]) for ref in (q_ref, k_ref, v_ref))
        first = lax.broadcasted_iota(jnp.int32, (frames, 128), 1) < HEAD
        zero = jnp.zeros_like(q)
        outs = []
        for j, own in enumerate((jnp.where(first, q, zero), jnp.where(first, zero, q))):
            probs = head_probs(own, k, far_ref[0], slope_ref[h * 2 + j])
            outs.append(jnp.dot(probs.astype(BF16), v, preferred_element_type=F32))
        out_ref[...] = by_source(jnp.where(first, outs[0], outs[1]), shape)

    def spec(offset):
        return pl.BlockSpec(shape, lambda m, h, s: (0, m, 0, h + offset))

    return pl.pallas_call(
        body,
        out_shape=jax.ShapeDtypeStruct((dp, micro, rows, width), BF16),
        grid_spec=pltpu.PrefetchScalarGridSpec(
            num_scalar_prefetch=1,
            grid=(micro, pairs),
            in_specs=[
                spec(0),
                spec(pairs),
                spec(2 * pairs),
                pl.BlockSpec((1, frames, frames), lambda m, h, s: (m, 0, 0)),
            ]
            + [ANY] * len(deps),
            out_specs=spec(0),
        ),
        compiler_params=pltpu.CompilerParams(vmem_limit_bytes=24 * 2**20),
        cost_estimate=pl.CostEstimate(flops=int(8 * 1.15e9), bytes_accessed=1024, transcendentals=0),
        name="attend",
    )(slopes, triple, triple, triple, far, *deps)


def attend_back(triple, grad, far, slopes, deps=()):
    dp, micro, rows, wide = triple.shape
    frames = dp * rows
    width = wide // 3
    pairs = width // 128
    shape = (dp, 1, rows, 128)
    scale = HEAD ** (-0.5)

    def turned(left, right):
        return lax.dot_general(left, right, (((0,), (0,)), ((), ())), preferred_element_type=F32)

    def body(slope_ref, q_ref, k_ref, v_ref, g_ref, far_ref, *refs):
        out_ref, token_ref = refs[-2:]
        token_ref[...] = jnp.zeros_like(token_ref)
        h = pl.program_id(1)
        q, k, v, g = (flat_frames(ref[...]) for ref in (q_ref, k_ref, v_ref, g_ref))
        first = lax.broadcasted_iota(jnp.int32, (frames, 128), 1) < HEAD
        zero = jnp.zeros_like(q)
        grads = []
        for j in range(2):
            own_q = jnp.where(first, q, zero) if j == 0 else jnp.where(first, zero, q)
            own_g = jnp.where(first, g, zero) if j == 0 else jnp.where(first, zero, g)
            scores = nt(k, own_q) * scale - slope_ref[h * 2 + j] * far_ref[0]
            raised = jnp.exp(scores - jnp.max(scores, axis=0, keepdims=True))
            probs = raised * (1.0 / jnp.sum(raised, axis=0, keepdims=True))
            back = nt(v, own_g)
            back = probs * (back - jnp.sum(back * probs, axis=0, keepdims=True))
            low = back.astype(BF16)
            grads.append(
                (
                    turned(low, k) * scale,
                    jnp.dot(low, q, preferred_element_type=F32) * scale,
                    jnp.dot(probs.astype(BF16), g, preferred_element_type=F32),
                )
            )
        for i in range(3):
            out_ref[i] = by_source(jnp.where(first, grads[0][i], grads[1][i]), shape)

    def spec(offset):
        return pl.BlockSpec(shape, lambda m, h, s: (0, m, 0, h + offset))

    return pl.pallas_call(
        body,
        out_shape=[jax.ShapeDtypeStruct((3, dp, micro, rows, width), BF16), TOKEN],
        grid_spec=pltpu.PrefetchScalarGridSpec(
            num_scalar_prefetch=1,
            grid=(micro, pairs),
            in_specs=[
                spec(0),
                spec(pairs),
                spec(2 * pairs),
                spec(0),
                pl.BlockSpec((1, frames, frames), lambda m, h, s: (m, 0, 0)),
            ]
            + [ANY] * len(deps),
            out_specs=[
                pl.BlockSpec((3,) + shape, lambda m, h, s: (0, 0, m, 0, h)),
                pl.BlockSpec(TOKEN.shape, lambda m, h, s: (0, 0)),
            ],
        ),
        compiler_params=pltpu.CompilerParams(vmem_limit_bytes=24 * 2**20),
        cost_estimate=pl.CostEstimate(flops=int(2 * 1.15e9), bytes_accessed=1024, transcendentals=0),
        name="attend_back",
    )(slopes, triple, triple, triple, grad, far, *deps)


def add_up(values):
    total = values[0].astype(F32)
    for value in values[1:]:
        total = total + value.astype(F32)
    return total.astype(BF16)


class Reduction:
    def __init__(self, pairs, d, dims, deps=()):
        self.pairs = [(left, right if right.ndim == 3 else right[None]) for left, right in pairs]
        self.d = d
        self.dims = dims
        self.sent, self.token = gradient_blocks(self.pairs, d, dims, deps=deps)

    def share(self):
        return flip(self.sent, 1)

    def own(self, got, deps=(), others=()):
        pairs = self.pairs + [pair for other, _ in others for pair in other.pairs]
        gots = [got] + [arrived for _, arrived in others]
        *self.parts, self.token = gradient_blocks(pairs, self.d, self.dims, gots, deps)

    def near(self):
        parts = self.parts
        return [flip(parts[0], 1 << self.dims[0]), flip(parts[2], 1 << self.dims[-1])]

    def near_landed(self, got):
        self.halves = []
        for side, order in ((0, self.dims), (1, self.dims[::-1])):
            stay = self.parts[2 * side + 1]
            left = [bit for bit in self.dims if bit != order[0]]
            shape = (2,) * len(left) + stay.shape[1:]
            values = [stay.reshape(shape), got[side].reshape(shape)]
            self.halves.append((values, list(order[1:]), left))

    def step(self):
        sends, self.stays = [], []
        for values, order, left in self.halves:
            at = left.index(order[0])
            sends.append(add_up([lax.index_in_dim(v, 1, at, keepdims=False) for v in values]))
            self.stays.append([lax.index_in_dim(v, 0, at, keepdims=False) for v in values])
        bits = [order[0] for _, order, _ in self.halves]
        return [flip(sends[0], 1 << bits[0]), flip(sends[1], 1 << bits[1])]

    def landed(self, got):
        halves = []
        for i, (_, order, left) in enumerate(self.halves):
            halves.append((self.stays[i] + [got[i]], order[1:], [b for b in left if b != order[0]]))
        self.halves = halves

    def cross(self):
        while len(self.halves[0][1]) > 1:
            self.landed(self.step())
        return self.step()

    def rows(self):
        self.value = jnp.concatenate([add_up(values) for values, _, _ in self.halves], axis=1)
        self.stage = 0
        return self.value

    def along(self):
        rep = lax.axis_size("rep")
        half = rep // 2
        k = self.stage
        if k < half - 1:
            pairs = [(k, k + 1), (rep - 1 - k, rep - 2 - k)]
        elif k == half - 1:
            pairs = [(k, k + 1), (k + 1, k)]
        else:
            i = rep - 2 - k
            pairs = [(i + 1, i), (rep - 2 - i, rep - 1 - i)]
        return lax.ppermute(self.value, "rep", pairs)

    def along_landed(self, got):
        rep = lax.axis_size("rep")
        z = lax.axis_index("rep")
        k = self.stage
        self.stage += 1
        if k < rep // 2:
            self.value = add_up([self.value, got])
        else:
            i = rep - 2 - k
            self.value = jnp.where((z == i) | (z == rep - 1 - i), got, self.value)

    def finish(self):
        while self.stage < lax.axis_size("rep") - 1:
            self.along_landed(self.along())
        return self.value.astype(F32)


class RepSum:
    def __init__(self, value):
        self.value = value
        self.bits = lax.axis_size("rep").bit_length() - 1
        self.steps = 2 * self.bits
        self.done = 0

    def mine(self):
        k = self.done
        bit = k if k < self.bits else self.steps - 1 - k
        z = lax.axis_index("rep")
        return bit, lax.bitwise_and(lax.shift_right_logical(z, bit), 1)

    def send(self):
        bit, mine = self.mine()
        if self.done >= self.bits:
            return rep_flip(self.value, 1 << bit)
        size = self.value.shape[0] // 2
        sent = lax.dynamic_slice_in_dim(self.value, (1 - mine) * size, size, 0)
        self.keep = lax.dynamic_slice_in_dim(self.value, mine * size, size, 0)
        return rep_flip(sent, 1 << bit)

    def landed(self, got):
        _, mine = self.mine()
        if self.done < self.bits:
            self.value = add_up([self.keep, got])
        else:
            lower = jnp.where(mine == 0, self.value, got)
            upper = jnp.where(mine == 0, got, self.value)
            self.value = jnp.concatenate([lower, upper], axis=0)
        self.done += 1


def nt(left, right):
    return lax.dot_general(left, right, (((1,), (1,)), ((), ())), preferred_element_type=F32)


def hidden_gradient(grad_result, w_down, slope, deps=()):
    total, width = grad_result.shape
    units = w_down.shape[0]
    tile = 512

    def body(grad_ref, w_ref, slope_ref, *refs):
        out_ref, sum_ref = refs[-2:]
        value = nt(grad_ref[...], w_ref[...]) * slope_ref[...].astype(F32)
        out_ref[...] = value.astype(BF16)
        sum_ref[...] = jnp.sum(value, axis=0, keepdims=True)

    return pl.pallas_call(
        body,
        out_shape=[
            jax.ShapeDtypeStruct((total, units), BF16),
            jax.ShapeDtypeStruct((1, units), F32),
        ],
        grid=(units // tile,),
        in_specs=[
            pl.BlockSpec((total, width), lambda c: (0, 0)),
            pl.BlockSpec((tile, width), lambda c: (c, 0)),
            pl.BlockSpec((total, tile), lambda c: (0, c)),
        ]
        + [ANY] * len(deps),
        out_specs=[
            pl.BlockSpec((total, tile), lambda c: (0, c)),
            pl.BlockSpec((1, tile), lambda c: (0, c)),
        ],
        compiler_params=pltpu.CompilerParams(vmem_limit_bytes=24 * 2**20),
        cost_estimate=pl.CostEstimate(flops=int(3 * 1.15e9), bytes_accessed=1024, transcendentals=0),
        name="hidden_gradient",
    )(grad_result, w_down, slope, *deps)


def mixed_gradient(hidden_low, w_up, w_out, mixed, grad_result, gain, deps=()):
    total, units = hidden_low.shape
    width = w_up.shape[0]
    tile = 256

    def body(low_ref, up_ref, out_w_ref, mixed_ref, result_ref, gain_ref, *outs):
        grad_ref, rounded_ref, attended_ref, sums_ref = outs[-4:]
        grad = nt(low_ref[...], up_ref[...])
        unit, scale = norm_parts(mixed_ref[...])
        result = result_ref[...].astype(F32)
        value = result + norm_back(grad, gain_ref[...], unit, scale)
        rounded = value.astype(BF16)
        grad_ref[...] = value
        rounded_ref[...] = rounded
        attended_ref[...] = nt(rounded, out_w_ref[...]).astype(BF16)

        @pl.when(pl.program_id(0) == 0)
        def _():
            sums_ref[...] = jnp.zeros_like(sums_ref)

        for i, terms in enumerate((value, grad * unit, grad, result)):
            sums_ref[pl.ds(i, 1), :] += jnp.sum(terms, axis=0, keepdims=True)

    rows = pl.BlockSpec((tile, width), lambda r: (r, 0))
    whole = [
        pl.BlockSpec((width, units), lambda r: (0, 0)),
        pl.BlockSpec((width, width), lambda r: (0, 0)),
    ]
    return pl.pallas_call(
        body,
        out_shape=[
            jax.ShapeDtypeStruct((total, width), F32),
            jax.ShapeDtypeStruct((total, width), BF16),
            jax.ShapeDtypeStruct((total, width), BF16),
            jax.ShapeDtypeStruct((8, width), F32),
        ],
        grid=(total // tile,),
        in_specs=[pl.BlockSpec((tile, units), lambda r: (r, 0))]
        + whole
        + [rows, rows, pl.BlockSpec((1, width), lambda r: (0, 0))]
        + [ANY] * len(deps),
        out_specs=[rows, rows, rows, pl.BlockSpec((8, width), lambda r: (0, 0))],
        compiler_params=pltpu.CompilerParams(vmem_limit_bytes=44 * 2**20),
        cost_estimate=pl.CostEstimate(flops=int(2 * 1.15e9), bytes_accessed=1024, transcendentals=0),
        name="mixed_gradient",
    )(hidden_low, w_up, w_out, mixed, grad_result, gain.reshape(1, width), *deps)


def normed_gradient(grad_triple, w_qkv, deps=()):
    three, total, width = grad_triple.shape
    tile = 256

    def body(grad_ref, w_ref, *refs):
        out_ref = refs[-1]
        value = nt(grad_ref[0], w_ref[:, pl.ds(0, width)])
        for i in range(1, three):
            value += nt(grad_ref[i], w_ref[:, pl.ds(i * width, width)])
        out_ref[...] = value.astype(BF16)

    return pl.pallas_call(
        body,
        out_shape=jax.ShapeDtypeStruct((total, width), BF16),
        grid=(total // tile,),
        in_specs=[
            pl.BlockSpec((three, tile, width), lambda r: (0, r, 0)),
            pl.BlockSpec((width, three * width), lambda r: (0, 0)),
        ]
        + [ANY] * len(deps),
        out_specs=pl.BlockSpec((tile, width), lambda r: (r, 0)),
        compiler_params=pltpu.CompilerParams(vmem_limit_bytes=24 * 2**20),
        cost_estimate=pl.CostEstimate(flops=int(2 * 1.15e9), bytes_accessed=1024, transcendentals=0),
        name="normed_gradient",
    )(grad_triple, w_qkv, *deps)


def matmul(left, right):
    return jnp.dot(left, right, preferred_element_type=F32)


def matmul_nt(left, right):
    return lax.dot_general(left, right, (((1,), (1,)), ((), ())), preferred_element_type=F32)


def matmul_tn(left, right):
    return lax.dot_general(left, right, (((0,), (0,)), ((), ())), preferred_element_type=F32)


def norm_parts(values):
    average = jnp.mean(values, axis=-1, keepdims=True)
    centred = values - average
    spread = jnp.mean(centred * centred, axis=-1, keepdims=True)
    scale = lax.rsqrt(spread + EPS)
    return centred * scale, scale


def norm_back(grad, gain, unit, scale):
    e = grad * gain
    return scale * (
        e
        - jnp.mean(e, axis=-1, keepdims=True)
        - unit * jnp.mean(e * unit, axis=-1, keepdims=True)
    )


def shards(
    inputs,
    skips,
    cotangent,
    dest_slot,
    pack_segments,
    block_live,
    counts,
    w_skip,
    b_skip,
    g_one,
    b_one,
    w_qkv,
    w_out,
    b_out,
    g_two,
    b_two,
    w_up,
    c_up,
    w_down,
    c_down,
):
    dp = lax.axis_size("dp")
    rep = lax.axis_size("rep")
    d = lax.axis_index("dp")
    z = lax.axis_index("rep")
    micro = inputs.shape[0]
    frames = inputs.shape[2]
    width = inputs.shape[3]
    blocks = dest_slot.shape[2]
    block = frames // blocks
    per_pair = blocks // dp
    total = micro * frames
    bits = dp.bit_length() - 1
    place = jnp.stack([z, lax.rem(d, 8)]).astype(jnp.int32)
    dims = list(range(1, bits))
    small = jnp.concatenate([dest_slot.reshape(-1), block_live.reshape(-1), counts.reshape(-1)])

    own_skip = own_chunk(place, width, [w_skip])
    own_skip, small = together(own_skip, small)
    z_skip = Fetch(own_skip)
    z_skip.rest()
    got = z_skip.send()
    every = small[None]
    for bit in range(bits):
        every = jnp.concatenate([every, flip(every, 1 << bit)], axis=0)
    z_mid = Fetch(own_chunk(place, width, [w_qkv, w_out], z_skip.held[1:]))
    z_mid.rest()
    z_skip.landed(got)

    run_skip = Spread(z_skip.far(), width, [every, z_mid.held[-1]])
    mid = z_mid.send()
    run_skip.near_landed(run_skip.near())

    span = micro * blocks
    numbers = every[:, : 2 * span].reshape(dp, 2 * micro, blocks)
    numbers = jnp.transpose(numbers, (1, 0, 2)).reshape(2 * micro, dp * blocks).astype(F32)
    count_total = jnp.sum(every[:, 2 * span]).astype(F32).reshape(1, 1)
    inner = jnp.arange(frames) % block
    live = inner[None] < jnp.repeat(block_live[:, 0, :], block, axis=1)
    codes = (2 * pack_segments[:, 0, :] + live).astype(F32)
    joined = jnp.concatenate([inputs.reshape(total, width), skips.reshape(total, width)], axis=1)
    far, far_turned, keep_wide, shuffle = plan_order(
        numbers[:micro], numbers[micro:], codes, d, block, [run_skip.pairs[0], joined]
    )
    keep_rows = keep_wide[:, :1]

    run_skip.cross_landed(run_skip.cross(), [shuffle, mid])

    z_mid.landed(mid)
    run_mid = Spread(z_mid.far(), width)
    full_skip, _ = assemble(
        w_skip, run_skip.parts(run_skip.share()), place, 0, 1, [run_mid.start[0]]
    )
    z_up = Fetch(own_chunk(place, width, [w_up], [run_mid.start[0]]))
    z_up.rest()
    base = matmul(joined, full_skip) + b_skip
    unit_one, scale_one = norm_parts(base)
    own_normed = (unit_one * g_one + b_one).astype(BF16)
    sent = matmul(shuffle, own_normed).astype(BF16)
    run_mid.near_landed(run_mid.near(), [sent, z_up.held[-1]])

    def exchange(values):
        values = values.reshape(dp, total // dp, width)
        got = lax.all_to_all(values, "dp", split_axis=0, concat_axis=0, tiled=True)
        return got.reshape(total, width)

    normed = exchange(sent)
    up = z_up.send([sent])
    z_down = Fetch(own_chunk(place, width, [w_down], [z_up.held[-1], sent]))
    z_down.rest()
    run_mid.cross_landed(run_mid.cross(), [up, z_down.held[-1], normed])
    z_up.landed(up)

    other = run_mid.share()
    run_up = Spread(z_up.far(), width, [run_mid.every])
    run_up.near_landed(run_up.near(), [other])
    shard_rows = w_qkv.shape[0] // 8
    parts_mid = run_mid.parts(other)
    full_qkv, _ = assemble(w_qkv, parts_mid, place, 0, 3)

    triple = matmul(normed, full_qkv).astype(BF16)
    triple = triple.reshape(dp, micro, per_pair * block, 3 * width)
    slopes = 2.0 ** (-8.0 * (jnp.arange(HEADS, dtype=F32) + 1.0) / HEADS)
    attended = attend(triple, far, slopes, [run_up.pairs[0]])
    down = z_down.send()
    run_up.cross_landed(run_up.cross(), [attended, down])
    z_down.landed(down)

    attended = exchange(attended)
    other = run_up.share()
    run_down = Spread(z_down.far(), width, [run_up.every])
    down = run_down.near()
    full_out, out_token = assemble(w_out, parts_mid, place, 3 * shard_rows, 1, [run_up.every])
    full_up, up_token = assemble(w_up, run_up.parts(other), place, 0, w_up.shape[1] // width)
    attended, out_token, up_token = together(attended, out_token, up_token)

    attended = matmul_tn(shuffle, attended).astype(BF16)
    mixed = base + matmul(attended, full_out) + (b_out + out_token[0, 0])
    unit_two, scale_two = norm_parts(mixed)
    normed_two = (unit_two * g_two + b_two).astype(BF16)
    count_total = count_total + up_token[:1, :1]
    for step in rep_steps(rep):
        count_total = count_total + rep_flip(count_total, step)
    share = counts[0, 0].astype(F32) * (dp * rep) / count_total[0, 0]
    run_down.near_landed(down, [up_token])
    down = run_down.cross()
    hidden = matmul(normed_two, full_up) + (c_up + run_down.token[0, 0])
    phi = 0.5 * (1.0 + lax.erf(hidden * (0.5**0.5)))
    active = (hidden * phi).astype(BF16)
    slope = (phi + hidden * jnp.exp(-0.5 * hidden * hidden) * ((2 * jnp.pi) ** -0.5)).astype(BF16)
    scaled = (cotangent.reshape(total, width).astype(F32) * share).astype(BF16)
    grad_result = scaled * keep_rows.astype(BF16)
    red_down = Reduction([(active, grad_result)], d, dims)

    down_got = red_down.share()
    run_down.cross_landed(down, [red_down.sent])
    full_down, _ = assemble(w_down, run_down.parts(run_down.share()), place, 0, 1)

    hidden_low, sum_hidden = hidden_gradient(grad_result, full_down, slope)
    red_up = Reduction([(normed_two, hidden_low)], d, dims)
    up_got = red_up.share()
    red_down.own(down_got, [red_up.sent])
    flying = red_down.near()
    grad_mixed, mixed_low, grad_attended, sums_mixed = mixed_gradient(
        hidden_low, full_up, full_out, mixed, grad_result, g_two, [red_down.token]
    )
    red_out = Reduction([(attended, mixed_low)], d, dims)
    out_got = red_out.share()
    flying, sums_mixed = together(flying, sums_mixed)
    red_down.near_landed(flying)

    down_flying = red_down.cross()
    sent = matmul(shuffle, grad_attended).astype(BF16)
    grad_attended = exchange(sent)
    red_up.own(up_got, [sent], [(red_out, out_got)])
    flying = red_up.near()
    down_flying, token = together(down_flying, red_up.token)
    red_down.landed(down_flying)
    red_down.rows()

    line = red_down.along()
    grad_attended = grad_attended.reshape(dp, micro, per_pair * block, width)
    grad_triple, token = attend_back(
        triple, grad_attended, far_turned, slopes, [red_down.value, token]
    )
    grad_triple = grad_triple.reshape(3, total, width)

    sent = normed_gradient(grad_triple, full_qkv)
    grad_normed = exchange(sent)
    flying, line, token = together(flying, line, token)
    red_mid = Reduction([(normed, grad_triple)], d, dims, [sent, token])
    grad_normed, token = together(grad_normed, red_mid.token)
    red_up.near_landed(flying)
    red_down.along_landed(line)
    up_flying = red_up.cross()
    line = red_down.along()

    mid_got = red_mid.share()
    grad_normed = matmul_tn(shuffle, grad_normed)
    grad_base = grad_mixed + norm_back(grad_normed, g_one, unit_one, scale_one)
    base_low = grad_base.astype(BF16)
    red_skip = Reduction([(joined, base_low)], d, dims, [token])
    skip_got = red_skip.share()
    vectors = (
        jnp.sum(grad_base, axis=0),
        jnp.sum(grad_normed * unit_one, axis=0),
        jnp.sum(grad_normed, axis=0),
        sums_mixed[0],
        sums_mixed[1],
        sums_mixed[2],
        sum_hidden[0],
        sums_mixed[3],
    )
    lengths = [v.shape[0] for v in vectors]
    summed = jnp.concatenate(vectors).reshape(-1, 128)
    for bit in range(bits - 1):
        summed = summed + flip(summed, 1 << bit)
    up_flying, token = together(up_flying, red_skip.token)
    red_up.landed(up_flying)
    red_up.rows()
    up_line = red_up.along()
    red_mid.own(mid_got, [token])
    summed, token = together(summed, red_mid.token)

    flying = red_mid.near()
    red_skip.own(skip_got, [token])
    skip_flying = red_skip.near()
    line, token = together(line, red_skip.token)
    red_down.along_landed(line)
    line = red_down.along()
    result = mixed + matmul(active, full_down) + (c_down + token[0, 0])
    output = (result * keep_rows).astype(BF16)
    grad_joined = matmul_nt(base_low, full_skip).astype(BF16)
    flying, up_line, grad_joined, summed = together(flying, up_line, grad_joined, summed)
    red_mid.near_landed(flying)
    red_up.along_landed(up_line)

    flying = red_mid.cross()
    up_line = red_up.along()
    flying, line, skip_flying, summed = together(flying, line, skip_flying, summed)
    red_down.along_landed(line)
    red_skip.near_landed(skip_flying)
    red_mid.landed(flying)

    mid_sum = RepSum(red_mid.rows())
    skip_flying = red_skip.cross()
    got = mid_sum.send()
    last = flip(summed, 1 << (bits - 1))
    got, up_line, skip_flying, last = together(got, up_line, skip_flying, last)
    mid_sum.landed(got)
    red_up.along_landed(up_line)
    red_skip.landed(skip_flying)
    summed = summed + last
    up_line = red_up.along()
    skip_columns = w_skip.shape[1]
    extra = jnp.pad(summed.reshape(-1), (0, -summed.size % (16 * rep * skip_columns)))
    extra = extra.reshape(-1, skip_columns).astype(BF16)
    skip_sum = RepSum(jnp.concatenate([red_skip.rows(), extra], axis=0))
    while mid_sum.done < mid_sum.steps:
        mid_got, skip_got = mid_sum.send(), skip_sum.send()
        if mid_sum.done == mid_sum.steps - 1:
            mid_got, skip_got, up_line = together(mid_got, skip_got, up_line)
        else:
            mid_got, skip_got = together(mid_got, skip_got)
        mid_sum.landed(mid_got)
        skip_sum.landed(skip_got)
    skip_sum.landed(skip_sum.send())
    red_up.along_landed(up_line)
    final_mid = mid_sum.value.astype(F32)
    final_skip = skip_sum.value.astype(F32)
    own_rows = w_skip.shape[0] * rep // dp
    summed = final_skip[own_rows:].reshape(-1)
    final_up = red_up.finish()
    units = c_up.shape[0]
    finals = [
        red_down.finish(),
        final_up[:, :units],
        final_up[:, units:],
        final_mid,
        final_skip[:own_rows],
    ]
    sums = []
    offset = 0
    for length in lengths:
        sums.append(summed[offset : offset + length])
        offset += length

    def as_owned(values):
        return values.reshape(inputs.shape)

    return (
        as_owned(output),
        as_owned(grad_joined[:, :width]),
        as_owned(grad_joined[:, width:]),
        finals[4],
        sums[0],
        sums[1],
        sums[2],
        finals[3],
        finals[2],
        sums[3],
        sums[4],
        sums[5],
        finals[1],
        sums[6],
        finals[0],
        sums[7],
    )


def solution(mesh):
    frames = P(None, "rep", "dp", None)
    slots = P(None, "rep", "dp")
    rows = P("rep", None)
    whole = P()
    in_specs = (
        (frames,) * 3
        + (slots,) * 3
        + (P("dp", "rep"), rows, whole, whole, whole, rows, rows)
        + (whole,) * 3
        + (rows, whole, rows, whole)
    )
    split = P("dp", None)
    out_specs = (
        (frames,) * 3
        + (split,)
        + (whole,) * 3
        + (split, split)
        + (whole,) * 3
        + (split, whole, split, whole)
    )
    return jax.shard_map(shards, mesh=mesh, in_specs=in_specs, out_specs=out_specs, check_vma=False)
```

```python
import jax
import jax.numpy as jnp
from jax import lax
from jax.experimental import pallas as pl
from jax.experimental.pallas import tpu as pltpu
from jax.sharding import PartitionSpec as P

HEADS = 16
HEAD = 64
EPS = 1e-05
F32 = jnp.float32
BF16 = jnp.bfloat16
TOKEN = jax.ShapeDtypeStruct((8, 128), F32)
ANY = pl.BlockSpec(memory_space=pl.ANY)
LIGHT = pl.CostEstimate(flops=1024, bytes_accessed=1024, transcendentals=0)


def flip(value, bit):
    n = lax.axis_size("dp")
    return lax.ppermute(value, "dp", [(i, i ^ bit) for i in range(n)])


def rep_flip(value, bit):
    n = lax.axis_size("rep")
    return lax.ppermute(value, "rep", [(i, i ^ bit) for i in range(n)])


def after(value, *earlier):
    return lax.optimization_barrier((value,) + earlier)[0]


def together(*values):
    return lax.optimization_barrier(values)


def assemble(w_local, parts, place, row_at, tiles, deps=()):
    rep = lax.axis_size("rep")
    shard_rows, columns = w_local.shape
    rows = shard_rows // 8
    tile = columns // tiles
    half = tile // 2
    chunk_rows = parts[0][0].shape[0] // (len(parts[0][1]) * (rep - 1))
    arrays = [part[0] for part in parts]
    count = 1 + sum(len(part[1]) for part in parts) * (rep - 1) * tiles

    def body(place_ref, local_ref, *refs):
        out_ref, token_ref, sems = refs[-3:]
        token_ref[...] = jnp.zeros_like(token_ref)
        z = place_ref[0]
        e = place_ref[1]
        copies = [
            pltpu.make_async_copy(
                local_ref,
                out_ref.at[pl.ds(pl.multiple_of(z * shard_rows, 16), shard_rows), :],
                sems.at[0],
            )
        ]
        for ref, (_, runs) in zip(refs, parts):
            for k, (side, rel) in enumerate(runs):
                chunk = jnp.bitwise_xor(e, rel)
                for s, apart in enumerate(far_order(rep), 1):
                    shard = jnp.bitwise_xor(z, apart)
                    start = pl.multiple_of(shard * shard_rows + chunk * rows, 16)
                    for t in range(tiles):
                        at = (k * (rep - 1) + s - 1) * chunk_rows + row_at + t * rows
                        copies.append(
                            pltpu.make_async_copy(
                                ref.at[pl.ds(at, rows), :],
                                out_ref.at[pl.ds(start, rows), pl.ds(t * tile + side * half, half)],
                                sems.at[len(copies)],
                            )
                        )
        for copy in copies:
            copy.start()
        for copy in copies:
            copy.wait()

    return pl.pallas_call(
        body,
        out_shape=[jax.ShapeDtypeStruct((shard_rows * rep, columns), w_local.dtype), TOKEN],
        grid=(1,),
        in_specs=[pl.BlockSpec(memory_space=pltpu.SMEM)] + [ANY] * (1 + len(parts) + len(deps)),
        out_specs=[
            pl.BlockSpec((shard_rows * rep, columns), lambda i: (0, 0)),
            pl.BlockSpec(TOKEN.shape, lambda i: (0, 0)),
        ],
        scratch_shapes=[pltpu.SemaphoreType.DMA((count,))],
        compiler_params=pltpu.CompilerParams(vmem_limit_bytes=26 * 2**20),
        cost_estimate=pl.CostEstimate(flops=int(1.5 * 1.15e9), bytes_accessed=1024, transcendentals=0),
        name="assemble",
    )(place, w_local, *arrays, *deps)


def own_chunk(place, width, shards_local, deps=()):
    items = []
    for which, w_local in enumerate(shards_local):
        for t in range(w_local.shape[1] // width):
            items.append((which, w_local.shape[0] // 8, t * width))
    total = sum(item[1] for item in items)

    def body(place_ref, *refs):
        out_ref, sems = refs[-2:]
        copies = []
        at = 0
        for which, rows, column in items:
            start = pl.multiple_of(place_ref[1] * rows, 16)
            copies.append(
                pltpu.make_async_copy(
                    refs[which].at[pl.ds(start, rows), pl.ds(column, width)],
                    out_ref.at[pl.ds(at, rows), :],
                    sems.at[len(copies)],
                )
            )
            at += rows
        for copy in copies:
            copy.start()
        for copy in copies:
            copy.wait()

    return pl.pallas_call(
        body,
        out_shape=jax.ShapeDtypeStruct((total, width), shards_local[0].dtype),
        grid=(1,),
        in_specs=[pl.BlockSpec(memory_space=pltpu.SMEM)]
        + [ANY] * (len(shards_local) + len(deps)),
        out_specs=pl.BlockSpec((total, width), lambda i: (0, 0)),
        scratch_shapes=[pltpu.SemaphoreType.DMA((len(items),))],
        compiler_params=pltpu.CompilerParams(vmem_limit_bytes=24 * 2**20),
        cost_estimate=LIGHT,
        name="own_chunk",
    )(place, *shards_local, *deps)


def pack(arrays, outs, deps=()):
    count = sum(len(out) for out in outs)

    def body(*refs):
        sources, targets = refs[: len(arrays)], refs[-2 - len(outs) : -2]
        token_ref, sems = refs[-2:]
        token_ref[...] = jnp.zeros_like(token_ref)
        copies = []
        for target, out in zip(targets, outs):
            at = 0
            for which, row, rows, column, columns in out:
                copies.append(
                    pltpu.make_async_copy(
                        sources[which].at[pl.ds(row, rows), pl.ds(column, columns)],
                        target.at[pl.ds(at, rows), :],
                        sems.at[len(copies)],
                    )
                )
                at += rows
        for copy in copies:
            copy.start()
        for copy in copies:
            copy.wait()

    return pl.pallas_call(
        body,
        out_shape=[
            jax.ShapeDtypeStruct((sum(item[2] for item in out), out[0][4]), arrays[0].dtype)
            for out in outs
        ]
        + [TOKEN],
        grid=(1,),
        in_specs=[ANY] * (len(arrays) + len(deps)),
        out_specs=[
            pl.BlockSpec((sum(item[2] for item in out), out[0][4]), lambda i: (0, 0))
            for out in outs
        ]
        + [pl.BlockSpec(TOKEN.shape, lambda i: (0, 0))],
        scratch_shapes=[pltpu.SemaphoreType.DMA((count,))],
        compiler_params=pltpu.CompilerParams(vmem_limit_bytes=24 * 2**20),
        cost_estimate=LIGHT,
        name="pack",
    )(*arrays, *deps)


def far_order(rep):
    order = [0]
    for bit in reversed(range(rep.bit_length() - 1)):
        order = order + [distance ^ (1 << bit) for distance in order]
    return order[1:]


class Spread:
    def __init__(self, gots, width, deps=()):
        self.half = width // 2
        rows = sum(got.shape[0] for got in gots)
        items = [(i, 0, got.shape[0]) for i, got in enumerate(gots)]
        *self.start, _ = pack(
            gots, [[item + (column, self.half) for item in items] for column in (0, self.half)], deps
        )
        self.n = rows

    def near(self):
        return [flip(self.start[0], 2), flip(self.start[1], 4)]

    def near_landed(self, got, deps=()):
        whole = [(i, 0, self.n, 0, self.half) for i in range(4)]
        *self.pairs, self.token = pack(
            [self.start[0], got[0], self.start[1], got[1]], [whole[:2], whole[2:]], deps
        )

    def cross(self):
        return [flip(self.pairs[0], 4), flip(self.pairs[1], 2)]

    def cross_landed(self, got, deps=()):
        whole = [(i, 0, 2 * self.n, 0, self.half) for i in range(4)]
        self.every, self.token = pack([self.pairs[0], got[0], self.pairs[1], got[1]], [whole], deps)

    def share(self):
        return flip(self.every, 1)

    def parts(self, other):
        runs = [(0, 0), (0, 2), (0, 4), (0, 6), (1, 0), (1, 4), (1, 2), (1, 6)]
        return [(self.every, runs), (other, [(side, rel | 1) for side, rel in runs])]


def rep_steps(rep):
    return [1 << bit for bit in reversed(range(rep.bit_length() - 1))]


class Fetch:
    def __init__(self, own):
        self.held = [own]
        self.steps = rep_steps(lax.axis_size("rep"))

    def send(self, deps=()):
        sent = self.held[0]
        if len(self.held) > 1:
            whole = [(i, 0, a.shape[0], 0, a.shape[1]) for i, a in enumerate(self.held)]
            sent, _ = pack(self.held, [whole], deps)
        return rep_flip(sent, self.steps[len(self.held) - 1])

    def landed(self, got):
        self.held.append(got)

    def rest(self):
        while len(self.held) < len(self.steps):
            self.landed(self.send())

    def far(self):
        return self.held[1:]


def plan_order(all_slots, all_live, codes, d, block, deps=()):
    micro, owners = all_slots.shape
    frames = codes.shape[1]
    blocks = frames // block
    dp = owners // blocks
    per_pair = blocks // dp
    total = micro * frames

    def column(row):
        return jnp.broadcast_to(row, (128, row.shape[1])).T[:, :1]

    def as_row(values):
        return jnp.broadcast_to(values, (values.shape[0], 128)).T[:1, :]

    def body(d_ref, slots_ref, live_ref, codes_ref, *refs):
        far_ref, turned_ref, keep_ref, shuffle_ref = refs[-4:]
        me = d_ref[0]
        lane = lax.broadcasted_iota(jnp.int32, (1, owners), 1)
        source = jnp.bitwise_xor(lax.div(lane, jnp.int32(blocks)), me)
        first_slot = (source * blocks).astype(F32) + lax.rem(lane, jnp.int32(blocks)).astype(F32)
        source_col = column(source.astype(F32))
        frame = lax.broadcasted_iota(jnp.int32, (frames, 1), 0)
        block_of = lax.div(frame, jnp.int32(block)).astype(F32)
        inner = lax.rem(frame, jnp.int32(block)).astype(F32)
        low = (me * blocks).astype(F32)
        rows = []
        for m in range(micro):
            slots = slots_ref[pl.ds(m, 1), :]
            slots_col = column(slots)
            same = source_col == source.astype(F32)
            rank = jnp.sum(jnp.where(same & (slots_col < slots), 1.0, 0.0), axis=0, keepdims=True)
            here = (slots >= low) & (slots < low + blocks)
            arrive = source.astype(F32) * per_pair + rank - (me * per_pair).astype(F32)
            arrive = jnp.where(here, arrive, -1.0)
            placed = jnp.sum(
                jnp.where(arrive == block_of, slots - low, 0.0), axis=1, keepdims=True
            )
            position = placed * block + inner
            at = lax.broadcasted_iota(jnp.int32, (1, frames), 1).astype(F32)
            code = jnp.sum(
                jnp.where(at == position, codes_ref[pl.ds(m, 1), :], 0.0), axis=1, keepdims=True
            )
            position_row, code_row = as_row(position), as_row(code)
            segment, segment_row = jnp.floor(code * 0.5), jnp.floor(code_row * 0.5)
            live_row = code_row - 2.0 * segment_row
            distance = jnp.abs(position - position_row)
            allowed = (segment == segment_row) & ((live_row > 0.5) | (distance < 0.5))
            far_ref[m] = jnp.where(allowed, distance, 1e32)
            live_col = code - 2.0 * segment
            allowed = (segment == segment_row) & ((live_col > 0.5) | (distance < 0.5))
            turned_ref[m] = jnp.where(allowed, distance, 1e32)
            own = lane < blocks
            mine = jnp.sum(
                jnp.where(own & (lane.astype(F32) == block_of), slots, 0.0), axis=1, keepdims=True
            )
            alive = jnp.sum(
                jnp.where(first_slot == mine, live_ref[pl.ds(m, 1), :], 0.0), axis=1, keepdims=True
            )
            keep_ref[pl.ds(m * frames, frames), :] = jnp.broadcast_to(
                jnp.where(inner < alive, 1.0, 0.0), (frames, 128)
            )
            my_rank = jnp.sum(
                jnp.where(own & (lane.astype(F32) == block_of), rank, 0.0), axis=1, keepdims=True
            )
            target = jnp.floor((my_rank + 0.5) / per_pair)
            row = (target * micro + m) * per_pair + (my_rank - target * per_pair)
            rows.append(as_row(row * block + inner))
        goal = jnp.concatenate(rows, axis=1)
        spot = lax.broadcasted_iota(jnp.int32, (total, total), 0).astype(F32)
        shuffle_ref[...] = jnp.where(spot == goal, 1.0, 0.0).astype(BF16)

    vmem = pl.BlockSpec(memory_space=pltpu.VMEM)
    return pl.pallas_call(
        body,
        out_shape=[
            jax.ShapeDtypeStruct((micro, frames, frames), F32),
            jax.ShapeDtypeStruct((micro, frames, frames), F32),
            jax.ShapeDtypeStruct((total, 128), F32),
            jax.ShapeDtypeStruct((total, total), BF16),
        ],
        in_specs=[pl.BlockSpec(memory_space=pltpu.SMEM), vmem, vmem, vmem] + [ANY] * len(deps),
        out_specs=[vmem, vmem, vmem, vmem],
        compiler_params=pltpu.CompilerParams(vmem_limit_bytes=24 * 2**20),
        cost_estimate=LIGHT,
        name="plan_order",
    )(d.reshape(1).astype(jnp.int32), all_slots, all_live, codes, *deps)


def gradient_blocks(pairs, d, dims, got=None, deps=()):
    dp = lax.axis_size("dp")
    total, all_rows = pairs[0][0].shape
    widths = [right.shape[2] for _, right in pairs]
    columns = sum(right.shape[0] * right.shape[2] for _, right in pairs)
    rows = all_rows // dp
    count = dp // 2
    odd = 1 if got is None else 0
    tile = min(min(widths), 512)
    splits = [width // tile for width in widths]
    tiles = [right.shape[0] * split for (_, right), split in zip(pairs, splits)]
    steps = sum(tiles)
    starts = [sum(tiles[:i]) for i in range(len(tiles))]

    def distance(p):
        rel = odd
        for k, bit in enumerate(dims):
            rel += ((p >> (len(dims) - 1 - k)) & 1) << bit
        return rel

    upper = [p for p in range(count) if p >= count // 2]
    lower = [p for p in range(count) if p < count // 2]
    odds = [p for p in range(count) if p % 2 == 1]
    evens = [p for p in range(count) if p % 2 == 0]
    chosen = (upper, lower, odds, evens)

    if rows % 128 != 0:
        products = []
        for left, right in pairs:
            flat = jnp.transpose(right, (1, 0, 2)).reshape(total, -1)
            products.append(matmul_tn(left, flat))
        product = jnp.concatenate(products, axis=1).reshape(dp, rows, columns)
        rel = jnp.array([distance(p) for p in range(count)], jnp.int32)
        product = product[jnp.bitwise_xor(rel, d)]
        token = jnp.zeros(TOKEN.shape, F32) + product[0, :1, :1]
        if got is None:
            return [product.astype(BF16), token]
        product = (product + jnp.concatenate(got, axis=2).astype(F32)).astype(BF16)
        half = columns // 2
        return [
            jnp.stack([product[p, :, side * half : (side + 1) * half] for p in ps])
            for side, ps in zip((0, 0, 1, 1), chosen)
        ] + [token]

    def body(d_ref, *refs):
        lefts = refs[: len(pairs)]
        rights = refs[len(pairs) : 2 * len(pairs)]
        got_refs = refs[2 * len(pairs) : 3 * len(pairs)]
        token_ref, turned_ref = refs[-2:]
        outs = refs[-3:-2] if got is None else refs[-6:-2]
        c = pl.program_id(0)

        @pl.when(c == 0)
        def _():
            token_ref[...] = jnp.zeros_like(token_ref)
            for i, left_ref in enumerate(lefts):
                for p in range(count):
                    at = pl.multiple_of(jnp.bitwise_xor(d_ref[0], distance(p)) * rows, 128)
                    turned_ref[i, pl.ds(p * rows, rows), :] = left_ref[:, pl.ds(at, rows)].T

        def piece(i, p):
            return jnp.dot(
                turned_ref[i, pl.ds(p * rows, rows), :], rights[i][0], preferred_element_type=F32
            )

        def write(i, half):
            for p in range(count):
                value = piece(i, p)
                if got is None:
                    outs[0][p] = value.astype(BF16)
                    continue
                value = (value + got_refs[i][p].astype(F32)).astype(BF16)
                for which in (2 * half, 2 * half + 1):
                    if p in chosen[which]:
                        outs[which][chosen[which].index(p)] = value

        for i in range(len(pairs)):
            for half in (0, 1):
                low = max(starts[i], half * (steps // 2))
                high = min(starts[i] + tiles[i], (half + 1) * (steps // 2))
                if low < high:
                    pl.when((c >= low) & (c < high))(lambda i=i, half=half: write(i, half))

    def right_spec(start, n, split):
        def at(c, d_ref):
            k = jnp.clip(c - start, 0, n - 1)
            return (lax.div(k, jnp.int32(split)), 0, lax.rem(k, jnp.int32(split)))

        return pl.BlockSpec((1, total, tile), at)

    in_specs = [pl.BlockSpec((total, all_rows), lambda c, d_ref: (0, 0))] * len(pairs)
    in_specs += [right_spec(*item) for item in zip(starts, tiles, splits)]
    args = [left for left, _ in pairs] + [right for _, right in pairs]
    if got is None:
        out_shape = [jax.ShapeDtypeStruct((count, rows, columns), BF16)]
        out_specs = [pl.BlockSpec((count, rows, tile), lambda c, d_ref: (0, 0, c))]
    else:
        for start, n in zip(starts, tiles):
            in_specs.append(
                pl.BlockSpec(
                    (count, rows, tile),
                    lambda c, d_ref, start=start, n=n: (0, 0, jnp.clip(c - start, 0, n - 1)),
                )
            )
        args += got
        out_shape = [jax.ShapeDtypeStruct((count // 2, rows, columns // 2), BF16)] * 4
        mid = steps // 2
        first = pl.BlockSpec(
            (count // 2, rows, tile), lambda c, d_ref: (0, 0, jnp.minimum(c, mid - 1))
        )
        second = pl.BlockSpec(
            (count // 2, rows, tile), lambda c, d_ref: (0, 0, jnp.maximum(c - mid, 0))
        )
        out_specs = [first, first, second, second]
    out_shape = out_shape + [TOKEN]
    out_specs = out_specs + [pl.BlockSpec(TOKEN.shape, lambda c, d_ref: (0, 0))]
    in_specs += [ANY] * len(deps)
    return pl.pallas_call(
        body,
        out_shape=out_shape,
        grid_spec=pltpu.PrefetchScalarGridSpec(
            num_scalar_prefetch=1,
            grid=(steps,),
            in_specs=in_specs,
            out_specs=out_specs,
            scratch_shapes=[pltpu.VMEM((len(pairs), count * rows, total), BF16)],
        ),
        compiler_params=pltpu.CompilerParams(vmem_limit_bytes=34 * 2**20),
        cost_estimate=pl.CostEstimate(flops=int(2.5 * 1.15e9), bytes_accessed=1024, transcendentals=0),
        name="gradient",
    )(d.reshape(1).astype(jnp.int32), *args, *deps)


def head_probs(q, k, far, slope):
    scores = lax.dot_general(q, k, (((1,), (1,)), ((), ())), preferred_element_type=F32)
    scores = scores * (HEAD ** (-0.5)) - slope * far
    raised = jnp.exp(scores - jnp.max(scores, axis=-1, keepdims=True))
    return raised * (1.0 / jnp.sum(raised, axis=-1, keepdims=True))


def flat_frames(block):
    sources, _, rows, lanes = block.shape
    if rows % 16 == 0:
        return block.reshape(sources * rows, lanes)
    return block.astype(F32).reshape(sources * rows, lanes).astype(BF16)


def by_source(value, like):
    sources, _, rows, lanes = like
    if rows % 16 == 0:
        return value.astype(BF16).reshape(sources, 1, rows, lanes)
    return value.reshape(sources, 1, rows, lanes).astype(BF16)


def attend(triple, far, slopes, deps=()):
    dp, micro, rows, wide = triple.shape
    frames = dp * rows
    width = wide // 3
    pairs = width // 128
    shape = (dp, 1, rows, 128)

    def body(slope_ref, q_ref, k_ref, v_ref, far_ref, *refs):
        out_ref = refs[-1]
        h = pl.program_id(1)
        q, k, v = (flat_frames(ref[...]) for ref in (q_ref, k_ref, v_ref))
        first = lax.broadcasted_iota(jnp.int32, (frames, 128), 1) < HEAD
        zero = jnp.zeros_like(q)
        outs = []
        for j, own in enumerate((jnp.where(first, q, zero), jnp.where(first, zero, q))):
            probs = head_probs(own, k, far_ref[0], slope_ref[h * 2 + j])
            outs.append(jnp.dot(probs.astype(BF16), v, preferred_element_type=F32))
        out_ref[...] = by_source(jnp.where(first, outs[0], outs[1]), shape)

    def spec(offset):
        return pl.BlockSpec(shape, lambda m, h, s: (0, m, 0, h + offset))

    return pl.pallas_call(
        body,
        out_shape=jax.ShapeDtypeStruct((dp, micro, rows, width), BF16),
        grid_spec=pltpu.PrefetchScalarGridSpec(
            num_scalar_prefetch=1,
            grid=(micro, pairs),
            in_specs=[
                spec(0),
                spec(pairs),
                spec(2 * pairs),
                pl.BlockSpec((1, frames, frames), lambda m, h, s: (m, 0, 0)),
            ]
            + [ANY] * len(deps),
            out_specs=spec(0),
        ),
        compiler_params=pltpu.CompilerParams(vmem_limit_bytes=24 * 2**20),
        cost_estimate=pl.CostEstimate(flops=int(8 * 1.15e9), bytes_accessed=1024, transcendentals=0),
        name="attend",
    )(slopes, triple, triple, triple, far, *deps)


def attend_back(triple, grad, far, slopes, deps=()):
    dp, micro, rows, wide = triple.shape
    frames = dp * rows
    width = wide // 3
    pairs = width // 128
    shape = (dp, 1, rows, 128)
    scale = HEAD ** (-0.5)

    def turned(left, right):
        return lax.dot_general(left, right, (((0,), (0,)), ((), ())), preferred_element_type=F32)

    def body(slope_ref, q_ref, k_ref, v_ref, g_ref, far_ref, *refs):
        out_ref, token_ref = refs[-2:]
        token_ref[...] = jnp.zeros_like(token_ref)
        h = pl.program_id(1)
        q, k, v, g = (flat_frames(ref[...]) for ref in (q_ref, k_ref, v_ref, g_ref))
        first = lax.broadcasted_iota(jnp.int32, (frames, 128), 1) < HEAD
        zero = jnp.zeros_like(q)
        grads = []
        for j in range(2):
            own_q = jnp.where(first, q, zero) if j == 0 else jnp.where(first, zero, q)
            own_g = jnp.where(first, g, zero) if j == 0 else jnp.where(first, zero, g)
            scores = nt(k, own_q) * scale - slope_ref[h * 2 + j] * far_ref[0]
            raised = jnp.exp(scores - jnp.max(scores, axis=0, keepdims=True))
            probs = raised * (1.0 / jnp.sum(raised, axis=0, keepdims=True))
            back = nt(v, own_g)
            back = probs * (back - jnp.sum(back * probs, axis=0, keepdims=True))
            low = back.astype(BF16)
            grads.append(
                (
                    turned(low, k) * scale,
                    jnp.dot(low, q, preferred_element_type=F32) * scale,
                    jnp.dot(probs.astype(BF16), g, preferred_element_type=F32),
                )
            )
        for i in range(3):
            out_ref[i] = by_source(jnp.where(first, grads[0][i], grads[1][i]), shape)

    def spec(offset):
        return pl.BlockSpec(shape, lambda m, h, s: (0, m, 0, h + offset))

    return pl.pallas_call(
        body,
        out_shape=[jax.ShapeDtypeStruct((3, dp, micro, rows, width), BF16), TOKEN],
        grid_spec=pltpu.PrefetchScalarGridSpec(
            num_scalar_prefetch=1,
            grid=(micro, pairs),
            in_specs=[
                spec(0),
                spec(pairs),
                spec(2 * pairs),
                spec(0),
                pl.BlockSpec((1, frames, frames), lambda m, h, s: (m, 0, 0)),
            ]
            + [ANY] * len(deps),
            out_specs=[
                pl.BlockSpec((3,) + shape, lambda m, h, s: (0, 0, m, 0, h)),
                pl.BlockSpec(TOKEN.shape, lambda m, h, s: (0, 0)),
            ],
        ),
        compiler_params=pltpu.CompilerParams(vmem_limit_bytes=24 * 2**20),
        cost_estimate=pl.CostEstimate(flops=int(2 * 1.15e9), bytes_accessed=1024, transcendentals=0),
        name="attend_back",
    )(slopes, triple, triple, triple, grad, far, *deps)


def add_up(values):
    total = values[0].astype(F32)
    for value in values[1:]:
        total = total + value.astype(F32)
    return total.astype(BF16)


class Reduction:
    def __init__(self, pairs, d, dims, deps=()):
        self.pairs = [(left, right if right.ndim == 3 else right[None]) for left, right in pairs]
        self.d = d
        self.dims = dims
        self.sent, self.token = gradient_blocks(self.pairs, d, dims, deps=deps)

    def share(self):
        return flip(self.sent, 1)

    def own(self, got, deps=(), others=()):
        pairs = self.pairs + [pair for other, _ in others for pair in other.pairs]
        gots = [got] + [arrived for _, arrived in others]
        *self.parts, self.token = gradient_blocks(pairs, self.d, self.dims, gots, deps)

    def near(self):
        parts = self.parts
        return [flip(parts[0], 1 << self.dims[0]), flip(parts[2], 1 << self.dims[-1])]

    def near_landed(self, got):
        self.halves = []
        for side, order in ((0, self.dims), (1, self.dims[::-1])):
            stay = self.parts[2 * side + 1]
            left = [bit for bit in self.dims if bit != order[0]]
            shape = (2,) * len(left) + stay.shape[1:]
            values = [stay.reshape(shape), got[side].reshape(shape)]
            self.halves.append((values, list(order[1:]), left))

    def step(self):
        sends, self.stays = [], []
        for values, order, left in self.halves:
            at = left.index(order[0])
            sends.append(add_up([lax.index_in_dim(v, 1, at, keepdims=False) for v in values]))
            self.stays.append([lax.index_in_dim(v, 0, at, keepdims=False) for v in values])
        bits = [order[0] for _, order, _ in self.halves]
        return [flip(sends[0], 1 << bits[0]), flip(sends[1], 1 << bits[1])]

    def landed(self, got):
        halves = []
        for i, (_, order, left) in enumerate(self.halves):
            halves.append((self.stays[i] + [got[i]], order[1:], [b for b in left if b != order[0]]))
        self.halves = halves

    def cross(self):
        while len(self.halves[0][1]) > 1:
            self.landed(self.step())
        return self.step()

    def rows(self):
        self.value = jnp.concatenate([add_up(values) for values, _, _ in self.halves], axis=1)
        self.stage = 0
        return self.value

    def along(self):
        rep = lax.axis_size("rep")
        half = rep // 2
        k = self.stage
        if k < half - 1:
            pairs = [(k, k + 1), (rep - 1 - k, rep - 2 - k)]
        elif k == half - 1:
            pairs = [(k, k + 1), (k + 1, k)]
        else:
            i = rep - 2 - k
            pairs = [(i + 1, i), (rep - 2 - i, rep - 1 - i)]
        return lax.ppermute(self.value, "rep", pairs)

    def along_landed(self, got):
        rep = lax.axis_size("rep")
        z = lax.axis_index("rep")
        k = self.stage
        self.stage += 1
        if k < rep // 2:
            self.value = add_up([self.value, got])
        else:
            i = rep - 2 - k
            self.value = jnp.where((z == i) | (z == rep - 1 - i), got, self.value)

    def finish(self):
        while self.stage < lax.axis_size("rep") - 1:
            self.along_landed(self.along())
        return self.value.astype(F32)


class RepSum:
    def __init__(self, value):
        self.value = value
        self.bits = lax.axis_size("rep").bit_length() - 1
        self.steps = 2 * self.bits
        self.done = 0

    def mine(self):
        k = self.done
        bit = k if k < self.bits else self.steps - 1 - k
        z = lax.axis_index("rep")
        return bit, lax.bitwise_and(lax.shift_right_logical(z, bit), 1)

    def send(self):
        bit, mine = self.mine()
        if self.done >= self.bits:
            return rep_flip(self.value, 1 << bit)
        size = self.value.shape[0] // 2
        sent = lax.dynamic_slice_in_dim(self.value, (1 - mine) * size, size, 0)
        self.keep = lax.dynamic_slice_in_dim(self.value, mine * size, size, 0)
        return rep_flip(sent, 1 << bit)

    def landed(self, got):
        _, mine = self.mine()
        if self.done < self.bits:
            self.value = add_up([self.keep, got])
        else:
            lower = jnp.where(mine == 0, self.value, got)
            upper = jnp.where(mine == 0, got, self.value)
            self.value = jnp.concatenate([lower, upper], axis=0)
        self.done += 1


def nt(left, right):
    return lax.dot_general(left, right, (((1,), (1,)), ((), ())), preferred_element_type=F32)


def hidden_gradient(grad_result, w_down, slope, deps=()):
    total, width = grad_result.shape
    units = w_down.shape[0]
    tile = 512

    def body(grad_ref, w_ref, slope_ref, *refs):
        out_ref, sum_ref = refs[-2:]
        value = nt(grad_ref[...], w_ref[...]) * slope_ref[...].astype(F32)
        out_ref[...] = value.astype(BF16)
        sum_ref[...] = jnp.sum(value, axis=0, keepdims=True)

    return pl.pallas_call(
        body,
        out_shape=[
            jax.ShapeDtypeStruct((total, units), BF16),
            jax.ShapeDtypeStruct((1, units), F32),
        ],
        grid=(units // tile,),
        in_specs=[
            pl.BlockSpec((total, width), lambda c: (0, 0)),
            pl.BlockSpec((tile, width), lambda c: (c, 0)),
            pl.BlockSpec((total, tile), lambda c: (0, c)),
        ]
        + [ANY] * len(deps),
        out_specs=[
            pl.BlockSpec((total, tile), lambda c: (0, c)),
            pl.BlockSpec((1, tile), lambda c: (0, c)),
        ],
        compiler_params=pltpu.CompilerParams(vmem_limit_bytes=24 * 2**20),
        cost_estimate=pl.CostEstimate(flops=int(3 * 1.15e9), bytes_accessed=1024, transcendentals=0),
        name="hidden_gradient",
    )(grad_result, w_down, slope, *deps)


def mixed_gradient(hidden_low, w_up, w_out, mixed, grad_result, gain, deps=()):
    total, units = hidden_low.shape
    width = w_up.shape[0]
    tile = 256

    def body(low_ref, up_ref, out_w_ref, mixed_ref, result_ref, gain_ref, *outs):
        grad_ref, rounded_ref, attended_ref, sums_ref = outs[-4:]
        grad = nt(low_ref[...], up_ref[...])
        unit, scale = norm_parts(mixed_ref[...])
        result = result_ref[...].astype(F32)
        value = result + norm_back(grad, gain_ref[...], unit, scale)
        rounded = value.astype(BF16)
        grad_ref[...] = value
        rounded_ref[...] = rounded
        attended_ref[...] = nt(rounded, out_w_ref[...]).astype(BF16)

        @pl.when(pl.program_id(0) == 0)
        def _():
            sums_ref[...] = jnp.zeros_like(sums_ref)

        for i, terms in enumerate((value, grad * unit, grad, result)):
            sums_ref[pl.ds(i, 1), :] += jnp.sum(terms, axis=0, keepdims=True)

    rows = pl.BlockSpec((tile, width), lambda r: (r, 0))
    whole = [
        pl.BlockSpec((width, units), lambda r: (0, 0)),
        pl.BlockSpec((width, width), lambda r: (0, 0)),
    ]
    return pl.pallas_call(
        body,
        out_shape=[
            jax.ShapeDtypeStruct((total, width), F32),
            jax.ShapeDtypeStruct((total, width), BF16),
            jax.ShapeDtypeStruct((total, width), BF16),
            jax.ShapeDtypeStruct((8, width), F32),
        ],
        grid=(total // tile,),
        in_specs=[pl.BlockSpec((tile, units), lambda r: (r, 0))]
        + whole
        + [rows, rows, pl.BlockSpec((1, width), lambda r: (0, 0))]
        + [ANY] * len(deps),
        out_specs=[rows, rows, rows, pl.BlockSpec((8, width), lambda r: (0, 0))],
        compiler_params=pltpu.CompilerParams(vmem_limit_bytes=44 * 2**20),
        cost_estimate=pl.CostEstimate(flops=int(2 * 1.15e9), bytes_accessed=1024, transcendentals=0),
        name="mixed_gradient",
    )(hidden_low, w_up, w_out, mixed, grad_result, gain.reshape(1, width), *deps)


def normed_gradient(grad_triple, w_qkv, deps=()):
    three, total, width = grad_triple.shape
    tile = 256

    def body(grad_ref, w_ref, *refs):
        out_ref = refs[-1]
        value = nt(grad_ref[0], w_ref[:, pl.ds(0, width)])
        for i in range(1, three):
            value += nt(grad_ref[i], w_ref[:, pl.ds(i * width, width)])
        out_ref[...] = value.astype(BF16)

    return pl.pallas_call(
        body,
        out_shape=jax.ShapeDtypeStruct((total, width), BF16),
        grid=(total // tile,),
        in_specs=[
            pl.BlockSpec((three, tile, width), lambda r: (0, r, 0)),
            pl.BlockSpec((width, three * width), lambda r: (0, 0)),
        ]
        + [ANY] * len(deps),
        out_specs=pl.BlockSpec((tile, width), lambda r: (r, 0)),
        compiler_params=pltpu.CompilerParams(vmem_limit_bytes=52 * 2**20),
        cost_estimate=pl.CostEstimate(flops=int(2 * 1.15e9), bytes_accessed=1024, transcendentals=0),
        name="normed_gradient",
    )(grad_triple, w_qkv, *deps)


def matmul(left, right):
    return jnp.dot(left, right, preferred_element_type=F32)


def matmul_nt(left, right):
    return lax.dot_general(left, right, (((1,), (1,)), ((), ())), preferred_element_type=F32)


def matmul_tn(left, right):
    return lax.dot_general(left, right, (((0,), (0,)), ((), ())), preferred_element_type=F32)


def norm_parts(values):
    average = jnp.mean(values, axis=-1, keepdims=True)
    centred = values - average
    spread = jnp.mean(centred * centred, axis=-1, keepdims=True)
    scale = lax.rsqrt(spread + EPS)
    return centred * scale, scale


def norm_back(grad, gain, unit, scale):
    e = grad * gain
    return scale * (
        e
        - jnp.mean(e, axis=-1, keepdims=True)
        - unit * jnp.mean(e * unit, axis=-1, keepdims=True)
    )


def shards(
    inputs,
    skips,
    cotangent,
    dest_slot,
    pack_segments,
    block_live,
    counts,
    w_skip,
    b_skip,
    g_one,
    b_one,
    w_qkv,
    w_out,
    b_out,
    g_two,
    b_two,
    w_up,
    c_up,
    w_down,
    c_down,
):
    dp = lax.axis_size("dp")
    rep = lax.axis_size("rep")
    d = lax.axis_index("dp")
    z = lax.axis_index("rep")
    micro = inputs.shape[0]
    frames = inputs.shape[2]
    width = inputs.shape[3]
    blocks = dest_slot.shape[2]
    block = frames // blocks
    per_pair = blocks // dp
    total = micro * frames
    bits = dp.bit_length() - 1
    place = jnp.stack([z, lax.rem(d, 8)]).astype(jnp.int32)
    dims = list(range(1, bits))

    own_skip = own_chunk(place, width, [w_skip])
    own_skip, slots_now, live_now = together(own_skip, dest_slot, block_live)
    small = jnp.concatenate([slots_now.reshape(-1), live_now.reshape(-1), counts.reshape(-1)])
    z_skip = Fetch(own_skip)
    z_skip.rest()
    got = z_skip.send()
    every = small[None]
    for bit in range(bits):
        every = jnp.concatenate([every, flip(every, 1 << bit)], axis=0)
    z_mid = Fetch(own_chunk(place, width, [w_qkv, w_out], z_skip.held[1:]))
    z_mid.rest()
    z_skip.landed(got)

    run_skip = Spread(z_skip.far(), width, [every, z_mid.held[-1]])
    mid = z_mid.send()
    run_skip.near_landed(run_skip.near())

    span = micro * blocks
    numbers = every[:, : 2 * span].reshape(dp, 2 * micro, blocks)
    numbers = jnp.transpose(numbers, (1, 0, 2)).reshape(2 * micro, dp * blocks).astype(F32)
    count_total = jnp.sum(every[:, 2 * span]).astype(F32).reshape(1, 1)
    inner = jnp.arange(frames) % block
    live = inner[None] < jnp.repeat(block_live[:, 0, :], block, axis=1)
    codes = (2 * pack_segments[:, 0, :] + live).astype(F32)
    joined = jnp.concatenate([inputs.reshape(total, width), skips.reshape(total, width)], axis=1)
    far, far_turned, keep_wide, shuffle = plan_order(
        numbers[:micro], numbers[micro:], codes, d, block, [run_skip.pairs[0], joined]
    )
    keep_rows = keep_wide[:, :1]

    run_skip.cross_landed(run_skip.cross(), [shuffle, mid])

    z_mid.landed(mid)
    run_mid = Spread(z_mid.far(), width)
    full_skip, _ = assemble(
        w_skip, run_skip.parts(run_skip.share()), place, 0, 1, [run_mid.start[0]]
    )
    z_up = Fetch(own_chunk(place, width, [w_up], [run_mid.start[0]]))
    z_up.rest()
    base = matmul(joined, full_skip) + b_skip
    unit_one, scale_one = norm_parts(base)
    own_normed = (unit_one * g_one + b_one).astype(BF16)
    sent = matmul(shuffle, own_normed).astype(BF16)
    run_mid.near_landed(run_mid.near(), [sent, z_up.held[-1]])

    def exchange(values):
        values = values.reshape(dp, total // dp, width)
        got = lax.all_to_all(values, "dp", split_axis=0, concat_axis=0, tiled=True)
        return got.reshape(total, width)

    normed = exchange(sent)
    up = z_up.send([sent])
    z_down = Fetch(own_chunk(place, width, [w_down], [z_up.held[-1], sent]))
    z_down.rest()
    run_mid.cross_landed(run_mid.cross(), [up, z_down.held[-1], normed])
    z_up.landed(up)

    other = run_mid.share()
    run_up = Spread(z_up.far(), width, [run_mid.every])
    run_up.near_landed(run_up.near(), [other])
    shard_rows = w_qkv.shape[0] // 8
    parts_mid = run_mid.parts(other)
    full_qkv, _ = assemble(w_qkv, parts_mid, place, 0, 3)

    triple = matmul(normed, full_qkv).astype(BF16)
    triple = triple.reshape(dp, micro, per_pair * block, 3 * width)
    slopes = 2.0 ** (-8.0 * (jnp.arange(HEADS, dtype=F32) + 1.0) / HEADS)
    attended = attend(triple, far, slopes, [run_up.pairs[0]])
    down = z_down.send()
    run_up.cross_landed(run_up.cross(), [attended, down])
    z_down.landed(down)

    attended = exchange(attended)
    other = run_up.share()
    run_down = Spread(z_down.far(), width, [run_up.every])
    down = run_down.near()
    full_out, out_token = assemble(w_out, parts_mid, place, 3 * shard_rows, 1, [run_up.every])
    full_up, up_token = assemble(w_up, run_up.parts(other), place, 0, w_up.shape[1] // width)
    attended, out_token, up_token = together(attended, out_token, up_token)

    attended = matmul_tn(shuffle, attended).astype(BF16)
    mixed = base + matmul(attended, full_out) + (b_out + out_token[0, 0])
    unit_two, scale_two = norm_parts(mixed)
    normed_two = (unit_two * g_two + b_two).astype(BF16)
    count_total = count_total + up_token[:1, :1]
    for step in rep_steps(rep):
        count_total = count_total + rep_flip(count_total, step)
    share = counts[0, 0].astype(F32) * (dp * rep) / count_total[0, 0]
    run_down.near_landed(down, [up_token])
    down = run_down.cross()
    hidden = matmul(normed_two, full_up) + (c_up + run_down.token[0, 0])
    phi = 0.5 * (1.0 + lax.erf(hidden * (0.5**0.5)))
    active = (hidden * phi).astype(BF16)
    slope = (phi + hidden * jnp.exp(-0.5 * hidden * hidden) * ((2 * jnp.pi) ** -0.5)).astype(BF16)
    scaled = (cotangent.reshape(total, width).astype(F32) * share).astype(BF16)
    grad_result = scaled * keep_rows.astype(BF16)
    red_down = Reduction([(active, grad_result)], d, dims)

    down_got = red_down.share()
    run_down.cross_landed(down, [red_down.sent])
    full_down, _ = assemble(w_down, run_down.parts(run_down.share()), place, 0, 1)

    hidden_low, sum_hidden = hidden_gradient(grad_result, full_down, slope)
    red_up = Reduction([(normed_two, hidden_low)], d, dims)
    up_got = red_up.share()
    red_down.own(down_got, [red_up.sent])
    flying = red_down.near()
    grad_mixed, mixed_low, grad_attended, sums_mixed = mixed_gradient(
        hidden_low, full_up, full_out, mixed, grad_result, g_two, [red_down.token]
    )
    red_out = Reduction([(attended, mixed_low)], d, dims)
    out_got = red_out.share()
    flying, sums_mixed = together(flying, sums_mixed)
    red_down.near_landed(flying)

    down_flying = red_down.cross()
    sent = matmul(shuffle, grad_attended).astype(BF16)
    grad_attended = exchange(sent)
    red_up.own(up_got, [sent], [(red_out, out_got)])
    flying = red_up.near()
    down_flying, token = together(down_flying, red_up.token)
    red_down.landed(down_flying)
    red_down.rows()

    line = red_down.along()
    grad_attended = grad_attended.reshape(dp, micro, per_pair * block, width)
    grad_triple, token = attend_back(
        triple, grad_attended, far_turned, slopes, [red_down.value, token]
    )
    grad_triple = grad_triple.reshape(3, total, width)

    sent = normed_gradient(grad_triple, full_qkv)
    grad_normed = exchange(sent)
    flying, line, token = together(flying, line, token)
    red_mid = Reduction([(normed, grad_triple)], d, dims, [sent, token])
    grad_normed, token = together(grad_normed, red_mid.token)
    red_up.near_landed(flying)
    red_down.along_landed(line)
    up_flying = red_up.cross()
    line = red_down.along()

    mid_got = red_mid.share()
    grad_normed = matmul_tn(shuffle, grad_normed)
    grad_base = grad_mixed + norm_back(grad_normed, g_one, unit_one, scale_one)
    base_low = grad_base.astype(BF16)
    red_skip = Reduction([(joined, base_low)], d, dims, [token])
    skip_got = red_skip.share()
    vectors = (
        jnp.sum(grad_base, axis=0),
        jnp.sum(grad_normed * unit_one, axis=0),
        jnp.sum(grad_normed, axis=0),
        sums_mixed[0],
        sums_mixed[1],
        sums_mixed[2],
        sum_hidden[0],
        sums_mixed[3],
    )
    lengths = [v.shape[0] for v in vectors]
    summed = jnp.concatenate(vectors).reshape(-1, 128)
    for bit in range(bits - 1):
        summed = summed + flip(summed, 1 << bit)
    up_flying, token = together(up_flying, red_skip.token)
    red_up.landed(up_flying)
    red_up.rows()
    up_line = red_up.along()
    red_mid.own(mid_got, [token])
    summed, token = together(summed, red_mid.token)

    flying = red_mid.near()
    red_skip.own(skip_got, [token])
    skip_flying = red_skip.near()
    line, token = together(line, red_skip.token)
    red_down.along_landed(line)
    line = red_down.along()
    result = mixed + matmul(active, full_down) + (c_down + token[0, 0])
    output = (result * keep_rows).astype(BF16)
    grad_joined = matmul_nt(base_low, full_skip).astype(BF16)
    flying, up_line, grad_joined, summed = together(flying, up_line, grad_joined, summed)
    red_mid.near_landed(flying)
    red_up.along_landed(up_line)

    flying = red_mid.cross()
    up_line = red_up.along()
    flying, line, skip_flying, summed = together(flying, line, skip_flying, summed)
    red_down.along_landed(line)
    red_skip.near_landed(skip_flying)
    red_mid.landed(flying)

    mid_sum = RepSum(red_mid.rows())
    skip_flying = red_skip.cross()
    got = mid_sum.send()
    last = flip(summed, 1 << (bits - 1))
    got, up_line, skip_flying, last = together(got, up_line, skip_flying, last)
    mid_sum.landed(got)
    red_up.along_landed(up_line)
    red_skip.landed(skip_flying)
    summed = summed + last
    up_line = red_up.along()
    skip_columns = w_skip.shape[1]
    extra = jnp.pad(summed.reshape(-1), (0, -summed.size % (16 * rep * skip_columns)))
    extra = extra.reshape(-1, skip_columns).astype(BF16)
    skip_sum = RepSum(jnp.concatenate([red_skip.rows(), extra], axis=0))
    while mid_sum.done < mid_sum.steps:
        mid_got, skip_got = mid_sum.send(), skip_sum.send()
        if mid_sum.done == mid_sum.steps - 2:
            mid_got, skip_got, up_line = together(mid_got, skip_got, up_line)
        else:
            mid_got, skip_got = together(mid_got, skip_got)
        mid_sum.landed(mid_got)
        skip_sum.landed(skip_got)
    skip_sum.landed(skip_sum.send())
    red_up.along_landed(up_line)
    final_mid = mid_sum.value.astype(F32)
    final_skip = skip_sum.value.astype(F32)
    own_rows = w_skip.shape[0] * rep // dp
    summed = final_skip[own_rows:].reshape(-1)
    final_up = red_up.finish()
    units = c_up.shape[0]
    finals = [
        red_down.finish(),
        final_up[:, :units],
        final_up[:, units:],
        final_mid,
        final_skip[:own_rows],
    ]
    sums = []
    offset = 0
    for length in lengths:
        sums.append(summed[offset : offset + length])
        offset += length

    def as_owned(values):
        return values.reshape(inputs.shape)

    return (
        as_owned(output),
        as_owned(grad_joined[:, :width]),
        as_owned(grad_joined[:, width:]),
        finals[4],
        sums[0],
        sums[1],
        sums[2],
        finals[3],
        finals[2],
        sums[3],
        sums[4],
        sums[5],
        finals[1],
        sums[6],
        finals[0],
        sums[7],
    )


def solution(mesh):
    frames = P(None, "rep", "dp", None)
    slots = P(None, "rep", "dp")
    rows = P("rep", None)
    whole = P()
    in_specs = (
        (frames,) * 3
        + (slots,) * 3
        + (P("dp", "rep"), rows, whole, whole, whole, rows, rows)
        + (whole,) * 3
        + (rows, whole, rows, whole)
    )
    split = P("dp", None)
    out_specs = (
        (frames,) * 3
        + (split,)
        + (whole,) * 3
        + (split, split)
        + (whole,) * 3
        + (split, whole, split, whole)
    )
    return jax.shard_map(shards, mesh=mesh, in_specs=in_specs, out_specs=out_specs, check_vma=False)
```

```python
import jax
import jax.numpy as jnp
from jax import lax
from jax.experimental import pallas as pl
from jax.experimental.pallas import tpu as pltpu
from jax.sharding import PartitionSpec as P

HEADS = 16
HEAD = 64
EPS = 1e-05
F32 = jnp.float32
BF16 = jnp.bfloat16
TOKEN = jax.ShapeDtypeStruct((8, 128), F32)
ANY = pl.BlockSpec(memory_space=pl.ANY)
LIGHT = pl.CostEstimate(flops=1024, bytes_accessed=1024, transcendentals=0)


def flip(value, bit):
    n = lax.axis_size("dp")
    return lax.ppermute(value, "dp", [(i, i ^ bit) for i in range(n)])


def rep_flip(value, bit):
    n = lax.axis_size("rep")
    return lax.ppermute(value, "rep", [(i, i ^ bit) for i in range(n)])


def after(value, *earlier):
    return lax.optimization_barrier((value,) + earlier)[0]


def together(*values):
    return lax.optimization_barrier(values)


def assemble(w_local, parts, place, row_at, tiles, deps=()):
    rep = lax.axis_size("rep")
    shard_rows, columns = w_local.shape
    rows = shard_rows // 8
    tile = columns // tiles
    half = tile // 2
    chunk_rows = parts[0][0].shape[0] // (len(parts[0][1]) * (rep - 1))
    arrays = [part[0] for part in parts]
    count = 1 + sum(len(part[1]) for part in parts) * (rep - 1) * tiles

    def body(place_ref, local_ref, *refs):
        out_ref, token_ref, sems = refs[-3:]
        token_ref[...] = jnp.zeros_like(token_ref)
        z = place_ref[0]
        e = place_ref[1]
        copies = [
            pltpu.make_async_copy(
                local_ref,
                out_ref.at[pl.ds(pl.multiple_of(z * shard_rows, 16), shard_rows), :],
                sems.at[0],
            )
        ]
        for ref, (_, runs) in zip(refs, parts):
            for k, (side, rel) in enumerate(runs):
                chunk = jnp.bitwise_xor(e, rel)
                for s, apart in enumerate(far_order(rep), 1):
                    shard = jnp.bitwise_xor(z, apart)
                    start = pl.multiple_of(shard * shard_rows + chunk * rows, 16)
                    for t in range(tiles):
                        at = (k * (rep - 1) + s - 1) * chunk_rows + row_at + t * rows
                        copies.append(
                            pltpu.make_async_copy(
                                ref.at[pl.ds(at, rows), :],
                                out_ref.at[pl.ds(start, rows), pl.ds(t * tile + side * half, half)],
                                sems.at[len(copies)],
                            )
                        )
        for copy in copies:
            copy.start()
        for copy in copies:
            copy.wait()

    return pl.pallas_call(
        body,
        out_shape=[jax.ShapeDtypeStruct((shard_rows * rep, columns), w_local.dtype), TOKEN],
        grid=(1,),
        in_specs=[pl.BlockSpec(memory_space=pltpu.SMEM)] + [ANY] * (1 + len(parts) + len(deps)),
        out_specs=[
            pl.BlockSpec((shard_rows * rep, columns), lambda i: (0, 0)),
            pl.BlockSpec(TOKEN.shape, lambda i: (0, 0)),
        ],
        scratch_shapes=[pltpu.SemaphoreType.DMA((count,))],
        compiler_params=pltpu.CompilerParams(vmem_limit_bytes=26 * 2**20),
        cost_estimate=pl.CostEstimate(flops=int(1.5 * 1.15e9), bytes_accessed=1024, transcendentals=0),
        name="assemble",
    )(place, w_local, *arrays, *deps)


def own_chunk(place, width, shards_local, deps=()):
    items = []
    for which, w_local in enumerate(shards_local):
        for t in range(w_local.shape[1] // width):
            items.append((which, w_local.shape[0] // 8, t * width))
    total = sum(item[1] for item in items)

    def body(place_ref, *refs):
        out_ref, sems = refs[-2:]
        copies = []
        at = 0
        for which, rows, column in items:
            start = pl.multiple_of(place_ref[1] * rows, 16)
            copies.append(
                pltpu.make_async_copy(
                    refs[which].at[pl.ds(start, rows), pl.ds(column, width)],
                    out_ref.at[pl.ds(at, rows), :],
                    sems.at[len(copies)],
                )
            )
            at += rows
        for copy in copies:
            copy.start()
        for copy in copies:
            copy.wait()

    return pl.pallas_call(
        body,
        out_shape=jax.ShapeDtypeStruct((total, width), shards_local[0].dtype),
        grid=(1,),
        in_specs=[pl.BlockSpec(memory_space=pltpu.SMEM)]
        + [ANY] * (len(shards_local) + len(deps)),
        out_specs=pl.BlockSpec((total, width), lambda i: (0, 0)),
        scratch_shapes=[pltpu.SemaphoreType.DMA((len(items),))],
        compiler_params=pltpu.CompilerParams(vmem_limit_bytes=24 * 2**20),
        cost_estimate=LIGHT,
        name="own_chunk",
    )(place, *shards_local, *deps)


def pack(arrays, outs, deps=()):
    count = sum(len(out) for out in outs)

    def body(*refs):
        sources, targets = refs[: len(arrays)], refs[-2 - len(outs) : -2]
        token_ref, sems = refs[-2:]
        token_ref[...] = jnp.zeros_like(token_ref)
        copies = []
        for target, out in zip(targets, outs):
            at = 0
            for which, row, rows, column, columns in out:
                copies.append(
                    pltpu.make_async_copy(
                        sources[which].at[pl.ds(row, rows), pl.ds(column, columns)],
                        target.at[pl.ds(at, rows), :],
                        sems.at[len(copies)],
                    )
                )
                at += rows
        for copy in copies:
            copy.start()
        for copy in copies:
            copy.wait()

    return pl.pallas_call(
        body,
        out_shape=[
            jax.ShapeDtypeStruct((sum(item[2] for item in out), out[0][4]), arrays[0].dtype)
            for out in outs
        ]
        + [TOKEN],
        grid=(1,),
        in_specs=[ANY] * (len(arrays) + len(deps)),
        out_specs=[
            pl.BlockSpec((sum(item[2] for item in out), out[0][4]), lambda i: (0, 0))
            for out in outs
        ]
        + [pl.BlockSpec(TOKEN.shape, lambda i: (0, 0))],
        scratch_shapes=[pltpu.SemaphoreType.DMA((count,))],
        compiler_params=pltpu.CompilerParams(vmem_limit_bytes=24 * 2**20),
        cost_estimate=LIGHT,
        name="pack",
    )(*arrays, *deps)


def far_order(rep):
    order = [0]
    for bit in reversed(range(rep.bit_length() - 1)):
        order = order + [distance ^ (1 << bit) for distance in order]
    return order[1:]


class Spread:
    def __init__(self, gots, width, deps=()):
        self.half = width // 2
        rows = sum(got.shape[0] for got in gots)
        items = [(i, 0, got.shape[0]) for i, got in enumerate(gots)]
        *self.start, _ = pack(
            gots, [[item + (column, self.half) for item in items] for column in (0, self.half)], deps
        )
        self.n = rows

    def near(self):
        return [flip(self.start[0], 2), flip(self.start[1], 4)]

    def near_landed(self, got, deps=()):
        whole = [(i, 0, self.n, 0, self.half) for i in range(4)]
        *self.pairs, self.token = pack(
            [self.start[0], got[0], self.start[1], got[1]], [whole[:2], whole[2:]], deps
        )

    def cross(self):
        return [flip(self.pairs[0], 4), flip(self.pairs[1], 2)]

    def cross_landed(self, got, deps=()):
        whole = [(i, 0, 2 * self.n, 0, self.half) for i in range(4)]
        self.every, self.token = pack([self.pairs[0], got[0], self.pairs[1], got[1]], [whole], deps)

    def share(self):
        return flip(self.every, 1)

    def parts(self, other):
        runs = [(0, 0), (0, 2), (0, 4), (0, 6), (1, 0), (1, 4), (1, 2), (1, 6)]
        return [(self.every, runs), (other, [(side, rel | 1) for side, rel in runs])]


def rep_steps(rep):
    return [1 << bit for bit in reversed(range(rep.bit_length() - 1))]


class Fetch:
    def __init__(self, own):
        self.held = [own]
        self.steps = rep_steps(lax.axis_size("rep"))

    def send(self, deps=()):
        sent = self.held[0]
        if len(self.held) > 1:
            whole = [(i, 0, a.shape[0], 0, a.shape[1]) for i, a in enumerate(self.held)]
            sent, _ = pack(self.held, [whole], deps)
        return rep_flip(sent, self.steps[len(self.held) - 1])

    def landed(self, got):
        self.held.append(got)

    def rest(self):
        while len(self.held) < len(self.steps):
            self.landed(self.send())

    def far(self):
        return self.held[1:]


def plan_order(all_slots, all_live, codes, d, block, deps=()):
    micro, owners = all_slots.shape
    frames = codes.shape[1]
    blocks = frames // block
    dp = owners // blocks
    per_pair = blocks // dp
    total = micro * frames

    def column(row):
        return jnp.broadcast_to(row, (128, row.shape[1])).T[:, :1]

    def as_row(values):
        return jnp.broadcast_to(values, (values.shape[0], 128)).T[:1, :]

    def body(d_ref, slots_ref, live_ref, codes_ref, *refs):
        far_ref, turned_ref, keep_ref, shuffle_ref = refs[-4:]
        me = d_ref[0]
        lane = lax.broadcasted_iota(jnp.int32, (1, owners), 1)
        source = jnp.bitwise_xor(lax.div(lane, jnp.int32(blocks)), me)
        first_slot = (source * blocks).astype(F32) + lax.rem(lane, jnp.int32(blocks)).astype(F32)
        source_col = column(source.astype(F32))
        frame = lax.broadcasted_iota(jnp.int32, (frames, 1), 0)
        block_of = lax.div(frame, jnp.int32(block)).astype(F32)
        inner = lax.rem(frame, jnp.int32(block)).astype(F32)
        low = (me * blocks).astype(F32)
        rows = []
        for m in range(micro):
            slots = slots_ref[pl.ds(m, 1), :]
            slots_col = column(slots)
            same = source_col == source.astype(F32)
            rank = jnp.sum(jnp.where(same & (slots_col < slots), 1.0, 0.0), axis=0, keepdims=True)
            here = (slots >= low) & (slots < low + blocks)
            arrive = source.astype(F32) * per_pair + rank - (me * per_pair).astype(F32)
            arrive = jnp.where(here, arrive, -1.0)
            placed = jnp.sum(
                jnp.where(arrive == block_of, slots - low, 0.0), axis=1, keepdims=True
            )
            position = placed * block + inner
            at = lax.broadcasted_iota(jnp.int32, (1, frames), 1).astype(F32)
            code = jnp.sum(
                jnp.where(at == position, codes_ref[pl.ds(m, 1), :], 0.0), axis=1, keepdims=True
            )
            position_row, code_row = as_row(position), as_row(code)
            segment, segment_row = jnp.floor(code * 0.5), jnp.floor(code_row * 0.5)
            live_row = code_row - 2.0 * segment_row
            distance = jnp.abs(position - position_row)
            allowed = (segment == segment_row) & ((live_row > 0.5) | (distance < 0.5))
            far_ref[m] = jnp.where(allowed, distance, 1e32)
            live_col = code - 2.0 * segment
            allowed = (segment == segment_row) & ((live_col > 0.5) | (distance < 0.5))
            turned_ref[m] = jnp.where(allowed, distance, 1e32)
            own = lane < blocks
            mine = jnp.sum(
                jnp.where(own & (lane.astype(F32) == block_of), slots, 0.0), axis=1, keepdims=True
            )
            alive = jnp.sum(
                jnp.where(first_slot == mine, live_ref[pl.ds(m, 1), :], 0.0), axis=1, keepdims=True
            )
            keep_ref[pl.ds(m * frames, frames), :] = jnp.broadcast_to(
                jnp.where(inner < alive, 1.0, 0.0), (frames, 128)
            )
            my_rank = jnp.sum(
                jnp.where(own & (lane.astype(F32) == block_of), rank, 0.0), axis=1, keepdims=True
            )
            target = jnp.floor((my_rank + 0.5) / per_pair)
            row = (target * micro + m) * per_pair + (my_rank - target * per_pair)
            rows.append(as_row(row * block + inner))
        goal = jnp.concatenate(rows, axis=1)
        spot = lax.broadcasted_iota(jnp.int32, (total, total), 0).astype(F32)
        shuffle_ref[...] = jnp.where(spot == goal, 1.0, 0.0).astype(BF16)

    vmem = pl.BlockSpec(memory_space=pltpu.VMEM)
    return pl.pallas_call(
        body,
        out_shape=[
            jax.ShapeDtypeStruct((micro, frames, frames), F32),
            jax.ShapeDtypeStruct((micro, frames, frames), F32),
            jax.ShapeDtypeStruct((total, 128), F32),
            jax.ShapeDtypeStruct((total, total), BF16),
        ],
        in_specs=[pl.BlockSpec(memory_space=pltpu.SMEM), vmem, vmem, vmem] + [ANY] * len(deps),
        out_specs=[vmem, vmem, vmem, vmem],
        compiler_params=pltpu.CompilerParams(vmem_limit_bytes=24 * 2**20),
        cost_estimate=LIGHT,
        name="plan_order",
    )(d.reshape(1).astype(jnp.int32), all_slots, all_live, codes, *deps)


def gradient_blocks(pairs, d, dims, got=None, deps=()):
    dp = lax.axis_size("dp")
    total, all_rows = pairs[0][0].shape
    widths = [right.shape[2] for _, right in pairs]
    columns = sum(right.shape[0] * right.shape[2] for _, right in pairs)
    rows = all_rows // dp
    count = dp // 2
    odd = 1 if got is None else 0
    tile = min(min(widths), 512)
    splits = [width // tile for width in widths]
    tiles = [right.shape[0] * split for (_, right), split in zip(pairs, splits)]
    steps = sum(tiles)
    starts = [sum(tiles[:i]) for i in range(len(tiles))]

    def distance(p):
        rel = odd
        for k, bit in enumerate(dims):
            rel += ((p >> (len(dims) - 1 - k)) & 1) << bit
        return rel

    upper = [p for p in range(count) if p >= count // 2]
    lower = [p for p in range(count) if p < count // 2]
    odds = [p for p in range(count) if p % 2 == 1]
    evens = [p for p in range(count) if p % 2 == 0]
    chosen = (upper, lower, odds, evens)

    if rows % 128 != 0:
        products = []
        for left, right in pairs:
            flat = jnp.transpose(right, (1, 0, 2)).reshape(total, -1)
            products.append(matmul_tn(left, flat))
        product = jnp.concatenate(products, axis=1).reshape(dp, rows, columns)
        rel = jnp.array([distance(p) for p in range(count)], jnp.int32)
        product = product[jnp.bitwise_xor(rel, d)]
        token = jnp.zeros(TOKEN.shape, F32) + product[0, :1, :1]
        if got is None:
            return [product.astype(BF16), token]
        product = (product + jnp.concatenate(got, axis=2).astype(F32)).astype(BF16)
        half = columns // 2
        return [
            jnp.stack([product[p, :, side * half : (side + 1) * half] for p in ps])
            for side, ps in zip((0, 0, 1, 1), chosen)
        ] + [token]

    def body(d_ref, *refs):
        lefts = refs[: len(pairs)]
        rights = refs[len(pairs) : 2 * len(pairs)]
        got_refs = refs[2 * len(pairs) : 3 * len(pairs)]
        token_ref, turned_ref = refs[-2:]
        outs = refs[-3:-2] if got is None else refs[-6:-2]
        c = pl.program_id(0)

        @pl.when(c == 0)
        def _():
            token_ref[...] = jnp.zeros_like(token_ref)
            for i, left_ref in enumerate(lefts):
                for p in range(count):
                    at = pl.multiple_of(jnp.bitwise_xor(d_ref[0], distance(p)) * rows, 128)
                    turned_ref[i, pl.ds(p * rows, rows), :] = left_ref[:, pl.ds(at, rows)].T

        def piece(i, p):
            return jnp.dot(
                turned_ref[i, pl.ds(p * rows, rows), :], rights[i][0], preferred_element_type=F32
            )

        def write(i, half):
            for p in range(count):
                value = piece(i, p)
                if got is None:
                    outs[0][p] = value.astype(BF16)
                    continue
                value = (value + got_refs[i][p].astype(F32)).astype(BF16)
                for which in (2 * half, 2 * half + 1):
                    if p in chosen[which]:
                        outs[which][chosen[which].index(p)] = value

        for i in range(len(pairs)):
            for half in (0, 1):
                low = max(starts[i], half * (steps // 2))
                high = min(starts[i] + tiles[i], (half + 1) * (steps // 2))
                if low < high:
                    pl.when((c >= low) & (c < high))(lambda i=i, half=half: write(i, half))

    def right_spec(start, n, split):
        def at(c, d_ref):
            k = jnp.clip(c - start, 0, n - 1)
            return (lax.div(k, jnp.int32(split)), 0, lax.rem(k, jnp.int32(split)))

        return pl.BlockSpec((1, total, tile), at)

    in_specs = [pl.BlockSpec((total, all_rows), lambda c, d_ref: (0, 0))] * len(pairs)
    in_specs += [right_spec(*item) for item in zip(starts, tiles, splits)]
    args = [left for left, _ in pairs] + [right for _, right in pairs]
    if got is None:
        out_shape = [jax.ShapeDtypeStruct((count, rows, columns), BF16)]
        out_specs = [pl.BlockSpec((count, rows, tile), lambda c, d_ref: (0, 0, c))]
    else:
        for start, n in zip(starts, tiles):
            in_specs.append(
                pl.BlockSpec(
                    (count, rows, tile),
                    lambda c, d_ref, start=start, n=n: (0, 0, jnp.clip(c - start, 0, n - 1)),
                )
            )
        args += got
        out_shape = [jax.ShapeDtypeStruct((count // 2, rows, columns // 2), BF16)] * 4
        mid = steps // 2
        first = pl.BlockSpec(
            (count // 2, rows, tile), lambda c, d_ref: (0, 0, jnp.minimum(c, mid - 1))
        )
        second = pl.BlockSpec(
            (count // 2, rows, tile), lambda c, d_ref: (0, 0, jnp.maximum(c - mid, 0))
        )
        out_specs = [first, first, second, second]
    out_shape = out_shape + [TOKEN]
    out_specs = out_specs + [pl.BlockSpec(TOKEN.shape, lambda c, d_ref: (0, 0))]
    in_specs += [ANY] * len(deps)
    return pl.pallas_call(
        body,
        out_shape=out_shape,
        grid_spec=pltpu.PrefetchScalarGridSpec(
            num_scalar_prefetch=1,
            grid=(steps,),
            in_specs=in_specs,
            out_specs=out_specs,
            scratch_shapes=[pltpu.VMEM((len(pairs), count * rows, total), BF16)],
        ),
        compiler_params=pltpu.CompilerParams(vmem_limit_bytes=34 * 2**20),
        cost_estimate=pl.CostEstimate(flops=int(2.5 * 1.15e9), bytes_accessed=1024, transcendentals=0),
        name="gradient",
    )(d.reshape(1).astype(jnp.int32), *args, *deps)


def head_probs(q, k, far, slope):
    scores = lax.dot_general(q, k, (((1,), (1,)), ((), ())), preferred_element_type=F32)
    scores = scores * (HEAD ** (-0.5)) - slope * far
    raised = jnp.exp(scores - jnp.max(scores, axis=-1, keepdims=True))
    return raised * (1.0 / jnp.sum(raised, axis=-1, keepdims=True))


def flat_frames(block):
    sources, _, rows, lanes = block.shape
    if rows % 16 == 0:
        return block.reshape(sources * rows, lanes)
    return block.astype(F32).reshape(sources * rows, lanes).astype(BF16)


def by_source(value, like):
    sources, _, rows, lanes = like
    if rows % 16 == 0:
        return value.astype(BF16).reshape(sources, 1, rows, lanes)
    return value.reshape(sources, 1, rows, lanes).astype(BF16)


def attend(triple, far, slopes, deps=()):
    dp, micro, rows, wide = triple.shape
    frames = dp * rows
    width = wide // 3
    pairs = width // 128
    shape = (dp, 1, rows, 128)

    def body(slope_ref, q_ref, k_ref, v_ref, far_ref, *refs):
        out_ref = refs[-1]
        h = pl.program_id(1)
        q, k, v = (flat_frames(ref[...]) for ref in (q_ref, k_ref, v_ref))
        first = lax.broadcasted_iota(jnp.int32, (frames, 128), 1) < HEAD
        zero = jnp.zeros_like(q)
        outs = []
        for j, own in enumerate((jnp.where(first, q, zero), jnp.where(first, zero, q))):
            probs = head_probs(own, k, far_ref[0], slope_ref[h * 2 + j])
            outs.append(jnp.dot(probs.astype(BF16), v, preferred_element_type=F32))
        out_ref[...] = by_source(jnp.where(first, outs[0], outs[1]), shape)

    def spec(offset):
        return pl.BlockSpec(shape, lambda m, h, s: (0, m, 0, h + offset))

    return pl.pallas_call(
        body,
        out_shape=jax.ShapeDtypeStruct((dp, micro, rows, width), BF16),
        grid_spec=pltpu.PrefetchScalarGridSpec(
            num_scalar_prefetch=1,
            grid=(micro, pairs),
            in_specs=[
                spec(0),
                spec(pairs),
                spec(2 * pairs),
                pl.BlockSpec((1, frames, frames), lambda m, h, s: (m, 0, 0)),
            ]
            + [ANY] * len(deps),
            out_specs=spec(0),
        ),
        compiler_params=pltpu.CompilerParams(vmem_limit_bytes=24 * 2**20),
        cost_estimate=pl.CostEstimate(flops=int(8 * 1.15e9), bytes_accessed=1024, transcendentals=0),
        name="attend",
    )(slopes, triple, triple, triple, far, *deps)


def attend_back(triple, grad, far, slopes, deps=()):
    dp, micro, rows, wide = triple.shape
    frames = dp * rows
    width = wide // 3
    pairs = width // 128
    shape = (dp, 1, rows, 128)
    scale = HEAD ** (-0.5)

    def turned(left, right):
        return lax.dot_general(left, right, (((0,), (0,)), ((), ())), preferred_element_type=F32)

    def body(slope_ref, q_ref, k_ref, v_ref, g_ref, far_ref, *refs):
        out_ref, token_ref = refs[-2:]
        token_ref[...] = jnp.zeros_like(token_ref)
        h = pl.program_id(1)
        q, k, v, g = (flat_frames(ref[...]) for ref in (q_ref, k_ref, v_ref, g_ref))
        first = lax.broadcasted_iota(jnp.int32, (frames, 128), 1) < HEAD
        zero = jnp.zeros_like(q)
        grads = []
        for j in range(2):
            own_q = jnp.where(first, q, zero) if j == 0 else jnp.where(first, zero, q)
            own_g = jnp.where(first, g, zero) if j == 0 else jnp.where(first, zero, g)
            scores = nt(k, own_q) * scale - slope_ref[h * 2 + j] * far_ref[0]
            raised = jnp.exp(scores - jnp.max(scores, axis=0, keepdims=True))
            probs = raised * (1.0 / jnp.sum(raised, axis=0, keepdims=True))
            back = nt(v, own_g)
            back = probs * (back - jnp.sum(back * probs, axis=0, keepdims=True))
            low = back.astype(BF16)
            grads.append(
                (
                    turned(low, k) * scale,
                    jnp.dot(low, q, preferred_element_type=F32) * scale,
                    jnp.dot(probs.astype(BF16), g, preferred_element_type=F32),
                )
            )
        for i in range(3):
            out_ref[i] = by_source(jnp.where(first, grads[0][i], grads[1][i]), shape)

    def spec(offset):
        return pl.BlockSpec(shape, lambda m, h, s: (0, m, 0, h + offset))

    return pl.pallas_call(
        body,
        out_shape=[jax.ShapeDtypeStruct((3, dp, micro, rows, width), BF16), TOKEN],
        grid_spec=pltpu.PrefetchScalarGridSpec(
            num_scalar_prefetch=1,
            grid=(micro, pairs),
            in_specs=[
                spec(0),
                spec(pairs),
                spec(2 * pairs),
                spec(0),
                pl.BlockSpec((1, frames, frames), lambda m, h, s: (m, 0, 0)),
            ]
            + [ANY] * len(deps),
            out_specs=[
                pl.BlockSpec((3,) + shape, lambda m, h, s: (0, 0, m, 0, h)),
                pl.BlockSpec(TOKEN.shape, lambda m, h, s: (0, 0)),
            ],
        ),
        compiler_params=pltpu.CompilerParams(vmem_limit_bytes=24 * 2**20),
        cost_estimate=pl.CostEstimate(flops=int(2 * 1.15e9), bytes_accessed=1024, transcendentals=0),
        name="attend_back",
    )(slopes, triple, triple, triple, grad, far, *deps)


def add_up(values):
    total = values[0].astype(F32)
    for value in values[1:]:
        total = total + value.astype(F32)
    return total.astype(BF16)


class Reduction:
    def __init__(self, pairs, d, dims, deps=()):
        self.pairs = [(left, right if right.ndim == 3 else right[None]) for left, right in pairs]
        self.d = d
        self.dims = dims
        self.sent, self.token = gradient_blocks(self.pairs, d, dims, deps=deps)

    def share(self):
        return flip(self.sent, 1)

    def own(self, got, deps=(), others=()):
        pairs = self.pairs + [pair for other, _ in others for pair in other.pairs]
        gots = [got] + [arrived for _, arrived in others]
        *self.parts, self.token = gradient_blocks(pairs, self.d, self.dims, gots, deps)

    def near(self):
        parts = self.parts
        return [flip(parts[0], 1 << self.dims[0]), flip(parts[2], 1 << self.dims[-1])]

    def near_landed(self, got):
        self.halves = []
        for side, order in ((0, self.dims), (1, self.dims[::-1])):
            stay = self.parts[2 * side + 1]
            left = [bit for bit in self.dims if bit != order[0]]
            shape = (2,) * len(left) + stay.shape[1:]
            values = [stay.reshape(shape), got[side].reshape(shape)]
            self.halves.append((values, list(order[1:]), left))

    def step(self):
        sends, self.stays = [], []
        for values, order, left in self.halves:
            at = left.index(order[0])
            sends.append(add_up([lax.index_in_dim(v, 1, at, keepdims=False) for v in values]))
            self.stays.append([lax.index_in_dim(v, 0, at, keepdims=False) for v in values])
        bits = [order[0] for _, order, _ in self.halves]
        return [flip(sends[0], 1 << bits[0]), flip(sends[1], 1 << bits[1])]

    def landed(self, got):
        halves = []
        for i, (_, order, left) in enumerate(self.halves):
            halves.append((self.stays[i] + [got[i]], order[1:], [b for b in left if b != order[0]]))
        self.halves = halves

    def cross(self):
        while len(self.halves[0][1]) > 1:
            self.landed(self.step())
        return self.step()

    def rows(self):
        self.value = jnp.concatenate([add_up(values) for values, _, _ in self.halves], axis=1)
        self.stage = 0
        return self.value

    def along(self):
        rep = lax.axis_size("rep")
        half = rep // 2
        k = self.stage
        if k < half - 1:
            pairs = [(k, k + 1), (rep - 1 - k, rep - 2 - k)]
        elif k == half - 1:
            pairs = [(k, k + 1), (k + 1, k)]
        else:
            i = rep - 2 - k
            pairs = [(i + 1, i), (rep - 2 - i, rep - 1 - i)]
        return lax.ppermute(self.value, "rep", pairs)

    def along_landed(self, got):
        rep = lax.axis_size("rep")
        z = lax.axis_index("rep")
        k = self.stage
        self.stage += 1
        if k < rep // 2:
            self.value = add_up([self.value, got])
        else:
            i = rep - 2 - k
            self.value = jnp.where((z == i) | (z == rep - 1 - i), got, self.value)

    def finish(self):
        while self.stage < lax.axis_size("rep") - 1:
            self.along_landed(self.along())
        return self.value.astype(F32)


class RepSum:
    def __init__(self, value):
        self.value = value
        self.bits = lax.axis_size("rep").bit_length() - 1
        self.steps = 2 * self.bits
        self.done = 0

    def mine(self):
        k = self.done
        bit = k if k < self.bits else self.steps - 1 - k
        z = lax.axis_index("rep")
        return bit, lax.bitwise_and(lax.shift_right_logical(z, bit), 1)

    def send(self):
        bit, mine = self.mine()
        if self.done >= self.bits:
            return rep_flip(self.value, 1 << bit)
        size = self.value.shape[0] // 2
        sent = lax.dynamic_slice_in_dim(self.value, (1 - mine) * size, size, 0)
        self.keep = lax.dynamic_slice_in_dim(self.value, mine * size, size, 0)
        return rep_flip(sent, 1 << bit)

    def landed(self, got):
        _, mine = self.mine()
        if self.done < self.bits:
            self.value = add_up([self.keep, got])
        else:
            lower = jnp.where(mine == 0, self.value, got)
            upper = jnp.where(mine == 0, got, self.value)
            self.value = jnp.concatenate([lower, upper], axis=0)
        self.done += 1


def nt(left, right):
    return lax.dot_general(left, right, (((1,), (1,)), ((), ())), preferred_element_type=F32)


def hidden_gradient(grad_result, w_down, slope, deps=()):
    total, width = grad_result.shape
    units = w_down.shape[0]
    tile = 512

    def body(grad_ref, w_ref, slope_ref, *refs):
        out_ref, sum_ref = refs[-2:]
        value = nt(grad_ref[...], w_ref[...]) * slope_ref[...].astype(F32)
        out_ref[...] = value.astype(BF16)
        sum_ref[...] = jnp.sum(value, axis=0, keepdims=True)

    return pl.pallas_call(
        body,
        out_shape=[
            jax.ShapeDtypeStruct((total, units), BF16),
            jax.ShapeDtypeStruct((1, units), F32),
        ],
        grid=(units // tile,),
        in_specs=[
            pl.BlockSpec((total, width), lambda c: (0, 0)),
            pl.BlockSpec((tile, width), lambda c: (c, 0)),
            pl.BlockSpec((total, tile), lambda c: (0, c)),
        ]
        + [ANY] * len(deps),
        out_specs=[
            pl.BlockSpec((total, tile), lambda c: (0, c)),
            pl.BlockSpec((1, tile), lambda c: (0, c)),
        ],
        compiler_params=pltpu.CompilerParams(vmem_limit_bytes=24 * 2**20),
        cost_estimate=pl.CostEstimate(flops=int(3 * 1.15e9), bytes_accessed=1024, transcendentals=0),
        name="hidden_gradient",
    )(grad_result, w_down, slope, *deps)


def mixed_gradient(hidden_low, w_up, w_out, mixed, grad_result, gain, deps=()):
    total, units = hidden_low.shape
    width = w_up.shape[0]
    tile = 256

    def body(low_ref, up_ref, out_w_ref, mixed_ref, result_ref, gain_ref, *outs):
        grad_ref, rounded_ref, attended_ref, sums_ref = outs[-4:]
        grad = nt(low_ref[...], up_ref[...])
        unit, scale = norm_parts(mixed_ref[...])
        result = result_ref[...].astype(F32)
        value = result + norm_back(grad, gain_ref[...], unit, scale)
        rounded = value.astype(BF16)
        grad_ref[...] = value
        rounded_ref[...] = rounded
        attended_ref[...] = nt(rounded, out_w_ref[...]).astype(BF16)

        @pl.when(pl.program_id(0) == 0)
        def _():
            sums_ref[...] = jnp.zeros_like(sums_ref)

        for i, terms in enumerate((value, grad * unit, grad, result)):
            sums_ref[pl.ds(i, 1), :] += jnp.sum(terms, axis=0, keepdims=True)

    rows = pl.BlockSpec((tile, width), lambda r: (r, 0))
    whole = [
        pl.BlockSpec((width, units), lambda r: (0, 0)),
        pl.BlockSpec((width, width), lambda r: (0, 0)),
    ]
    return pl.pallas_call(
        body,
        out_shape=[
            jax.ShapeDtypeStruct((total, width), F32),
            jax.ShapeDtypeStruct((total, width), BF16),
            jax.ShapeDtypeStruct((total, width), BF16),
            jax.ShapeDtypeStruct((8, width), F32),
        ],
        grid=(total // tile,),
        in_specs=[pl.BlockSpec((tile, units), lambda r: (r, 0))]
        + whole
        + [rows, rows, pl.BlockSpec((1, width), lambda r: (0, 0))]
        + [ANY] * len(deps),
        out_specs=[rows, rows, rows, pl.BlockSpec((8, width), lambda r: (0, 0))],
        compiler_params=pltpu.CompilerParams(vmem_limit_bytes=44 * 2**20),
        cost_estimate=pl.CostEstimate(flops=int(2 * 1.15e9), bytes_accessed=1024, transcendentals=0),
        name="mixed_gradient",
    )(hidden_low, w_up, w_out, mixed, grad_result, gain.reshape(1, width), *deps)


def normed_gradient(grad_triple, w_qkv, deps=()):
    three, total, width = grad_triple.shape
    tile = 256

    def body(grad_ref, w_ref, *refs):
        out_ref = refs[-1]
        value = nt(grad_ref[0], w_ref[:, pl.ds(0, width)])
        for i in range(1, three):
            value += nt(grad_ref[i], w_ref[:, pl.ds(i * width, width)])
        out_ref[...] = value.astype(BF16)

    return pl.pallas_call(
        body,
        out_shape=jax.ShapeDtypeStruct((total, width), BF16),
        grid=(total // tile,),
        in_specs=[
            pl.BlockSpec((three, tile, width), lambda r: (0, r, 0)),
            pl.BlockSpec((width, three * width), lambda r: (0, 0)),
        ]
        + [ANY] * len(deps),
        out_specs=pl.BlockSpec((tile, width), lambda r: (r, 0)),
        compiler_params=pltpu.CompilerParams(vmem_limit_bytes=24 * 2**20),
        cost_estimate=pl.CostEstimate(flops=int(2 * 1.15e9), bytes_accessed=1024, transcendentals=0),
        name="normed_gradient",
    )(grad_triple, w_qkv, *deps)


def matmul(left, right):
    return jnp.dot(left, right, preferred_element_type=F32)


def matmul_nt(left, right):
    return lax.dot_general(left, right, (((1,), (1,)), ((), ())), preferred_element_type=F32)


def matmul_tn(left, right):
    return lax.dot_general(left, right, (((0,), (0,)), ((), ())), preferred_element_type=F32)


def norm_parts(values):
    average = jnp.mean(values, axis=-1, keepdims=True)
    centred = values - average
    spread = jnp.mean(centred * centred, axis=-1, keepdims=True)
    scale = lax.rsqrt(spread + EPS)
    return centred * scale, scale


def norm_back(grad, gain, unit, scale):
    e = grad * gain
    return scale * (
        e
        - jnp.mean(e, axis=-1, keepdims=True)
        - unit * jnp.mean(e * unit, axis=-1, keepdims=True)
    )


def shards(
    inputs,
    skips,
    cotangent,
    dest_slot,
    pack_segments,
    block_live,
    counts,
    w_skip,
    b_skip,
    g_one,
    b_one,
    w_qkv,
    w_out,
    b_out,
    g_two,
    b_two,
    w_up,
    c_up,
    w_down,
    c_down,
):
    dp = lax.axis_size("dp")
    rep = lax.axis_size("rep")
    d = lax.axis_index("dp")
    z = lax.axis_index("rep")
    micro = inputs.shape[0]
    frames = inputs.shape[2]
    width = inputs.shape[3]
    blocks = dest_slot.shape[2]
    block = frames // blocks
    per_pair = blocks // dp
    total = micro * frames
    bits = dp.bit_length() - 1
    place = jnp.stack([z, lax.rem(d, 8)]).astype(jnp.int32)
    dims = list(range(1, bits))
    small = jnp.concatenate([dest_slot.reshape(-1), block_live.reshape(-1), counts.reshape(-1)])

    own_skip = own_chunk(place, width, [w_skip])
    own_skip, small = together(own_skip, small)
    z_skip = Fetch(own_skip)
    z_skip.rest()
    got = z_skip.send()
    every = small[None]
    for bit in range(bits):
        every = jnp.concatenate([every, flip(every, 1 << bit)], axis=0)
    z_mid = Fetch(own_chunk(place, width, [w_qkv, w_out], z_skip.held[1:]))
    z_mid.rest()
    z_skip.landed(got)

    run_skip = Spread(z_skip.far(), width, [every, z_mid.held[-1]])
    mid = z_mid.send()
    run_skip.near_landed(run_skip.near())

    span = micro * blocks
    numbers = every[:, : 2 * span].reshape(dp, 2 * micro, blocks)
    numbers = jnp.transpose(numbers, (1, 0, 2)).reshape(2 * micro, dp * blocks).astype(F32)
    count_total = jnp.sum(every[:, 2 * span]).astype(F32).reshape(1, 1)
    inner = jnp.arange(frames) % block
    live = inner[None] < jnp.repeat(block_live[:, 0, :], block, axis=1)
    codes = (2 * pack_segments[:, 0, :] + live).astype(F32)
    joined = jnp.concatenate([inputs.reshape(total, width), skips.reshape(total, width)], axis=1)
    far, far_turned, keep_wide, shuffle = plan_order(
        numbers[:micro], numbers[micro:], codes, d, block, [run_skip.pairs[0], joined]
    )
    keep_rows = keep_wide[:, :1]

    run_skip.cross_landed(run_skip.cross(), [shuffle, mid])

    z_mid.landed(mid)
    run_mid = Spread(z_mid.far(), width)
    full_skip, _ = assemble(
        w_skip, run_skip.parts(run_skip.share()), place, 0, 1, [run_mid.start[0]]
    )
    z_up = Fetch(own_chunk(place, width, [w_up], [run_mid.start[0]]))
    z_up.rest()
    base = matmul(joined, full_skip) + b_skip
    unit_one, scale_one = norm_parts(base)
    own_normed = (unit_one * g_one + b_one).astype(BF16)
    sent = matmul(shuffle, own_normed).astype(BF16)
    run_mid.near_landed(run_mid.near(), [sent, z_up.held[-1]])

    def exchange(values):
        values = values.reshape(dp, total // dp, width)
        got = lax.all_to_all(values, "dp", split_axis=0, concat_axis=0, tiled=True)
        return got.reshape(total, width)

    normed = exchange(sent)
    up = z_up.send([sent])
    z_down = Fetch(own_chunk(place, width, [w_down], [z_up.held[-1], sent]))
    z_down.rest()
    run_mid.cross_landed(run_mid.cross(), [up, z_down.held[-1], normed])
    z_up.landed(up)

    other = run_mid.share()
    run_up = Spread(z_up.far(), width, [run_mid.every])
    run_up.near_landed(run_up.near(), [other])
    shard_rows = w_qkv.shape[0] // 8
    parts_mid = run_mid.parts(other)
    full_qkv, _ = assemble(w_qkv, parts_mid, place, 0, 3)

    triple = matmul(normed, full_qkv).astype(BF16)
    triple = triple.reshape(dp, micro, per_pair * block, 3 * width)
    slopes = 2.0 ** (-8.0 * (jnp.arange(HEADS, dtype=F32) + 1.0) / HEADS)
    attended = attend(triple, far, slopes, [run_up.pairs[0]])
    down = z_down.send()
    run_up.cross_landed(run_up.cross(), [attended, down])
    z_down.landed(down)

    attended = exchange(attended)
    other = run_up.share()
    run_down = Spread(z_down.far(), width, [run_up.every])
    down = run_down.near()
    full_out, out_token = assemble(w_out, parts_mid, place, 3 * shard_rows, 1, [run_up.every])
    full_up, up_token = assemble(w_up, run_up.parts(other), place, 0, w_up.shape[1] // width)
    attended, out_token, up_token = together(attended, out_token, up_token)

    attended = matmul_tn(shuffle, attended).astype(BF16)
    mixed = base + matmul(attended, full_out) + (b_out + out_token[0, 0])
    unit_two, scale_two = norm_parts(mixed)
    normed_two = (unit_two * g_two + b_two).astype(BF16)
    count_total = count_total + up_token[:1, :1]
    for step in rep_steps(rep):
        count_total = count_total + rep_flip(count_total, step)
    share = counts[0, 0].astype(F32) * (dp * rep) / count_total[0, 0]
    run_down.near_landed(down, [up_token])
    down = run_down.cross()
    hidden = matmul(normed_two, full_up) + (c_up + run_down.token[0, 0])
    phi = 0.5 * (1.0 + lax.erf(hidden * (0.5**0.5)))
    active = (hidden * phi).astype(BF16)
    slope = (phi + hidden * jnp.exp(-0.5 * hidden * hidden) * ((2 * jnp.pi) ** -0.5)).astype(BF16)
    scaled = (cotangent.reshape(total, width).astype(F32) * share).astype(BF16)
    grad_result = scaled * keep_rows.astype(BF16)
    red_down = Reduction([(active, grad_result)], d, dims)

    down_got = red_down.share()
    run_down.cross_landed(down, [red_down.sent])
    full_down, _ = assemble(w_down, run_down.parts(run_down.share()), place, 0, 1)

    hidden_low, sum_hidden = hidden_gradient(grad_result, full_down, slope)
    red_up = Reduction([(normed_two, hidden_low)], d, dims)
    up_got = red_up.share()
    red_down.own(down_got, [red_up.sent])
    flying = red_down.near()
    grad_mixed, mixed_low, grad_attended, sums_mixed = mixed_gradient(
        hidden_low, full_up, full_out, mixed, grad_result, g_two, [red_down.token]
    )
    red_out = Reduction([(attended, mixed_low)], d, dims)
    out_got = red_out.share()
    flying, sums_mixed = together(flying, sums_mixed)
    red_down.near_landed(flying)

    down_flying = red_down.cross()
    sent = matmul(shuffle, grad_attended).astype(BF16)
    grad_attended = exchange(sent)
    red_up.own(up_got, [sent], [(red_out, out_got)])
    flying = red_up.near()
    down_flying, token = together(down_flying, red_up.token)
    red_down.landed(down_flying)
    red_down.rows()

    line = red_down.along()
    grad_attended = grad_attended.reshape(dp, micro, per_pair * block, width)
    grad_triple, token = attend_back(
        triple, grad_attended, far_turned, slopes, [red_down.value, token]
    )
    grad_triple = grad_triple.reshape(3, total, width)

    sent = normed_gradient(grad_triple, full_qkv)
    grad_normed = exchange(sent)
    flying, line, token = together(flying, line, token)
    red_mid = Reduction([(normed, grad_triple)], d, dims, [sent, token])
    grad_normed, token = together(grad_normed, red_mid.token)
    red_up.near_landed(flying)
    red_down.along_landed(line)
    up_flying = red_up.cross()
    line = red_down.along()

    mid_got = red_mid.share()
    grad_normed = matmul_tn(shuffle, grad_normed)
    grad_base = grad_mixed + norm_back(grad_normed, g_one, unit_one, scale_one)
    base_low = grad_base.astype(BF16)
    red_skip = Reduction([(joined, base_low)], d, dims, [token])
    skip_got = red_skip.share()
    vectors = (
        jnp.sum(grad_base, axis=0),
        jnp.sum(grad_normed * unit_one, axis=0),
        jnp.sum(grad_normed, axis=0),
        sums_mixed[0],
        sums_mixed[1],
        sums_mixed[2],
        sum_hidden[0],
        sums_mixed[3],
    )
    lengths = [v.shape[0] for v in vectors]
    summed = jnp.concatenate(vectors).reshape(-1, 128)
    for bit in range(bits - 1):
        summed = summed + flip(summed, 1 << bit)
    up_flying, token = together(up_flying, red_skip.token)
    red_up.landed(up_flying)
    red_up.rows()
    up_line = red_up.along()
    red_mid.own(mid_got, [token])
    summed, token = together(summed, red_mid.token)

    flying = red_mid.near()
    red_skip.own(skip_got, [token])
    skip_flying = red_skip.near()
    line, token = together(line, red_skip.token)
    red_down.along_landed(line)
    line = red_down.along()
    result = mixed + matmul(active, full_down) + (c_down + token[0, 0])
    output = (result * keep_rows).astype(BF16)
    grad_joined = matmul_nt(base_low, full_skip).astype(BF16)
    flying, up_line, grad_joined, summed = together(flying, up_line, grad_joined, summed)
    red_mid.near_landed(flying)
    red_up.along_landed(up_line)

    flying = red_mid.cross()
    up_line = red_up.along()
    flying, line, skip_flying, summed = together(flying, line, skip_flying, summed)
    red_down.along_landed(line)
    red_skip.near_landed(skip_flying)
    red_mid.landed(flying)

    mid_sum = RepSum(red_mid.rows())
    skip_flying = red_skip.cross()
    got = mid_sum.send()
    last = flip(summed, 1 << (bits - 1))
    got, up_line, skip_flying, last = together(got, up_line, skip_flying, last)
    mid_sum.landed(got)
    red_up.along_landed(up_line)
    red_skip.landed(skip_flying)
    summed = summed + last
    up_line = red_up.along()
    skip_columns = w_skip.shape[1]
    extra = jnp.pad(summed.reshape(-1), (0, -summed.size % (16 * rep * skip_columns)))
    extra = extra.reshape(-1, skip_columns).astype(BF16)
    skip_sum = RepSum(jnp.concatenate([red_skip.rows(), extra], axis=0))
    while mid_sum.done < mid_sum.steps:
        mid_got, skip_got = mid_sum.send(), skip_sum.send()
        if mid_sum.done == 1:
            mid_got, skip_got, up_line = together(mid_got, skip_got, up_line)
        else:
            mid_got, skip_got = together(mid_got, skip_got)
        mid_sum.landed(mid_got)
        skip_sum.landed(skip_got)
    skip_sum.landed(skip_sum.send())
    red_up.along_landed(up_line)
    final_mid = mid_sum.value.astype(F32)
    final_skip = skip_sum.value.astype(F32)
    own_rows = w_skip.shape[0] * rep // dp
    summed = final_skip[own_rows:].reshape(-1)
    final_up = red_up.finish()
    units = c_up.shape[0]
    finals = [
        red_down.finish(),
        final_up[:, :units],
        final_up[:, units:],
        final_mid,
        final_skip[:own_rows],
    ]
    sums = []
    offset = 0
    for length in lengths:
        sums.append(summed[offset : offset + length])
        offset += length

    def as_owned(values):
        return values.reshape(inputs.shape)

    return (
        as_owned(output),
        as_owned(grad_joined[:, :width]),
        as_owned(grad_joined[:, width:]),
        finals[4],
        sums[0],
        sums[1],
        sums[2],
        finals[3],
        finals[2],
        sums[3],
        sums[4],
        sums[5],
        finals[1],
        sums[6],
        finals[0],
        sums[7],
    )


def solution(mesh):
    frames = P(None, "rep", "dp", None)
    slots = P(None, "rep", "dp")
    rows = P("rep", None)
    whole = P()
    in_specs = (
        (frames,) * 3
        + (slots,) * 3
        + (P("dp", "rep"), rows, whole, whole, whole, rows, rows)
        + (whole,) * 3
        + (rows, whole, rows, whole)
    )
    split = P("dp", None)
    out_specs = (
        (frames,) * 3
        + (split,)
        + (whole,) * 3
        + (split, split)
        + (whole,) * 3
        + (split, whole, split, whole)
    )
    return jax.shard_map(shards, mesh=mesh, in_specs=in_specs, out_specs=out_specs, check_vma=False)
```

```python
import jax
import jax.numpy as jnp
from jax import lax
from jax.experimental import pallas as pl
from jax.experimental.pallas import tpu as pltpu
from jax.sharding import PartitionSpec as P

HEADS = 16
HEAD = 64
EPS = 1e-05
F32 = jnp.float32
BF16 = jnp.bfloat16
TOKEN = jax.ShapeDtypeStruct((8, 128), F32)
ANY = pl.BlockSpec(memory_space=pl.ANY)
LIGHT = pl.CostEstimate(flops=1024, bytes_accessed=1024, transcendentals=0)


def flip(value, bit):
    n = lax.axis_size("dp")
    return lax.ppermute(value, "dp", [(i, i ^ bit) for i in range(n)])


def rep_flip(value, bit):
    n = lax.axis_size("rep")
    return lax.ppermute(value, "rep", [(i, i ^ bit) for i in range(n)])


def after(value, *earlier):
    return lax.optimization_barrier((value,) + earlier)[0]


def together(*values):
    return lax.optimization_barrier(values)


def assemble(w_local, parts, place, row_at, tiles, deps=()):
    rep = lax.axis_size("rep")
    shard_rows, columns = w_local.shape
    rows = shard_rows // 8
    tile = columns // tiles
    half = tile // 2
    chunk_rows = parts[0][0].shape[0] // (len(parts[0][1]) * (rep - 1))
    arrays = [part[0] for part in parts]
    count = 1 + sum(len(part[1]) for part in parts) * (rep - 1) * tiles

    def body(place_ref, local_ref, *refs):
        out_ref, token_ref, sems = refs[-3:]
        token_ref[...] = jnp.zeros_like(token_ref)
        z = place_ref[0]
        e = place_ref[1]
        copies = [
            pltpu.make_async_copy(
                local_ref,
                out_ref.at[pl.ds(pl.multiple_of(z * shard_rows, 16), shard_rows), :],
                sems.at[0],
            )
        ]
        for ref, (_, runs) in zip(refs, parts):
            for k, (side, rel) in enumerate(runs):
                chunk = jnp.bitwise_xor(e, rel)
                for s, apart in enumerate(far_order(rep), 1):
                    shard = jnp.bitwise_xor(z, apart)
                    start = pl.multiple_of(shard * shard_rows + chunk * rows, 16)
                    for t in range(tiles):
                        at = (k * (rep - 1) + s - 1) * chunk_rows + row_at + t * rows
                        copies.append(
                            pltpu.make_async_copy(
                                ref.at[pl.ds(at, rows), :],
                                out_ref.at[pl.ds(start, rows), pl.ds(t * tile + side * half, half)],
                                sems.at[len(copies)],
                            )
                        )
        for copy in copies:
            copy.start()
        for copy in copies:
            copy.wait()

    return pl.pallas_call(
        body,
        out_shape=[jax.ShapeDtypeStruct((shard_rows * rep, columns), w_local.dtype), TOKEN],
        grid=(1,),
        in_specs=[pl.BlockSpec(memory_space=pltpu.SMEM)] + [ANY] * (1 + len(parts) + len(deps)),
        out_specs=[
            pl.BlockSpec((shard_rows * rep, columns), lambda i: (0, 0)),
            pl.BlockSpec(TOKEN.shape, lambda i: (0, 0)),
        ],
        scratch_shapes=[pltpu.SemaphoreType.DMA((count,))],
        compiler_params=pltpu.CompilerParams(vmem_limit_bytes=26 * 2**20),
        cost_estimate=pl.CostEstimate(flops=int(1.5 * 1.15e9), bytes_accessed=1024, transcendentals=0),
        name="assemble",
    )(place, w_local, *arrays, *deps)


def own_chunk(place, width, shards_local, deps=()):
    items = []
    for which, w_local in enumerate(shards_local):
        for t in range(w_local.shape[1] // width):
            items.append((which, w_local.shape[0] // 8, t * width))
    total = sum(item[1] for item in items)

    def body(place_ref, *refs):
        out_ref, sems = refs[-2:]
        copies = []
        at = 0
        for which, rows, column in items:
            start = pl.multiple_of(place_ref[1] * rows, 16)
            copies.append(
                pltpu.make_async_copy(
                    refs[which].at[pl.ds(start, rows), pl.ds(column, width)],
                    out_ref.at[pl.ds(at, rows), :],
                    sems.at[len(copies)],
                )
            )
            at += rows
        for copy in copies:
            copy.start()
        for copy in copies:
            copy.wait()

    return pl.pallas_call(
        body,
        out_shape=jax.ShapeDtypeStruct((total, width), shards_local[0].dtype),
        grid=(1,),
        in_specs=[pl.BlockSpec(memory_space=pltpu.SMEM)]
        + [ANY] * (len(shards_local) + len(deps)),
        out_specs=pl.BlockSpec((total, width), lambda i: (0, 0)),
        scratch_shapes=[pltpu.SemaphoreType.DMA((len(items),))],
        compiler_params=pltpu.CompilerParams(vmem_limit_bytes=24 * 2**20),
        cost_estimate=LIGHT,
        name="own_chunk",
    )(place, *shards_local, *deps)


def pack(arrays, outs, deps=()):
    count = sum(len(out) for out in outs)

    def body(*refs):
        sources, targets = refs[: len(arrays)], refs[-2 - len(outs) : -2]
        token_ref, sems = refs[-2:]
        token_ref[...] = jnp.zeros_like(token_ref)
        copies = []
        for target, out in zip(targets, outs):
            at = 0
            for which, row, rows, column, columns in out:
                copies.append(
                    pltpu.make_async_copy(
                        sources[which].at[pl.ds(row, rows), pl.ds(column, columns)],
                        target.at[pl.ds(at, rows), :],
                        sems.at[len(copies)],
                    )
                )
                at += rows
        for copy in copies:
            copy.start()
        for copy in copies:
            copy.wait()

    return pl.pallas_call(
        body,
        out_shape=[
            jax.ShapeDtypeStruct((sum(item[2] for item in out), out[0][4]), arrays[0].dtype)
            for out in outs
        ]
        + [TOKEN],
        grid=(1,),
        in_specs=[ANY] * (len(arrays) + len(deps)),
        out_specs=[
            pl.BlockSpec((sum(item[2] for item in out), out[0][4]), lambda i: (0, 0))
            for out in outs
        ]
        + [pl.BlockSpec(TOKEN.shape, lambda i: (0, 0))],
        scratch_shapes=[pltpu.SemaphoreType.DMA((count,))],
        compiler_params=pltpu.CompilerParams(vmem_limit_bytes=24 * 2**20),
        cost_estimate=LIGHT,
        name="pack",
    )(*arrays, *deps)


def far_order(rep):
    order = [0]
    for bit in reversed(range(rep.bit_length() - 1)):
        order = order + [distance ^ (1 << bit) for distance in order]
    return order[1:]


class Spread:
    def __init__(self, gots, width, deps=()):
        self.half = width // 2
        rows = sum(got.shape[0] for got in gots)
        items = [(i, 0, got.shape[0]) for i, got in enumerate(gots)]
        *self.start, _ = pack(
            gots, [[item + (column, self.half) for item in items] for column in (0, self.half)], deps
        )
        self.n = rows

    def near(self):
        return [flip(self.start[0], 2), flip(self.start[1], 4)]

    def near_landed(self, got, deps=()):
        whole = [(i, 0, self.n, 0, self.half) for i in range(4)]
        *self.pairs, self.token = pack(
            [self.start[0], got[0], self.start[1], got[1]], [whole[:2], whole[2:]], deps
        )

    def cross(self):
        return [flip(self.pairs[0], 4), flip(self.pairs[1], 2)]

    def cross_landed(self, got, deps=()):
        whole = [(i, 0, 2 * self.n, 0, self.half) for i in range(4)]
        self.every, self.token = pack([self.pairs[0], got[0], self.pairs[1], got[1]], [whole], deps)

    def share(self):
        return flip(self.every, 1)

    def parts(self, other):
        runs = [(0, 0), (0, 2), (0, 4), (0, 6), (1, 0), (1, 4), (1, 2), (1, 6)]
        return [(self.every, runs), (other, [(side, rel | 1) for side, rel in runs])]


def rep_steps(rep):
    return [1 << bit for bit in reversed(range(rep.bit_length() - 1))]


class Fetch:
    def __init__(self, own):
        self.held = [own]
        self.steps = rep_steps(lax.axis_size("rep"))

    def send(self, deps=()):
        sent = self.held[0]
        if len(self.held) > 1:
            whole = [(i, 0, a.shape[0], 0, a.shape[1]) for i, a in enumerate(self.held)]
            sent, _ = pack(self.held, [whole], deps)
        return rep_flip(sent, self.steps[len(self.held) - 1])

    def landed(self, got):
        self.held.append(got)

    def rest(self):
        while len(self.held) < len(self.steps):
            self.landed(self.send())

    def far(self):
        return self.held[1:]


def plan_order(all_slots, all_live, codes, d, block, deps=()):
    micro, owners = all_slots.shape
    frames = codes.shape[1]
    blocks = frames // block
    dp = owners // blocks
    per_pair = blocks // dp
    total = micro * frames

    def column(row):
        return jnp.broadcast_to(row, (128, row.shape[1])).T[:, :1]

    def as_row(values):
        return jnp.broadcast_to(values, (values.shape[0], 128)).T[:1, :]

    def body(d_ref, slots_ref, live_ref, codes_ref, *refs):
        far_ref, turned_ref, keep_ref, shuffle_ref = refs[-4:]
        me = d_ref[0]
        lane = lax.broadcasted_iota(jnp.int32, (1, owners), 1)
        source = jnp.bitwise_xor(lax.div(lane, jnp.int32(blocks)), me)
        first_slot = (source * blocks).astype(F32) + lax.rem(lane, jnp.int32(blocks)).astype(F32)
        source_col = column(source.astype(F32))
        frame = lax.broadcasted_iota(jnp.int32, (frames, 1), 0)
        block_of = lax.div(frame, jnp.int32(block)).astype(F32)
        inner = lax.rem(frame, jnp.int32(block)).astype(F32)
        low = (me * blocks).astype(F32)
        rows = []
        for m in range(micro):
            slots = slots_ref[pl.ds(m, 1), :]
            slots_col = column(slots)
            same = source_col == source.astype(F32)
            rank = jnp.sum(jnp.where(same & (slots_col < slots), 1.0, 0.0), axis=0, keepdims=True)
            here = (slots >= low) & (slots < low + blocks)
            arrive = source.astype(F32) * per_pair + rank - (me * per_pair).astype(F32)
            arrive = jnp.where(here, arrive, -1.0)
            placed = jnp.sum(
                jnp.where(arrive == block_of, slots - low, 0.0), axis=1, keepdims=True
            )
            position = placed * block + inner
            at = lax.broadcasted_iota(jnp.int32, (1, frames), 1).astype(F32)
            code = jnp.sum(
                jnp.where(at == position, codes_ref[pl.ds(m, 1), :], 0.0), axis=1, keepdims=True
            )
            position_row, code_row = as_row(position), as_row(code)
            segment, segment_row = jnp.floor(code * 0.5), jnp.floor(code_row * 0.5)
            live_row = code_row - 2.0 * segment_row
            distance = jnp.abs(position - position_row)
            allowed = (segment == segment_row) & ((live_row > 0.5) | (distance < 0.5))
            far_ref[m] = jnp.where(allowed, distance, 1e32)
            live_col = code - 2.0 * segment
            allowed = (segment == segment_row) & ((live_col > 0.5) | (distance < 0.5))
            turned_ref[m] = jnp.where(allowed, distance, 1e32)
            own = lane < blocks
            mine = jnp.sum(
                jnp.where(own & (lane.astype(F32) == block_of), slots, 0.0), axis=1, keepdims=True
            )
            alive = jnp.sum(
                jnp.where(first_slot == mine, live_ref[pl.ds(m, 1), :], 0.0), axis=1, keepdims=True
            )
            keep_ref[pl.ds(m * frames, frames), :] = jnp.broadcast_to(
                jnp.where(inner < alive, 1.0, 0.0), (frames, 128)
            )
            my_rank = jnp.sum(
                jnp.where(own & (lane.astype(F32) == block_of), rank, 0.0), axis=1, keepdims=True
            )
            target = jnp.floor((my_rank + 0.5) / per_pair)
            row = (target * micro + m) * per_pair + (my_rank - target * per_pair)
            rows.append(as_row(row * block + inner))
        goal = jnp.concatenate(rows, axis=1)
        spot = lax.broadcasted_iota(jnp.int32, (total, total), 0).astype(F32)
        shuffle_ref[...] = jnp.where(spot == goal, 1.0, 0.0).astype(BF16)

    vmem = pl.BlockSpec(memory_space=pltpu.VMEM)
    return pl.pallas_call(
        body,
        out_shape=[
            jax.ShapeDtypeStruct((micro, frames, frames), F32),
            jax.ShapeDtypeStruct((micro, frames, frames), F32),
            jax.ShapeDtypeStruct((total, 128), F32),
            jax.ShapeDtypeStruct((total, total), BF16),
        ],
        in_specs=[pl.BlockSpec(memory_space=pltpu.SMEM), vmem, vmem, vmem] + [ANY] * len(deps),
        out_specs=[vmem, vmem, vmem, vmem],
        compiler_params=pltpu.CompilerParams(vmem_limit_bytes=24 * 2**20),
        cost_estimate=LIGHT,
        name="plan_order",
    )(d.reshape(1).astype(jnp.int32), all_slots, all_live, codes, *deps)


def gradient_blocks(pairs, d, dims, got=None, deps=()):
    dp = lax.axis_size("dp")
    total, all_rows = pairs[0][0].shape
    widths = [right.shape[2] for _, right in pairs]
    columns = sum(right.shape[0] * right.shape[2] for _, right in pairs)
    rows = all_rows // dp
    count = dp // 2
    odd = 1 if got is None else 0
    tile = min(min(widths), 512)
    splits = [width // tile for width in widths]
    tiles = [right.shape[0] * split for (_, right), split in zip(pairs, splits)]
    steps = sum(tiles)
    starts = [sum(tiles[:i]) for i in range(len(tiles))]

    def distance(p):
        rel = odd
        for k, bit in enumerate(dims):
            rel += ((p >> (len(dims) - 1 - k)) & 1) << bit
        return rel

    upper = [p for p in range(count) if p >= count // 2]
    lower = [p for p in range(count) if p < count // 2]
    odds = [p for p in range(count) if p % 2 == 1]
    evens = [p for p in range(count) if p % 2 == 0]
    chosen = (upper, lower, odds, evens)

    if rows % 128 != 0:
        products = []
        for left, right in pairs:
            flat = jnp.transpose(right, (1, 0, 2)).reshape(total, -1)
            products.append(matmul_tn(left, flat))
        product = jnp.concatenate(products, axis=1).reshape(dp, rows, columns)
        rel = jnp.array([distance(p) for p in range(count)], jnp.int32)
        product = product[jnp.bitwise_xor(rel, d)]
        token = jnp.zeros(TOKEN.shape, F32) + product[0, :1, :1]
        if got is None:
            return [product.astype(BF16), token]
        product = (product + jnp.concatenate(got, axis=2).astype(F32)).astype(BF16)
        half = columns // 2
        return [
            jnp.stack([product[p, :, side * half : (side + 1) * half] for p in ps])
            for side, ps in zip((0, 0, 1, 1), chosen)
        ] + [token]

    def body(d_ref, *refs):
        lefts = refs[: len(pairs)]
        rights = refs[len(pairs) : 2 * len(pairs)]
        got_refs = refs[2 * len(pairs) : 3 * len(pairs)]
        token_ref, turned_ref = refs[-2:]
        outs = refs[-3:-2] if got is None else refs[-6:-2]
        c = pl.program_id(0)

        @pl.when(c == 0)
        def _():
            token_ref[...] = jnp.zeros_like(token_ref)
            for i, left_ref in enumerate(lefts):
                for p in range(count):
                    at = pl.multiple_of(jnp.bitwise_xor(d_ref[0], distance(p)) * rows, 128)
                    turned_ref[i, pl.ds(p * rows, rows), :] = left_ref[:, pl.ds(at, rows)].T

        def piece(i, p):
            return jnp.dot(
                turned_ref[i, pl.ds(p * rows, rows), :], rights[i][0], preferred_element_type=F32
            )

        def write(i, half):
            for p in range(count):
                value = piece(i, p)
                if got is None:
                    outs[0][p] = value.astype(BF16)
                    continue
                value = (value + got_refs[i][p].astype(F32)).astype(BF16)
                for which in (2 * half, 2 * half + 1):
                    if p in chosen[which]:
                        outs[which][chosen[which].index(p)] = value

        for i in range(len(pairs)):
            for half in (0, 1):
                low = max(starts[i], half * (steps // 2))
                high = min(starts[i] + tiles[i], (half + 1) * (steps // 2))
                if low < high:
                    pl.when((c >= low) & (c < high))(lambda i=i, half=half: write(i, half))

    def right_spec(start, n, split):
        def at(c, d_ref):
            k = jnp.clip(c - start, 0, n - 1)
            return (lax.div(k, jnp.int32(split)), 0, lax.rem(k, jnp.int32(split)))

        return pl.BlockSpec((1, total, tile), at)

    in_specs = [pl.BlockSpec((total, all_rows), lambda c, d_ref: (0, 0))] * len(pairs)
    in_specs += [right_spec(*item) for item in zip(starts, tiles, splits)]
    args = [left for left, _ in pairs] + [right for _, right in pairs]
    if got is None:
        out_shape = [jax.ShapeDtypeStruct((count, rows, columns), BF16)]
        out_specs = [pl.BlockSpec((count, rows, tile), lambda c, d_ref: (0, 0, c))]
    else:
        for start, n in zip(starts, tiles):
            in_specs.append(
                pl.BlockSpec(
                    (count, rows, tile),
                    lambda c, d_ref, start=start, n=n: (0, 0, jnp.clip(c - start, 0, n - 1)),
                )
            )
        args += got
        out_shape = [jax.ShapeDtypeStruct((count // 2, rows, columns // 2), BF16)] * 4
        mid = steps // 2
        first = pl.BlockSpec(
            (count // 2, rows, tile), lambda c, d_ref: (0, 0, jnp.minimum(c, mid - 1))
        )
        second = pl.BlockSpec(
            (count // 2, rows, tile), lambda c, d_ref: (0, 0, jnp.maximum(c - mid, 0))
        )
        out_specs = [first, first, second, second]
    out_shape = out_shape + [TOKEN]
    out_specs = out_specs + [pl.BlockSpec(TOKEN.shape, lambda c, d_ref: (0, 0))]
    in_specs += [ANY] * len(deps)
    return pl.pallas_call(
        body,
        out_shape=out_shape,
        grid_spec=pltpu.PrefetchScalarGridSpec(
            num_scalar_prefetch=1,
            grid=(steps,),
            in_specs=in_specs,
            out_specs=out_specs,
            scratch_shapes=[pltpu.VMEM((len(pairs), count * rows, total), BF16)],
        ),
        compiler_params=pltpu.CompilerParams(vmem_limit_bytes=34 * 2**20),
        cost_estimate=pl.CostEstimate(flops=int(2.5 * 1.15e9), bytes_accessed=1024, transcendentals=0),
        name="gradient",
    )(d.reshape(1).astype(jnp.int32), *args, *deps)


def head_probs(q, k, far, slope):
    scores = lax.dot_general(q, k, (((1,), (1,)), ((), ())), preferred_element_type=F32)
    scores = scores * (HEAD ** (-0.5)) - slope * far
    raised = jnp.exp(scores - jnp.max(scores, axis=-1, keepdims=True))
    return raised * (1.0 / jnp.sum(raised, axis=-1, keepdims=True))


def flat_frames(block):
    sources, _, rows, lanes = block.shape
    if rows % 16 == 0:
        return block.reshape(sources * rows, lanes)
    return block.astype(F32).reshape(sources * rows, lanes).astype(BF16)


def by_source(value, like):
    sources, _, rows, lanes = like
    if rows % 16 == 0:
        return value.astype(BF16).reshape(sources, 1, rows, lanes)
    return value.reshape(sources, 1, rows, lanes).astype(BF16)


def attend(triple, far, slopes, deps=()):
    dp, micro, rows, wide = triple.shape
    frames = dp * rows
    width = wide // 3
    pairs = width // 128
    shape = (dp, 1, rows, 128)

    def body(slope_ref, q_ref, k_ref, v_ref, far_ref, *refs):
        out_ref = refs[-1]
        h = pl.program_id(1)
        q, k, v = (flat_frames(ref[...]) for ref in (q_ref, k_ref, v_ref))
        first = lax.broadcasted_iota(jnp.int32, (frames, 128), 1) < HEAD
        zero = jnp.zeros_like(q)
        outs = []
        for j, own in enumerate((jnp.where(first, q, zero), jnp.where(first, zero, q))):
            probs = head_probs(own, k, far_ref[0], slope_ref[h * 2 + j])
            outs.append(jnp.dot(probs.astype(BF16), v, preferred_element_type=F32))
        out_ref[...] = by_source(jnp.where(first, outs[0], outs[1]), shape)

    def spec(offset):
        return pl.BlockSpec(shape, lambda m, h, s: (0, m, 0, h + offset))

    return pl.pallas_call(
        body,
        out_shape=jax.ShapeDtypeStruct((dp, micro, rows, width), BF16),
        grid_spec=pltpu.PrefetchScalarGridSpec(
            num_scalar_prefetch=1,
            grid=(micro, pairs),
            in_specs=[
                spec(0),
                spec(pairs),
                spec(2 * pairs),
                pl.BlockSpec((1, frames, frames), lambda m, h, s: (m, 0, 0)),
            ]
            + [ANY] * len(deps),
            out_specs=spec(0),
        ),
        compiler_params=pltpu.CompilerParams(vmem_limit_bytes=24 * 2**20),
        cost_estimate=pl.CostEstimate(flops=int(8 * 1.15e9), bytes_accessed=1024, transcendentals=0),
        name="attend",
    )(slopes, triple, triple, triple, far, *deps)


def attend_back(triple, grad, far, slopes, deps=()):
    dp, micro, rows, wide = triple.shape
    frames = dp * rows
    width = wide // 3
    pairs = width // 128
    shape = (dp, 1, rows, 128)
    scale = HEAD ** (-0.5)

    def turned(left, right):
        return lax.dot_general(left, right, (((0,), (0,)), ((), ())), preferred_element_type=F32)

    def body(slope_ref, q_ref, k_ref, v_ref, g_ref, far_ref, *refs):
        out_ref, token_ref = refs[-2:]
        token_ref[...] = jnp.zeros_like(token_ref)
        h = pl.program_id(1)
        q, k, v, g = (flat_frames(ref[...]) for ref in (q_ref, k_ref, v_ref, g_ref))
        first = lax.broadcasted_iota(jnp.int32, (frames, 128), 1) < HEAD
        zero = jnp.zeros_like(q)
        grads = []
        for j in range(2):
            own_q = jnp.where(first, q, zero) if j == 0 else jnp.where(first, zero, q)
            own_g = jnp.where(first, g, zero) if j == 0 else jnp.where(first, zero, g)
            scores = nt(k, own_q) * scale - slope_ref[h * 2 + j] * far_ref[0]
            raised = jnp.exp(scores - jnp.max(scores, axis=0, keepdims=True))
            probs = raised * (1.0 / jnp.sum(raised, axis=0, keepdims=True))
            back = nt(v, own_g)
            back = probs * (back - jnp.sum(back * probs, axis=0, keepdims=True))
            low = back.astype(BF16)
            grads.append(
                (
                    turned(low, k) * scale,
                    jnp.dot(low, q, preferred_element_type=F32) * scale,
                    jnp.dot(probs.astype(BF16), g, preferred_element_type=F32),
                )
            )
        for i in range(3):
            out_ref[i] = by_source(jnp.where(first, grads[0][i], grads[1][i]), shape)

    def spec(offset):
        return pl.BlockSpec(shape, lambda m, h, s: (0, m, 0, h + offset))

    return pl.pallas_call(
        body,
        out_shape=[jax.ShapeDtypeStruct((3, dp, micro, rows, width), BF16), TOKEN],
        grid_spec=pltpu.PrefetchScalarGridSpec(
            num_scalar_prefetch=1,
            grid=(micro, pairs),
            in_specs=[
                spec(0),
                spec(pairs),
                spec(2 * pairs),
                spec(0),
                pl.BlockSpec((1, frames, frames), lambda m, h, s: (m, 0, 0)),
            ]
            + [ANY] * len(deps),
            out_specs=[
                pl.BlockSpec((3,) + shape, lambda m, h, s: (0, 0, m, 0, h)),
                pl.BlockSpec(TOKEN.shape, lambda m, h, s: (0, 0)),
            ],
        ),
        compiler_params=pltpu.CompilerParams(vmem_limit_bytes=24 * 2**20),
        cost_estimate=pl.CostEstimate(flops=int(2 * 1.15e9), bytes_accessed=1024, transcendentals=0),
        name="attend_back",
    )(slopes, triple, triple, triple, grad, far, *deps)


def add_up(values):
    total = values[0].astype(F32)
    for value in values[1:]:
        total = total + value.astype(F32)
    return total.astype(BF16)


class Reduction:
    def __init__(self, pairs, d, dims, deps=()):
        self.pairs = [(left, right if right.ndim == 3 else right[None]) for left, right in pairs]
        self.d = d
        self.dims = dims
        self.sent, self.token = gradient_blocks(self.pairs, d, dims, deps=deps)

    def share(self):
        return flip(self.sent, 1)

    def own(self, got, deps=(), others=()):
        pairs = self.pairs + [pair for other, _ in others for pair in other.pairs]
        gots = [got] + [arrived for _, arrived in others]
        *self.parts, self.token = gradient_blocks(pairs, self.d, self.dims, gots, deps)

    def near(self):
        parts = self.parts
        return [flip(parts[0], 1 << self.dims[0]), flip(parts[2], 1 << self.dims[-1])]

    def near_landed(self, got):
        self.halves = []
        for side, order in ((0, self.dims), (1, self.dims[::-1])):
            stay = self.parts[2 * side + 1]
            left = [bit for bit in self.dims if bit != order[0]]
            shape = (2,) * len(left) + stay.shape[1:]
            values = [stay.reshape(shape), got[side].reshape(shape)]
            self.halves.append((values, list(order[1:]), left))

    def step(self):
        sends, self.stays = [], []
        for values, order, left in self.halves:
            at = left.index(order[0])
            sends.append(add_up([lax.index_in_dim(v, 1, at, keepdims=False) for v in values]))
            self.stays.append([lax.index_in_dim(v, 0, at, keepdims=False) for v in values])
        bits = [order[0] for _, order, _ in self.halves]
        return [flip(sends[0], 1 << bits[0]), flip(sends[1], 1 << bits[1])]

    def landed(self, got):
        halves = []
        for i, (_, order, left) in enumerate(self.halves):
            halves.append((self.stays[i] + [got[i]], order[1:], [b for b in left if b != order[0]]))
        self.halves = halves

    def cross(self):
        while len(self.halves[0][1]) > 1:
            self.landed(self.step())
        return self.step()

    def rows(self):
        self.value = jnp.concatenate([add_up(values) for values, _, _ in self.halves], axis=1)
        self.stage = 0
        return self.value

    def along(self):
        rep = lax.axis_size("rep")
        half = rep // 2
        k = self.stage
        if k < half - 1:
            pairs = [(k, k + 1), (rep - 1 - k, rep - 2 - k)]
        elif k == half - 1:
            pairs = [(k, k + 1), (k + 1, k)]
        else:
            i = rep - 2 - k
            pairs = [(i + 1, i), (rep - 2 - i, rep - 1 - i)]
        return lax.ppermute(self.value, "rep", pairs)

    def along_landed(self, got):
        rep = lax.axis_size("rep")
        z = lax.axis_index("rep")
        k = self.stage
        self.stage += 1
        if k < rep // 2:
            self.value = add_up([self.value, got])
        else:
            i = rep - 2 - k
            self.value = jnp.where((z == i) | (z == rep - 1 - i), got, self.value)

    def finish(self):
        while self.stage < lax.axis_size("rep") - 1:
            self.along_landed(self.along())
        return self.value.astype(F32)


class RepSum:
    def __init__(self, value):
        self.value = value
        self.bits = lax.axis_size("rep").bit_length() - 1
        self.steps = 2 * self.bits
        self.done = 0

    def mine(self):
        k = self.done
        bit = k if k < self.bits else self.steps - 1 - k
        z = lax.axis_index("rep")
        return bit, lax.bitwise_and(lax.shift_right_logical(z, bit), 1)

    def send(self):
        bit, mine = self.mine()
        if self.done >= self.bits:
            return rep_flip(self.value, 1 << bit)
        size = self.value.shape[0] // 2
        sent = lax.dynamic_slice_in_dim(self.value, (1 - mine) * size, size, 0)
        self.keep = lax.dynamic_slice_in_dim(self.value, mine * size, size, 0)
        return rep_flip(sent, 1 << bit)

    def landed(self, got):
        _, mine = self.mine()
        if self.done < self.bits:
            self.value = add_up([self.keep, got])
        else:
            lower = jnp.where(mine == 0, self.value, got)
            upper = jnp.where(mine == 0, got, self.value)
            self.value = jnp.concatenate([lower, upper], axis=0)
        self.done += 1


def nt(left, right):
    return lax.dot_general(left, right, (((1,), (1,)), ((), ())), preferred_element_type=F32)


def hidden_gradient(grad_result, w_down, slope, deps=()):
    total, width = grad_result.shape
    units = w_down.shape[0]
    tile = 512

    def body(grad_ref, w_ref, slope_ref, *refs):
        out_ref, sum_ref = refs[-2:]
        value = nt(grad_ref[...], w_ref[...]) * slope_ref[...].astype(F32)
        out_ref[...] = value.astype(BF16)
        sum_ref[...] = jnp.sum(value, axis=0, keepdims=True)

    return pl.pallas_call(
        body,
        out_shape=[
            jax.ShapeDtypeStruct((total, units), BF16),
            jax.ShapeDtypeStruct((1, units), F32),
        ],
        grid=(units // tile,),
        in_specs=[
            pl.BlockSpec((total, width), lambda c: (0, 0)),
            pl.BlockSpec((tile, width), lambda c: (c, 0)),
            pl.BlockSpec((total, tile), lambda c: (0, c)),
        ]
        + [ANY] * len(deps),
        out_specs=[
            pl.BlockSpec((total, tile), lambda c: (0, c)),
            pl.BlockSpec((1, tile), lambda c: (0, c)),
        ],
        compiler_params=pltpu.CompilerParams(vmem_limit_bytes=24 * 2**20),
        cost_estimate=pl.CostEstimate(flops=int(3 * 1.15e9), bytes_accessed=1024, transcendentals=0),
        name="hidden_gradient",
    )(grad_result, w_down, slope, *deps)


def mixed_gradient(hidden_low, w_up, w_out, mixed, grad_result, gain, deps=()):
    total, units = hidden_low.shape
    width = w_up.shape[0]
    tile = 256

    def body(low_ref, up_ref, out_w_ref, mixed_ref, result_ref, gain_ref, *outs):
        grad_ref, rounded_ref, attended_ref, sums_ref = outs[-4:]
        grad = nt(low_ref[...], up_ref[...])
        unit, scale = norm_parts(mixed_ref[...])
        result = result_ref[...].astype(F32)
        value = result + norm_back(grad, gain_ref[...], unit, scale)
        rounded = value.astype(BF16)
        grad_ref[...] = value
        rounded_ref[...] = rounded
        attended_ref[...] = nt(rounded, out_w_ref[...]).astype(BF16)

        @pl.when(pl.program_id(0) == 0)
        def _():
            sums_ref[...] = jnp.zeros_like(sums_ref)

        for i, terms in enumerate((value, grad * unit, grad, result)):
            sums_ref[pl.ds(i, 1), :] += jnp.sum(terms, axis=0, keepdims=True)

    rows = pl.BlockSpec((tile, width), lambda r: (r, 0))
    whole = [
        pl.BlockSpec((width, units), lambda r: (0, 0)),
        pl.BlockSpec((width, width), lambda r: (0, 0)),
    ]
    return pl.pallas_call(
        body,
        out_shape=[
            jax.ShapeDtypeStruct((total, width), F32),
            jax.ShapeDtypeStruct((total, width), BF16),
            jax.ShapeDtypeStruct((total, width), BF16),
            jax.ShapeDtypeStruct((8, width), F32),
        ],
        grid=(total // tile,),
        in_specs=[pl.BlockSpec((tile, units), lambda r: (r, 0))]
        + whole
        + [rows, rows, pl.BlockSpec((1, width), lambda r: (0, 0))]
        + [ANY] * len(deps),
        out_specs=[rows, rows, rows, pl.BlockSpec((8, width), lambda r: (0, 0))],
        compiler_params=pltpu.CompilerParams(vmem_limit_bytes=44 * 2**20),
        cost_estimate=pl.CostEstimate(flops=int(2 * 1.15e9), bytes_accessed=1024, transcendentals=0),
        name="mixed_gradient",
    )(hidden_low, w_up, w_out, mixed, grad_result, gain.reshape(1, width), *deps)


def normed_gradient(grad_triple, w_qkv, deps=()):
    three, total, width = grad_triple.shape
    tile = 256

    def body(grad_ref, w_ref, *refs):
        out_ref = refs[-1]
        value = nt(grad_ref[0], w_ref[:, pl.ds(0, width)])
        for i in range(1, three):
            value += nt(grad_ref[i], w_ref[:, pl.ds(i * width, width)])
        out_ref[...] = value.astype(BF16)

    return pl.pallas_call(
        body,
        out_shape=jax.ShapeDtypeStruct((total, width), BF16),
        grid=(total // tile,),
        in_specs=[
            pl.BlockSpec((three, tile, width), lambda r: (0, r, 0)),
            pl.BlockSpec((width, three * width), lambda r: (0, 0)),
        ]
        + [ANY] * len(deps),
        out_specs=pl.BlockSpec((tile, width), lambda r: (r, 0)),
        compiler_params=pltpu.CompilerParams(vmem_limit_bytes=24 * 2**20),
        cost_estimate=pl.CostEstimate(flops=int(2 * 1.15e9), bytes_accessed=1024, transcendentals=0),
        name="normed_gradient",
    )(grad_triple, w_qkv, *deps)


def matmul(left, right):
    return jnp.dot(left, right, preferred_element_type=F32)


def matmul_nt(left, right):
    return lax.dot_general(left, right, (((1,), (1,)), ((), ())), preferred_element_type=F32)


def matmul_tn(left, right):
    return lax.dot_general(left, right, (((0,), (0,)), ((), ())), preferred_element_type=F32)


def norm_parts(values):
    average = jnp.mean(values, axis=-1, keepdims=True)
    centred = values - average
    spread = jnp.mean(centred * centred, axis=-1, keepdims=True)
    scale = lax.rsqrt(spread + EPS)
    return centred * scale, scale


def norm_back(grad, gain, unit, scale):
    e = grad * gain
    return scale * (
        e
        - jnp.mean(e, axis=-1, keepdims=True)
        - unit * jnp.mean(e * unit, axis=-1, keepdims=True)
    )


def shards(
    inputs,
    skips,
    cotangent,
    dest_slot,
    pack_segments,
    block_live,
    counts,
    w_skip,
    b_skip,
    g_one,
    b_one,
    w_qkv,
    w_out,
    b_out,
    g_two,
    b_two,
    w_up,
    c_up,
    w_down,
    c_down,
):
    dp = lax.axis_size("dp")
    rep = lax.axis_size("rep")
    d = lax.axis_index("dp")
    z = lax.axis_index("rep")
    micro = inputs.shape[0]
    frames = inputs.shape[2]
    width = inputs.shape[3]
    blocks = dest_slot.shape[2]
    block = frames // blocks
    per_pair = blocks // dp
    total = micro * frames
    bits = dp.bit_length() - 1
    place = jnp.stack([z, lax.rem(d, 8)]).astype(jnp.int32)
    dims = list(range(1, bits))
    small = jnp.concatenate([dest_slot.reshape(-1), block_live.reshape(-1), counts.reshape(-1)])

    own_skip = own_chunk(place, width, [w_skip])
    own_skip, small = together(own_skip, small)
    z_skip = Fetch(own_skip)
    z_skip.rest()
    got = z_skip.send()
    every = small[None]
    for bit in range(bits):
        every = jnp.concatenate([every, flip(every, 1 << bit)], axis=0)
    z_mid = Fetch(own_chunk(place, width, [w_qkv, w_out], z_skip.held[1:]))
    z_mid.rest()
    z_skip.landed(got)

    run_skip = Spread(z_skip.far(), width, [every, z_mid.held[-1]])
    mid = z_mid.send()
    run_skip.near_landed(run_skip.near())

    span = micro * blocks
    numbers = every[:, : 2 * span].reshape(dp, 2 * micro, blocks)
    numbers = jnp.transpose(numbers, (1, 0, 2)).reshape(2 * micro, dp * blocks).astype(F32)
    count_total = jnp.sum(every[:, 2 * span]).astype(F32).reshape(1, 1)
    inner = jnp.arange(frames) % block
    live = inner[None] < jnp.repeat(block_live[:, 0, :], block, axis=1)
    codes = (2 * pack_segments[:, 0, :] + live).astype(F32)
    joined = jnp.concatenate([inputs.reshape(total, width), skips.reshape(total, width)], axis=1)
    far, far_turned, keep_wide, shuffle = plan_order(
        numbers[:micro], numbers[micro:], codes, d, block, [run_skip.pairs[0], joined]
    )
    keep_rows = keep_wide[:, :1]

    run_skip.cross_landed(run_skip.cross(), [shuffle, mid])

    z_mid.landed(mid)
    run_mid = Spread(z_mid.far(), width)
    full_skip, _ = assemble(
        w_skip, run_skip.parts(run_skip.share()), place, 0, 1, [run_mid.start[0]]
    )
    z_up = Fetch(own_chunk(place, width, [w_up], [run_mid.start[0]]))
    z_up.rest()
    base = matmul(joined, full_skip) + b_skip
    unit_one, scale_one = norm_parts(base)
    own_normed = (unit_one * g_one + b_one).astype(BF16)
    sent = matmul(shuffle, own_normed).astype(BF16)
    run_mid.near_landed(run_mid.near(), [sent, z_up.held[-1]])

    def exchange(values):
        values = values.reshape(dp, total // dp, width)
        got = lax.all_to_all(values, "dp", split_axis=0, concat_axis=0, tiled=True)
        return got.reshape(total, width)

    normed = exchange(sent)
    up = z_up.send([sent])
    z_down = Fetch(own_chunk(place, width, [w_down], [z_up.held[-1], sent]))
    z_down.rest()
    run_mid.cross_landed(run_mid.cross(), [up, z_down.held[-1], normed])
    z_up.landed(up)

    other = run_mid.share()
    run_up = Spread(z_up.far(), width, [run_mid.every])
    run_up.near_landed(run_up.near(), [other])
    shard_rows = w_qkv.shape[0] // 8
    parts_mid = run_mid.parts(other)
    full_qkv, _ = assemble(w_qkv, parts_mid, place, 0, 3)

    triple = matmul(normed, full_qkv).astype(BF16)
    triple = triple.reshape(dp, micro, per_pair * block, 3 * width)
    slopes = 2.0 ** (-8.0 * (jnp.arange(HEADS, dtype=F32) + 1.0) / HEADS)
    attended = attend(triple, far, slopes, [run_up.pairs[0]])
    down = z_down.send()
    run_up.cross_landed(run_up.cross(), [attended, down])
    z_down.landed(down)

    attended = exchange(attended)
    other = run_up.share()
    run_down = Spread(z_down.far(), width, [run_up.every])
    down = run_down.near()
    full_out, out_token = assemble(w_out, parts_mid, place, 3 * shard_rows, 1, [run_up.every])
    full_up, up_token = assemble(w_up, run_up.parts(other), place, 0, w_up.shape[1] // width)
    attended, out_token, up_token = together(attended, out_token, up_token)

    attended = matmul_tn(shuffle, attended).astype(BF16)
    mixed = base + matmul(attended, full_out) + (b_out + out_token[0, 0])
    unit_two, scale_two = norm_parts(mixed)
    normed_two = (unit_two * g_two + b_two).astype(BF16)
    count_total = count_total + up_token[:1, :1]
    for step in rep_steps(rep):
        count_total = count_total + rep_flip(count_total, step)
    share = counts[0, 0].astype(F32) * (dp * rep) / count_total[0, 0]
    run_down.near_landed(down, [up_token])
    down = run_down.cross()
    hidden = matmul(normed_two, full_up) + (c_up + run_down.token[0, 0])
    phi = 0.5 * (1.0 + lax.erf(hidden * (0.5**0.5)))
    active = (hidden * phi).astype(BF16)
    slope = (phi + hidden * jnp.exp(-0.5 * hidden * hidden) * ((2 * jnp.pi) ** -0.5)).astype(BF16)
    scaled = (cotangent.reshape(total, width).astype(F32) * share).astype(BF16)
    grad_result = scaled * keep_rows.astype(BF16)
    red_down = Reduction([(active, grad_result)], d, dims)

    down_got = red_down.share()
    run_down.cross_landed(down, [red_down.sent])
    full_down, _ = assemble(w_down, run_down.parts(run_down.share()), place, 0, 1)

    hidden_low, sum_hidden = hidden_gradient(grad_result, full_down, slope)
    red_up = Reduction([(normed_two, hidden_low)], d, dims)
    up_got = red_up.share()
    red_down.own(down_got, [red_up.sent])
    flying = red_down.near()
    grad_mixed, mixed_low, grad_attended, sums_mixed = mixed_gradient(
        hidden_low, full_up, full_out, mixed, grad_result, g_two, [red_down.token]
    )
    red_out = Reduction([(attended, mixed_low)], d, dims)
    out_got = red_out.share()
    flying, sums_mixed = together(flying, sums_mixed)
    red_down.near_landed(flying)

    down_flying = red_down.cross()
    sent = matmul(shuffle, grad_attended).astype(BF16)
    grad_attended = exchange(sent)
    red_up.own(up_got, [sent], [(red_out, out_got)])
    flying = red_up.near()
    down_flying, token = together(down_flying, red_up.token)
    red_down.landed(down_flying)
    red_down.rows()

    line = red_down.along()
    grad_attended = grad_attended.reshape(dp, micro, per_pair * block, width)
    grad_triple, token = attend_back(
        triple, grad_attended, far_turned, slopes, [red_down.value, token]
    )
    grad_triple = grad_triple.reshape(3, total, width)

    sent = normed_gradient(grad_triple, full_qkv)
    grad_normed = exchange(sent)
    flying, line, token = together(flying, line, token)
    red_mid = Reduction([(normed, grad_triple)], d, dims, [sent, token])
    grad_normed, token = together(grad_normed, red_mid.token)
    red_up.near_landed(flying)
    red_down.along_landed(line)
    up_flying = red_up.cross()
    line = red_down.along()

    mid_got = red_mid.share()
    grad_normed = matmul_tn(shuffle, grad_normed)
    grad_base = grad_mixed + norm_back(grad_normed, g_one, unit_one, scale_one)
    base_low = grad_base.astype(BF16)
    red_skip = Reduction([(joined, base_low)], d, dims, [token])
    skip_got = red_skip.share()
    vectors = (
        jnp.sum(grad_base, axis=0),
        jnp.sum(grad_normed * unit_one, axis=0),
        jnp.sum(grad_normed, axis=0),
        sums_mixed[0],
        sums_mixed[1],
        sums_mixed[2],
        sum_hidden[0],
        sums_mixed[3],
    )
    lengths = [v.shape[0] for v in vectors]
    summed = jnp.concatenate(vectors).reshape(-1, 128)
    summed = summed + flip(summed, 1)
    up_flying, token, summed = together(up_flying, red_skip.token, summed)
    for bit in range(1, bits - 1):
        summed = summed + flip(summed, 1 << bit)
    red_up.landed(up_flying)
    red_up.rows()
    up_line = red_up.along()
    red_mid.own(mid_got, [token])
    summed, token = together(summed, red_mid.token)

    flying = red_mid.near()
    red_skip.own(skip_got, [token])
    skip_flying = red_skip.near()
    line, token = together(line, red_skip.token)
    red_down.along_landed(line)
    line = red_down.along()
    result = mixed + matmul(active, full_down) + (c_down + token[0, 0])
    output = (result * keep_rows).astype(BF16)
    grad_joined = (matmul_nt(base_low, full_skip) + token[0, 0]).astype(BF16)
    flying, up_line, grad_joined, summed = together(flying, up_line, grad_joined, summed)
    red_mid.near_landed(flying)
    red_up.along_landed(up_line)

    flying = red_mid.cross()
    up_line = red_up.along()
    flying, line, skip_flying, summed = together(flying, line, skip_flying, summed)
    red_down.along_landed(line)
    red_skip.near_landed(skip_flying)
    red_mid.landed(flying)

    mid_sum = RepSum(red_mid.rows())
    skip_flying = red_skip.cross()
    got = mid_sum.send()
    last = flip(summed, 1 << (bits - 1))
    got, up_line, skip_flying, last = together(got, up_line, skip_flying, last)
    mid_sum.landed(got)
    red_up.along_landed(up_line)
    red_skip.landed(skip_flying)
    summed = summed + last
    up_line = red_up.along()
    skip_columns = w_skip.shape[1]
    extra = jnp.pad(summed.reshape(-1), (0, -summed.size % (16 * rep * skip_columns)))
    extra = extra.reshape(-1, skip_columns).astype(BF16)
    skip_sum = RepSum(jnp.concatenate([red_skip.rows(), extra], axis=0))
    while mid_sum.done < mid_sum.steps:
        mid_got, skip_got = mid_sum.send(), skip_sum.send()
        if mid_sum.done == 1:
            mid_got, skip_got, up_line = together(mid_got, skip_got, up_line)
        else:
            mid_got, skip_got = together(mid_got, skip_got)
        mid_sum.landed(mid_got)
        skip_sum.landed(skip_got)
    skip_sum.landed(skip_sum.send())
    red_up.along_landed(up_line)
    final_mid = mid_sum.value.astype(F32)
    final_skip = skip_sum.value.astype(F32)
    own_rows = w_skip.shape[0] * rep // dp
    summed = final_skip[own_rows:].reshape(-1)
    final_up = red_up.finish()
    units = c_up.shape[0]
    finals = [
        red_down.finish(),
        final_up[:, :units],
        final_up[:, units:],
        final_mid,
        final_skip[:own_rows],
    ]
    sums = []
    offset = 0
    for length in lengths:
        sums.append(summed[offset : offset + length])
        offset += length

    def as_owned(values):
        return values.reshape(inputs.shape)

    return (
        as_owned(output),
        as_owned(grad_joined[:, :width]),
        as_owned(grad_joined[:, width:]),
        finals[4],
        sums[0],
        sums[1],
        sums[2],
        finals[3],
        finals[2],
        sums[3],
        sums[4],
        sums[5],
        finals[1],
        sums[6],
        finals[0],
        sums[7],
    )


def solution(mesh):
    frames = P(None, "rep", "dp", None)
    slots = P(None, "rep", "dp")
    rows = P("rep", None)
    whole = P()
    in_specs = (
        (frames,) * 3
        + (slots,) * 3
        + (P("dp", "rep"), rows, whole, whole, whole, rows, rows)
        + (whole,) * 3
        + (rows, whole, rows, whole)
    )
    split = P("dp", None)
    out_specs = (
        (frames,) * 3
        + (split,)
        + (whole,) * 3
        + (split, split)
        + (whole,) * 3
        + (split, whole, split, whole)
    )
    return jax.shard_map(shards, mesh=mesh, in_specs=in_specs, out_specs=out_specs, check_vma=False)
```
